32 devices in a mesh: img: 16 (over z, x, core), row: 2 (over y).
Axes of the slice: x: 2, y: 2, z: 4, core: 2. Of those that a mesh axis runs over, the one named last changes fastest.
Arguments:
- tokens: bfloat16 [16, 24, 24, 768], P('img', 'row'), may hold values from -6 to 6
- cotangent: bfloat16 [16, 24, 24, 768], P('img', 'row'), may hold values from -4 to 4
- valid: int32 [16], P('img'), may hold values 0 or 1
- params: float32 [7102464], P(('img', 'row')), may hold values from -3 to 3, as said below
- first_moment: float32 [7102464], P(('img', 'row')), as said below
- second_moment: float32 [7102464], P(('img', 'row')), as said below
Outputs:
- block_output: bfloat16 [16, 24, 24, 768], P('img', 'row')
- input_grad: float32 [16, 24, 24, 768], P('img', 'row')
- new_params: float32 [7102464], P(('img', 'row'))
- new_params_low: bfloat16 [7102464], P(('img', 'row'))
- new_first: float32 [7102464], P(('img', 'row'))
- new_second: float32 [7102464], P(('img', 'row'))
The draws below stay inside these ranges and needn't reach their ends.
Inputs may be any that keep to these rules, and one draw needn't show every extreme that they name: `params`: entries past 7100568 are zero; the gains lie between 0.5 and 1.5. `first_moment`: both signs occur. `second_moment`: every entry is positive.
All inputs are finite; a program needn't handle non-finite values. No bound on the sum of `valid` on one device may be relied on, other than what follows from the above.
Results may differ from the reference program's by a relative error of at most 0.012.
Values may be sent and summed in bfloat16 or wider, within the bound.
No kernel may reach another device: no remote copies, remote signals or barrier semaphores. Data moves between devices by JAX's collectives and lax.ppermute only.
A program may use at most 192 MiB of HBM per device.

```python
import jax
import jax.numpy as jnp
from jax import lax

D = 768
FF = 3072
HEADS = 24
HEAD_DIM = 32
WIN = 12
SHIFT = 6
SIDE = 24
STEP = 4
TABLE_ROWS = 529
IMAGES = 16
TOKENS = 9216
PARAMS = 7102464


def scale_table(position):
    entries = [(3 * D * D, D ** (-0.5), 0.0), (D * D, 4.0 * D ** (-0.5), 0.0), (D * FF, D ** (-0.5), 0.0), (FF * D, FF ** (-0.5), 0.0), (TABLE_ROWS * HEADS, 1.0, 0.0), (3 * D, 0.3, 0.0), (D, 0.3, 0.0), (FF, 0.3, 0.0), (D, 0.3, 0.0), (D, 0.15, 1.0), (D, 0.3, 0.0), (D, 0.15, 1.0), (D, 0.3, 0.0)]
    spread = jnp.zeros(position.shape, jnp.float32)
    centre = jnp.zeros(position.shape, jnp.float32)
    offset = 0
    for span_len, deviation, level in entries:
        inside = (position >= offset) & (position < offset + span_len)
        spread = jnp.where(inside, jnp.float32(deviation), spread)
        centre = jnp.where(inside, jnp.float32(level), centre)
        offset = offset + span_len
    return (spread, centre)


def draw_params(key, part):
    key = jax.random.fold_in(key, 11)
    position = jnp.arange(PARAMS, dtype=jnp.int32)
    spread, centre = scale_table(position)
    noise = jnp.clip(jax.random.normal(key, (PARAMS,), jnp.float32), -3.0, 3.0)
    return centre + spread * noise


def draw_first_moment(key, part):
    key = jax.random.fold_in(key, 23)
    size_scale = 0.8 * jnp.sqrt(jnp.float32(TOKENS))
    noise = jnp.clip(jax.random.normal(key, (PARAMS,), jnp.float32), -3.0, 3.0)
    return size_scale * noise


def draw_second_moment(key, part):
    key = jax.random.fold_in(key, 37)
    size_scale = 0.8 * jnp.sqrt(jnp.float32(TOKENS))
    factor = jnp.exp(jax.random.uniform(key, (PARAMS,), jnp.float32, 0.0, 1.3862944))
    return size_scale * size_scale * factor


def draw_cotangent(key, part):
    key = jax.random.fold_in(key, 41)
    noise_key = jax.random.fold_in(key, 0)
    values = jnp.clip(jax.random.normal(noise_key, (IMAGES, SIDE, SIDE, D), jnp.float32), -4.0, 4.0)
    return values.astype(jnp.bfloat16)


def touch_ends(values, rng, smallest, high):
    index_at = [jax.random.randint(jax.random.fold_in(rng, axis), (), 0, length) for axis, length in enumerate(values.shape)]
    longest = values.shape.index(max(values.shape))
    neighbour = index_at[:longest] + [(index_at[longest] + 1) % values.shape[longest]] + index_at[longest + 1:]
    return values.at[tuple(index_at)].set(smallest).at[tuple(neighbour)].set(high)


def block_levels(stream_key, dims, cuts, smallest, high):
    def one(dim, shards_of):
        heights = jax.random.uniform(jax.random.fold_in(jax.random.fold_in(stream_key, 6), dim), (shards_of,), jnp.float32, smallest / len(cuts), high / len(cuts))
        return jnp.repeat(jnp.exp(heights), dims[dim] // shards_of).reshape((-1,) + (1,) * (len(dims) - dim - 1))

    level = one(*cuts[0])
    for cut in cuts[1:]:
        level = level * one(*cut)
    return level


def normal_values(key, shape, width, limit, cuts=(), held_as=jnp.bfloat16):
    level = block_levels(key, shape, cuts, -0.22, 0.18) if cuts else 1.0
    values = jax.random.normal(key, shape, jnp.float32) * width * level
    return jnp.minimum(jnp.maximum(values, -limit), limit).astype(held_as)


def setup_inputs(seed: int = 0) -> dict:
    keys = jax.random.split(jax.random.key(seed), 7)
    tokens = normal_values(keys[0], (IMAGES, SIDE, SIDE, D), 1.0, 6.0, ((0, 16), (1, 2)))
    cotangent = draw_cotangent(jax.random.fold_in(keys[6], 71), 0)
    valid = touch_ends((jax.random.randint(keys[2], (IMAGES,), 0, 8) < 7).astype(jnp.int32), jax.random.fold_in(keys[2], 1), 0, 1)
    params = draw_params(jax.random.fold_in(keys[6], 71), 0)
    first_moment = draw_first_moment(jax.random.fold_in(keys[6], 71), 0)
    second_moment = draw_second_moment(jax.random.fold_in(keys[6], 71), 0)
    return dict(tokens=tokens, cotangent=cotangent, valid=valid, params=params, first_moment=first_moment, second_moment=second_moment)


@jax.custom_vjp
def low(v):
    return lax.optimization_barrier(v.astype(jnp.bfloat16)).astype(jnp.float32)

@jax.custom_vjp
def low_back(v):
    return v

def low_keep(v):
    return (low(v), None)

def low_pass(kept, grad):
    return (grad,)

def back_keep(v):
    return (v, None)

def back_low(kept, grad):
    return (low(grad),)
low.defvjp(low_keep, low_pass)
low_back.defvjp(back_keep, back_low)
EPSILON = 1e-05
MASKED = -100.0
DECAY = 0.05
ADAM_EPS = 1e-08
BETA_ONE = 0.5
BETA_TWO = 0.5
HIGH = lax.Precision.HIGHEST

def piece_shapes():
    return [(D, 3 * D), (D, D), (D, FF), (FF, D), (TABLE_ROWS, HEADS), (3 * D,), (D,), (FF,), (D,), (D,), (D,), (D,), (D,)]

def unpack(flat_vec):
    pieces = []
    offset = 0
    for shape_one in piece_shapes():
        amount = 1
        for extent in shape_one:
            amount = amount * extent
        pieces.append(lax.slice_in_dim(flat_vec, offset, offset + amount).reshape(shape_one))
        offset = offset + amount
    return pieces

def step_rates(position):
    rate_list = [D ** (-0.5), 4.0 * D ** (-0.5), D ** (-0.5), FF ** (-0.5), 1.0, 0.3, 0.3, 0.3, 0.3, 0.4, 0.3, 0.4, 0.3]
    result = jnp.zeros(position.shape, jnp.float32)
    offset = 0
    for shape_one, rate_one in zip(piece_shapes(), rate_list):
        amount = 1
        for extent in shape_one:
            amount = amount * extent
        inside = (position >= offset) & (position < offset + amount)
        result = jnp.where(inside, jnp.float32(rate_one), result)
        offset = offset + amount
    return result

def layer_norm(values, gain_vec, shift_vec):
    centre = lax.optimization_barrier(jnp.mean(values, -1, keepdims=True))
    centred = values - centre
    spread = lax.optimization_barrier(jnp.mean(centred * centred, -1, keepdims=True))
    return centred * lax.rsqrt(spread + EPSILON) * gain_vec + shift_vec

def region_of(coord):
    return jnp.where(coord < SIDE - WIN, 0, jnp.where(coord < SIDE - SHIFT, 1, 2))

def relative_index():
    cell_index = jnp.arange(WIN * WIN, dtype=jnp.int32)
    row_part = cell_index // WIN
    col_part = cell_index % WIN
    return ((row_part[:, None] - row_part[None, :] + WIN - 1) * (2 * WIN - 1) + (col_part[:, None] - col_part[None, :] + WIN - 1)).astype(jnp.int32)

def window_mask(row_first):
    row_coord = row_first + jnp.arange(WIN, dtype=jnp.int32)
    col_coord = jnp.arange(SIDE, dtype=jnp.int32)
    region_ids = 3 * region_of(row_coord)[:, None] + region_of(col_coord)[None, :]
    region_ids = region_ids.reshape(WIN, SIDE // WIN, WIN).transpose(1, 0, 2).reshape(SIDE // WIN, WIN * WIN)
    same = region_ids[:, :, None] == region_ids[:, None, :]
    return jnp.where(same, 0.0, MASKED).astype(jnp.float32)

def window_block(pieces, full_mask, portion):
    w_qkv, w_proj, w_up, w_down, bias_table, b_qkv, b_proj, b_up, b_down, gain_one, shift_one, gain_two, shift_two = pieces
    img_count = portion.shape[0]
    normed = low_back(low(layer_norm(portion, gain_one, shift_one)))
    rolled = jnp.roll(normed, (-SHIFT, -SHIFT), (1, 2))
    windows = rolled.reshape(img_count, SIDE // WIN, WIN, SIDE // WIN, WIN, D).transpose(0, 1, 3, 2, 4, 5)
    windows = windows.reshape(-1, WIN * WIN, D)
    packed = jnp.einsum('wtc,cf->wtf', windows, w_qkv, precision=HIGH) + b_qkv
    packed = low_back(low(packed))
    heads_view = packed.reshape(windows.shape[0], WIN * WIN, 3, HEADS, HEAD_DIM)
    queries = heads_view[:, :, 0]
    keys_all = heads_view[:, :, 1]
    values_all = heads_view[:, :, 2]
    raw_scores = low_back(jnp.einsum('wqhd,wkhd->whqk', queries, keys_all, precision=HIGH))
    bias_full = bias_table[relative_index()].transpose(2, 0, 1)
    region_mask = jnp.tile(full_mask, (img_count, 1, 1))
    scores = raw_scores * HEAD_DIM ** (-0.5) + bias_full[None] + region_mask[:, None]
    row_top = lax.optimization_barrier(jnp.max(scores, -1, keepdims=True))
    exponent = jnp.exp(scores - row_top)
    attn_probs = low(exponent / lax.optimization_barrier(jnp.sum(exponent, -1, keepdims=True)))
    attn_mixed = jnp.einsum('whqk,wkhd->wqhd', attn_probs, values_all, precision=HIGH)
    attn_mixed = low_back(low(attn_mixed)).reshape(-1, WIN * WIN, D)
    branch = jnp.einsum('wtc,cf->wtf', attn_mixed, w_proj, precision=HIGH) + b_proj
    branch = low_back(low(branch))
    branch_grid = branch.reshape(img_count, SIDE // WIN, SIDE // WIN, WIN, WIN, D).transpose(0, 1, 3, 2, 4, 5)
    branch_grid = branch_grid.reshape(img_count, SIDE, SIDE, D)
    middle = portion + jnp.roll(branch_grid, (SHIFT, SHIFT), (1, 2))
    hidden_in = low(layer_norm(middle, gain_two, shift_two))
    upward = low_back(jnp.einsum('abcd,df->abcf', hidden_in, w_up, precision=HIGH) + b_up)
    active = low(jax.nn.gelu(upward, approximate=False))
    return middle + jnp.einsum('abcf,fd->abcd', active, w_down, precision=HIGH) + b_down

def reference(tokens, cotangent, valid, params, first_moment, second_moment):
    flat_low = params.astype(jnp.bfloat16).astype(jnp.float32)
    images = tokens.astype(jnp.float32)
    grad_out = cotangent.astype(jnp.float32) * valid.astype(jnp.float32)[:, None, None, None]
    group_size = 4 if IMAGES % 4 == 0 else 1
    full_mask = jnp.concatenate([window_mask(0), window_mask(WIN)], 0)

    def forward(flat_vec, every_image):
        pieces = unpack(flat_vec)
        step_fn = jax.checkpoint(lambda portion: window_block(pieces, full_mask, portion))
        grouped = every_image.reshape(IMAGES // group_size, group_size, SIDE, SIDE, D)
        return lax.map(step_fn, grouped).reshape(every_image.shape)
    output, pull_back = jax.vjp(forward, flat_low, images)
    grad_flat, input_grad = pull_back(grad_out)
    position = jnp.arange(PARAMS, dtype=jnp.int32)
    step_rate = step_rates(position)
    new_first = BETA_ONE * first_moment + (1.0 - BETA_ONE) * grad_flat
    new_second = BETA_TWO * second_moment + (1.0 - BETA_TWO) * grad_flat * grad_flat
    fixed_first = new_first / (1.0 - BETA_ONE ** STEP)
    fixed_second = new_second / (1.0 - BETA_TWO ** STEP)
    new_params = params - step_rate * (fixed_first / (jnp.sqrt(fixed_second) + ADAM_EPS) + DECAY * params)
    return (output.astype(jnp.bfloat16), input_grad, new_params, new_params.astype(jnp.bfloat16), new_first, new_second)
```

```python
import math

import jax
import jax.numpy as jnp
from jax import lax
from jax.experimental import pallas as pl
from jax.experimental.pallas import tpu as pltpu
from jax.sharding import PartitionSpec as P

D = 768
FF = 3072
HEADS = 24
HEAD_DIM = 32
WIN = 12
SHIFT = 6
SIDE = 24
STEP = 4
TABLE_ROWS = 529


EPSILON = 1e-05
MASKED = -100.0
DECAY = 0.05
ADAM_EPS = 1e-08
BETA_ONE = 0.5
BETA_TWO = 0.5


def from_partner(block, axis, apart):
    count = lax.axis_size(axis)
    route = []
    for low in range(count):
        high = low | 1 << apart
        if high != low and high < count:
            route += [(low, high), (high, low)]
    return lax.ppermute(block, axis, route)


def piece_shapes():
    return [
        (D, 3 * D),
        (D, D),
        (D, FF),
        (FF, D),
        (TABLE_ROWS, HEADS),
        (3 * D,),
        (D,),
        (FF,),
        (D,),
        (D,),
        (D,),
        (D,),
        (D,),
    ]


def unpack(flat_vec):
    pieces = []
    offset = 0
    for shape_one in piece_shapes():
        amount = math.prod(shape_one)
        pieces.append(lax.slice_in_dim(flat_vec, offset, offset + amount).reshape(shape_one))
        offset = offset + amount
    return pieces


def step_rates(position):
    rate_list = [
        D ** (-0.5),
        4.0 * D ** (-0.5),
        D ** (-0.5),
        FF ** (-0.5),
        1.0,
        0.3,
        0.3,
        0.3,
        0.3,
        0.4,
        0.3,
        0.4,
        0.3,
    ]
    result = jnp.zeros(position.shape, jnp.float32)
    offset = 0
    for shape_one, rate_one in zip(piece_shapes(), rate_list):
        amount = math.prod(shape_one)
        inside = (position >= offset) & (position < offset + amount)
        result = jnp.where(inside, jnp.float32(rate_one), result)
        offset = offset + amount
    return result


def layer_norm(values, gain_vec, shift_vec):
    centre = jnp.mean(values, -1, keepdims=True)
    centred = values - centre
    spread = jnp.mean(centred * centred, -1, keepdims=True)
    return centred * lax.rsqrt(spread + EPSILON) * gain_vec + shift_vec


def region_of(coord):
    return jnp.where(coord < SIDE - WIN, 0, jnp.where(coord < SIDE - SHIFT, 1, 2))


def relative_index():
    cell_index = jnp.arange(WIN * WIN, dtype=jnp.int32)
    row_part = cell_index // WIN
    col_part = cell_index % WIN
    return (row_part[:, None] - row_part[None, :] + WIN - 1) * (2 * WIN - 1) + (
        col_part[:, None] - col_part[None, :] + WIN - 1
    )


def window_mask(row_first):
    row_coord = row_first + jnp.arange(WIN, dtype=jnp.int32)
    col_coord = jnp.arange(SIDE, dtype=jnp.int32)
    region_ids = 3 * region_of(row_coord)[:, None] + region_of(col_coord)[None, :]
    region_ids = (
        region_ids.reshape(WIN, SIDE // WIN, WIN).transpose(1, 0, 2).reshape(SIDE // WIN, WIN * WIN)
    )
    same = region_ids[:, :, None] == region_ids[:, None, :]
    return jnp.where(same, 0.0, MASKED).astype(jnp.float32)


def to_windows(grid_rows):
    img_count = grid_rows.shape[0]
    width = grid_rows.shape[-1]
    shaped = grid_rows.reshape(img_count, WIN, SIDE // WIN, WIN, width).transpose(0, 2, 1, 3, 4)
    return shaped.reshape(img_count * (SIDE // WIN), WIN * WIN, width)


def from_windows(window_rows, img_count):
    width = window_rows.shape[-1]
    shaped = window_rows.reshape(img_count, SIDE // WIN, WIN, WIN, width).transpose(0, 2, 1, 3, 4)
    return shaped.reshape(img_count, WIN, SIDE, width)


BF16 = jnp.bfloat16
F32 = jnp.float32
BOTH = ("img", "row")
ROWS = 9248
TILE = 16
WINDOW = 304
WIDE = 2 * D // 4
VMEM_MOST = 60 * 1024 * 1024


def contract_rows(left_op, right_op):
    summed_dims = tuple(range(left_op.ndim - 1))
    return lax.dot_general(
        left_op,
        right_op,
        ((summed_dims, summed_dims), ((), ())),
        preferred_element_type=jnp.float32,
    )


def times_transposed(left_op, right_op):
    return lax.dot_general(
        left_op,
        right_op,
        (((left_op.ndim - 1,), (1,)), ((), ())),
        preferred_element_type=jnp.float32,
    )


def swap(block, mask, only=None):
    count = lax.axis_size(BOTH)
    route = [(d, d ^ mask) for d in range(count) if only is None or only(d)]
    return lax.ppermute(block, BOTH, route)


def params_call(**more):
    return pltpu.CompilerParams(vmem_limit_bytes=VMEM_MOST, **more)


def vmem(count):
    return [pl.BlockSpec(memory_space=pltpu.VMEM)] * count


SMEM_SPEC = pl.BlockSpec(memory_space=pltpu.SMEM)
ANY_SPEC = pl.BlockSpec(memory_space=pl.ANY)


def first_tile(device):
    return (289 * device) // TILE


def prep_body(me_ref, own_ref, out_ref, wide_ref):
    shift = me_ref[0] % TILE
    wide_ref[0:96] = jnp.zeros((96, 128), F32)
    wide_ref[1824:1920] = jnp.zeros((96, 128), F32)
    wide_ref[96:1830] = own_ref[...]
    for j in range(6):
        picked = wide_ref[pl.ds(96 - 6 * shift + j, WINDOW, stride=6), :]
        out_ref[:, 128 * j : 128 * (j + 1)] = picked.astype(BF16)


def window_of(me, own_flat):
    return pl.pallas_call(
        prep_body,
        out_shape=jax.ShapeDtypeStruct((WINDOW, D), BF16),
        in_specs=[SMEM_SPEC] + vmem(1),
        out_specs=vmem(1)[0],
        scratch_shapes=[pltpu.VMEM((1920, 128), F32)],
        compiler_params=params_call(),
        name="own_window",
    )(me, own_flat.reshape(-1, 128))


def mixer(groups, per):
    size = groups * per
    row = lax.broadcasted_iota(jnp.int32, (size, size), 0)
    col = lax.broadcasted_iota(jnp.int32, (size, size), 1)
    return (col == groups * (row % per) + row // per).astype(F32).astype(BF16)


def unmixer(groups, per):
    size = groups * per
    row = lax.broadcasted_iota(jnp.int32, (size, size), 0)
    col = lax.broadcasted_iota(jnp.int32, (size, size), 1)
    return (row == groups * (col % per) + col // per).astype(F32).astype(BF16)


def assemble_body(me_ref, *refs):
    parts = refs[:32]
    qkv_ref, proj_ref, up_ref, down_ref, tail_ref = refs[32:37]
    flat_ref, edge_ref, main_sem, edge_sem = refs[37:]
    me = me_ref[0]
    copies = []
    for m in range(32):
        start = pl.multiple_of(first_tile(me ^ m) * TILE, TILE)
        main = pltpu.make_async_copy(
            parts[m].at[pl.ds(TILE, WINDOW - TILE)],
            flat_ref.at[pl.ds(start + TILE, WINDOW - TILE)],
            main_sem.at[m],
        )
        edge = pltpu.make_async_copy(parts[m].at[pl.ds(0, TILE)], edge_ref.at[m], edge_sem.at[m])
        main.start()
        edge.start()
        copies += [main, edge]
    flat_ref[0:TILE] = jnp.zeros((TILE, D), BF16)
    middle = first_tile(16) * TILE
    flat_ref[middle : middle + TILE] = jnp.zeros((TILE, D), BF16)
    for copy in copies:
        copy.wait()
    for m in range(32):
        start = pl.multiple_of(first_tile(me ^ m) * TILE, TILE)
        flat_ref[pl.ds(start, TILE)] += edge_ref[m]
    mix = mixer(3, 64)

    def qkv_step(t, carry):
        rows = flat_ref[pl.ds(pl.multiple_of(192 * t, 64), 192)]
        out = jnp.dot(mix, rows, preferred_element_type=F32).astype(BF16)
        for j in range(3):
            qkv_ref[j, pl.ds(pl.multiple_of(64 * t, 64), 64)] = out[64 * j : 64 * (j + 1)]
        return carry

    lax.fori_loop(0, 12, qkv_step, 0)
    proj_ref[...] = flat_ref[2304:3072]
    mix_up = mixer(4, 48)

    def up_step(t, carry):
        rows = flat_ref[pl.ds(pl.multiple_of(3072 + 192 * t, 64), 192)]
        out = jnp.dot(mix_up, rows, preferred_element_type=F32).astype(BF16)
        for j in range(4):
            up_ref[j, pl.ds(pl.multiple_of(48 * t, 16), 48)] = out[48 * j : 48 * (j + 1)]
        return carry

    lax.fori_loop(0, 16, up_step, 0)

    def down_step(t, carry):
        at = pl.multiple_of(256 * t, 256)
        down_ref[pl.ds(at, 256)] = flat_ref[pl.ds(pl.multiple_of(6144 + 256 * t, 256), 256)]
        return carry

    lax.fori_loop(0, 12, down_step, 0)
    tail_ref[...] = flat_ref[9216:9248]


def gather_windows(me, own):
    parts = [None] * 32
    parts[0] = own
    for z in (8, 16, 24):
        parts[z] = swap(own, z)
    for z in (0, 8, 16, 24):
        parts[z | 4] = swap(parts[z], 4)
        parts[z | 1] = swap(parts[z], 1)
        left = swap(parts[z | 4][:, :384], 1)
        right = swap(parts[z | 1][:, 384:], 4)
        parts[z | 5] = jnp.concatenate([left, right], 1)
        for xy in (0, 4, 1, 5):
            parts[z | xy | 2] = swap(parts[z | xy], 2)
    return pl.pallas_call(
        assemble_body,
        out_shape=[
            jax.ShapeDtypeStruct((3, D, D), BF16),
            jax.ShapeDtypeStruct((D, D), BF16),
            jax.ShapeDtypeStruct((4, D, D), BF16),
            jax.ShapeDtypeStruct((FF, D), BF16),
            jax.ShapeDtypeStruct((32, D), BF16),
        ],
        in_specs=[SMEM_SPEC] + [ANY_SPEC] * 32,
        out_specs=vmem(5),
        scratch_shapes=[
            pltpu.VMEM((ROWS, D), BF16),
            pltpu.VMEM((32, TILE, D), BF16),
            pltpu.SemaphoreType.DMA((32,)),
            pltpu.SemaphoreType.DMA((32,)),
        ],
        compiler_params=params_call(),
        name="assemble",
    )(me, *parts)


def plane_rows(plane):
    low = (289 * 8 * plane) // TILE * TILE
    high = (289 * (8 * plane + 7)) // TILE * TILE + WINDOW
    return low, high


def spread_body(plane, kinds, me_ref, *refs):
    given = refs[: len(kinds)]
    keep_ref, send_ref, flat_ref = refs[len(kinds) :]
    low, high = plane_rows(plane)
    span = high - low
    me = me_ref[0]
    for kind, ref in zip(kinds, given):
        if kind == "qkv":
            mix = unmixer(3, 64)
            for t in range(12):
                rows = jnp.concatenate([ref[j, 64 * t : 64 * (t + 1)] for j in range(3)], 0)
                flat_ref[192 * t : 192 * (t + 1)] = jnp.dot(
                    mix, rows, preferred_element_type=F32
                ).astype(BF16)
        elif kind == "up":
            mix = unmixer(4, 48)
            for t in range(16):
                at = 3072 + 192 * t
                if at + 192 <= low or at >= high:
                    continue
                rows = jnp.concatenate([ref[j, 48 * t : 48 * (t + 1)] for j in range(4)], 0)
                out = jnp.dot(mix, rows, preferred_element_type=F32).astype(BF16)
                a, b = max(at, low), min(at + 192, high)
                flat_ref[a - low : b - low] = out[a - at : b - at]
        else:
            base, count = (2304, D) if kind == "proj" else (6144, FF)
            a, b = max(base, low), min(base + count, high)
            flat_ref[a - low : b - low] = ref[a - base : b - base]
    if high > 9216:
        flat_ref[9216 - low : high - low] = jnp.zeros((high - 9216, D), BF16)
    for ref, flip in ((keep_ref, 0), (send_ref, 2)):
        for s, bits in enumerate((0, 1, 4, 5)):
            device = 8 * plane + ((me & 7) ^ (bits | flip))
            start = pl.multiple_of(first_tile(device) * TILE - low, TILE)
            ref[s] = flat_ref[pl.ds(start, WINDOW)]


def spread(me, plane, **given):
    low, high = plane_rows(plane)
    shape = jax.ShapeDtypeStruct((4, WINDOW, D), BF16)
    body = lambda *refs: spread_body(plane, tuple(given), *refs)
    return pl.pallas_call(
        body,
        out_shape=[shape, shape],
        in_specs=[SMEM_SPEC] + vmem(len(given)),
        out_specs=vmem(2),
        scratch_shapes=[pltpu.VMEM((high - low, D), BF16)],
        compiler_params=params_call(),
        name="spread_" + "_".join(given),
    )(me, *given.values())


def added(one, two):
    return (one.astype(F32) + two.astype(F32)).astype(BF16)


def reduce_plane(plane, keep, send):
    total = added(keep, swap(send, 2)).reshape(2, 2, WINDOW, D)
    left, right = total[..., :384], total[..., 384:]
    from_x = swap(left[1], 4)
    from_y = swap(right[:, 1], 1)
    left = added(left[0], from_x)
    right = added(right[:, 0], from_y)
    left = added(left[0], swap(left[1], 1))
    right = added(right[0], swap(right[1], 4))
    mine = jnp.concatenate([left, right], 1)
    terms = [mine]
    for z in (1, 2, 3):
        terms.append(swap(mine, 8 * z, lambda d: d // 8 == plane ^ z))
    return terms


def adam_body(me_ref, *refs):
    terms = refs[:16]
    tail_ref, params_ref, first_ref, second_ref = refs[16:20]
    out_params, out_low, out_first, out_second, flat_ref, grad_ref, copy_ref, sems = refs[20:]
    me = me_ref[0]
    shift = me % TILE
    for plane in range(4):

        @pl.when(me // 8 == plane)
        def _():
            copies = [
                pltpu.make_async_copy(terms[4 * plane + z], copy_ref.at[z], sems.at[z])
                for z in range(4)
            ]
            for copy in copies:
                copy.start()
            for copy in copies:
                copy.wait()

    for j in range(6):
        terms_j = [copy_ref[z, :, 128 * j : 128 * (j + 1)].astype(F32) for z in range(4)]
        flat_ref[pl.ds(j, WINDOW, stride=6), :] = (terms_j[0] + terms_j[1]) + (
            terms_j[2] + terms_j[3]
        )
    grad_ref[...] = flat_ref[pl.ds(6 * shift, 1734), :]

    @pl.when(me == 31)
    def _():
        grad_ref[1542:1734, :] += tail_ref[...]

    grad = grad_ref[...]
    position = (
        me * 221952
        + lax.broadcasted_iota(jnp.int32, grad.shape, 0) * 128
        + lax.broadcasted_iota(jnp.int32, grad.shape, 1)
    )
    params = params_ref[...]
    new = adam_step(params, first_ref[...], second_ref[...], grad, position)
    out_params[...] = new[0]
    out_low[...] = new[0].astype(BF16)
    out_first[...] = new[1]
    out_second[...] = new[2]


def adam_step(params, first_moment, second_moment, grad, position):
    step_rate = step_rates(position)
    new_first = BETA_ONE * first_moment + (1.0 - BETA_ONE) * grad
    new_second = BETA_TWO * second_moment + (1.0 - BETA_TWO) * grad * grad
    fixed_first = new_first / (1.0 - BETA_ONE**STEP)
    fixed_second = new_second / (1.0 - BETA_TWO**STEP)
    new_params = params - step_rate * (
        fixed_first / (jnp.sqrt(fixed_second) + ADAM_EPS) + DECAY * params
    )
    return new_params, new_first, new_second


def adam(me, terms, tail, params, first_moment, second_moment):
    lines = (1734, 128)
    args = [one.reshape(lines) for one in (params, first_moment, second_moment)]
    outs = pl.pallas_call(
        adam_body,
        out_shape=[
            jax.ShapeDtypeStruct(lines, F32),
            jax.ShapeDtypeStruct(lines, BF16),
            jax.ShapeDtypeStruct(lines, F32),
            jax.ShapeDtypeStruct(lines, F32),
        ],
        in_specs=[SMEM_SPEC] + [ANY_SPEC] * 16 + vmem(4),
        out_specs=vmem(4),
        scratch_shapes=[
            pltpu.VMEM((6 * WINDOW, 128), F32),
            pltpu.VMEM(lines, F32),
            pltpu.VMEM((4, WINDOW, D), BF16),
            pltpu.SemaphoreType.DMA((4,)),
        ],
        compiler_params=params_call(),
        name="adam",
    )(me, *terms, tail, *args)
    return [one.reshape(-1) for one in outs]


def sum_tail(tail):
    tail = tail + swap(tail, 2)
    tail = (tail + swap(tail, 4)) + (swap(tail, 1) + swap(tail, 5))
    return (tail + swap(tail, 8)) + (swap(tail, 16) + swap(tail, 24))


def table_picks():
    col = jnp.arange(WIN * 384, dtype=jnp.int32)
    m = col % 384
    wanted = (22 - m // WIN) * 23 + col // 384 - m % WIN + WIN - 1
    wanted = jnp.where(m < 276, wanted, -1)
    return (jnp.arange(TABLE_ROWS, dtype=jnp.int32)[:, None] == wanted[None, :]).astype(BF16)


def bias_of(table):
    strips = lax.dot_general(
        table, table_picks(), (((0,), (0,)), ((), ())), preferred_element_type=F32
    ).reshape(HEADS, WIN, 384)
    rows = [strips[:, :, 12 * (11 - i) : 12 * (11 - i) + 144] for i in range(WIN)]
    return jnp.stack(rows, 1).reshape(HEADS, 144, 144)


def table_grad_of(pair_sums):
    shaped = pair_sums.reshape(HEADS, WIN, WIN, 144)
    strips = 0.0
    for i in range(WIN):
        low = 12 * (11 - i)
        strips = strips + jnp.pad(shaped[:, i], ((0, 0), (0, 0), (low, 240 - low)))
    picked = lax.dot_general(
        strips.reshape(HEADS, WIN * 384),
        table_picks().astype(F32),
        (((1,), (1,)), ((), ())),
        precision=lax.Precision.HIGHEST,
        preferred_element_type=F32,
    )
    return picked.T


def heads_of(block):
    return block.reshape(-1, WIN * WIN, HEADS, HEAD_DIM)


def shards(tokens, cotangent, valid, params, first_moment, second_moment):
    img_count = tokens.shape[0]
    win_count = img_count * (SIDE // WIN)
    tile_len = WIN * WIN
    quick = lax.axis_size("img") == 16 and lax.axis_size("row") == 2
    if quick:
        me = lax.axis_index(BOTH).astype(jnp.int32).reshape(1)
        w_qkv, w_proj, w_up, w_down, tail = gather_windows(me, window_of(me, params))
        tail = tail.reshape(-1)
    else:
        gathered = lax.all_gather(params.astype(BF16), BOTH, axis=0, tiled=True)
        whole = unpack(gathered)
        w_qkv = whole[0].reshape(D, 3, D).transpose(1, 0, 2)
        w_proj = whole[1]
        w_up = whole[2].reshape(D, 4, D).transpose(1, 0, 2)
        w_down = whole[3]
        tail = gathered[9216 * D :]
    small = []
    offset = 0
    for shape_one in piece_shapes()[4:]:
        amount = math.prod(shape_one)
        small.append(tail[offset : offset + amount].reshape(shape_one))
        offset += amount
    bias_table, b_qkv, b_proj, b_up, b_down, gain_one, shift_one, gain_two, shift_two = small
    tokens_in = from_partner(tokens[:, :SHIFT], "row", 0)
    shifted = jnp.roll(jnp.concatenate([tokens[:, SHIFT:], tokens_in], 1), -SHIFT, 2)
    token_windows = to_windows(shifted).reshape(-1, D).astype(F32)
    normed, norm_pull = jax.vjp(
        layer_norm, token_windows, gain_one.astype(F32), shift_one.astype(F32)
    )
    windows = normed.astype(BF16)
    packed = [
        (
            jnp.dot(windows, w_qkv[j], preferred_element_type=F32)
            + b_qkv[D * j : D * (j + 1)].astype(F32)
        ).astype(BF16)
        for j in range(3)
    ]
    queries, keys_all, values_all = [heads_of(one) for one in packed]
    bias_full = bias_of(bias_table)
    region_mask = jnp.tile(window_mask(lax.axis_index("row") * WIN), (img_count, 1, 1))
    raw_scores = jnp.einsum("wqhd,wkhd->whqk", queries, keys_all, preferred_element_type=F32)
    scores = raw_scores * HEAD_DIM ** (-0.5) + bias_full[None] + region_mask[:, None]
    row_top = jnp.max(scores, -1, keepdims=True)
    exponent = jnp.exp(scores - row_top)
    row_total = jnp.sum(exponent, -1, keepdims=True)
    probs = exponent / row_total
    attn_probs = probs.astype(BF16)
    attn_mixed = jnp.einsum(
        "whqk,wkhd->wqhd", attn_probs, values_all, preferred_element_type=F32
    )
    attn_mixed = attn_mixed.astype(BF16).reshape(-1, D)
    branch = (
        jnp.dot(attn_mixed, w_proj, preferred_element_type=F32) + b_proj.astype(F32)
    ).astype(BF16)
    branch_grid = jnp.roll(
        from_windows(branch.reshape(win_count, tile_len, D), img_count), SHIFT, 2
    )
    returned = from_partner(branch_grid[:, SHIFT:], "row", 0)
    images = tokens.astype(F32)
    middle = images + jnp.concatenate([returned, branch_grid[:, :SHIFT]], 1).astype(F32)
    middle = middle.reshape(-1, D)
    normed_two, norm_two_pull = jax.vjp(
        layer_norm, middle, gain_two.astype(F32), shift_two.astype(F32)
    )
    hidden_in = normed_two.astype(BF16)
    grad_out = (cotangent * valid.astype(BF16)[:, None, None, None]).reshape(-1, D)
    output = middle + b_down.astype(F32)
    grad_hidden = 0.0
    grads_up, grads_down, grads_bup = [], [], []
    for j in range(4):
        upward = jnp.dot(hidden_in, w_up[j], preferred_element_type=F32) + b_up[
            D * j : D * (j + 1)
        ].astype(F32)
        active_full, gelu_pull = jax.vjp(
            lambda values: jax.nn.gelu(values, approximate=False), upward
        )
        active = active_full.astype(BF16)
        down_part = w_down[D * j : D * (j + 1)]
        output = output + jnp.dot(active, down_part, preferred_element_type=F32)
        grads_down.append(contract_rows(active, grad_out).astype(BF16))
        grad_up = gelu_pull(times_transposed(grad_out, down_part))[0].astype(BF16)
        grads_up.append(contract_rows(hidden_in, grad_up).astype(BF16))
        grads_bup.append(jnp.sum(grad_up.astype(F32), 0))
        grad_hidden = grad_hidden + times_transposed(grad_up, w_up[j])
    grad_w_down = jnp.concatenate(grads_down, 0)
    grad_w_up = jnp.stack(grads_up, 0)
    if quick:
        terms = reduce_plane(3, *spread(me, 3, down=grad_w_down))
        terms = reduce_plane(2, *spread(me, 2, up=grad_w_up, down=grad_w_down)) + terms
    grad_b_down = jnp.sum(grad_out.astype(F32), 0)
    grad_middle_ln, grad_gain_two, grad_shift_two = norm_two_pull(grad_hidden)
    grad_middle = grad_out.astype(F32) + grad_middle_ln
    middle_low = grad_middle.astype(BF16).reshape(tokens.shape)
    arrived = from_partner(middle_low[:, :SHIFT], "row", 0)
    grad_grid = jnp.roll(jnp.concatenate([middle_low[:, SHIFT:], arrived], 1), -SHIFT, 2)
    grad_branch = to_windows(grad_grid).reshape(-1, D)
    grad_w_proj = contract_rows(attn_mixed, grad_branch).astype(BF16)
    if quick:
        terms = reduce_plane(1, *spread(me, 1, proj=grad_w_proj, up=grad_w_up)) + terms
    grad_b_proj = jnp.sum(grad_branch.astype(F32), 0)
    grad_attn = heads_of(times_transposed(grad_branch, w_proj).astype(BF16))
    grad_values = jnp.einsum("whqk,wqhd->wkhd", attn_probs, grad_attn, preferred_element_type=F32)
    grad_probs = jnp.einsum("wqhd,wkhd->whqk", grad_attn, values_all, preferred_element_type=F32)
    grad_scores = probs * (grad_probs - jnp.sum(probs * grad_probs, -1, keepdims=True))
    grad_table = table_grad_of(jnp.sum(grad_scores, 0))
    grad_raw = (grad_scores * HEAD_DIM ** (-0.5)).astype(BF16)
    grad_queries = jnp.einsum("whqk,wkhd->wqhd", grad_raw, keys_all, preferred_element_type=F32)
    grad_keys = jnp.einsum("whqk,wqhd->wkhd", grad_raw, queries, preferred_element_type=F32)
    grad_packed = [
        one.astype(BF16).reshape(-1, D) for one in (grad_queries, grad_keys, grad_values)
    ]
    grad_w_qkv = jnp.stack([contract_rows(windows, one).astype(BF16) for one in grad_packed], 0)
    if quick:
        terms = reduce_plane(0, *spread(me, 0, qkv=grad_w_qkv, proj=grad_w_proj)) + terms
    grad_b_qkv = jnp.concatenate([jnp.sum(one.astype(F32), 0) for one in grad_packed])
    grad_windows = sum(times_transposed(one, w_qkv[j]) for j, one in enumerate(grad_packed))
    grad_tokens, grad_gain_one, grad_shift_one = norm_pull(grad_windows)
    grad_tokens = grad_tokens.astype(BF16).reshape(win_count, tile_len, D)
    grad_shifted = jnp.roll(from_windows(grad_tokens, img_count), SHIFT, 2)
    arrived_two = from_partner(grad_shifted[:, SHIFT:], "row", 0)
    input_grad = grad_middle.reshape(tokens.shape) + jnp.concatenate(
        [arrived_two, grad_shifted[:, :SHIFT]], 1
    ).astype(F32)
    small_grads = [
        grad_table,
        grad_b_qkv,
        grad_b_proj,
        jnp.concatenate(grads_bup),
        grad_b_down,
        grad_gain_one,
        grad_shift_one,
        grad_gain_two,
        grad_shift_two,
    ]
    tail_grad = jnp.concatenate([one.reshape(-1) for one in small_grads])
    if quick:
        tail_grad = jnp.pad(tail_grad, (0, 32 * D - tail_grad.shape[0])).reshape(192, 128)
        new = adam(me, terms, sum_tail(tail_grad), params, first_moment, second_moment)
    else:
        flat = [
            grad_w_qkv.transpose(1, 0, 2),
            grad_w_proj,
            grad_w_up.transpose(1, 0, 2),
            grad_w_down,
            tail_grad,
        ]
        flat = jnp.concatenate([one.astype(F32).reshape(-1) for one in flat])
        flat = jnp.pad(flat, (0, gathered.shape[0] - flat.shape[0]))
        mine = lax.psum_scatter(flat, BOTH, scatter_dimension=0, tiled=True)
        length = params.shape[0]
        position = lax.axis_index(BOTH) * length + jnp.arange(length, dtype=jnp.int32)
        new = adam_step(params, first_moment, second_moment, mine, position)
        new = [new[0], new[0].astype(BF16), new[1], new[2]]
    return (output.astype(BF16).reshape(tokens.shape), input_grad, *new)


def solution(mesh):
    return jax.shard_map(
        shards,
        mesh=mesh,
        in_specs=(
            P("img", "row", None, None),
            P("img", "row", None, None),
            P("img"),
            P(("img", "row")),
            P(("img", "row")),
            P(("img", "row")),
        ),
        out_specs=(
            P("img", "row", None, None),
            P("img", "row", None, None),
            P(("img", "row")),
            P(("img", "row")),
            P(("img", "row")),
            P(("img", "row")),
        ),
        check_vma=False,
    )
```

```python
import functools
import math

import jax
import jax.numpy as jnp
from jax import lax
from jax.experimental import pallas as pl
from jax.experimental.pallas import tpu as pltpu
from jax.sharding import PartitionSpec as P

D = 768
FF = 3072
HEADS = 24
HEAD_DIM = 32
WIN = 12
SHIFT = 6
SIDE = 24
STEP = 4
TABLE_ROWS = 529


EPSILON = 1e-05
MASKED = -100.0
DECAY = 0.05
ADAM_EPS = 1e-08
BETA_ONE = 0.5
BETA_TWO = 0.5


def from_partner(block, axis, apart):
    count = lax.axis_size(axis)
    route = []
    for low in range(count):
        high = low | 1 << apart
        if high != low and high < count:
            route += [(low, high), (high, low)]
    return lax.ppermute(block, axis, route)


def piece_shapes():
    return [
        (D, 3 * D),
        (D, D),
        (D, FF),
        (FF, D),
        (TABLE_ROWS, HEADS),
        (3 * D,),
        (D,),
        (FF,),
        (D,),
        (D,),
        (D,),
        (D,),
        (D,),
    ]


def unpack(flat_vec):
    pieces = []
    offset = 0
    for shape_one in piece_shapes():
        amount = math.prod(shape_one)
        pieces.append(lax.slice_in_dim(flat_vec, offset, offset + amount).reshape(shape_one))
        offset = offset + amount
    return pieces


def step_rates(position):
    rate_list = [
        D ** (-0.5),
        4.0 * D ** (-0.5),
        D ** (-0.5),
        FF ** (-0.5),
        1.0,
        0.3,
        0.3,
        0.3,
        0.3,
        0.4,
        0.3,
        0.4,
        0.3,
    ]
    result = jnp.zeros(position.shape, jnp.float32)
    offset = 0
    for shape_one, rate_one in zip(piece_shapes(), rate_list):
        amount = math.prod(shape_one)
        inside = (position >= offset) & (position < offset + amount)
        result = jnp.where(inside, jnp.float32(rate_one), result)
        offset = offset + amount
    return result


def layer_norm(values, gain_vec, shift_vec):
    centre = jnp.mean(values, -1, keepdims=True)
    centred = values - centre
    spread = jnp.mean(centred * centred, -1, keepdims=True)
    return centred * lax.rsqrt(spread + EPSILON) * gain_vec + shift_vec


def region_of(coord):
    return jnp.where(coord < SIDE - WIN, 0, jnp.where(coord < SIDE - SHIFT, 1, 2))


def relative_index():
    cell_index = jnp.arange(WIN * WIN, dtype=jnp.int32)
    row_part = cell_index // WIN
    col_part = cell_index % WIN
    return (row_part[:, None] - row_part[None, :] + WIN - 1) * (2 * WIN - 1) + (
        col_part[:, None] - col_part[None, :] + WIN - 1
    )


def window_mask(row_first):
    row_coord = row_first + jnp.arange(WIN, dtype=jnp.int32)
    col_coord = jnp.arange(SIDE, dtype=jnp.int32)
    region_ids = 3 * region_of(row_coord)[:, None] + region_of(col_coord)[None, :]
    region_ids = (
        region_ids.reshape(WIN, SIDE // WIN, WIN).transpose(1, 0, 2).reshape(SIDE // WIN, WIN * WIN)
    )
    same = region_ids[:, :, None] == region_ids[:, None, :]
    return jnp.where(same, 0.0, MASKED).astype(jnp.float32)


def to_windows(grid_rows):
    img_count = grid_rows.shape[0]
    width = grid_rows.shape[-1]
    shaped = grid_rows.reshape(img_count, WIN, SIDE // WIN, WIN, width).transpose(0, 2, 1, 3, 4)
    return shaped.reshape(img_count * (SIDE // WIN), WIN * WIN, width)


def from_windows(window_rows, img_count):
    width = window_rows.shape[-1]
    shaped = window_rows.reshape(img_count, SIDE // WIN, WIN, WIN, width).transpose(0, 2, 1, 3, 4)
    return shaped.reshape(img_count, WIN, SIDE, width)


BF16 = jnp.bfloat16
F32 = jnp.float32
BOTH = ("img", "row")
ROWS = 9248
TILE = 16
WINDOW = 304
WIDE = 2 * D // 4
VMEM_MOST = 60 * 1024 * 1024


def contract_rows(left_op, right_op):
    summed_dims = tuple(range(left_op.ndim - 1))
    return lax.dot_general(
        left_op,
        right_op,
        ((summed_dims, summed_dims), ((), ())),
        preferred_element_type=jnp.float32,
    )


def times_transposed(left_op, right_op):
    return lax.dot_general(
        left_op,
        right_op,
        (((left_op.ndim - 1,), (1,)), ((), ())),
        preferred_element_type=jnp.float32,
    )


def scores_of(queries, keys_all, bias_full, region_mask):
    raw_scores = jnp.einsum(
        "wqhd,wkhd->whqk", queries, keys_all, preferred_element_type=jnp.float32
    )
    return raw_scores * HEAD_DIM ** (-0.5) + bias_full[None] + region_mask[:, None]


def shards_general(tokens, cotangent, valid, params, first_moment, second_moment):
    img_count = tokens.shape[0]
    win_count = img_count * (SIDE // WIN)
    tile_len = WIN * WIN
    gathered = lax.all_gather(params.astype(jnp.bfloat16), ("img", "row"), axis=0, tiled=True)
    (
        w_qkv,
        w_proj,
        w_up,
        w_down,
        bias_table,
        b_qkv,
        b_proj,
        b_up,
        b_down,
        gain_one,
        shift_one,
        gain_two,
        shift_two,
    ) = unpack(gathered)
    images = tokens.astype(jnp.float32)
    normed, norm_pull = jax.vjp(
        layer_norm, images, gain_one.astype(jnp.float32), shift_one.astype(jnp.float32)
    )
    normed_low = normed.astype(jnp.bfloat16)
    incoming = from_partner(normed_low[:, :SHIFT], "row", 0)
    shifted = jnp.roll(jnp.concatenate([normed_low[:, SHIFT:], incoming], 1), -SHIFT, 2)
    windows = to_windows(shifted)
    packed = (
        jnp.dot(windows, w_qkv, preferred_element_type=jnp.float32) + b_qkv.astype(jnp.float32)
    ).astype(jnp.bfloat16)
    heads_view = packed.reshape(win_count, tile_len, 3, HEADS, HEAD_DIM)
    queries = heads_view[:, :, 0]
    keys_all = heads_view[:, :, 1]
    values_all = heads_view[:, :, 2]
    rel_index = relative_index()
    bias_full = bias_table.astype(jnp.float32)[rel_index].transpose(2, 0, 1)
    region_mask = jnp.tile(window_mask(lax.axis_index("row") * WIN), (img_count, 1, 1))
    scores = scores_of(queries, keys_all, bias_full, region_mask)
    row_top = jnp.max(scores, -1, keepdims=True)
    exponent = jnp.exp(scores - row_top)
    row_total = jnp.sum(exponent, -1, keepdims=True)
    log_total = row_top + jnp.log(row_total)
    attn_probs = (exponent / row_total).astype(jnp.bfloat16)
    attn_mixed = jnp.einsum(
        "whqk,wkhd->wqhd", attn_probs, values_all, preferred_element_type=jnp.float32
    )
    attn_mixed = attn_mixed.astype(jnp.bfloat16).reshape(win_count, tile_len, D)
    branch = (
        jnp.dot(attn_mixed, w_proj, preferred_element_type=jnp.float32) + b_proj.astype(jnp.float32)
    ).astype(jnp.bfloat16)
    branch_grid = jnp.roll(from_windows(branch, img_count), SHIFT, 2)
    returned = from_partner(branch_grid[:, SHIFT:], "row", 0)
    middle = images + jnp.concatenate([returned, branch_grid[:, :SHIFT]], 1).astype(jnp.float32)
    normed_two, norm_two_pull = jax.vjp(
        layer_norm, middle, gain_two.astype(jnp.float32), shift_two.astype(jnp.float32)
    )
    hidden_in = normed_two.astype(jnp.bfloat16)
    upward = jnp.dot(hidden_in, w_up, preferred_element_type=jnp.float32) + b_up.astype(jnp.float32)
    active_full, gelu_pull = jax.vjp(lambda values: jax.nn.gelu(values, approximate=False), upward)
    active = active_full.astype(jnp.bfloat16)
    output = (
        middle
        + jnp.dot(active, w_down, preferred_element_type=jnp.float32)
        + b_down.astype(jnp.float32)
    )
    regathered = lax.all_gather(params.astype(jnp.bfloat16), ("img", "row"), axis=0, tiled=True)
    fresh = unpack(regathered)
    w_qkv, w_proj, w_up, w_down = (fresh[0], fresh[1], fresh[2], fresh[3])
    grad_out = cotangent * valid.astype(jnp.bfloat16)[:, None, None, None]
    grad_w_down = contract_rows(active, grad_out)
    grad_b_down = jnp.sum(grad_out.astype(jnp.float32), (0, 1, 2))
    grad_active = times_transposed(grad_out, w_down)
    grad_up = gelu_pull(grad_active)[0].astype(jnp.bfloat16)
    grad_w_up = contract_rows(hidden_in, grad_up)
    grad_b_up = jnp.sum(grad_up.astype(jnp.float32), (0, 1, 2))
    grad_hidden = times_transposed(grad_up, w_up)
    grad_middle_ln, grad_gain_two, grad_shift_two = norm_two_pull(grad_hidden)
    grad_middle = grad_out.astype(jnp.float32) + grad_middle_ln
    middle_low = grad_middle.astype(jnp.bfloat16)
    arrived = from_partner(middle_low[:, :SHIFT], "row", 0)
    grad_grid = jnp.roll(jnp.concatenate([middle_low[:, SHIFT:], arrived], 1), -SHIFT, 2)
    grad_branch = to_windows(grad_grid)
    grad_w_proj = contract_rows(attn_mixed, grad_branch)
    grad_b_proj = jnp.sum(grad_branch.astype(jnp.float32), (0, 1))
    grad_attn = times_transposed(grad_branch, w_proj).astype(jnp.bfloat16)
    grad_attn = grad_attn.reshape(win_count, tile_len, HEADS, HEAD_DIM)
    again_scores = scores_of(queries, keys_all, bias_full, region_mask)
    again_probs = jnp.exp(again_scores - log_total)
    grad_values = jnp.einsum(
        "whqk,wqhd->wkhd",
        again_probs.astype(jnp.bfloat16),
        grad_attn,
        preferred_element_type=jnp.float32,
    )
    grad_probs = jnp.einsum(
        "wqhd,wkhd->whqk", grad_attn, values_all, preferred_element_type=jnp.float32
    )
    grad_scores = again_probs * (grad_probs - jnp.sum(again_probs * grad_probs, -1, keepdims=True))
    pair_sums = jnp.sum(grad_scores, 0).transpose(1, 2, 0).reshape(tile_len * tile_len, HEADS)
    grad_table = jax.ops.segment_sum(pair_sums, rel_index.reshape(-1), TABLE_ROWS)
    grad_raw = (grad_scores * HEAD_DIM ** (-0.5)).astype(jnp.bfloat16)
    grad_queries = jnp.einsum(
        "whqk,wkhd->wqhd", grad_raw, keys_all, preferred_element_type=jnp.float32
    )
    grad_keys = jnp.einsum("whqk,wqhd->wkhd", grad_raw, queries, preferred_element_type=jnp.float32)
    grad_packed = jnp.stack([grad_queries, grad_keys, grad_values], 2).astype(jnp.bfloat16)
    grad_packed = grad_packed.reshape(win_count, tile_len, 3 * D)
    grad_w_qkv = contract_rows(windows, grad_packed)
    grad_b_qkv = jnp.sum(grad_packed.astype(jnp.float32), (0, 1))
    grad_windows = times_transposed(grad_packed, w_qkv).astype(jnp.bfloat16)
    grad_shifted = jnp.roll(from_windows(grad_windows, img_count), SHIFT, 2)
    arrived_two = from_partner(grad_shifted[:, SHIFT:], "row", 0)
    grad_normed = jnp.concatenate([arrived_two, grad_shifted[:, :SHIFT]], 1).astype(jnp.float32)
    grad_images_ln, grad_gain_one, grad_shift_one = norm_pull(grad_normed)
    input_grad = grad_middle + grad_images_ln
    grad_list = [
        grad_w_qkv,
        grad_w_proj,
        grad_w_up,
        grad_w_down,
        grad_table,
        grad_b_qkv,
        grad_b_proj,
        grad_b_up,
        grad_b_down,
        grad_gain_one,
        grad_shift_one,
        grad_gain_two,
        grad_shift_two,
    ]
    grad_flat = jnp.concatenate([grad_one.reshape(-1) for grad_one in grad_list])
    grad_flat = jnp.pad(grad_flat, (0, gathered.shape[0] - grad_flat.shape[0]))
    grad_shard = lax.psum_scatter(grad_flat, ("img", "row"), scatter_dimension=0, tiled=True)
    shard_len = params.shape[0]
    position = lax.axis_index(("img", "row")) * shard_len + jnp.arange(shard_len, dtype=jnp.int32)
    step_rate = step_rates(position)
    new_first = BETA_ONE * first_moment + (1.0 - BETA_ONE) * grad_shard
    new_second = BETA_TWO * second_moment + (1.0 - BETA_TWO) * grad_shard * grad_shard
    fixed_first = new_first / (1.0 - BETA_ONE**STEP)
    fixed_second = new_second / (1.0 - BETA_TWO**STEP)
    new_params = params - step_rate * (
        fixed_first / (jnp.sqrt(fixed_second) + ADAM_EPS) + DECAY * params
    )
    return (
        output.astype(jnp.bfloat16),
        input_grad,
        new_params,
        new_params.astype(jnp.bfloat16),
        new_first,
        new_second,
    )


BF16 = jnp.bfloat16
F32 = jnp.float32
BOTH = ("img", "row")
TILE = 16
WINDOW = 304
LEN = 2 * WIN * WIN
QUADS = HEADS // 4
SPAN = 4 * WIN * WIN


def swap(block, mask, only=None):
    count = lax.axis_size(BOTH)
    route = [(d, d ^ mask) for d in range(count) if only is None or only(d)]
    return lax.ppermute(block, BOTH, route)


def params_call(mebibytes):
    return pltpu.CompilerParams(vmem_limit_bytes=mebibytes << 20)


def vmem(count):
    return [pl.BlockSpec(memory_space=pltpu.VMEM)] * count


SMEM_SPEC = pl.BlockSpec(memory_space=pltpu.SMEM)
ANY_SPEC = pl.BlockSpec(memory_space=pl.ANY)


def first_tile(device):
    return (289 * device) // TILE


def prep_body(me_ref, own_ref, out_ref, spare_ref, wide_ref):
    shift = me_ref[0] % TILE
    wide_ref[0:96] = jnp.zeros((96, 128), F32)
    wide_ref[1824:1920] = jnp.zeros((96, 128), F32)
    wide_ref[96:1830] = own_ref[...]
    for j in range(6):
        picked = wide_ref[pl.ds(96 - 6 * shift + j, WINDOW, stride=6), :]
        out_ref[:, 128 * j : 128 * (j + 1)] = picked.astype(BF16)
        spare_ref[:, 128 * j : 128 * (j + 1)] = picked.astype(BF16)


def window_of(me, own_flat):
    return pl.pallas_call(
        prep_body,
        out_shape=[jax.ShapeDtypeStruct((WINDOW, D), BF16)] * 2,
        in_specs=[SMEM_SPEC] + vmem(1),
        out_specs=vmem(2),
        scratch_shapes=[pltpu.VMEM((1920, 128), F32)],
        compiler_params=params_call(8),
        name="own_window",
    )(me, own_flat.reshape(-1, 128))


def mixer(groups, per):
    size = groups * per
    row = lax.broadcasted_iota(jnp.int32, (size, size), 0)
    col = lax.broadcasted_iota(jnp.int32, (size, size), 1)
    return (col == groups * (row % per) + row // per).astype(F32).astype(BF16)


def unmixer(groups, per):
    size = groups * per
    row = lax.broadcasted_iota(jnp.int32, (size, size), 0)
    col = lax.broadcasted_iota(jnp.int32, (size, size), 1)
    return (row == groups * (col % per) + col // per).astype(F32).astype(BF16)


def plane_rows(plane):
    low = first_tile(8 * plane) * TILE
    high = first_tile(8 * plane + 7) * TILE + WINDOW
    return low, high


def gate(value, *others):
    def body(*refs):
        pass

    return pl.pallas_call(
        body,
        out_shape=jax.ShapeDtypeStruct(value.shape, value.dtype),
        in_specs=[ANY_SPEC] * (1 + len(others)),
        out_specs=ANY_SPEC,
        input_output_aliases={0: 0},
        cost_estimate=pl.CostEstimate(flops=1, bytes_accessed=1, transcendentals=0),
        name="gate",
    )(value, *others)


def cross(block, zero, one):
    count = lax.axis_size(BOTH)
    return lax.ppermute(block, BOTH, [(d, d ^ (one if d & 2 else zero)) for d in range(count)])


def gather_windows(own, spare, rows, bias_maker):
    me = lax.axis_index(BOTH)
    got = {0: own}
    first, second, third = {}, {}, {}
    tail = own[WINDOW - 32 :]
    have = 31

    def hop(tail, have, mask):
        tail = jnp.where(me & have == have, tail, jnp.zeros_like(tail))
        return tail + swap(tail, mask, lambda d: d & have == have), have ^ mask

    got[8] = swap(own, 8)
    first[0] = cross(own, 4, 1)
    second[0] = cross(own, 1, 4)
    got[16] = swap(own, 16)
    third[0] = cross(first[0], 1, 4)
    first[8] = cross(got[8], 4, 1)
    second[8] = cross(got[8], 1, 4)
    tail = gate(tail, first[0])
    tail, have = hop(tail, have, 16)
    tail, have = hop(tail, have, 8)
    got_rows = from_partner(gate(rows, second[0]), "row", 0)
    got[24] = swap(gate(spare, got[16]), 24)
    tail, have = hop(tail, have, 4)
    tail, have = hop(tail, have, 1)
    third[8] = cross(first[8], 1, 4)
    first[16] = cross(got[16], 4, 1)
    second[16] = cross(got[16], 1, 4)
    tail, have = hop(tail, have, 2)
    made = bias_maker(tail)
    third[16] = cross(first[16], 1, 4)
    got[24] = gate(got[24], *made, got_rows)
    first[24] = cross(got[24], 4, 1)
    second[24] = cross(got[24], 1, 4)
    third[24] = cross(first[24], 1, 4)
    blocks, places = [], []
    for z in (0, 8, 16, 24):
        four = [got[z], first[z], second[z], third[z]]
        masks = [(z, z), (z | 4, z | 1), (z | 1, z | 4), (z | 5, z | 5)]
        for n in range(4):
            places.append((len(blocks) + n, None, *masks[n]))
        other = swap(stacked(four), 2)
        for n, (zero, one) in enumerate(masks):
            places.append((len(blocks) + 4, n, one | 2, zero | 2))
        blocks += [*four, other]
    return blocks, places, made, got_rows


def stacked_body(*refs):
    count = len(refs) - 2
    copies = [
        pltpu.make_async_copy(refs[i], refs[count].at[i], refs[count + 1].at[i])
        for i in range(count)
    ]
    for copy in copies:
        copy.start()
    for copy in copies:
        copy.wait()


def stacked(blocks):
    return pl.pallas_call(
        stacked_body,
        out_shape=like(len(blocks), WINDOW, D),
        in_specs=[ANY_SPEC] * len(blocks),
        out_specs=vmem(1)[0],
        scratch_shapes=[pltpu.SemaphoreType.DMA((len(blocks),))],
        compiler_params=params_call(8),
        cost_estimate=pl.CostEstimate(flops=1, bytes_accessed=1, transcendentals=0),
        name="stacked",
    )(*blocks)


class Loader:

    def __init__(self, me, parts, places, first, last, flat_ref, edge_ref, main_sem, edge_sem):
        self.me, self.parts, self.first, self.last = me, parts, first, last
        self.places = places
        self.flat_ref, self.edge_ref = flat_ref, edge_ref
        self.main_sem, self.edge_sem = main_sem, edge_sem
        self.base = first_tile(first) * TILE

    def place(self, m):
        _, _, zero, one = self.places[m]
        device = self.me ^ jnp.where((self.me & 2) == 0, zero, one)
        start = pl.multiple_of(first_tile(device) * TILE - self.base, TILE)
        return start, (device >= self.first) & (device <= self.last)

    def copies(self, m, start):
        block, slot = self.places[m][:2]
        part = self.parts[block] if slot is None else self.parts[block].at[slot]
        main = pltpu.make_async_copy(
            part.at[pl.ds(TILE, WINDOW - TILE)],
            self.flat_ref.at[pl.ds(start + TILE, WINDOW - TILE)],
            self.main_sem.at[m],
        )
        edge = pltpu.make_async_copy(
            part.at[pl.ds(0, TILE)], self.edge_ref.at[m], self.edge_sem.at[m]
        )
        return main, edge

    def start(self):
        for m in range(32):
            start, wanted = self.place(m)

            @pl.when(wanted)
            def _():
                for copy in self.copies(m, start):
                    copy.start()

        for device in (self.first, 16):
            if self.first <= device <= self.last:
                at = first_tile(device) * TILE - self.base
                self.flat_ref[at : at + TILE] = jnp.zeros((TILE, D), BF16)

    def wait(self):
        for m in range(32):
            start, wanted = self.place(m)

            @pl.when(wanted)
            def _():
                for copy in self.copies(m, start):
                    copy.wait()

        for m in range(32):
            start, wanted = self.place(m)

            @pl.when(wanted)
            def _():
                self.flat_ref[pl.ds(start, TILE)] += self.edge_ref[m]


def loader_scratch(first, last):
    rows = first_tile(last) * TILE + WINDOW - first_tile(first) * TILE
    return [
        pltpu.VMEM((rows, D), BF16),
        pltpu.VMEM((32, TILE, D), BF16),
        pltpu.SemaphoreType.DMA((32,)),
        pltpu.SemaphoreType.DMA((32,)),
    ]


def unmix_rows(flat_ref, out_ref, base, groups, per, steps):
    mix = mixer(groups, per)
    size = groups * per
    for t in range(steps):
        rows = flat_ref[base + size * t : base + size * (t + 1)]
        out = jnp.dot(mix, rows, preferred_element_type=F32).astype(BF16)
        for j in range(groups):
            out_ref[j, per * t : per * (t + 1)] = out[per * j : per * (j + 1)]


def mix_rows(in_ref, flat_ref, base, groups, per, steps):
    mix = unmixer(groups, per)
    size = groups * per
    for t in range(steps):
        rows = jnp.concatenate([in_ref[j, per * t : per * (t + 1)] for j in range(groups)], 0)
        out = jnp.dot(mix, rows, preferred_element_type=F32).astype(BF16)
        flat_ref[base + size * t : base + size * (t + 1)] = out


def cut_windows(me, plane, flat_ref, base, keeps, send_ref):
    for flip in (2, 0):
        for s in range(4):
            first = jnp.where(((me ^ flip) & 2) == 0, 4, 1)
            away = (first if s & 2 else 0) + (5 - first if s & 1 else 0)
            device = 8 * plane + ((me & 7) ^ (away | flip))
            start = pl.multiple_of(first_tile(device) * TILE - base, TILE)
            window = flat_ref[pl.ds(start, WINDOW)]
            if flip:
                send_ref[s] = window
            else:
                keeps[s // 2][s % 2] = window


WINDOWS = [
    jax.ShapeDtypeStruct((2, WINDOW, D), BF16),
    jax.ShapeDtypeStruct((2, WINDOW, D), BF16),
    jax.ShapeDtypeStruct((4, WINDOW, D), BF16),
]


def like(*shape, dtype=BF16):
    return jax.ShapeDtypeStruct(shape, dtype)


def call(body, name, outs, out_any, ins, in_any, scratch, limit):
    n_in, n_out = len(ins) - 1, len(outs)
    return pl.pallas_call(
        body,
        out_shape=outs,
        in_specs=[SMEM_SPEC] + vmem(n_in - in_any) + [ANY_SPEC] * in_any,
        out_specs=vmem(n_out - out_any) + [ANY_SPEC] * out_any,
        scratch_shapes=scratch,
        compiler_params=params_call(limit),
        cost_estimate=pl.CostEstimate(flops=1, bytes_accessed=1, transcendentals=0),
        name=name,
    )(*ins)


def normal_parts(values):
    centre = jnp.mean(values, -1, keepdims=True)
    centred = values - centre
    spread = jnp.mean(centred * centred, -1, keepdims=True)
    scale = lax.rsqrt(spread + EPSILON)
    return centred * scale, scale


def normal_pull(n, scale, grad, gain):
    e = grad * gain
    return scale * (
        e - jnp.mean(e, -1, keepdims=True) - n * jnp.mean(e * n, -1, keepdims=True)
    )


def over_heads(block):
    head = lax.broadcasted_iota(jnp.int32, block.shape, 1) // HEAD_DIM
    return jnp.concatenate([jnp.where(head == h, block, jnp.zeros_like(block)) for h in range(4)], 0)


def own_columns(block):
    head = lax.broadcasted_iota(jnp.int32, (144, 128), 1) // HEAD_DIM
    out = block[0:144]
    for h in range(1, 4):
        out = jnp.where(head == h, block[144 * h : 144 * (h + 1)], out)
    return out


def contract(one, two, a, b):
    return lax.dot_general(one, two, (((a,), (b,)), ((), ())), preferred_element_type=F32)


def lay(out_ref, near, far):
    for i in range(WIN):
        ref, k = (near, 24 * i) if i < SHIFT else (far, 24 * (i - SHIFT))
        out_ref[12 * i : 12 * i + 12] = ref[k + 6 : k + 18]
        out_ref[144 + 12 * i : 150 + 12 * i] = ref[k + 18 : k + 24]
        out_ref[150 + 12 * i : 156 + 12 * i] = ref[k : k + 6]


def unlay(ref, near, far):
    for i in range(WIN):
        out_ref, k = (near, 24 * i) if i < SHIFT else (far, 24 * (i - SHIFT))
        out_ref[k + 6 : k + 18] = ref[12 * i : 12 * i + 12]
        out_ref[k + 18 : k + 24] = ref[144 + 12 * i : 150 + 12 * i]
        out_ref[k : k + 6] = ref[150 + 12 * i : 156 + 12 * i]


HALF = LEN // 2
LAY_SCRATCH = [pltpu.VMEM((LEN, D), F32), pltpu.VMEM((HALF, D), F32), pltpu.VMEM((HALF, D), F32)]


def attend_body(places, me_ref, tokens_ref, rows_ref, vecs_ref, strips_ref, mask_ref, *refs):
    parts = refs[:20]
    windows_ref, laid_ref, packed_ref, attn_ref, probs_ref, near_ref, far_ref, qkv_ref, proj_ref = refs[20:29]
    flat_ref, edge_ref, main_sem, edge_sem, wide_ref, one_ref, two_ref, bias_ref = refs[29:]
    loader = Loader(me_ref[0], parts, places, 0, 10, flat_ref, edge_ref, main_sem, edge_sem)
    loader.start()
    one_ref[...] = tokens_ref[HALF:LEN].astype(F32)
    two_ref[...] = rows_ref[...].astype(F32)
    lay(wide_ref, one_ref, two_ref)
    laid = wide_ref[...]
    laid_ref[...] = laid.astype(BF16)
    n, _ = normal_parts(laid)
    windows_ref[...] = (n * vecs_ref[9:10] + vecs_ref[10:11]).astype(BF16)
    loader.wait()
    unmix_rows(flat_ref, qkv_ref, 0, 3, 64, 12)
    proj_ref[...] = flat_ref[2304:3072]

    def project(j, carry):
        packed_ref[j] = (
            jnp.dot(windows_ref[...], qkv_ref[j], preferred_element_type=F32)
            + vecs_ref[pl.ds(j, 1)]
        ).astype(BF16)
        return carry

    lax.fori_loop(0, 3, project, 0)

    def quad(g, carry):
        lanes = pl.ds(pl.multiple_of(128 * g, 128), 128)
        for h in range(4):
            for i in range(WIN):
                low = 12 * (11 - i)
                bias_ref[12 * i : 12 * i + 12, 144 * h : 144 * (h + 1)] = strips_ref[
                    4 * g + h, 0:12, low : low + 144
                ]
        for w in range(2):
            rows = pl.ds(144 * w, 144)
            queries = over_heads(packed_ref[0, rows, lanes])
            scores = contract(packed_ref[1, rows, lanes], queries, 1, 1)
            scores = scores * HEAD_DIM ** (-0.5) + bias_ref[...] + mask_ref[w]
            top = jnp.max(scores, 0, keepdims=True)
            exponent = jnp.exp(scores - top)
            total = jnp.sum(exponent, 0, keepdims=True)
            probs = (exponent * (1.0 / total)).astype(BF16)
            probs_ref[2 * g + w] = probs
            mixed = contract(probs, packed_ref[2, rows, lanes], 0, 0)
            attn_ref[rows, lanes] = own_columns(mixed).astype(BF16)
        return carry

    lax.fori_loop(0, QUADS, quad, 0)
    wide_ref[...] = (
        jnp.dot(attn_ref[...], proj_ref[...], preferred_element_type=F32) + vecs_ref[3:4]
    )
    unlay(wide_ref, one_ref, two_ref)
    near_ref[...] = one_ref[...].astype(BF16)
    far_ref[...] = two_ref[...].astype(BF16)


def attend(me, tokens, rows, vecs, bias, mask, parts, places):
    return call(
        functools.partial(attend_body, places),
        "attention_forward",
        [
            like(LEN, D),
            like(LEN, D),
            like(3, LEN, D),
            like(LEN, D),
            like(2 * QUADS, 144, SPAN),
            like(HALF, D),
            like(HALF, D),
            like(3, D, D),
            like(D, D),
        ],
        0,
        [me, tokens, rows, vecs, bias, mask, *parts],
        20,
        loader_scratch(0, 10) + LAY_SCRATCH + [pltpu.VMEM((144, SPAN), F32)],
        36,
    )


def middle_of(tokens_ref, back_ref, near_ref):
    branch = jnp.concatenate([back_ref[...].astype(F32), near_ref[...].astype(F32)], 0)
    return tokens_ref[...].astype(F32) + branch


def feed_body(places, me_ref, valid_ref, tokens_ref, back_ref, near_ref, cotangent_ref, vecs_ref, *refs):
    parts = refs[:20]
    hidden_ref, active_ref, gradup_ref, up_ref, sums_ref, down_ref, low_ref, low_keep, high_keep, send_ref = refs[20:30]
    flat_ref, edge_ref, main_sem, edge_sem, grad_ref = refs[30:]
    me = me_ref[0]
    loader = Loader(me, parts, places, 10, 31, flat_ref, edge_ref, main_sem, edge_sem)
    loader.start()
    n, _ = normal_parts(middle_of(tokens_ref, back_ref, near_ref))
    hidden_ref[...] = (n * vecs_ref[11:12] + vecs_ref[12:13]).astype(BF16)
    grad_out = cotangent_ref[...] * valid_ref[0].astype(F32).astype(BF16)
    grad_ref[3072:3104] = jnp.zeros((32, D), BF16)
    loader.wait()
    unmix_rows(flat_ref, up_ref, 3072 - loader.base, 4, 48, 16)
    down_at = 6144 - loader.base
    down_ref[...] = flat_ref[down_at : down_at + FF]

    def step(j, carry):
        at = pl.multiple_of(D * j, D)
        down = flat_ref[pl.ds(down_at + at, D)]
        upward = jnp.dot(hidden_ref[...], up_ref[j], preferred_element_type=F32)
        upward = upward + vecs_ref[pl.ds(4 + j, 1)]
        grad_active = contract(grad_out, down, 1, 1)
        share = 0.5 * (1.0 + lax.erf(upward * (0.5**0.5)))
        density = jnp.exp(-0.5 * upward * upward) * ((2.0 * math.pi) ** (-0.5))
        active = (upward * share).astype(BF16)
        grad_up = (grad_active * (share + upward * density)).astype(BF16)
        active_ref[j] = active
        gradup_ref[j] = grad_up
        sums_ref[pl.ds(j, 1)] = jnp.sum(grad_up.astype(F32), 0, keepdims=True)
        grad_ref[pl.ds(at, D)] = contract(active, grad_out, 0, 0).astype(BF16)
        return carry

    lax.fori_loop(0, 4, step, 0)
    cut_windows(me, 3, grad_ref, 6144, (low_keep, high_keep), send_ref)
    low_ref[...] = grad_ref[0:800]
    sums_ref[4:5] = jnp.sum(grad_out.astype(F32), 0, keepdims=True)


def feed(me, valid, tokens, back, near, cotangent, vecs, parts, places):
    body = functools.partial(feed_body, places)
    n_in = 5
    outs = [
        like(LEN, D),
        like(4, LEN, D),
        like(4, LEN, D),
        like(4, D, D),
        like(8, D, dtype=F32),
        like(FF, D),
        like(800, D),
        *WINDOWS,
    ]
    return pl.pallas_call(
        body,
        out_shape=outs,
        in_specs=[SMEM_SPEC] * 2 + vmem(n_in) + [ANY_SPEC] * 20,
        out_specs=vmem(10),
        scratch_shapes=loader_scratch(10, 31)
        + [pltpu.VMEM((3104, D), BF16)],
        compiler_params=params_call(44),
        cost_estimate=pl.CostEstimate(flops=1, bytes_accessed=1, transcendentals=0),
        name="feed_forward",
    )(me, valid, tokens, back, near, cotangent, vecs, *parts)


def middle_body(me_ref, valid_ref, tokens_ref, back_ref, near_ref, cotangent_ref, vecs_ref, gradup_ref, up_ref, grad_ref, far_out, near_out, sums_ref):
    n, scale = normal_parts(middle_of(tokens_ref, back_ref, near_ref))
    grad_hidden = contract(gradup_ref[0], up_ref[0], 1, 1)
    for j in range(1, 4):
        grad_hidden = grad_hidden + contract(gradup_ref[j], up_ref[j], 1, 1)
    sums_ref[0:1] = jnp.sum(grad_hidden * n, 0, keepdims=True)
    sums_ref[1:2] = jnp.sum(grad_hidden, 0, keepdims=True)
    grad_out = (cotangent_ref[...] * valid_ref[0].astype(F32).astype(BF16)).astype(F32)
    grad = grad_out + normal_pull(n, scale, grad_hidden, vecs_ref[11:12])
    grad_ref[...] = grad
    far_out[...] = grad[:HALF].astype(BF16)
    near_out[...] = grad[HALF:].astype(BF16)


def middle_grad(me, valid, tokens, back, near, cotangent, vecs, grad_up, w_up):
    return pl.pallas_call(
        middle_body,
        out_shape=[like(LEN, D, dtype=F32), like(HALF, D), like(HALF, D), like(8, D, dtype=F32)],
        in_specs=[SMEM_SPEC] * 2 + vmem(7),
        out_specs=vmem(4),
        compiler_params=params_call(28),
        cost_estimate=pl.CostEstimate(flops=1, bytes_accessed=1, transcendentals=0),
        name="middle_grad",
    )(me, valid, tokens, back, near, cotangent, vecs, grad_up, w_up)


def up_body(me_ref, hidden_ref, gradup_ref, low_ref, tie_ref, proj_ref, low_keep, high_keep, send_ref, quad_ref, flat_ref):
    me = me_ref[0]

    def step(j, carry):
        quad_ref[j] = contract(hidden_ref[...], gradup_ref[j], 0, 0).astype(BF16)
        return carry

    lax.fori_loop(0, 4, step, 0)
    flat_ref[3072:3872] = low_ref[...]
    mix_rows(quad_ref, flat_ref, 0, 4, 48, 16)
    cut_windows(me, 2, flat_ref, 3072, (low_keep, high_keep), send_ref)
    proj_ref[...] = flat_ref[0:1552]


def up_grad(me, hidden, grad_up, low, tie):
    return call(
        up_body,
        "up_grad",
        [like(1552, D), *WINDOWS],
        0,
        [me, hidden, grad_up, low, tie],
        1,
        [
            pltpu.VMEM((4, D, D), BF16),
            pltpu.VMEM((3872, D), BF16),
        ],
        28,
    )


def proj_body(me_ref, near_ref, far_ref, attn_ref, proj_ref, high_ref, tie_ref, back_ref, sums_ref, edge_ref, low_keep, high_keep, send_ref, flat_ref, wide_ref, one_ref, two_ref):
    me = me_ref[0]
    one_ref[...] = near_ref[...].astype(F32)
    two_ref[...] = far_ref[...].astype(F32)
    lay(wide_ref, one_ref, two_ref)
    grad = wide_ref[...].astype(BF16)
    flat_ref[0:768] = contract(attn_ref[...], grad, 0, 0).astype(BF16)
    flat_ref[768:2320] = high_ref[...]
    cut_windows(me, 1, flat_ref, 2304, (low_keep, high_keep), send_ref)
    edge_ref[...] = flat_ref[0:16]
    back_ref[...] = contract(grad, proj_ref[...], 1, 1).astype(BF16)
    sums_ref[0:1] = jnp.sum(grad.astype(F32), 0, keepdims=True)


def proj_grad(me, near, far, attn, w_proj, high, tie):
    return call(
        proj_body,
        "proj_grad",
        [like(LEN, D), like(8, D, dtype=F32), like(16, D), *WINDOWS],
        0,
        [me, near, far, attn, w_proj, high, tie],
        1,
        [pltpu.VMEM((2320, D), BF16)] + LAY_SCRATCH,
        24,
    )


def unattend_quads(quads, packed_ref, grad_ref, attn_ref, probs_ref, back_ref, strips_ref, pairs_ref):
    strips_ref[...] = jnp.zeros_like(strips_ref)

    def quad(g, carry):
        lanes = pl.ds(pl.multiple_of(128 * g, 128), 128)
        for w in range(2):
            rows = pl.ds(144 * w, 144)
            queries = over_heads(packed_ref[0, rows, lanes])
            keys = packed_ref[1, rows, lanes]
            values = packed_ref[2, rows, lanes]
            grad = grad_ref[rows, lanes]
            product = -(attn_ref[rows, lanes].astype(F32) * grad.astype(F32)).astype(BF16)
            grads = over_heads(grad)
            left = jnp.concatenate([values, jnp.ones_like(values)], 1)
            right = jnp.concatenate([grads, over_heads(product)], 1)
            probs = probs_ref[2 * g + w]
            grad_scores = probs.astype(F32) * contract(left, right, 1, 1)
            if w == 0:
                pairs_ref[...] = grad_scores
            else:
                pairs_ref[...] += grad_scores
            raw = (grad_scores * HEAD_DIM ** (-0.5)).astype(BF16)
            back_ref[0, rows, lanes] = own_columns(contract(raw, keys, 0, 0)).astype(BF16)
            back_ref[1, rows, lanes] = jnp.dot(
                raw, queries, preferred_element_type=F32
            ).astype(BF16)
            back_ref[2, rows, lanes] = jnp.dot(
                probs, grads, preferred_element_type=F32
            ).astype(BF16)
        for h in range(4):
            for i in range(WIN):
                low = 12 * (11 - i)
                strips_ref[4 * (g - quads[0]) + h, 0:12, low : low + 144] += pairs_ref[
                    12 * i : 12 * i + 12, 144 * h : 144 * (h + 1)
                ]
        return carry

    lax.fori_loop(*quads, quad, 0)


def unattend_body(me_ref, packed_ref, grad_ref, attn_ref, probs_ref, tie_ref, back_ref, strips_ref, pairs_ref):
    unattend_quads((0, QUADS), packed_ref, grad_ref, attn_ref, probs_ref, back_ref, strips_ref, pairs_ref)


def qkv_body(me_ref, windows_ref, edge_ref, back_ref, tie_ref, sums_ref, low_keep, high_keep, send_ref, trio_ref, flat_ref):
    me = me_ref[0]

    def step(j, carry):
        trio_ref[j] = contract(windows_ref[...], back_ref[j], 0, 0).astype(BF16)
        sums_ref[pl.ds(j, 1)] = jnp.sum(back_ref[j].astype(F32), 0, keepdims=True)
        return carry

    lax.fori_loop(0, 3, step, 0)
    mix_rows(trio_ref, flat_ref, 0, 3, 64, 12)
    flat_ref[2304:2320] = edge_ref[...]
    cut_windows(me, 0, flat_ref, 0, (low_keep, high_keep), send_ref)


def unattend(me, packed, grad, attn, probs, tie):
    return call(
        unattend_body,
        "attention_backward",
        [like(3, LEN, D), like(HEADS, WIN, 384, dtype=F32)],
        0,
        [me, packed, grad, attn, probs, tie],
        1,
        [pltpu.VMEM((144, SPAN), F32)],
        24,
    )


def qkv_grad(me, windows, edge, back, tie):
    return call(
        qkv_body,
        "qkv_grad",
        [like(8, D, dtype=F32), *WINDOWS],
        0,
        [me, windows, edge, back, tie],
        1,
        [
            pltpu.VMEM((3, D, D), BF16),
            pltpu.VMEM((2320, D), BF16),
        ],
        24,
    )


def token_body(me_ref, back_ref, qkv_ref, laid_ref, vecs_ref, tie_ref, near_out, far_out, sums_ref, wide_ref, one_ref, two_ref):
    grad = contract(back_ref[0], qkv_ref[0], 1, 1)
    for j in (1, 2):
        grad = grad + contract(back_ref[j], qkv_ref[j], 1, 1)
    n, scale = normal_parts(laid_ref[...].astype(F32))
    sums_ref[0:1] = jnp.sum(grad * n, 0, keepdims=True)
    sums_ref[1:2] = jnp.sum(grad, 0, keepdims=True)
    wide_ref[...] = normal_pull(n, scale, grad, vecs_ref[9:10])
    unlay(wide_ref, one_ref, two_ref)
    near_out[...] = one_ref[...].astype(BF16)
    far_out[...] = two_ref[...].astype(BF16)


def token_grad(me, back, w_qkv, laid, vecs, tie):
    return call(
        token_body,
        "token_grad",
        [like(HALF, D), like(HALF, D), like(8, D, dtype=F32)],
        0,
        [me, back, w_qkv, laid, vecs, tie],
        1,
        LAY_SCRATCH,
        20,
    )


def output_body(me_ref, tokens_ref, back_ref, near_ref, vecs_ref, active_ref, down_ref, tie_ref, out_ref):
    total = middle_of(tokens_ref, back_ref, near_ref) + vecs_ref[8:9]
    for j in range(4):
        total = total + jnp.dot(
            active_ref[j], down_ref[D * j : D * (j + 1)], preferred_element_type=F32
        )
    out_ref[...] = total.astype(BF16)


def block_output(me, tokens, back, near, vecs, active, w_down, tie):
    return call(
        output_body,
        "block_output",
        [like(LEN, D)],
        0,
        [me, tokens, back, near, vecs, active, w_down, tie],
        1,
        [],
        28,
    )[0]


def sum_body(slots, lows, *refs):
    for i in range(slots):
        total = refs[0][lows[0] + i].astype(F32)
        for ref, low in zip(refs[1 : len(lows)], lows[1:]):
            total = total + ref[low + i].astype(F32)
        refs[-1][i] = total.astype(BF16)


def sum_slots(slots, terms, *ties):
    return pl.pallas_call(
        functools.partial(sum_body, slots, [low for _, low in terms]),
        out_shape=like(slots, WINDOW, D),
        in_specs=vmem(len(terms)) + [ANY_SPEC] * len(ties),
        out_specs=vmem(1)[0],
        compiler_params=params_call(16),
        cost_estimate=pl.CostEstimate(flops=1, bytes_accessed=1, transcendentals=0),
        name="sum_slots",
    )(*[one for one, _ in terms], *ties)


def arranged_body(me_ref, high_ref, low_ref, own_ref, other_ref):
    odd = (me_ref[0] // 8) % 2 == 1

    @pl.when(odd)
    def _():
        own_ref[...] = high_ref[0]
        other_ref[...] = low_ref[0]

    @pl.when(jnp.logical_not(odd))
    def _():
        own_ref[...] = low_ref[0]
        other_ref[...] = high_ref[0]


def arranged(me, high, low):
    return call(
        arranged_body, "arranged", [like(WINDOW, D), like(WINDOW, D)], 0, [me, high, low], 0, [], 12
    )


def sum_two(one, two, *ties):
    def body(one_ref, two_ref, *refs):
        refs[-1][...] = (one_ref[...].astype(F32) + two_ref[...].astype(F32)).astype(BF16)

    return pl.pallas_call(
        body,
        out_shape=like(WINDOW, D),
        in_specs=vmem(2) + [ANY_SPEC] * len(ties),
        out_specs=vmem(1)[0],
        compiler_params=params_call(12),
        cost_estimate=pl.CostEstimate(flops=1, bytes_accessed=1, transcendentals=0),
        name="sum_two",
    )(one, two, *ties)


def to_half(block, upper):
    return swap(block, 16, lambda d: (d // 16 == 1) != upper)


def adam_body(me_ref, *refs):
    terms = refs[:4]
    tail_ref, params_ref, first_ref, second_ref = refs[4:8]
    out_params, out_low, out_first, out_second, flat_ref, grad_ref, copy_ref, sems = refs[8:]
    me = me_ref[0]
    shift = me % TILE
    for upper in range(2):

        @pl.when(me // 16 == upper)
        def _():
            copies = [
                pltpu.make_async_copy(terms[2 * upper + z], copy_ref.at[z], sems.at[z])
                for z in range(2)
            ]
            for copy in copies:
                copy.start()
            for copy in copies:
                copy.wait()

    for j in range(6):
        terms_j = [copy_ref[z, :, 128 * j : 128 * (j + 1)].astype(F32) for z in range(2)]
        flat_ref[pl.ds(j, WINDOW, stride=6), :] = terms_j[0] + terms_j[1]
    grad_ref[...] = flat_ref[pl.ds(6 * shift, 1734), :]

    @pl.when(me == 31)
    def _():
        grad_ref[1542:1734, :] += tail_ref[...]

    grad = grad_ref[...]
    position = (
        me * 221952
        + lax.broadcasted_iota(jnp.int32, grad.shape, 0) * 128
        + lax.broadcasted_iota(jnp.int32, grad.shape, 1)
    )
    step_rate = step_rates(position)
    new_first = BETA_ONE * first_ref[...] + (1.0 - BETA_ONE) * grad
    new_second = BETA_TWO * second_ref[...] + (1.0 - BETA_TWO) * grad * grad
    fixed_first = new_first / (1.0 - BETA_ONE**STEP)
    fixed_second = new_second / (1.0 - BETA_TWO**STEP)
    params = params_ref[...]
    new_params = params - step_rate * (
        fixed_first / (jnp.sqrt(fixed_second) + ADAM_EPS) + DECAY * params
    )
    out_params[...] = new_params
    out_low[...] = new_params.astype(BF16)
    out_first[...] = new_first
    out_second[...] = new_second


def adam(me, terms, tail, params, first_moment, second_moment):
    lines = (1734, 128)
    args = [one.reshape(lines) for one in (params, first_moment, second_moment)]
    outs = pl.pallas_call(
        adam_body,
        out_shape=[
            jax.ShapeDtypeStruct(lines, F32),
            jax.ShapeDtypeStruct(lines, BF16),
            jax.ShapeDtypeStruct(lines, F32),
            jax.ShapeDtypeStruct(lines, F32),
        ],
        in_specs=[SMEM_SPEC] + [ANY_SPEC] * 4 + vmem(4),
        out_specs=vmem(4),
        scratch_shapes=[
            pltpu.VMEM((6 * WINDOW, 128), F32),
            pltpu.VMEM(lines, F32),
            pltpu.VMEM((2, WINDOW, D), BF16),
            pltpu.SemaphoreType.DMA((2,)),
        ],
        compiler_params=params_call(28),
        name="adam",
    )(me, *terms, tail, *args)
    return [one.reshape(-1) for one in outs]


def table_picks():
    col = jnp.arange(WIN * 384, dtype=jnp.int32)
    m = col % 384
    wanted = (m // WIN) * 23 + m % WIN - col // 384 + WIN - 1
    wanted = jnp.where(m < 276, wanted, -1)
    return (jnp.arange(TABLE_ROWS, dtype=jnp.int32)[None, :] == wanted[:, None]).astype(BF16)


def bias_of(table):
    return lax.dot_general(
        table, table_picks(), (((0,), (1,)), ((), ())), preferred_element_type=F32
    ).reshape(HEADS, WIN, 384)


def table_grad_of(strips):
    picked = lax.dot_general(
        strips.reshape(HEADS, WIN * 384),
        table_picks().astype(F32),
        (((1,), (0,)), ((), ())),
        precision=lax.Precision.HIGHEST,
        preferred_element_type=F32,
    )
    return picked.T


def shards(tokens, cotangent, valid, params, first_moment, second_moment):
    if lax.axis_size("img") != 16 or lax.axis_size("row") != 2:
        return shards_general(tokens, cotangent, valid, params, first_moment, second_moment)
    me = lax.axis_index(BOTH).astype(jnp.int32).reshape(1)
    flat_tokens = tokens.reshape(LEN, D)
    flat_cotangent = cotangent.reshape(LEN, D)
    own, spare = window_of(me, params)
    mask = jnp.tile(window_mask(lax.axis_index("row") * WIN), (1, 1, 4))
    amount = TABLE_ROWS * HEADS

    def bias_maker(tail):
        tail = tail.reshape(-1)
        bias = bias_of(tail[:amount].reshape(TABLE_ROWS, HEADS))
        return bias, tail[amount : amount + 13 * D].reshape(13, D).astype(F32), mask

    parts, places, (bias, vecs, mask), rows = gather_windows(
        own, spare, flat_tokens[:HALF], bias_maker
    )
    windows, laid, packed, attn, probs, near, far, w_qkv, w_proj = attend(
        me, flat_tokens, rows, vecs, bias, mask, parts, places
    )
    back = from_partner(far, "row", 0)
    hidden, active, grad_up, w_up, sums_up, w_down, low, low_three, high_three, send = feed(
        me, valid, flat_tokens, back, near, flat_cotangent, vecs, parts, places
    )
    core_three = swap(send, 2)
    grad_middle, far_grad, near_grad, sums_two = middle_grad(
        me, valid, flat_tokens, back, near, flat_cotangent, vecs, grad_up, w_up
    )
    far_grad = from_partner(far_grad, "row", 0)
    sent = sum_slots(2, [(high_three, 0), (core_three, 2)], near_grad)
    x_three = cross(sent, 4, 1)
    high, low_two, high_two, send = up_grad(me, hidden, grad_up, low, sent)
    core_two = swap(send, 2)
    sent = sum_slots(1, [(low_three, 1), (core_three, 1), (x_three, 1)], high)
    y_three = cross(sent, 1, 4)
    grad_attn, sums_proj, edge, low_one, high_one, send = proj_grad(
        me, near_grad, far_grad, attn, w_proj, high, sent
    )
    core_one = swap(send, 2)
    three = sum_slots(1, [(low_three, 0), (core_three, 0), (x_three, 0), (y_three, 0)], edge)
    sent = sum_slots(2, [(high_two, 0), (core_two, 2)], three)
    x_two = cross(sent, 4, 1)
    grad_packed, strips = unattend(me, packed, grad_attn, attn, probs, sent)
    sent = sum_slots(1, [(low_two, 1), (core_two, 1), (x_two, 1)], grad_packed)
    y_two = cross(sent, 1, 4)
    sent = sum_slots(2, [(high_one, 0), (core_one, 2)], sent)
    x_one = cross(sent, 4, 1)
    sums_qkv, low_zero, high_zero, send = qkv_grad(me, windows, edge, grad_packed, sent)
    core_zero = swap(send, 2)
    two = sum_slots(1, [(low_two, 0), (core_two, 0), (x_two, 0), (y_two, 0)], sums_qkv)
    upper, other = arranged(me, three, two)
    z_upper = swap(other, 8)
    sent = sum_slots(1, [(low_one, 1), (core_one, 1), (x_one, 1)], upper)
    y_one = cross(sent, 1, 4)
    sent = sum_slots(2, [(high_zero, 0), (core_zero, 2)], sent)
    x_zero = cross(sent, 4, 1)
    near_in, far_in, sums_one = token_grad(me, grad_packed, w_qkv, laid, vecs, sent)
    upper = sum_two(upper, z_upper, near_in)
    far_upper = to_half(upper, True)
    strips = gate(strips, upper)
    small = [
        table_grad_of(strips).reshape(-1),
        sums_qkv[:3].reshape(-1),
        sums_proj[0],
        sums_up[:4].reshape(-1),
        sums_up[4],
        sums_one[0],
        sums_one[1],
        sums_two[0],
        sums_two[1],
    ]
    small = jnp.concatenate(small)
    small = jnp.pad(small, (0, 32 * D - small.shape[0])).reshape(192, 128)
    small = small + swap(small, 2)
    sent = sum_slots(1, [(low_zero, 1), (core_zero, 1), (x_zero, 1)], small)
    y_zero = cross(sent, 1, 4)
    small = gate(small, sent)
    small = small + swap(small, 4)
    small = small + swap(small, 1)
    one = sum_slots(1, [(low_one, 0), (core_one, 0), (x_one, 0), (y_one, 0)], small)
    zero = sum_slots(1, [(low_zero, 0), (core_zero, 0), (x_zero, 0), (y_zero, 0)], one)
    lower, other = arranged(me, one, zero)
    z_lower = swap(other, 8)
    far_in = from_partner(gate(far_in, lower), "row", 0)
    output = block_output(me, flat_tokens, back, near, vecs, active, w_down, lower)
    lower = sum_two(lower, z_lower, output, far_in)
    far_lower = to_half(lower, False)
    small = gate(small, lower)
    small = small + to_half(small, True)
    small = small + swap(small, 8, lambda d: d // 8 == 2)
    input_grad = grad_middle + jnp.concatenate([far_in, near_in], 0).astype(F32)
    terms = [lower, far_lower, upper, far_upper]
    new = adam(me, terms, small, params, first_moment, second_moment)
    return (output.reshape(tokens.shape), input_grad.reshape(tokens.shape), *new)


def solution(mesh):
    return jax.shard_map(
        shards,
        mesh=mesh,
        in_specs=(
            P("img", "row", None, None),
            P("img", "row", None, None),
            P("img"),
            P(("img", "row")),
            P(("img", "row")),
            P(("img", "row")),
        ),
        out_specs=(
            P("img", "row", None, None),
            P("img", "row", None, None),
            P(("img", "row")),
            P(("img", "row")),
            P(("img", "row")),
            P(("img", "row")),
        ),
        check_vma=False,
    )
```

```python
import functools
import math

import jax
import jax.numpy as jnp
from jax import lax
from jax.experimental import pallas as pl
from jax.experimental.pallas import tpu as pltpu
from jax.sharding import PartitionSpec as P

D = 768
FF = 3072
HEADS = 24
HEAD_DIM = 32
WIN = 12
SHIFT = 6
SIDE = 24
STEP = 4
TABLE_ROWS = 529


EPSILON = 1e-05
MASKED = -100.0
DECAY = 0.05
ADAM_EPS = 1e-08
BETA_ONE = 0.5
BETA_TWO = 0.5


def from_partner(block, axis, apart):
    count = lax.axis_size(axis)
    route = []
    for low in range(count):
        high = low | 1 << apart
        if high != low and high < count:
            route += [(low, high), (high, low)]
    return lax.ppermute(block, axis, route)


def piece_shapes():
    return [
        (D, 3 * D),
        (D, D),
        (D, FF),
        (FF, D),
        (TABLE_ROWS, HEADS),
        (3 * D,),
        (D,),
        (FF,),
        (D,),
        (D,),
        (D,),
        (D,),
        (D,),
    ]


def unpack(flat_vec):
    pieces = []
    offset = 0
    for shape_one in piece_shapes():
        amount = math.prod(shape_one)
        pieces.append(lax.slice_in_dim(flat_vec, offset, offset + amount).reshape(shape_one))
        offset = offset + amount
    return pieces


def step_rates(position):
    rate_list = [
        D ** (-0.5),
        4.0 * D ** (-0.5),
        D ** (-0.5),
        FF ** (-0.5),
        1.0,
        0.3,
        0.3,
        0.3,
        0.3,
        0.4,
        0.3,
        0.4,
        0.3,
    ]
    result = jnp.zeros(position.shape, jnp.float32)
    offset = 0
    for shape_one, rate_one in zip(piece_shapes(), rate_list):
        amount = math.prod(shape_one)
        inside = (position >= offset) & (position < offset + amount)
        result = jnp.where(inside, jnp.float32(rate_one), result)
        offset = offset + amount
    return result


def layer_norm(values, gain_vec, shift_vec):
    centre = jnp.mean(values, -1, keepdims=True)
    centred = values - centre
    spread = jnp.mean(centred * centred, -1, keepdims=True)
    return centred * lax.rsqrt(spread + EPSILON) * gain_vec + shift_vec


def region_of(coord):
    return jnp.where(coord < SIDE - WIN, 0, jnp.where(coord < SIDE - SHIFT, 1, 2))


def relative_index():
    cell_index = jnp.arange(WIN * WIN, dtype=jnp.int32)
    row_part = cell_index // WIN
    col_part = cell_index % WIN
    return (row_part[:, None] - row_part[None, :] + WIN - 1) * (2 * WIN - 1) + (
        col_part[:, None] - col_part[None, :] + WIN - 1
    )


def window_mask(row_first):
    row_coord = row_first + jnp.arange(WIN, dtype=jnp.int32)
    col_coord = jnp.arange(SIDE, dtype=jnp.int32)
    region_ids = 3 * region_of(row_coord)[:, None] + region_of(col_coord)[None, :]
    region_ids = (
        region_ids.reshape(WIN, SIDE // WIN, WIN).transpose(1, 0, 2).reshape(SIDE // WIN, WIN * WIN)
    )
    same = region_ids[:, :, None] == region_ids[:, None, :]
    return jnp.where(same, 0.0, MASKED).astype(jnp.float32)


def to_windows(grid_rows):
    img_count = grid_rows.shape[0]
    width = grid_rows.shape[-1]
    shaped = grid_rows.reshape(img_count, WIN, SIDE // WIN, WIN, width).transpose(0, 2, 1, 3, 4)
    return shaped.reshape(img_count * (SIDE // WIN), WIN * WIN, width)


def from_windows(window_rows, img_count):
    width = window_rows.shape[-1]
    shaped = window_rows.reshape(img_count, SIDE // WIN, WIN, WIN, width).transpose(0, 2, 1, 3, 4)
    return shaped.reshape(img_count, WIN, SIDE, width)


BF16 = jnp.bfloat16
F32 = jnp.float32
BOTH = ("img", "row")
ROWS = 9248
TILE = 16
WINDOW = 304
WIDE = 2 * D // 4
VMEM_MOST = 60 * 1024 * 1024


def contract_rows(left_op, right_op):
    summed_dims = tuple(range(left_op.ndim - 1))
    return lax.dot_general(
        left_op,
        right_op,
        ((summed_dims, summed_dims), ((), ())),
        preferred_element_type=jnp.float32,
    )


def times_transposed(left_op, right_op):
    return lax.dot_general(
        left_op,
        right_op,
        (((left_op.ndim - 1,), (1,)), ((), ())),
        preferred_element_type=jnp.float32,
    )


def scores_of(queries, keys_all, bias_full, region_mask):
    raw_scores = jnp.einsum(
        "wqhd,wkhd->whqk", queries, keys_all, preferred_element_type=jnp.float32
    )
    return raw_scores * HEAD_DIM ** (-0.5) + bias_full[None] + region_mask[:, None]


def shards_general(tokens, cotangent, valid, params, first_moment, second_moment):
    img_count = tokens.shape[0]
    win_count = img_count * (SIDE // WIN)
    tile_len = WIN * WIN
    gathered = lax.all_gather(params.astype(jnp.bfloat16), ("img", "row"), axis=0, tiled=True)
    (
        w_qkv,
        w_proj,
        w_up,
        w_down,
        bias_table,
        b_qkv,
        b_proj,
        b_up,
        b_down,
        gain_one,
        shift_one,
        gain_two,
        shift_two,
    ) = unpack(gathered)
    images = tokens.astype(jnp.float32)
    normed, norm_pull = jax.vjp(
        layer_norm, images, gain_one.astype(jnp.float32), shift_one.astype(jnp.float32)
    )
    normed_low = normed.astype(jnp.bfloat16)
    incoming = from_partner(normed_low[:, :SHIFT], "row", 0)
    shifted = jnp.roll(jnp.concatenate([normed_low[:, SHIFT:], incoming], 1), -SHIFT, 2)
    windows = to_windows(shifted)
    packed = (
        jnp.dot(windows, w_qkv, preferred_element_type=jnp.float32) + b_qkv.astype(jnp.float32)
    ).astype(jnp.bfloat16)
    heads_view = packed.reshape(win_count, tile_len, 3, HEADS, HEAD_DIM)
    queries = heads_view[:, :, 0]
    keys_all = heads_view[:, :, 1]
    values_all = heads_view[:, :, 2]
    rel_index = relative_index()
    bias_full = bias_table.astype(jnp.float32)[rel_index].transpose(2, 0, 1)
    region_mask = jnp.tile(window_mask(lax.axis_index("row") * WIN), (img_count, 1, 1))
    scores = scores_of(queries, keys_all, bias_full, region_mask)
    row_top = jnp.max(scores, -1, keepdims=True)
    exponent = jnp.exp(scores - row_top)
    row_total = jnp.sum(exponent, -1, keepdims=True)
    log_total = row_top + jnp.log(row_total)
    attn_probs = (exponent / row_total).astype(jnp.bfloat16)
    attn_mixed = jnp.einsum(
        "whqk,wkhd->wqhd", attn_probs, values_all, preferred_element_type=jnp.float32
    )
    attn_mixed = attn_mixed.astype(jnp.bfloat16).reshape(win_count, tile_len, D)
    branch = (
        jnp.dot(attn_mixed, w_proj, preferred_element_type=jnp.float32) + b_proj.astype(jnp.float32)
    ).astype(jnp.bfloat16)
    branch_grid = jnp.roll(from_windows(branch, img_count), SHIFT, 2)
    returned = from_partner(branch_grid[:, SHIFT:], "row", 0)
    middle = images + jnp.concatenate([returned, branch_grid[:, :SHIFT]], 1).astype(jnp.float32)
    normed_two, norm_two_pull = jax.vjp(
        layer_norm, middle, gain_two.astype(jnp.float32), shift_two.astype(jnp.float32)
    )
    hidden_in = normed_two.astype(jnp.bfloat16)
    upward = jnp.dot(hidden_in, w_up, preferred_element_type=jnp.float32) + b_up.astype(jnp.float32)
    active_full, gelu_pull = jax.vjp(lambda values: jax.nn.gelu(values, approximate=False), upward)
    active = active_full.astype(jnp.bfloat16)
    output = (
        middle
        + jnp.dot(active, w_down, preferred_element_type=jnp.float32)
        + b_down.astype(jnp.float32)
    )
    regathered = lax.all_gather(params.astype(jnp.bfloat16), ("img", "row"), axis=0, tiled=True)
    fresh = unpack(regathered)
    w_qkv, w_proj, w_up, w_down = (fresh[0], fresh[1], fresh[2], fresh[3])
    grad_out = cotangent * valid.astype(jnp.bfloat16)[:, None, None, None]
    grad_w_down = contract_rows(active, grad_out)
    grad_b_down = jnp.sum(grad_out.astype(jnp.float32), (0, 1, 2))
    grad_active = times_transposed(grad_out, w_down)
    grad_up = gelu_pull(grad_active)[0].astype(jnp.bfloat16)
    grad_w_up = contract_rows(hidden_in, grad_up)
    grad_b_up = jnp.sum(grad_up.astype(jnp.float32), (0, 1, 2))
    grad_hidden = times_transposed(grad_up, w_up)
    grad_middle_ln, grad_gain_two, grad_shift_two = norm_two_pull(grad_hidden)
    grad_middle = grad_out.astype(jnp.float32) + grad_middle_ln
    middle_low = grad_middle.astype(jnp.bfloat16)
    arrived = from_partner(middle_low[:, :SHIFT], "row", 0)
    grad_grid = jnp.roll(jnp.concatenate([middle_low[:, SHIFT:], arrived], 1), -SHIFT, 2)
    grad_branch = to_windows(grad_grid)
    grad_w_proj = contract_rows(attn_mixed, grad_branch)
    grad_b_proj = jnp.sum(grad_branch.astype(jnp.float32), (0, 1))
    grad_attn = times_transposed(grad_branch, w_proj).astype(jnp.bfloat16)
    grad_attn = grad_attn.reshape(win_count, tile_len, HEADS, HEAD_DIM)
    again_scores = scores_of(queries, keys_all, bias_full, region_mask)
    again_probs = jnp.exp(again_scores - log_total)
    grad_values = jnp.einsum(
        "whqk,wqhd->wkhd",
        again_probs.astype(jnp.bfloat16),
        grad_attn,
        preferred_element_type=jnp.float32,
    )
    grad_probs = jnp.einsum(
        "wqhd,wkhd->whqk", grad_attn, values_all, preferred_element_type=jnp.float32
    )
    grad_scores = again_probs * (grad_probs - jnp.sum(again_probs * grad_probs, -1, keepdims=True))
    pair_sums = jnp.sum(grad_scores, 0).transpose(1, 2, 0).reshape(tile_len * tile_len, HEADS)
    grad_table = jax.ops.segment_sum(pair_sums, rel_index.reshape(-1), TABLE_ROWS)
    grad_raw = (grad_scores * HEAD_DIM ** (-0.5)).astype(jnp.bfloat16)
    grad_queries = jnp.einsum(
        "whqk,wkhd->wqhd", grad_raw, keys_all, preferred_element_type=jnp.float32
    )
    grad_keys = jnp.einsum("whqk,wqhd->wkhd", grad_raw, queries, preferred_element_type=jnp.float32)
    grad_packed = jnp.stack([grad_queries, grad_keys, grad_values], 2).astype(jnp.bfloat16)
    grad_packed = grad_packed.reshape(win_count, tile_len, 3 * D)
    grad_w_qkv = contract_rows(windows, grad_packed)
    grad_b_qkv = jnp.sum(grad_packed.astype(jnp.float32), (0, 1))
    grad_windows = times_transposed(grad_packed, w_qkv).astype(jnp.bfloat16)
    grad_shifted = jnp.roll(from_windows(grad_windows, img_count), SHIFT, 2)
    arrived_two = from_partner(grad_shifted[:, SHIFT:], "row", 0)
    grad_normed = jnp.concatenate([arrived_two, grad_shifted[:, :SHIFT]], 1).astype(jnp.float32)
    grad_images_ln, grad_gain_one, grad_shift_one = norm_pull(grad_normed)
    input_grad = grad_middle + grad_images_ln
    grad_list = [
        grad_w_qkv,
        grad_w_proj,
        grad_w_up,
        grad_w_down,
        grad_table,
        grad_b_qkv,
        grad_b_proj,
        grad_b_up,
        grad_b_down,
        grad_gain_one,
        grad_shift_one,
        grad_gain_two,
        grad_shift_two,
    ]
    grad_flat = jnp.concatenate([grad_one.reshape(-1) for grad_one in grad_list])
    grad_flat = jnp.pad(grad_flat, (0, gathered.shape[0] - grad_flat.shape[0]))
    grad_shard = lax.psum_scatter(grad_flat, ("img", "row"), scatter_dimension=0, tiled=True)
    shard_len = params.shape[0]
    position = lax.axis_index(("img", "row")) * shard_len + jnp.arange(shard_len, dtype=jnp.int32)
    step_rate = step_rates(position)
    new_first = BETA_ONE * first_moment + (1.0 - BETA_ONE) * grad_shard
    new_second = BETA_TWO * second_moment + (1.0 - BETA_TWO) * grad_shard * grad_shard
    fixed_first = new_first / (1.0 - BETA_ONE**STEP)
    fixed_second = new_second / (1.0 - BETA_TWO**STEP)
    new_params = params - step_rate * (
        fixed_first / (jnp.sqrt(fixed_second) + ADAM_EPS) + DECAY * params
    )
    return (
        output.astype(jnp.bfloat16),
        input_grad,
        new_params,
        new_params.astype(jnp.bfloat16),
        new_first,
        new_second,
    )


BF16 = jnp.bfloat16
F32 = jnp.float32
BOTH = ("img", "row")
TILE = 16
WINDOW = 304
LEN = 2 * WIN * WIN
QUADS = HEADS // 4
SPAN = 4 * WIN * WIN


def swap(block, mask, only=None):
    count = lax.axis_size(BOTH)
    route = [(d, d ^ mask) for d in range(count) if only is None or only(d)]
    return lax.ppermute(block, BOTH, route)


def params_call(mebibytes):
    return pltpu.CompilerParams(vmem_limit_bytes=mebibytes << 20)


def vmem(count):
    return [pl.BlockSpec(memory_space=pltpu.VMEM)] * count


SMEM_SPEC = pl.BlockSpec(memory_space=pltpu.SMEM)
ANY_SPEC = pl.BlockSpec(memory_space=pl.ANY)


def first_tile(device):
    return (289 * device) // TILE


def prep_body(me_ref, own_ref, out_ref, spare_ref, extra_ref, wide_ref):
    shift = me_ref[0] % TILE
    wide_ref[0:96] = jnp.zeros((96, 128), F32)
    wide_ref[1824:1920] = jnp.zeros((96, 128), F32)
    wide_ref[96:1830] = own_ref[...]
    for j in range(6):
        picked = wide_ref[pl.ds(96 - 6 * shift + j, WINDOW, stride=6), :]
        out_ref[:, 128 * j : 128 * (j + 1)] = picked.astype(BF16)
        spare_ref[:, 128 * j : 128 * (j + 1)] = picked.astype(BF16)
        extra_ref[:, 128 * j : 128 * (j + 1)] = picked.astype(BF16)


def window_of(me, own_flat):
    return pl.pallas_call(
        prep_body,
        out_shape=[jax.ShapeDtypeStruct((WINDOW, D), BF16)] * 3,
        in_specs=[SMEM_SPEC] + vmem(1),
        out_specs=vmem(3),
        scratch_shapes=[pltpu.VMEM((1920, 128), F32)],
        compiler_params=params_call(8),
        name="own_window",
    )(me, own_flat.reshape(-1, 128))


def mixer(groups, per):
    size = groups * per
    row = lax.broadcasted_iota(jnp.int32, (size, size), 0)
    col = lax.broadcasted_iota(jnp.int32, (size, size), 1)
    return (col == groups * (row % per) + row // per).astype(F32).astype(BF16)


def unmixer(groups, per):
    size = groups * per
    row = lax.broadcasted_iota(jnp.int32, (size, size), 0)
    col = lax.broadcasted_iota(jnp.int32, (size, size), 1)
    return (row == groups * (col % per) + col // per).astype(F32).astype(BF16)


def plane_rows(plane):
    low = first_tile(8 * plane) * TILE
    high = first_tile(8 * plane + 7) * TILE + WINDOW
    return low, high


def gate(value, *others):
    def body(*refs):
        pass

    return pl.pallas_call(
        body,
        out_shape=jax.ShapeDtypeStruct(value.shape, value.dtype),
        in_specs=[ANY_SPEC] * (1 + len(others)),
        out_specs=ANY_SPEC,
        input_output_aliases={0: 0},
        cost_estimate=cost(0),
        name="gate",
    )(value, *others)


def cross(block, zero, one):
    count = lax.axis_size(BOTH)
    return lax.ppermute(block, BOTH, [(d, d ^ (one if d & 2 else zero)) for d in range(count)])


def gather_windows(own, spare, extra, rows, bias_maker):
    me = lax.axis_index(BOTH)
    got = {0: own}
    first, second, third = {}, {}, {}
    tail = own[WINDOW - 32 :]
    have = 31

    def hop(tail, have, mask):
        tail = jnp.where(me & have == have, tail, jnp.zeros_like(tail))
        return tail + swap(tail, mask, lambda d: d & have == have), have ^ mask

    for mask in (2, 4, 1):
        tail, have = hop(tail, have, mask)

    def exchange(z):
        first[z] = cross(got[z], 4, 1)
        second[z] = cross(got[z], 1, 4)
        third[z] = cross(first[z], 1, 4)

    got[8] = swap(own, 8)
    exchange(0)
    got[16] = swap(gate(spare, first[0]), 16)
    got[8] = gate(got[8], first[0], second[0], tail)
    exchange(8)
    from_three = lambda d: d // 8 == 3
    tail = jnp.where(me // 8 == 3, tail, jnp.zeros_like(tail))
    tail = tail + swap(tail, 8, from_three) + swap(tail, 16, from_three) + swap(tail, 24, from_three)
    got_rows = from_partner(gate(rows, second[0]), "row", 0)
    got[24] = swap(gate(extra, got[16]), 24)
    got[16] = gate(got[16], first[8], second[8], third[0], tail)
    exchange(16)
    made = bias_maker(tail)
    got[24] = gate(got[24], first[16], second[16], third[8], *made, got_rows)
    exchange(24)
    blocks, places = [], []
    for z in (0, 8, 16, 24):
        four = [got[z], first[z], second[z], third[z]]
        masks = [(z, z), (z | 4, z | 1), (z | 1, z | 4), (z | 5, z | 5)]
        for n in range(4):
            places.append((len(blocks) + n, None, *masks[n]))
        other = swap(stacked(four), 2)
        for n, (zero, one) in enumerate(masks):
            places.append((len(blocks) + 4, n, one | 2, zero | 2))
        blocks += [*four, other]
    return blocks, places, made, got_rows


def stacked_body(*refs):
    for i, ref in enumerate(refs[:-1]):
        refs[-1][i] = ref[...]


def stacked(blocks):
    return pl.pallas_call(
        stacked_body,
        out_shape=like(len(blocks), WINDOW, D),
        in_specs=vmem(len(blocks)),
        out_specs=vmem(1)[0],
        compiler_params=params_call(4),
        cost_estimate=cost(0),
        name="stacked",
    )(*blocks)


def load_windows(me, parts, places, first, last, flat_ref):
    base = first_tile(first) * TILE
    for device in (first, 16):
        if first <= device <= last:
            at = first_tile(device) * TILE - base
            flat_ref[at : at + TILE] = jnp.zeros((TILE, D), BF16)

    def each(act):
        for block, slot, zero, one in places:
            device = me ^ jnp.where((me & 2) == 0, zero, one)
            start = pl.multiple_of(first_tile(device) * TILE - base, TILE)
            part = parts[block] if slot is None else parts[block].at[slot]

            @pl.when((device >= first) & (device <= last))
            def _():
                act(part, start)

    def main(part, start):
        flat_ref[pl.ds(start + TILE, WINDOW - TILE)] = part[TILE:WINDOW]

    def edge(part, start):
        flat_ref[pl.ds(start, TILE)] += part[0:TILE]

    each(main)
    each(edge)


def flat_scratch(first, last):
    return pltpu.VMEM(
        (first_tile(last) * TILE + WINDOW - first_tile(first) * TILE, D), BF16
    )


def unmix_rows(flat_ref, out_ref, base, groups, per, steps):
    mix = mixer(groups, per)
    size = groups * per
    for t in range(steps):
        rows = flat_ref[base + size * t : base + size * (t + 1)]
        out = jnp.dot(mix, rows, preferred_element_type=F32).astype(BF16)
        for j in range(groups):
            out_ref[j, per * t : per * (t + 1)] = out[per * j : per * (j + 1)]


def mix_rows(in_ref, flat_ref, base, groups, per, steps):
    mix = unmixer(groups, per)
    size = groups * per
    for t in range(steps):
        rows = jnp.concatenate([in_ref[j, per * t : per * (t + 1)] for j in range(groups)], 0)
        out = jnp.dot(mix, rows, preferred_element_type=F32).astype(BF16)
        flat_ref[base + size * t : base + size * (t + 1)] = out


def cut_windows(me, plane, flat_ref, base, keeps, sends):
    for flip in (2, 0):
        for s in range(4):
            first = jnp.where(((me ^ flip) & 2) == 0, 4, 1)
            away = (first if s & 2 else 0) + (5 - first if s & 1 else 0)
            device = 8 * plane + ((me & 7) ^ (away | flip))
            start = pl.multiple_of(first_tile(device) * TILE - base, TILE)
            window = flat_ref[pl.ds(start, WINDOW)]
            (sends if flip else keeps)[s // 2][s % 2] = window


def cost(microseconds):
    return pl.CostEstimate(
        flops=int(1e9 * microseconds),
        bytes_accessed=int(3.2e6 * microseconds),
        transcendentals=0,
    )


WINDOWS = [jax.ShapeDtypeStruct((2, WINDOW, D), BF16)] * 4


def like(*shape, dtype=BF16):
    return jax.ShapeDtypeStruct(shape, dtype)


def call(body, name, ins, outs, scratch, limit, ties=(), us=0, far=0):
    n_in, n_tie, n_out = len(ins), len(ties), len(outs)
    first_out = n_in + n_tie

    def wrapped(*refs):
        body(*refs[:n_in], *refs[first_out : first_out + n_out], *refs[first_out + n_out + 1 :])
        token_ref = refs[first_out + n_out]
        token_ref[...] = jnp.zeros_like(token_ref)

    specs = [SMEM_SPEC if one.dtype == jnp.int32 else vmem(1)[0] for one in ins]
    return pl.pallas_call(
        wrapped,
        out_shape=[*outs, like(8, 128, dtype=F32)],
        in_specs=specs + vmem(n_tie),
        out_specs=vmem(n_out - far)
        + [pl.BlockSpec(memory_space=pltpu.HBM)] * far
        + vmem(1),
        scratch_shapes=scratch,
        compiler_params=params_call(limit),
        cost_estimate=cost(us),
        name=name,
    )(*ins, *ties)


def pause(*ties, us=4):
    return call(lambda: None, "pause", [], [], [], 4, ties, us)[0]


def normal_parts(values):
    centre = jnp.mean(values, -1, keepdims=True)
    centred = values - centre
    spread = jnp.mean(centred * centred, -1, keepdims=True)
    scale = lax.rsqrt(spread + EPSILON)
    return centred * scale, scale


def normal_pull(n, scale, grad, gain):
    e = grad * gain
    return scale * (
        e - jnp.mean(e, -1, keepdims=True) - n * jnp.mean(e * n, -1, keepdims=True)
    )


def over_heads(block):
    head = lax.broadcasted_iota(jnp.int32, block.shape, 1) // HEAD_DIM
    return jnp.concatenate([jnp.where(head == h, block, jnp.zeros_like(block)) for h in range(4)], 0)


def own_columns(block):
    head = lax.broadcasted_iota(jnp.int32, (144, 128), 1) // HEAD_DIM
    out = block[0:144]
    for h in range(1, 4):
        out = jnp.where(head == h, block[144 * h : 144 * (h + 1)], out)
    return out


def contract(one, two, a, b):
    return lax.dot_general(one, two, (((a,), (b,)), ((), ())), preferred_element_type=F32)


def lay(out_ref, near, far):
    for i in range(WIN):
        ref, k = (near, 24 * i) if i < SHIFT else (far, 24 * (i - SHIFT))
        out_ref[12 * i : 12 * i + 12] = ref[k + 6 : k + 18]
        out_ref[144 + 12 * i : 150 + 12 * i] = ref[k + 18 : k + 24]
        out_ref[150 + 12 * i : 156 + 12 * i] = ref[k : k + 6]


def unlay(ref, near, far):
    for i in range(WIN):
        out_ref, k = (near, 24 * i) if i < SHIFT else (far, 24 * (i - SHIFT))
        out_ref[k + 6 : k + 18] = ref[12 * i : 12 * i + 12]
        out_ref[k + 18 : k + 24] = ref[144 + 12 * i : 150 + 12 * i]
        out_ref[k : k + 6] = ref[150 + 12 * i : 156 + 12 * i]


HALF = LEN // 2
LAY_SCRATCH = [pltpu.VMEM((LEN, D), F32), pltpu.VMEM((HALF, D), F32), pltpu.VMEM((HALF, D), F32)]


def attend_body(places, me_ref, tokens_ref, rows_ref, vecs_ref, strips_ref, mask_ref, *refs):
    parts = refs[:20]
    windows_ref, packed_ref, attn_ref, probs_ref, near_ref, far_ref, proj_ref, qkv_out, laid_out = refs[20:29]
    flat_ref, wide_ref, one_ref, two_ref, bias_ref, qkv_ref, laid_ref, sems = refs[29:]
    load_windows(me_ref[0], parts, places, 0, 10, flat_ref)
    one_ref[...] = tokens_ref[HALF:LEN].astype(F32)
    two_ref[...] = rows_ref[...].astype(F32)
    lay(wide_ref, one_ref, two_ref)
    laid = wide_ref[...]
    laid_ref[...] = laid.astype(BF16)
    n, _ = normal_parts(laid)
    windows_ref[...] = (n * vecs_ref[9:10] + vecs_ref[10:11]).astype(BF16)
    unmix_rows(flat_ref, qkv_ref, 0, 3, 64, 12)
    copies = [
        pltpu.make_async_copy(qkv_ref, qkv_out, sems.at[0]),
        pltpu.make_async_copy(laid_ref, laid_out, sems.at[1]),
    ]
    for copy in copies:
        copy.start()
    proj_ref[...] = flat_ref[2304:3072]

    def project(j, carry):
        packed_ref[j] = (
            jnp.dot(windows_ref[...], qkv_ref[j], preferred_element_type=F32)
            + vecs_ref[pl.ds(j, 1)]
        ).astype(BF16)
        return carry

    lax.fori_loop(0, 3, project, 0)

    def quad(g, carry):
        lanes = pl.ds(pl.multiple_of(128 * g, 128), 128)
        for h in range(4):
            for i in range(WIN):
                low = 12 * (11 - i)
                bias_ref[12 * i : 12 * i + 12, 144 * h : 144 * (h + 1)] = strips_ref[
                    4 * g + h, 0:12, low : low + 144
                ]
        for w in range(2):
            rows = pl.ds(144 * w, 144)
            queries = over_heads(packed_ref[0, rows, lanes])
            scores = contract(packed_ref[1, rows, lanes], queries, 1, 1)
            scores = scores * HEAD_DIM ** (-0.5) + bias_ref[...] + mask_ref[w]
            top = jnp.max(scores, 0, keepdims=True)
            exponent = jnp.exp(scores - top)
            total = jnp.sum(exponent, 0, keepdims=True)
            probs = (exponent * (1.0 / total)).astype(BF16)
            probs_ref[2 * g + w] = probs
            mixed = contract(probs, packed_ref[2, rows, lanes], 0, 0)
            attn_ref[rows, lanes] = own_columns(mixed).astype(BF16)
        return carry

    lax.fori_loop(0, QUADS, quad, 0)
    wide_ref[...] = (
        jnp.dot(attn_ref[...], proj_ref[...], preferred_element_type=F32) + vecs_ref[3:4]
    )
    unlay(wide_ref, one_ref, two_ref)
    near_ref[...] = one_ref[...].astype(BF16)
    far_ref[...] = two_ref[...].astype(BF16)
    for copy in copies:
        copy.wait()


def attend(me, tokens, rows, vecs, bias, mask, parts, places):
    return call(
        functools.partial(attend_body, places),
        "attention_forward",
        [me, tokens, rows, vecs, bias, mask, *parts],
        [
            like(LEN, D),
            like(3, LEN, D),
            like(LEN, D),
            like(2 * QUADS, 144, SPAN),
            like(HALF, D),
            like(HALF, D),
            like(D, D),
            like(3, D, D),
            like(LEN, D),
        ],
        [flat_scratch(0, 10)]
        + LAY_SCRATCH
        + [
            pltpu.VMEM((144, SPAN), F32),
            pltpu.VMEM((3, D, D), BF16),
            pltpu.VMEM((LEN, D), BF16),
            pltpu.SemaphoreType.DMA((2,)),
        ],
        18,
        far=2,
    )


def middle_of(tokens_ref, back_ref, near_ref):
    branch = jnp.concatenate([back_ref[...].astype(F32), near_ref[...].astype(F32)], 0)
    return tokens_ref[...].astype(F32) + branch


def feed_weights_body(places, me_ref, *refs):
    parts = refs[:20]
    up_ref, down_ref, flat_ref = refs[20:]
    load_windows(me_ref[0], parts, places, 10, 31, flat_ref)
    base = first_tile(10) * TILE
    unmix_rows(flat_ref, up_ref, 3072 - base, 4, 48, 16)
    down_ref[...] = flat_ref[6144 - base : 6144 - base + FF]


def feed_weights(me, parts, places, *ties):
    return call(
        functools.partial(feed_weights_body, places),
        "feed_weights",
        [me, *parts],
        [like(4, D, D), like(FF, D)],
        [flat_scratch(10, 31)],
        14,
        ties,
    )


def feed_body(me_ref, valid_ref, tokens_ref, back_ref, near_ref, cotangent_ref, vecs_ref, up_ref, down_ref, hidden_ref, active_ref, gradup_ref, sums_ref, low_ref, low_keep, high_keep, low_send, high_send, grad_ref):
    me = me_ref[0]
    n, _ = normal_parts(middle_of(tokens_ref, back_ref, near_ref))
    hidden_ref[...] = (n * vecs_ref[11:12] + vecs_ref[12:13]).astype(BF16)
    grad_out = cotangent_ref[...] * valid_ref[0].astype(F32).astype(BF16)
    grad_ref[3072:3104] = jnp.zeros((32, D), BF16)

    def step(j, carry):
        at = pl.multiple_of(D * j, D)
        down = down_ref[pl.ds(at, D)]
        upward = jnp.dot(hidden_ref[...], up_ref[j], preferred_element_type=F32)
        upward = upward + vecs_ref[pl.ds(4 + j, 1)]
        grad_active = contract(grad_out, down, 1, 1)
        share = 0.5 * (1.0 + lax.erf(upward * (0.5**0.5)))
        density = jnp.exp(-0.5 * upward * upward) * ((2.0 * math.pi) ** (-0.5))
        active = (upward * share).astype(BF16)
        grad_up = (grad_active * (share + upward * density)).astype(BF16)
        active_ref[j] = active
        gradup_ref[j] = grad_up
        sums_ref[pl.ds(j, 1)] = jnp.sum(grad_up.astype(F32), 0, keepdims=True)
        grad_ref[pl.ds(at, D)] = contract(active, grad_out, 0, 0).astype(BF16)
        return carry

    lax.fori_loop(0, 4, step, 0)
    cut_windows(me, 3, grad_ref, 6144, (low_keep, high_keep), (low_send, high_send))
    low_ref[...] = grad_ref[0:800]
    sums_ref[4:5] = jnp.sum(grad_out.astype(F32), 0, keepdims=True)


def feed(me, valid, tokens, back, near, cotangent, vecs, w_up, w_down):
    return call(
        feed_body,
        "feed_forward",
        [me, valid, tokens, back, near, cotangent, vecs, w_up, w_down],
        [
            like(LEN, D),
            like(4, LEN, D),
            like(4, LEN, D),
            like(8, D, dtype=F32),
            like(800, D),
            *WINDOWS,
        ],
        [pltpu.VMEM((3104, D), BF16)],
        16,
    )


def middle_body(me_ref, valid_ref, tokens_ref, back_ref, near_ref, cotangent_ref, vecs_ref, gradup_ref, up_ref, grad_ref, far_out, near_out, sums_ref):
    n, scale = normal_parts(middle_of(tokens_ref, back_ref, near_ref))
    grad_hidden = contract(gradup_ref[0], up_ref[0], 1, 1)
    for j in range(1, 4):
        grad_hidden = grad_hidden + contract(gradup_ref[j], up_ref[j], 1, 1)
    sums_ref[0:1] = jnp.sum(grad_hidden * n, 0, keepdims=True)
    sums_ref[1:2] = jnp.sum(grad_hidden, 0, keepdims=True)
    grad_out = (cotangent_ref[...] * valid_ref[0].astype(F32).astype(BF16)).astype(F32)
    grad = grad_out + normal_pull(n, scale, grad_hidden, vecs_ref[11:12])
    grad_ref[...] = grad
    far_out[...] = grad[:HALF].astype(BF16)
    near_out[...] = grad[HALF:].astype(BF16)


def middle_grad(me, valid, tokens, back, near, cotangent, vecs, grad_up, w_up):
    return call(
        middle_body,
        "middle_grad",
        [me, valid, tokens, back, near, cotangent, vecs, grad_up, w_up],
        [like(LEN, D, dtype=F32), like(HALF, D), like(HALF, D), like(8, D, dtype=F32)],
        [],
        12,
    )


def up_body(me_ref, hidden_ref, gradup_ref, low_ref, proj_ref, low_keep, high_keep, low_send, high_send, quad_ref, flat_ref):
    me = me_ref[0]

    def step(j, carry):
        quad_ref[j] = contract(hidden_ref[...], gradup_ref[j], 0, 0).astype(BF16)
        return carry

    lax.fori_loop(0, 4, step, 0)
    flat_ref[3072:3872] = low_ref[...]
    mix_rows(quad_ref, flat_ref, 0, 4, 48, 16)
    cut_windows(me, 2, flat_ref, 3072, (low_keep, high_keep), (low_send, high_send))
    proj_ref[...] = flat_ref[0:1552]


def up_grad(me, hidden, grad_up, low, *ties):
    return call(
        up_body,
        "up_grad",
        [me, hidden, grad_up, low],
        [like(1552, D), *WINDOWS],
        [pltpu.VMEM((4, D, D), BF16), pltpu.VMEM((3872, D), BF16)],
        16,
        ties,
    )


def proj_body(me_ref, near_ref, far_ref, attn_ref, proj_ref, high_ref, back_ref, sums_ref, edge_ref, low_keep, high_keep, low_send, high_send, flat_ref, wide_ref, one_ref, two_ref):
    me = me_ref[0]
    one_ref[...] = near_ref[...].astype(F32)
    two_ref[...] = far_ref[...].astype(F32)
    lay(wide_ref, one_ref, two_ref)
    grad = wide_ref[...].astype(BF16)
    flat_ref[0:768] = contract(attn_ref[...], grad, 0, 0).astype(BF16)
    flat_ref[768:2320] = high_ref[...]
    cut_windows(me, 1, flat_ref, 2304, (low_keep, high_keep), (low_send, high_send))
    edge_ref[...] = flat_ref[0:16]
    back_ref[...] = contract(grad, proj_ref[...], 1, 1).astype(BF16)
    sums_ref[0:1] = jnp.sum(grad.astype(F32), 0, keepdims=True)


def proj_grad(me, near, far, attn, w_proj, high, *ties):
    return call(
        proj_body,
        "proj_grad",
        [me, near, far, attn, w_proj, high],
        [like(LEN, D), like(8, D, dtype=F32), like(16, D), *WINDOWS],
        [pltpu.VMEM((2320, D), BF16)] + LAY_SCRATCH,
        12,
        ties,
    )


def unattend_quads(quads, packed_ref, grad_ref, attn_ref, probs_ref, back_ref, strips_ref, pairs_ref):
    strips_ref[...] = jnp.zeros_like(strips_ref)

    def quad(g, carry):
        lanes = pl.ds(pl.multiple_of(128 * g, 128), 128)
        for w in range(2):
            rows = pl.ds(144 * w, 144)
            queries = over_heads(packed_ref[0, rows, lanes])
            keys = packed_ref[1, rows, lanes]
            values = packed_ref[2, rows, lanes]
            grad = grad_ref[rows, lanes]
            product = -(attn_ref[rows, lanes].astype(F32) * grad.astype(F32)).astype(BF16)
            grads = over_heads(grad)
            left = jnp.concatenate([values, jnp.ones_like(values)], 1)
            right = jnp.concatenate([grads, over_heads(product)], 1)
            probs = probs_ref[2 * g + w]
            grad_scores = probs.astype(F32) * contract(left, right, 1, 1)
            if w == 0:
                pairs_ref[...] = grad_scores
            else:
                pairs_ref[...] += grad_scores
            raw = (grad_scores * HEAD_DIM ** (-0.5)).astype(BF16)
            back_ref[0, rows, lanes] = own_columns(contract(raw, keys, 0, 0)).astype(BF16)
            back_ref[1, rows, lanes] = jnp.dot(
                raw, queries, preferred_element_type=F32
            ).astype(BF16)
            back_ref[2, rows, lanes] = jnp.dot(
                probs, grads, preferred_element_type=F32
            ).astype(BF16)
        for h in range(4):
            for i in range(WIN):
                low = 12 * (11 - i)
                strips_ref[4 * (g - quads[0]) + h, 0:12, low : low + 144] += pairs_ref[
                    12 * i : 12 * i + 12, 144 * h : 144 * (h + 1)
                ]
        return carry

    lax.fori_loop(*quads, quad, 0)


def unattend_body(me_ref, packed_ref, grad_ref, attn_ref, probs_ref, back_ref, strips_ref, pairs_ref):
    unattend_quads((0, QUADS), packed_ref, grad_ref, attn_ref, probs_ref, back_ref, strips_ref, pairs_ref)


def qkv_body(me_ref, windows_ref, edge_ref, back_ref, sums_ref, low_keep, high_keep, low_send, high_send, trio_ref, flat_ref):
    me = me_ref[0]

    def step(j, carry):
        trio_ref[j] = contract(windows_ref[...], back_ref[j], 0, 0).astype(BF16)
        sums_ref[pl.ds(j, 1)] = jnp.sum(back_ref[j].astype(F32), 0, keepdims=True)
        return carry

    lax.fori_loop(0, 3, step, 0)
    mix_rows(trio_ref, flat_ref, 0, 3, 64, 12)
    flat_ref[2304:2320] = edge_ref[...]
    cut_windows(me, 0, flat_ref, 0, (low_keep, high_keep), (low_send, high_send))


def unattend(me, packed, grad, attn, probs, *ties):
    return call(
        unattend_body,
        "attention_backward",
        [me, packed, grad, attn, probs],
        [like(3, LEN, D), like(HEADS, WIN, 384, dtype=F32)],
        [pltpu.VMEM((144, SPAN), F32)],
        10,
        ties,
    )


def qkv_grad(me, windows, edge, back, *ties):
    return call(
        qkv_body,
        "qkv_grad",
        [me, windows, edge, back],
        [like(8, D, dtype=F32), *WINDOWS],
        [pltpu.VMEM((3, D, D), BF16), pltpu.VMEM((2320, D), BF16)],
        12,
        ties,
    )


def token_body(me_ref, back_ref, qkv_ref, laid_ref, vecs_ref, near_out, far_out, sums_ref, wide_ref, one_ref, two_ref):
    grad = contract(back_ref[0], qkv_ref[0], 1, 1)
    for j in (1, 2):
        grad = grad + contract(back_ref[j], qkv_ref[j], 1, 1)
    n, scale = normal_parts(laid_ref[...].astype(F32))
    sums_ref[0:1] = jnp.sum(grad * n, 0, keepdims=True)
    sums_ref[1:2] = jnp.sum(grad, 0, keepdims=True)
    wide_ref[...] = normal_pull(n, scale, grad, vecs_ref[9:10])
    unlay(wide_ref, one_ref, two_ref)
    near_out[...] = one_ref[...].astype(BF16)
    far_out[...] = two_ref[...].astype(BF16)


def token_grad(me, back, w_qkv, laid, vecs, *ties):
    return call(
        token_body,
        "token_grad",
        [me, back, w_qkv, laid, vecs],
        [like(HALF, D), like(HALF, D), like(8, D, dtype=F32)],
        LAY_SCRATCH,
        10,
        ties,
    )


def output_body(me_ref, tokens_ref, back_ref, near_ref, vecs_ref, active_ref, down_ref, out_ref):
    total = middle_of(tokens_ref, back_ref, near_ref) + vecs_ref[8:9]
    for j in range(4):
        total = total + jnp.dot(
            active_ref[j], down_ref[D * j : D * (j + 1)], preferred_element_type=F32
        )
    out_ref[...] = total.astype(BF16)


def block_output(me, tokens, back, near, vecs, active, w_down, *ties):
    return call(
        output_body,
        "block_output",
        [me, tokens, back, near, vecs, active, w_down],
        [like(LEN, D)],
        [],
        10,
        ties,
    )


def sum_body(slots, lows, *refs):
    for i in range(slots):
        total = refs[0][lows[0] + i].astype(F32)
        for ref, low in zip(refs[1 : len(lows)], lows[1:]):
            total = total + ref[low + i].astype(F32)
        refs[-1][i] = total.astype(BF16)


def sum_slots(slots, terms, *ties):
    return call(
        functools.partial(sum_body, slots, [low for _, low in terms]),
        "sum_slots",
        [one for one, _ in terms],
        [like(slots, WINDOW, D)],
        [],
        6,
        ties,
    )


def split_body(low_ref, core_ref, x_ref, sent_ref, kept_ref):
    for slot, ref in ((1, sent_ref), (0, kept_ref)):
        total = low_ref[slot].astype(F32) + core_ref[slot].astype(F32)
        ref[...] = (total + x_ref[slot].astype(F32)).astype(BF16)


def split_sum(low, core, x, *ties):
    return call(
        split_body, "split_sum", [low, core, x], [like(WINDOW, D), like(WINDOW, D)], [], 6, ties
    )


def three_body(me_ref, high_ref, low_ref, low_y_ref, own_ref, other_ref):
    low = (low_ref[...].astype(F32) + low_y_ref[...].astype(F32)).astype(BF16)
    odd = (me_ref[0] // 8) % 2 == 1

    @pl.when(odd)
    def _():
        own_ref[...] = high_ref[...]
        other_ref[...] = low

    @pl.when(jnp.logical_not(odd))
    def _():
        own_ref[...] = low
        other_ref[...] = high_ref[...]


def sum_three(me, high, low, low_y, *ties):
    return call(
        three_body,
        "sum_three",
        [me, high, low, low_y],
        [like(WINDOW, D), like(WINDOW, D)],
        [],
        8,
        ties,
    )


def sum_two(one, two, *ties):
    def body(one_ref, two_ref, out_ref):
        out_ref[...] = (one_ref[...].astype(F32) + two_ref[...].astype(F32)).astype(BF16)

    return call(body, "sum_two", [one, two], [like(WINDOW, D)], [], 6, ties)


def to_half(block, upper):
    return swap(block, 16, lambda d: (d // 16 == 1) != upper)


def small_body(strips_ref, qkv_ref, proj_ref, up_ref, one_ref, two_ref, out_ref, rows_ref):
    out_ref[...] = jnp.zeros_like(out_ref)
    out_ref[0:3] = qkv_ref[0:3]
    out_ref[3:4] = proj_ref[0:1]
    out_ref[4:9] = up_ref[0:5]
    out_ref[9:11] = one_ref[0:2]
    out_ref[11:13] = two_ref[0:2]
    for j in range(WIN):
        rows_ref[24 * j : 24 * (j + 1)] = strips_ref[:, j, :]
    rows = rows_ref[...]
    high = rows.astype(BF16)
    low = (rows - high.astype(F32)).astype(BF16)
    m = lax.broadcasted_iota(jnp.int32, (384, 640), 0)
    n = lax.broadcasted_iota(jnp.int32, (384, 640), 1)
    spread = ((n == 23 * (m // WIN) + m % WIN) & (m < 276)).astype(F32).astype(BF16)
    wide = jnp.dot(high, spread, preferred_element_type=F32) + jnp.dot(
        low, spread, preferred_element_type=F32
    )
    total = wide[264:288]
    for j in range(WIN - 1):
        total = total + pltpu.roll(wide[24 * j : 24 * (j + 1)], 11 - j, 1)
    out_ref[16:40, 0:640] = total


def small_grads(strips, qkv, proj, up, one, two, *ties):
    return call(
        small_body,
        "small_grads",
        [strips, qkv, proj, up, one, two],
        [like(40, D, dtype=F32)],
        [pltpu.VMEM((288, 384), F32)],
        8,
        ties,
    )


def lines_body(small_ref, out_ref, table_ref, vec_ref, line_ref):
    table = jnp.concatenate([small_ref[16:40, 0:640], jnp.zeros((104, 640), F32)], 0)
    table_ref[...] = table.T
    wide = jnp.zeros((40, 384), F32)
    for q in range(16):
        rows = table_ref[pl.ds(q, 40, stride=16), :]
        padded = jnp.concatenate([rows, jnp.zeros((40, 256), F32)], 1)
        wide = wide + (pltpu.roll(padded, 24 * q, 1) if q else padded)
    line_ref[...] = jnp.zeros_like(line_ref)
    for c in range(3):
        line_ref[pl.ds(c, 40, stride=3), :] = wide[:, 128 * c : 128 * (c + 1)]
    for c in range(6):
        vec_ref[pl.ds(c, 16, stride=6), :] = small_ref[0:16, 128 * c : 128 * (c + 1)]
    rolled = pltpu.roll(vec_ref[...], 24, 1)
    lane = lax.broadcasted_iota(jnp.int32, rolled.shape, 1)
    line_ref[99:195] += jnp.where(lane >= 24, rolled, 0.0)
    line_ref[100:196] += jnp.where(lane < 24, rolled, 0.0)
    out_ref[...] = line_ref[0:192]


def small_lines(small):
    return call(
        lines_body,
        "small_lines",
        [small],
        [like(192, 128, dtype=F32)],
        [pltpu.VMEM((640, 128), F32), pltpu.VMEM((96, 128), F32), pltpu.VMEM((200, 128), F32)],
        8,
    )[0]


def adam_body(me_ref, *refs):
    terms = refs[:5]
    tail_ref, params_ref, first_ref, second_ref = refs[5:9]
    out_params, out_low, out_first, out_second, flat_ref, grad_ref, copy_ref, sems = refs[9:]
    me = me_ref[0]
    shift = me % TILE
    for which, own_terms in enumerate((terms[0:2], terms[2:3], terms[3:5])):

        @pl.when(jnp.minimum(me // 8, 2) == which)
        def _():
            copies = [
                pltpu.make_async_copy(term, copy_ref.at[z], sems.at[z])
                for z, term in enumerate(own_terms)
            ]
            if len(own_terms) == 1:
                copy_ref[1] = jnp.zeros((WINDOW, D), BF16)
            for copy in copies:
                copy.start()
            for copy in copies:
                copy.wait()

    for j in range(6):
        terms_j = [copy_ref[z, :, 128 * j : 128 * (j + 1)].astype(F32) for z in range(2)]
        flat_ref[pl.ds(j, WINDOW, stride=6), :] = terms_j[0] + terms_j[1]
    grad_ref[...] = flat_ref[pl.ds(6 * shift, 1734), :]

    @pl.when(me == 31)
    def _():
        grad_ref[1542:1734, :] += tail_ref[...]

    grad = grad_ref[...]
    position = (
        me * 221952
        + lax.broadcasted_iota(jnp.int32, grad.shape, 0) * 128
        + lax.broadcasted_iota(jnp.int32, grad.shape, 1)
    )
    step_rate = step_rates(position)
    new_first = BETA_ONE * first_ref[...] + (1.0 - BETA_ONE) * grad
    new_second = BETA_TWO * second_ref[...] + (1.0 - BETA_TWO) * grad * grad
    fixed_first = new_first / (1.0 - BETA_ONE**STEP)
    fixed_second = new_second / (1.0 - BETA_TWO**STEP)
    params = params_ref[...]
    new_params = params - step_rate * (
        fixed_first / (jnp.sqrt(fixed_second) + ADAM_EPS) + DECAY * params
    )
    out_params[...] = new_params
    out_low[...] = new_params.astype(BF16)
    out_first[...] = new_first
    out_second[...] = new_second


def adam(me, terms, tail, params, first_moment, second_moment):
    lines = (1734, 128)
    args = [one.reshape(lines) for one in (params, first_moment, second_moment)]
    outs = pl.pallas_call(
        adam_body,
        out_shape=[
            jax.ShapeDtypeStruct(lines, F32),
            jax.ShapeDtypeStruct(lines, BF16),
            jax.ShapeDtypeStruct(lines, F32),
            jax.ShapeDtypeStruct(lines, F32),
        ],
        in_specs=[SMEM_SPEC] + [ANY_SPEC] * 5 + vmem(4),
        out_specs=vmem(4),
        scratch_shapes=[
            pltpu.VMEM((6 * WINDOW, 128), F32),
            pltpu.VMEM(lines, F32),
            pltpu.VMEM((2, WINDOW, D), BF16),
            pltpu.SemaphoreType.DMA((2,)),
        ],
        compiler_params=params_call(12),
        name="adam",
    )(me, *terms, tail, *args)
    return [one.reshape(-1) for one in outs]


def table_picks():
    col = jnp.arange(WIN * 384, dtype=jnp.int32)
    m = col % 384
    wanted = (m // WIN) * 23 + m % WIN - col // 384 + WIN - 1
    wanted = jnp.where(m < 276, wanted, -1)
    return (jnp.arange(TABLE_ROWS, dtype=jnp.int32)[None, :] == wanted[:, None]).astype(BF16)


def bias_of(table):
    return lax.dot_general(
        table, table_picks(), (((0,), (1,)), ((), ())), preferred_element_type=F32
    ).reshape(HEADS, WIN, 384)


def shards(tokens, cotangent, valid, params, first_moment, second_moment):
    if lax.axis_size("img") != 16 or lax.axis_size("row") != 2:
        return shards_general(tokens, cotangent, valid, params, first_moment, second_moment)
    me = lax.axis_index(BOTH).astype(jnp.int32).reshape(1)
    flat_tokens = tokens.reshape(LEN, D)
    flat_cotangent = cotangent.reshape(LEN, D)
    own, spare, extra = window_of(me, params)
    mask = jnp.tile(window_mask(lax.axis_index("row") * WIN), (1, 1, 4))
    amount = TABLE_ROWS * HEADS

    def bias_maker(tail):
        tail = tail.reshape(-1)
        bias = bias_of(tail[:amount].reshape(TABLE_ROWS, HEADS))
        return bias, tail[amount : amount + 13 * D].reshape(13, D).astype(F32), mask

    parts, places, (bias, vecs, mask), rows = gather_windows(
        own, spare, extra, flat_tokens[:HALF], bias_maker
    )
    windows, packed, attn, probs, near, far, w_proj, w_qkv, laid, token = attend(
        me, flat_tokens, rows, vecs, bias, mask, parts, places
    )
    back = from_partner(far, "row", 0)
    w_up, w_down, _ = feed_weights(me, parts, places, pause(token))
    hidden, active, grad_up, sums_up, low, low_three, high_three, low_send, high_send, token = feed(
        me, valid, flat_tokens, back, near, flat_cotangent, vecs, w_up, w_down
    )
    core_high_three, core_low_three = swap(high_send, 2), swap(low_send, 2)
    grad_middle, far_grad, near_grad, sums_two, token = middle_grad(
        me, valid, flat_tokens, back, near, flat_cotangent, vecs, grad_up, w_up
    )
    far_grad = from_partner(far_grad, "row", 0)
    sent, token = sum_slots(2, [(high_three, 0), (core_high_three, 0)], pause(token))
    x_three = cross(sent, 4, 1)
    high, low_two, high_two, low_send, high_send, token = up_grad(
        me, hidden, grad_up, low, pause(token)
    )
    core_high_two, core_low_two = swap(high_send, 2), swap(low_send, 2)
    sent, three, token = split_sum(low_three, core_low_three, x_three, token)
    y_three = cross(sent, 1, 4)
    sent, token = sum_slots(2, [(high_two, 0), (core_high_two, 0)], pause(token))
    x_two = cross(sent, 4, 1)
    grad_attn, sums_proj, edge, low_one, high_one, low_send, high_send, token = proj_grad(
        me, near_grad, far_grad, attn, w_proj, high, pause(token)
    )
    core_high_one, core_low_one = swap(high_send, 2), swap(low_send, 2)
    grad_packed, strips, token = unattend(me, packed, grad_attn, attn, probs, pause(token))
    three, token = sum_two(three, y_three, token)
    sent, two, token = split_sum(low_two, core_low_two, x_two, token)
    y_two = cross(sent, 1, 4)
    sent, token = sum_slots(2, [(high_one, 0), (core_high_one, 0)], pause(token))
    x_one = cross(sent, 4, 1)
    sums_qkv, low_zero, high_zero, low_send, high_send, token = qkv_grad(
        me, windows, edge, grad_packed, pause(token)
    )
    core_high_zero, core_low_zero = swap(high_send, 2), swap(low_send, 2)
    upper, other, token = sum_three(me, three, two, y_two, token)
    z_upper = swap(other, 8)
    sent, one, token = split_sum(low_one, core_low_one, x_one, token)
    y_one = cross(sent, 1, 4)
    sent, token = sum_slots(2, [(high_zero, 0), (core_high_zero, 0)], pause(token, us=12))
    x_zero = cross(sent, 4, 1)
    near_in, far_in, sums_one, token = token_grad(
        me, grad_packed, w_qkv, laid, vecs, pause(token)
    )
    upper, token = sum_two(upper, z_upper, token)
    far_upper = to_half(upper, True)
    one, token = sum_two(one, y_one, token)
    z_one = swap(one, 8, lambda d: d // 8 in (0, 2))
    small, token = small_grads(strips, sums_qkv, sums_proj, sums_up, sums_one, sums_two, token)
    small = small + swap(small, 2)
    sent, zero, token = split_sum(low_zero, core_low_zero, x_zero, token)
    y_zero = cross(sent, 1, 4)
    one, token = sum_two(one, z_one, token)
    far_one = swap(one, 16, lambda d: d // 8 == 3)
    zero, token = sum_two(zero, y_zero, token)
    z_zero = swap(zero, 8, lambda d: d // 8 in (1, 3))
    small = gate(small, token)
    small = (small + swap(small, 4)) + (swap(small, 1) + swap(small, 5))
    far_in = from_partner(gate(far_in, token), "row", 0)
    output, token = block_output(
        me, flat_tokens, back, near, vecs, active, w_down, token
    )
    one, token = sum_two(one, far_one, token)
    zero, token = sum_two(zero, z_zero, token)
    far_zero = swap(zero, 16, lambda d: d // 8 == 2)
    small = gate(small, token)
    small = small + to_half(small, True)
    small = small_lines(small + swap(small, 8, lambda d: d // 8 == 2))
    input_grad = grad_middle + jnp.concatenate([far_in, near_in], 0).astype(F32)
    terms = [zero, far_zero, one, upper, far_upper]
    new = adam(me, terms, small, params, first_moment, second_moment)
    return (output.reshape(tokens.shape), input_grad.reshape(tokens.shape), *new)


def solution(mesh):
    return jax.shard_map(
        shards,
        mesh=mesh,
        in_specs=(
            P("img", "row", None, None),
            P("img", "row", None, None),
            P("img"),
            P(("img", "row")),
            P(("img", "row")),
            P(("img", "row")),
        ),
        out_specs=(
            P("img", "row", None, None),
            P("img", "row", None, None),
            P(("img", "row")),
            P(("img", "row")),
            P(("img", "row")),
            P(("img", "row")),
        ),
        check_vma=False,
    )
```

```python
import functools
import math

import jax
import jax.numpy as jnp
from jax import lax
from jax.experimental import pallas as pl
from jax.experimental.pallas import tpu as pltpu
from jax.sharding import PartitionSpec as P

D = 768
FF = 3072
HEADS = 24
HEAD_DIM = 32
WIN = 12
SHIFT = 6
SIDE = 24
STEP = 4
TABLE_ROWS = 529


EPSILON = 1e-05
MASKED = -100.0
DECAY = 0.05
ADAM_EPS = 1e-08
BETA_ONE = 0.5
BETA_TWO = 0.5


def from_partner(block, axis, apart):
    count = lax.axis_size(axis)
    route = []
    for low in range(count):
        high = low | 1 << apart
        if high != low and high < count:
            route += [(low, high), (high, low)]
    return lax.ppermute(block, axis, route)


def piece_shapes():
    return [
        (D, 3 * D),
        (D, D),
        (D, FF),
        (FF, D),
        (TABLE_ROWS, HEADS),
        (3 * D,),
        (D,),
        (FF,),
        (D,),
        (D,),
        (D,),
        (D,),
        (D,),
    ]


def unpack(flat_vec):
    pieces = []
    offset = 0
    for shape_one in piece_shapes():
        amount = math.prod(shape_one)
        pieces.append(lax.slice_in_dim(flat_vec, offset, offset + amount).reshape(shape_one))
        offset = offset + amount
    return pieces


def step_rates(position):
    rate_list = [
        D ** (-0.5),
        4.0 * D ** (-0.5),
        D ** (-0.5),
        FF ** (-0.5),
        1.0,
        0.3,
        0.3,
        0.3,
        0.3,
        0.4,
        0.3,
        0.4,
        0.3,
    ]
    result = jnp.zeros(position.shape, jnp.float32)
    offset = 0
    for shape_one, rate_one in zip(piece_shapes(), rate_list):
        amount = math.prod(shape_one)
        inside = (position >= offset) & (position < offset + amount)
        result = jnp.where(inside, jnp.float32(rate_one), result)
        offset = offset + amount
    return result


def layer_norm(values, gain_vec, shift_vec):
    centre = jnp.mean(values, -1, keepdims=True)
    centred = values - centre
    spread = jnp.mean(centred * centred, -1, keepdims=True)
    return centred * lax.rsqrt(spread + EPSILON) * gain_vec + shift_vec


def region_of(coord):
    return jnp.where(coord < SIDE - WIN, 0, jnp.where(coord < SIDE - SHIFT, 1, 2))


def relative_index():
    cell_index = jnp.arange(WIN * WIN, dtype=jnp.int32)
    row_part = cell_index // WIN
    col_part = cell_index % WIN
    return (row_part[:, None] - row_part[None, :] + WIN - 1) * (2 * WIN - 1) + (
        col_part[:, None] - col_part[None, :] + WIN - 1
    )


def window_mask(row_first):
    row_coord = row_first + jnp.arange(WIN, dtype=jnp.int32)
    col_coord = jnp.arange(SIDE, dtype=jnp.int32)
    region_ids = 3 * region_of(row_coord)[:, None] + region_of(col_coord)[None, :]
    region_ids = (
        region_ids.reshape(WIN, SIDE // WIN, WIN).transpose(1, 0, 2).reshape(SIDE // WIN, WIN * WIN)
    )
    same = region_ids[:, :, None] == region_ids[:, None, :]
    return jnp.where(same, 0.0, MASKED).astype(jnp.float32)


def to_windows(grid_rows):
    img_count = grid_rows.shape[0]
    width = grid_rows.shape[-1]
    shaped = grid_rows.reshape(img_count, WIN, SIDE // WIN, WIN, width).transpose(0, 2, 1, 3, 4)
    return shaped.reshape(img_count * (SIDE // WIN), WIN * WIN, width)


def from_windows(window_rows, img_count):
    width = window_rows.shape[-1]
    shaped = window_rows.reshape(img_count, SIDE // WIN, WIN, WIN, width).transpose(0, 2, 1, 3, 4)
    return shaped.reshape(img_count, WIN, SIDE, width)


BF16 = jnp.bfloat16
F32 = jnp.float32
BOTH = ("img", "row")
ROWS = 9248
TILE = 16
WINDOW = 304
WIDE = 2 * D // 4
VMEM_MOST = 60 * 1024 * 1024


def contract_rows(left_op, right_op):
    summed_dims = tuple(range(left_op.ndim - 1))
    return lax.dot_general(
        left_op,
        right_op,
        ((summed_dims, summed_dims), ((), ())),
        preferred_element_type=jnp.float32,
    )


def times_transposed(left_op, right_op):
    return lax.dot_general(
        left_op,
        right_op,
        (((left_op.ndim - 1,), (1,)), ((), ())),
        preferred_element_type=jnp.float32,
    )


def scores_of(queries, keys_all, bias_full, region_mask):
    raw_scores = jnp.einsum(
        "wqhd,wkhd->whqk", queries, keys_all, preferred_element_type=jnp.float32
    )
    return raw_scores * HEAD_DIM ** (-0.5) + bias_full[None] + region_mask[:, None]


def shards_general(tokens, cotangent, valid, params, first_moment, second_moment):
    img_count = tokens.shape[0]
    win_count = img_count * (SIDE // WIN)
    tile_len = WIN * WIN
    gathered = lax.all_gather(params.astype(jnp.bfloat16), ("img", "row"), axis=0, tiled=True)
    (
        w_qkv,
        w_proj,
        w_up,
        w_down,
        bias_table,
        b_qkv,
        b_proj,
        b_up,
        b_down,
        gain_one,
        shift_one,
        gain_two,
        shift_two,
    ) = unpack(gathered)
    images = tokens.astype(jnp.float32)
    normed, norm_pull = jax.vjp(
        layer_norm, images, gain_one.astype(jnp.float32), shift_one.astype(jnp.float32)
    )
    normed_low = normed.astype(jnp.bfloat16)
    incoming = from_partner(normed_low[:, :SHIFT], "row", 0)
    shifted = jnp.roll(jnp.concatenate([normed_low[:, SHIFT:], incoming], 1), -SHIFT, 2)
    windows = to_windows(shifted)
    packed = (
        jnp.dot(windows, w_qkv, preferred_element_type=jnp.float32) + b_qkv.astype(jnp.float32)
    ).astype(jnp.bfloat16)
    heads_view = packed.reshape(win_count, tile_len, 3, HEADS, HEAD_DIM)
    queries = heads_view[:, :, 0]
    keys_all = heads_view[:, :, 1]
    values_all = heads_view[:, :, 2]
    rel_index = relative_index()
    bias_full = bias_table.astype(jnp.float32)[rel_index].transpose(2, 0, 1)
    region_mask = jnp.tile(window_mask(lax.axis_index("row") * WIN), (img_count, 1, 1))
    scores = scores_of(queries, keys_all, bias_full, region_mask)
    row_top = jnp.max(scores, -1, keepdims=True)
    exponent = jnp.exp(scores - row_top)
    row_total = jnp.sum(exponent, -1, keepdims=True)
    log_total = row_top + jnp.log(row_total)
    attn_probs = (exponent / row_total).astype(jnp.bfloat16)
    attn_mixed = jnp.einsum(
        "whqk,wkhd->wqhd", attn_probs, values_all, preferred_element_type=jnp.float32
    )
    attn_mixed = attn_mixed.astype(jnp.bfloat16).reshape(win_count, tile_len, D)
    branch = (
        jnp.dot(attn_mixed, w_proj, preferred_element_type=jnp.float32) + b_proj.astype(jnp.float32)
    ).astype(jnp.bfloat16)
    branch_grid = jnp.roll(from_windows(branch, img_count), SHIFT, 2)
    returned = from_partner(branch_grid[:, SHIFT:], "row", 0)
    middle = images + jnp.concatenate([returned, branch_grid[:, :SHIFT]], 1).astype(jnp.float32)
    normed_two, norm_two_pull = jax.vjp(
        layer_norm, middle, gain_two.astype(jnp.float32), shift_two.astype(jnp.float32)
    )
    hidden_in = normed_two.astype(jnp.bfloat16)
    upward = jnp.dot(hidden_in, w_up, preferred_element_type=jnp.float32) + b_up.astype(jnp.float32)
    active_full, gelu_pull = jax.vjp(lambda values: jax.nn.gelu(values, approximate=False), upward)
    active = active_full.astype(jnp.bfloat16)
    output = (
        middle
        + jnp.dot(active, w_down, preferred_element_type=jnp.float32)
        + b_down.astype(jnp.float32)
    )
    regathered = lax.all_gather(params.astype(jnp.bfloat16), ("img", "row"), axis=0, tiled=True)
    fresh = unpack(regathered)
    w_qkv, w_proj, w_up, w_down = (fresh[0], fresh[1], fresh[2], fresh[3])
    grad_out = cotangent * valid.astype(jnp.bfloat16)[:, None, None, None]
    grad_w_down = contract_rows(active, grad_out)
    grad_b_down = jnp.sum(grad_out.astype(jnp.float32), (0, 1, 2))
    grad_active = times_transposed(grad_out, w_down)
    grad_up = gelu_pull(grad_active)[0].astype(jnp.bfloat16)
    grad_w_up = contract_rows(hidden_in, grad_up)
    grad_b_up = jnp.sum(grad_up.astype(jnp.float32), (0, 1, 2))
    grad_hidden = times_transposed(grad_up, w_up)
    grad_middle_ln, grad_gain_two, grad_shift_two = norm_two_pull(grad_hidden)
    grad_middle = grad_out.astype(jnp.float32) + grad_middle_ln
    middle_low = grad_middle.astype(jnp.bfloat16)
    arrived = from_partner(middle_low[:, :SHIFT], "row", 0)
    grad_grid = jnp.roll(jnp.concatenate([middle_low[:, SHIFT:], arrived], 1), -SHIFT, 2)
    grad_branch = to_windows(grad_grid)
    grad_w_proj = contract_rows(attn_mixed, grad_branch)
    grad_b_proj = jnp.sum(grad_branch.astype(jnp.float32), (0, 1))
    grad_attn = times_transposed(grad_branch, w_proj).astype(jnp.bfloat16)
    grad_attn = grad_attn.reshape(win_count, tile_len, HEADS, HEAD_DIM)
    again_scores = scores_of(queries, keys_all, bias_full, region_mask)
    again_probs = jnp.exp(again_scores - log_total)
    grad_values = jnp.einsum(
        "whqk,wqhd->wkhd",
        again_probs.astype(jnp.bfloat16),
        grad_attn,
        preferred_element_type=jnp.float32,
    )
    grad_probs = jnp.einsum(
        "wqhd,wkhd->whqk", grad_attn, values_all, preferred_element_type=jnp.float32
    )
    grad_scores = again_probs * (grad_probs - jnp.sum(again_probs * grad_probs, -1, keepdims=True))
    pair_sums = jnp.sum(grad_scores, 0).transpose(1, 2, 0).reshape(tile_len * tile_len, HEADS)
    grad_table = jax.ops.segment_sum(pair_sums, rel_index.reshape(-1), TABLE_ROWS)
    grad_raw = (grad_scores * HEAD_DIM ** (-0.5)).astype(jnp.bfloat16)
    grad_queries = jnp.einsum(
        "whqk,wkhd->wqhd", grad_raw, keys_all, preferred_element_type=jnp.float32
    )
    grad_keys = jnp.einsum("whqk,wqhd->wkhd", grad_raw, queries, preferred_element_type=jnp.float32)
    grad_packed = jnp.stack([grad_queries, grad_keys, grad_values], 2).astype(jnp.bfloat16)
    grad_packed = grad_packed.reshape(win_count, tile_len, 3 * D)
    grad_w_qkv = contract_rows(windows, grad_packed)
    grad_b_qkv = jnp.sum(grad_packed.astype(jnp.float32), (0, 1))
    grad_windows = times_transposed(grad_packed, w_qkv).astype(jnp.bfloat16)
    grad_shifted = jnp.roll(from_windows(grad_windows, img_count), SHIFT, 2)
    arrived_two = from_partner(grad_shifted[:, SHIFT:], "row", 0)
    grad_normed = jnp.concatenate([arrived_two, grad_shifted[:, :SHIFT]], 1).astype(jnp.float32)
    grad_images_ln, grad_gain_one, grad_shift_one = norm_pull(grad_normed)
    input_grad = grad_middle + grad_images_ln
    grad_list = [
        grad_w_qkv,
        grad_w_proj,
        grad_w_up,
        grad_w_down,
        grad_table,
        grad_b_qkv,
        grad_b_proj,
        grad_b_up,
        grad_b_down,
        grad_gain_one,
        grad_shift_one,
        grad_gain_two,
        grad_shift_two,
    ]
    grad_flat = jnp.concatenate([grad_one.reshape(-1) for grad_one in grad_list])
    grad_flat = jnp.pad(grad_flat, (0, gathered.shape[0] - grad_flat.shape[0]))
    grad_shard = lax.psum_scatter(grad_flat, ("img", "row"), scatter_dimension=0, tiled=True)
    shard_len = params.shape[0]
    position = lax.axis_index(("img", "row")) * shard_len + jnp.arange(shard_len, dtype=jnp.int32)
    step_rate = step_rates(position)
    new_first = BETA_ONE * first_moment + (1.0 - BETA_ONE) * grad_shard
    new_second = BETA_TWO * second_moment + (1.0 - BETA_TWO) * grad_shard * grad_shard
    fixed_first = new_first / (1.0 - BETA_ONE**STEP)
    fixed_second = new_second / (1.0 - BETA_TWO**STEP)
    new_params = params - step_rate * (
        fixed_first / (jnp.sqrt(fixed_second) + ADAM_EPS) + DECAY * params
    )
    return (
        output.astype(jnp.bfloat16),
        input_grad,
        new_params,
        new_params.astype(jnp.bfloat16),
        new_first,
        new_second,
    )


BF16 = jnp.bfloat16
F32 = jnp.float32
BOTH = ("img", "row")
TILE = 16
WINDOW = 304
LEN = 2 * WIN * WIN
QUADS = HEADS // 4
SPAN = 4 * WIN * WIN


def swap(block, mask, only=None):
    count = lax.axis_size(BOTH)
    route = [(d, d ^ mask) for d in range(count) if only is None or only(d)]
    return lax.ppermute(block, BOTH, route)


def params_call(mebibytes):
    return pltpu.CompilerParams(vmem_limit_bytes=mebibytes << 20)


def vmem(count):
    return [pl.BlockSpec(memory_space=pltpu.VMEM)] * count


SMEM_SPEC = pl.BlockSpec(memory_space=pltpu.SMEM)
ANY_SPEC = pl.BlockSpec(memory_space=pl.ANY)


def first_tile(device):
    return (289 * device) // TILE


def prep_body(me_ref, own_ref, out_ref, spare_ref, extra_ref, wide_ref):
    shift = me_ref[0] % TILE
    wide_ref[0:96] = jnp.zeros((96, 128), F32)
    wide_ref[1824:1920] = jnp.zeros((96, 128), F32)
    wide_ref[96:1830] = own_ref[...]
    for j in range(6):
        picked = wide_ref[pl.ds(96 - 6 * shift + j, WINDOW, stride=6), :]
        out_ref[:, 128 * j : 128 * (j + 1)] = picked.astype(BF16)
        spare_ref[:, 128 * j : 128 * (j + 1)] = picked.astype(BF16)
        extra_ref[:, 128 * j : 128 * (j + 1)] = picked.astype(BF16)


def window_of(me, own_flat):
    return pl.pallas_call(
        prep_body,
        out_shape=[jax.ShapeDtypeStruct((WINDOW, D), BF16)] * 3,
        in_specs=[SMEM_SPEC] + vmem(1),
        out_specs=vmem(3),
        scratch_shapes=[pltpu.VMEM((1920, 128), F32)],
        compiler_params=params_call(8),
        name="own_window",
    )(me, own_flat.reshape(-1, 128))


def mixer(groups, per):
    size = groups * per
    row = lax.broadcasted_iota(jnp.int32, (size, size), 0)
    col = lax.broadcasted_iota(jnp.int32, (size, size), 1)
    return (col == groups * (row % per) + row // per).astype(F32).astype(BF16)


def unmixer(groups, per):
    size = groups * per
    row = lax.broadcasted_iota(jnp.int32, (size, size), 0)
    col = lax.broadcasted_iota(jnp.int32, (size, size), 1)
    return (row == groups * (col % per) + col // per).astype(F32).astype(BF16)


def plane_rows(plane):
    low = first_tile(8 * plane) * TILE
    high = first_tile(8 * plane + 7) * TILE + WINDOW
    return low, high


def gate(value, *others):
    def body(*refs):
        pass

    return pl.pallas_call(
        body,
        out_shape=jax.ShapeDtypeStruct(value.shape, value.dtype),
        in_specs=[ANY_SPEC] * (1 + len(others)),
        out_specs=ANY_SPEC,
        input_output_aliases={0: 0},
        cost_estimate=cost(0),
        name="gate",
    )(value, *others)


def cross(block, zero, one):
    count = lax.axis_size(BOTH)
    return lax.ppermute(block, BOTH, [(d, d ^ (one if d & 2 else zero)) for d in range(count)])


def gather_windows(own, spare, extra, rows, *early):
    got = {0: own}
    first, second, third = {}, {}, {}

    def exchange(z):
        first[z] = cross(got[z], 4, 1)
        second[z] = cross(got[z], 1, 4)
        third[z] = cross(first[z], 1, 4)

    got[8] = swap(own, 8)
    first[0] = cross(own, 4, 1)
    second[0] = cross(own, 1, 4)
    spare = gate(spare, got[8])
    got[16] = swap(spare, 16)
    first[0] = gate(first[0], spare)
    third[0] = cross(first[0], 1, 4)
    got_rows = from_partner(rows, "row", 0)
    got[8] = gate(got[8], first[0], second[0], got_rows)
    exchange(8)
    got[24] = swap(gate(extra, got[16]), 24)
    got[16] = gate(got[16], first[8], second[8], third[0])
    exchange(16)
    got[24] = gate(got[24], first[16], second[16], third[8], *early)
    exchange(24)
    blocks, places = [], []
    for z in (0, 8, 16, 24):
        own_some = [got[z], first[z], second[z], third[z]]
        masks = ((z, z), (z | 4, z | 1), (z | 1, z | 4), (z | 5, z | 5))
        if z == 24:
            places.append((len(blocks), None, *masks[3]))
            places.append((len(blocks) + 1, None, masks[3][1] | 2, masks[3][0] | 2))
            last = own_some.pop()
            blocks += [last, swap(last, 2)]
        own_some = stacked(own_some)
        for n in range(own_some.shape[0]):
            zero, one = masks[n]
            places.append((len(blocks), n, zero, one))
            places.append((len(blocks) + 1, n, one | 2, zero | 2))
        blocks += [own_some, swap(own_some, 2)]
    return blocks, places, got_rows


def stacked_body(*refs):
    for i, ref in enumerate(refs[:-1]):
        refs[-1][i] = ref[...]


def stacked(blocks):
    return pl.pallas_call(
        stacked_body,
        out_shape=like(len(blocks), WINDOW, D),
        in_specs=vmem(len(blocks)),
        out_specs=vmem(1)[0],
        compiler_params=params_call(4),
        cost_estimate=cost(0),
        name="stacked",
    )(*blocks)


def load_windows(me, parts, places, first, last, flat_ref):
    base = first_tile(first) * TILE
    for device in (first, 16):
        if first <= device <= last:
            at = first_tile(device) * TILE - base
            flat_ref[at : at + TILE] = jnp.zeros((TILE, D), BF16)

    def each(act):
        for block, slot, zero, one in places:
            device = me ^ jnp.where((me & 2) == 0, zero, one)
            start = pl.multiple_of(first_tile(device) * TILE - base, TILE)
            part = parts[block] if slot is None else parts[block].at[slot]

            @pl.when((device >= first) & (device <= last))
            def _():
                act(part, start)

    def main(part, start):
        def step(i, carry):
            at = pl.multiple_of(48 * i + TILE, TILE)
            to = pl.multiple_of(start + at, TILE)
            flat_ref[pl.ds(to, 48)] = part[pl.ds(at, 48)]
            return carry

        lax.fori_loop(0, 6, step, 0)

    def edge(part, start):
        flat_ref[pl.ds(start, TILE)] += part[0:TILE]

    each(main)
    each(edge)


def load_small(me, parts, places, tail_ref):
    for block, slot, zero, one in places:
        part = parts[block] if slot is None else parts[block].at[slot]

        @pl.when(me ^ jnp.where((me & 2) == 0, zero, one) == 31)
        def _():
            tail_ref[...] = part[WINDOW - 32 : WINDOW]


def flat_scratch(first, last):
    return pltpu.VMEM(
        (first_tile(last) * TILE + WINDOW - first_tile(first) * TILE, D), BF16
    )


def unmix_rows(flat_ref, out_ref, base, groups, per, steps):
    mix = mixer(groups, per)
    size = groups * per
    for t in range(steps):
        rows = flat_ref[base + size * t : base + size * (t + 1)]
        out = jnp.dot(mix, rows, preferred_element_type=F32).astype(BF16)
        for j in range(groups):
            out_ref[j, per * t : per * (t + 1)] = out[per * j : per * (j + 1)]


def mix_rows(in_ref, flat_ref, base, groups, per, steps):
    mix = unmixer(groups, per)
    size = groups * per
    for t in range(steps):
        rows = jnp.concatenate([in_ref[j, per * t : per * (t + 1)] for j in range(groups)], 0)
        out = jnp.dot(mix, rows, preferred_element_type=F32).astype(BF16)
        flat_ref[base + size * t : base + size * (t + 1)] = out


def cut_windows(me, plane, flat_ref, base, keeps, sends):
    for flip in (2, 0):
        for s in range(4):
            first = jnp.where(((me ^ flip) & 2) == 0, 4, 1)
            away = (first if s & 2 else 0) + (5 - first if s & 1 else 0)
            device = 8 * plane + ((me & 7) ^ (away | flip))
            start = pl.multiple_of(first_tile(device) * TILE - base, TILE)
            window = flat_ref[pl.ds(start, WINDOW)]
            (sends if flip else keeps)[s // 2][s % 2] = window


def cost(microseconds):
    return pl.CostEstimate(
        flops=int(1e9 * microseconds),
        bytes_accessed=int(3.2e6 * microseconds),
        transcendentals=0,
    )


WINDOWS = [jax.ShapeDtypeStruct((2, WINDOW, D), BF16)] * 4


def like(*shape, dtype=BF16):
    return jax.ShapeDtypeStruct(shape, dtype)


def call(body, name, ins, outs, scratch, limit, ties=(), us=0, far=0):
    n_in, n_tie, n_out = len(ins), len(ties), len(outs)
    first_out = n_in + n_tie

    def wrapped(*refs):
        body(*refs[:n_in], *refs[first_out : first_out + n_out], *refs[first_out + n_out + 1 :])
        token_ref = refs[first_out + n_out]
        token_ref[...] = jnp.zeros_like(token_ref)

    specs = [SMEM_SPEC if one.dtype == jnp.int32 else vmem(1)[0] for one in ins]
    return pl.pallas_call(
        wrapped,
        out_shape=[*outs, like(8, 128, dtype=F32)],
        in_specs=specs + vmem(n_tie),
        out_specs=vmem(n_out - far)
        + [pl.BlockSpec(memory_space=pltpu.HBM)] * far
        + vmem(1),
        scratch_shapes=scratch,
        compiler_params=params_call(limit),
        cost_estimate=cost(us),
        name=name,
    )(*ins, *ties)


def pause(*ties, us=4):
    return call(lambda: None, "pause", [], [], [], 4, ties, us)[0]


def normal_parts(values):
    centre = jnp.mean(values, -1, keepdims=True)
    centred = values - centre
    spread = jnp.mean(centred * centred, -1, keepdims=True)
    scale = lax.rsqrt(spread + EPSILON)
    return centred * scale, scale


def normal_pull(n, scale, grad, gain):
    e = grad * gain
    return scale * (
        e - jnp.mean(e, -1, keepdims=True) - n * jnp.mean(e * n, -1, keepdims=True)
    )


def over_heads(block):
    head = lax.broadcasted_iota(jnp.int32, block.shape, 1) // HEAD_DIM
    return jnp.concatenate([jnp.where(head == h, block, jnp.zeros_like(block)) for h in range(4)], 0)


def own_columns(block):
    head = lax.broadcasted_iota(jnp.int32, (144, 128), 1) // HEAD_DIM
    out = block[0:144]
    for h in range(1, 4):
        out = jnp.where(head == h, block[144 * h : 144 * (h + 1)], out)
    return out


def contract(one, two, a, b):
    return lax.dot_general(one, two, (((a,), (b,)), ((), ())), preferred_element_type=F32)


def lay(out_ref, near, far):
    for i in range(WIN):
        ref, k = (near, 24 * i) if i < SHIFT else (far, 24 * (i - SHIFT))
        out_ref[12 * i : 12 * i + 12] = ref[k + 6 : k + 18]
        out_ref[144 + 12 * i : 150 + 12 * i] = ref[k + 18 : k + 24]
        out_ref[150 + 12 * i : 156 + 12 * i] = ref[k : k + 6]


def unlay(ref, near, far):
    for i in range(WIN):
        out_ref, k = (near, 24 * i) if i < SHIFT else (far, 24 * (i - SHIFT))
        out_ref[k + 6 : k + 18] = ref[12 * i : 12 * i + 12]
        out_ref[k + 18 : k + 24] = ref[144 + 12 * i : 150 + 12 * i]
        out_ref[k : k + 6] = ref[150 + 12 * i : 156 + 12 * i]


HALF = LEN // 2
LAY_SCRATCH = [pltpu.VMEM((LEN, D), F32), pltpu.VMEM((HALF, D), F32), pltpu.VMEM((HALF, D), F32)]


def unpack_small(tail_ref, vecs_ref, strips_ref, wide_ref, shift_ref):
    tail = tail_ref[...].astype(F32)
    rolled = pltpu.roll(tail, 360, 1)
    below = pltpu.roll(rolled, 31, 0)
    lane = lax.broadcasted_iota(jnp.int32, (16, D), 1)
    vecs_ref[...] = jnp.where(lane < 360, rolled[16:32], below[16:32])
    cell = lax.broadcasted_iota(jnp.int32, (32, D), 1) // HEADS
    which = lax.broadcasted_iota(jnp.int32, (32, D), 0)
    for r in range(17):
        row = jnp.broadcast_to(tail[r : r + 1], (32, D))
        wide_ref[32 * r : 32 * (r + 1)] = jnp.where(cell == which, row, 0.0).astype(BF16)
    lane = lax.broadcasted_iota(jnp.int32, (D, 128), 0)
    head = lax.broadcasted_iota(jnp.int32, (D, 128), 1)
    pick = (lane % HEADS == head).astype(F32).astype(BF16)
    table = jnp.dot(wide_ref[0:544], pick, preferred_element_type=F32)
    row = lax.broadcasted_iota(jnp.int32, table.shape, 0)
    table = jnp.where(row < TABLE_ROWS, table, 0.0)
    table = jnp.concatenate([table, jnp.zeros((96, 128), F32)], 0).T[0:HEADS]
    for j in range(WIN):
        moved = pltpu.roll(table, 629 + j, 1) if j < 11 else table
        shift_ref[24 * j : 24 * (j + 1), 0:640] = moved
    strips = contract(shift_ref[:, 0:640].astype(BF16), table_spread(), 1, 1)
    for j in range(WIN):
        strips_ref[:, j, :] = strips[24 * j : 24 * (j + 1)]


def table_spread():
    m = lax.broadcasted_iota(jnp.int32, (384, 640), 0)
    n = lax.broadcasted_iota(jnp.int32, (384, 640), 1)
    return ((n == 23 * (m // WIN) + m % WIN) & (m < 276)).astype(F32).astype(BF16)


def attend_body(places, me_ref, tokens_ref, rows_ref, mask_ref, *refs):
    parts = refs[:10]
    windows_ref, packed_ref, attn_ref, probs_ref, near_ref, far_ref, proj_ref, vecs_ref, qkv_out, laid_out = refs[10:20]
    flat_ref, wide_ref, one_ref, two_ref, bias_ref, qkv_ref, laid_ref, sems, tail_ref, strips_ref = refs[20:]
    load_small(me_ref[0], parts, places, tail_ref)
    unpack_small(tail_ref, vecs_ref, strips_ref, flat_ref, wide_ref)
    load_windows(me_ref[0], parts, places, 0, 10, flat_ref)
    one_ref[...] = tokens_ref[HALF:LEN].astype(F32)
    two_ref[...] = rows_ref[...].astype(F32)
    lay(wide_ref, one_ref, two_ref)
    laid = wide_ref[...]
    laid_ref[...] = laid.astype(BF16)
    n, _ = normal_parts(laid)
    windows_ref[...] = (n * vecs_ref[9:10] + vecs_ref[10:11]).astype(BF16)
    unmix_rows(flat_ref, qkv_ref, 0, 3, 64, 12)
    copies = [
        pltpu.make_async_copy(qkv_ref, qkv_out, sems.at[0]),
        pltpu.make_async_copy(laid_ref, laid_out, sems.at[1]),
    ]
    for copy in copies:
        copy.start()
    proj_ref[...] = flat_ref[2304:3072]

    def project(j, carry):
        packed_ref[j] = (
            jnp.dot(windows_ref[...], qkv_ref[j], preferred_element_type=F32)
            + vecs_ref[pl.ds(j, 1)]
        ).astype(BF16)
        return carry

    lax.fori_loop(0, 3, project, 0)

    def quad(g, carry):
        lanes = pl.ds(pl.multiple_of(128 * g, 128), 128)
        for h in range(4):
            for i in range(WIN):
                low = 12 * (11 - i)
                bias_ref[12 * i : 12 * i + 12, 144 * h : 144 * (h + 1)] = strips_ref[
                    4 * g + h, 0:12, low : low + 144
                ]
        for w in range(2):
            rows = pl.ds(144 * w, 144)
            queries = over_heads(packed_ref[0, rows, lanes])
            scores = contract(packed_ref[1, rows, lanes], queries, 1, 1)
            scores = scores * HEAD_DIM ** (-0.5) + bias_ref[...] + mask_ref[w]
            top = jnp.max(scores, 0, keepdims=True)
            exponent = jnp.exp(scores - top)
            total = jnp.sum(exponent, 0, keepdims=True)
            probs = (exponent * (1.0 / total)).astype(BF16)
            probs_ref[2 * g + w] = probs
            mixed = contract(probs, packed_ref[2, rows, lanes], 0, 0)
            attn_ref[rows, lanes] = own_columns(mixed).astype(BF16)
        return carry

    lax.fori_loop(0, QUADS, quad, 0)
    wide_ref[...] = (
        jnp.dot(attn_ref[...], proj_ref[...], preferred_element_type=F32) + vecs_ref[3:4]
    )
    unlay(wide_ref, one_ref, two_ref)
    near_ref[...] = one_ref[...].astype(BF16)
    far_ref[...] = two_ref[...].astype(BF16)
    for copy in copies:
        copy.wait()


def attend(me, tokens, rows, mask, parts, places):
    return call(
        functools.partial(attend_body, places),
        "attention_forward",
        [me, tokens, rows, mask, *parts],
        [
            like(LEN, D),
            like(3, LEN, D),
            like(LEN, D),
            like(2 * QUADS, 144, SPAN),
            like(HALF, D),
            like(HALF, D),
            like(D, D),
            like(16, D, dtype=F32),
            like(3, D, D),
            like(LEN, D),
        ],
        [flat_scratch(0, 10)]
        + LAY_SCRATCH
        + [
            pltpu.VMEM((144, SPAN), F32),
            pltpu.VMEM((3, D, D), BF16),
            pltpu.VMEM((LEN, D), BF16),
            pltpu.SemaphoreType.DMA((2,)),
            pltpu.VMEM((32, D), BF16),
            pltpu.VMEM((HEADS, WIN, 384), F32),
        ],
        22,
        far=2,
    )


def middle_of(tokens_ref, back_ref, near_ref):
    branch = jnp.concatenate([back_ref[...].astype(F32), near_ref[...].astype(F32)], 0)
    return tokens_ref[...].astype(F32) + branch


def feed_weights_body(places, me_ref, *refs):
    parts = refs[:10]
    up_ref, down_ref, flat_ref = refs[10:]
    load_windows(me_ref[0], parts, places, 10, 31, flat_ref)
    base = first_tile(10) * TILE
    unmix_rows(flat_ref, up_ref, 3072 - base, 4, 48, 16)

    def step(i, carry):
        at = pl.multiple_of(64 * i, 64)
        down_ref[pl.ds(at, 64)] = flat_ref[pl.ds(pl.multiple_of(6144 - base + at, TILE), 64)]
        return carry

    lax.fori_loop(0, 48, step, 0)


def feed_weights(me, parts, places, *ties):
    return call(
        functools.partial(feed_weights_body, places),
        "feed_weights",
        [me, *parts],
        [like(4, D, D), like(FF, D)],
        [flat_scratch(10, 31)],
        20,
        ties,
    )


def feed_body(me_ref, valid_ref, tokens_ref, back_ref, near_ref, cotangent_ref, vecs_ref, up_ref, down_ref, hidden_ref, active_ref, gradup_ref, sums_ref, low_ref, low_keep, high_keep, low_send, high_send, grad_ref):
    me = me_ref[0]
    n, _ = normal_parts(middle_of(tokens_ref, back_ref, near_ref))
    hidden_ref[...] = (n * vecs_ref[11:12] + vecs_ref[12:13]).astype(BF16)
    grad_out = cotangent_ref[...] * valid_ref[0].astype(F32).astype(BF16)
    grad_ref[3072:3104] = jnp.zeros((32, D), BF16)

    def step(j, carry):
        at = pl.multiple_of(D * j, D)
        down = down_ref[pl.ds(at, D)]
        upward = jnp.dot(hidden_ref[...], up_ref[j], preferred_element_type=F32)
        upward = upward + vecs_ref[pl.ds(4 + j, 1)]
        grad_active = contract(grad_out, down, 1, 1)
        share = 0.5 * (1.0 + lax.erf(upward * (0.5**0.5)))
        density = jnp.exp(-0.5 * upward * upward) * ((2.0 * math.pi) ** (-0.5))
        active = (upward * share).astype(BF16)
        grad_up = (grad_active * (share + upward * density)).astype(BF16)
        active_ref[j] = active
        gradup_ref[j] = grad_up
        sums_ref[pl.ds(j, 1)] = jnp.sum(grad_up.astype(F32), 0, keepdims=True)
        grad_ref[pl.ds(at, D)] = contract(active, grad_out, 0, 0).astype(BF16)
        return carry

    lax.fori_loop(0, 4, step, 0)
    cut_windows(me, 3, grad_ref, 6144, (low_keep, high_keep), (low_send, high_send))
    low_ref[...] = grad_ref[0:800]
    sums_ref[4:5] = jnp.sum(grad_out.astype(F32), 0, keepdims=True)


def feed(me, valid, tokens, back, near, cotangent, vecs, w_up, w_down):
    return call(
        feed_body,
        "feed_forward",
        [me, valid, tokens, back, near, cotangent, vecs, w_up, w_down],
        [
            like(LEN, D),
            like(4, LEN, D),
            like(4, LEN, D),
            like(8, D, dtype=F32),
            like(800, D),
            *WINDOWS,
        ],
        [pltpu.VMEM((3104, D), BF16)],
        16,
    )


def middle_body(me_ref, valid_ref, tokens_ref, back_ref, near_ref, cotangent_ref, vecs_ref, gradup_ref, up_ref, grad_ref, far_out, near_out, sums_ref):
    n, scale = normal_parts(middle_of(tokens_ref, back_ref, near_ref))
    grad_hidden = contract(gradup_ref[0], up_ref[0], 1, 1)
    for j in range(1, 4):
        grad_hidden = grad_hidden + contract(gradup_ref[j], up_ref[j], 1, 1)
    sums_ref[0:1] = jnp.sum(grad_hidden * n, 0, keepdims=True)
    sums_ref[1:2] = jnp.sum(grad_hidden, 0, keepdims=True)
    grad_out = (cotangent_ref[...] * valid_ref[0].astype(F32).astype(BF16)).astype(F32)
    grad = grad_out + normal_pull(n, scale, grad_hidden, vecs_ref[11:12])
    grad_ref[...] = grad
    far_out[...] = grad[:HALF].astype(BF16)
    near_out[...] = grad[HALF:].astype(BF16)


def middle_grad(me, valid, tokens, back, near, cotangent, vecs, grad_up, w_up):
    return call(
        middle_body,
        "middle_grad",
        [me, valid, tokens, back, near, cotangent, vecs, grad_up, w_up],
        [like(LEN, D, dtype=F32), like(HALF, D), like(HALF, D), like(8, D, dtype=F32)],
        [],
        12,
    )


def up_body(me_ref, hidden_ref, gradup_ref, low_ref, proj_ref, low_keep, high_keep, low_send, high_send, quad_ref, flat_ref):
    me = me_ref[0]

    def step(j, carry):
        quad_ref[j] = contract(hidden_ref[...], gradup_ref[j], 0, 0).astype(BF16)
        return carry

    lax.fori_loop(0, 4, step, 0)
    flat_ref[3072:3872] = low_ref[...]
    mix_rows(quad_ref, flat_ref, 0, 4, 48, 16)
    cut_windows(me, 2, flat_ref, 3072, (low_keep, high_keep), (low_send, high_send))
    proj_ref[...] = flat_ref[0:1552]


def up_grad(me, hidden, grad_up, low, *ties):
    return call(
        up_body,
        "up_grad",
        [me, hidden, grad_up, low],
        [like(1552, D), *WINDOWS],
        [pltpu.VMEM((4, D, D), BF16), pltpu.VMEM((3872, D), BF16)],
        16,
        ties,
    )


def proj_body(me_ref, near_ref, far_ref, attn_ref, proj_ref, high_ref, back_ref, sums_ref, edge_ref, low_keep, high_keep, low_send, high_send, flat_ref, wide_ref, one_ref, two_ref):
    me = me_ref[0]
    one_ref[...] = near_ref[...].astype(F32)
    two_ref[...] = far_ref[...].astype(F32)
    lay(wide_ref, one_ref, two_ref)
    grad = wide_ref[...].astype(BF16)
    flat_ref[0:768] = contract(attn_ref[...], grad, 0, 0).astype(BF16)
    flat_ref[768:2320] = high_ref[...]
    cut_windows(me, 1, flat_ref, 2304, (low_keep, high_keep), (low_send, high_send))
    edge_ref[...] = flat_ref[0:16]
    back_ref[...] = contract(grad, proj_ref[...], 1, 1).astype(BF16)
    sums_ref[0:1] = jnp.sum(grad.astype(F32), 0, keepdims=True)


def proj_grad(me, near, far, attn, w_proj, high, *ties):
    return call(
        proj_body,
        "proj_grad",
        [me, near, far, attn, w_proj, high],
        [like(LEN, D), like(8, D, dtype=F32), like(16, D), *WINDOWS],
        [pltpu.VMEM((2320, D), BF16)] + LAY_SCRATCH,
        12,
        ties,
    )


def unattend_quads(quads, packed_ref, grad_ref, attn_ref, probs_ref, back_ref, strips_ref, pairs_ref):
    strips_ref[...] = jnp.zeros_like(strips_ref)

    def quad(g, carry):
        lanes = pl.ds(pl.multiple_of(128 * g, 128), 128)
        for w in range(2):
            rows = pl.ds(144 * w, 144)
            queries = over_heads(packed_ref[0, rows, lanes])
            keys = packed_ref[1, rows, lanes]
            values = packed_ref[2, rows, lanes]
            grad = grad_ref[rows, lanes]
            product = -(attn_ref[rows, lanes].astype(F32) * grad.astype(F32)).astype(BF16)
            grads = over_heads(grad)
            left = jnp.concatenate([values, jnp.ones_like(values)], 1)
            right = jnp.concatenate([grads, over_heads(product)], 1)
            probs = probs_ref[2 * g + w]
            grad_scores = probs.astype(F32) * contract(left, right, 1, 1)
            if w == 0:
                pairs_ref[...] = grad_scores
            else:
                pairs_ref[...] += grad_scores
            raw = (grad_scores * HEAD_DIM ** (-0.5)).astype(BF16)
            back_ref[0, rows, lanes] = own_columns(contract(raw, keys, 0, 0)).astype(BF16)
            back_ref[1, rows, lanes] = jnp.dot(
                raw, queries, preferred_element_type=F32
            ).astype(BF16)
            back_ref[2, rows, lanes] = jnp.dot(
                probs, grads, preferred_element_type=F32
            ).astype(BF16)
        for h in range(4):
            for i in range(WIN):
                low = 12 * (11 - i)
                strips_ref[4 * (g - quads[0]) + h, 0:12, low : low + 144] += pairs_ref[
                    12 * i : 12 * i + 12, 144 * h : 144 * (h + 1)
                ]
        return carry

    lax.fori_loop(*quads, quad, 0)


def unattend_body(me_ref, packed_ref, grad_ref, attn_ref, probs_ref, back_ref, strips_ref, pairs_ref):
    unattend_quads((0, QUADS), packed_ref, grad_ref, attn_ref, probs_ref, back_ref, strips_ref, pairs_ref)


def qkv_body(me_ref, windows_ref, edge_ref, back_ref, sums_ref, low_keep, high_keep, low_send, high_send, trio_ref, flat_ref):
    me = me_ref[0]

    def step(j, carry):
        trio_ref[j] = contract(windows_ref[...], back_ref[j], 0, 0).astype(BF16)
        sums_ref[pl.ds(j, 1)] = jnp.sum(back_ref[j].astype(F32), 0, keepdims=True)
        return carry

    lax.fori_loop(0, 3, step, 0)
    mix_rows(trio_ref, flat_ref, 0, 3, 64, 12)
    flat_ref[2304:2320] = edge_ref[...]
    cut_windows(me, 0, flat_ref, 0, (low_keep, high_keep), (low_send, high_send))


def unattend(me, packed, grad, attn, probs, *ties):
    return call(
        unattend_body,
        "attention_backward",
        [me, packed, grad, attn, probs],
        [like(3, LEN, D), like(HEADS, WIN, 384, dtype=F32)],
        [pltpu.VMEM((144, SPAN), F32)],
        10,
        ties,
    )


def qkv_grad(me, windows, edge, back, *ties):
    return call(
        qkv_body,
        "qkv_grad",
        [me, windows, edge, back],
        [like(8, D, dtype=F32), *WINDOWS],
        [pltpu.VMEM((3, D, D), BF16), pltpu.VMEM((2320, D), BF16)],
        12,
        ties,
    )


def token_body(me_ref, back_ref, qkv_ref, laid_ref, vecs_ref, near_out, far_out, sums_ref, wide_ref, one_ref, two_ref):
    grad = contract(back_ref[0], qkv_ref[0], 1, 1)
    for j in (1, 2):
        grad = grad + contract(back_ref[j], qkv_ref[j], 1, 1)
    n, scale = normal_parts(laid_ref[...].astype(F32))
    sums_ref[0:1] = jnp.sum(grad * n, 0, keepdims=True)
    sums_ref[1:2] = jnp.sum(grad, 0, keepdims=True)
    wide_ref[...] = normal_pull(n, scale, grad, vecs_ref[9:10])
    unlay(wide_ref, one_ref, two_ref)
    near_out[...] = one_ref[...].astype(BF16)
    far_out[...] = two_ref[...].astype(BF16)


def token_grad(me, back, w_qkv, laid, vecs, *ties):
    return call(
        token_body,
        "token_grad",
        [me, back, w_qkv, laid, vecs],
        [like(HALF, D), like(HALF, D), like(8, D, dtype=F32)],
        LAY_SCRATCH,
        10,
        ties,
    )


def output_body(me_ref, tokens_ref, back_ref, near_ref, vecs_ref, active_ref, down_ref, out_ref):
    total = middle_of(tokens_ref, back_ref, near_ref) + vecs_ref[8:9]
    for j in range(4):
        total = total + jnp.dot(
            active_ref[j], down_ref[D * j : D * (j + 1)], preferred_element_type=F32
        )
    out_ref[...] = total.astype(BF16)


def block_output(me, tokens, back, near, vecs, active, w_down, *ties):
    return call(
        output_body,
        "block_output",
        [me, tokens, back, near, vecs, active, w_down],
        [like(LEN, D)],
        [],
        10,
        ties,
    )


def sum_body(slots, lows, *refs):
    for i in range(slots):
        total = refs[0][lows[0] + i].astype(F32)
        for ref, low in zip(refs[1 : len(lows)], lows[1:]):
            total = total + ref[low + i].astype(F32)
        refs[-1][i] = total.astype(BF16)


def sum_slots(slots, terms, *ties):
    return call(
        functools.partial(sum_body, slots, [low for _, low in terms]),
        "sum_slots",
        [one for one, _ in terms],
        [like(slots, WINDOW, D)],
        [],
        6,
        ties,
    )


def split_body(low_ref, core_ref, x_ref, sent_ref, kept_ref):
    for slot, ref in ((1, sent_ref), (0, kept_ref)):
        total = low_ref[slot].astype(F32) + core_ref[slot].astype(F32)
        ref[...] = (total + x_ref[slot].astype(F32)).astype(BF16)


def split_sum(low, core, x, *ties):
    return call(
        split_body, "split_sum", [low, core, x], [like(WINDOW, D), like(WINDOW, D)], [], 6, ties
    )


def three_body(me_ref, high_ref, high_y_ref, low_ref, low_y_ref, own_ref, other_ref):
    high = (high_ref[...].astype(F32) + high_y_ref[...].astype(F32)).astype(BF16)
    low = (low_ref[...].astype(F32) + low_y_ref[...].astype(F32)).astype(BF16)
    odd = (me_ref[0] // 8) % 2 == 1

    @pl.when(odd)
    def _():
        own_ref[...] = high
        other_ref[...] = low

    @pl.when(jnp.logical_not(odd))
    def _():
        own_ref[...] = low
        other_ref[...] = high


def sum_three(me, high, high_y, low, low_y, *ties):
    return call(
        three_body,
        "sum_three",
        [me, high, high_y, low, low_y],
        [like(WINDOW, D), like(WINDOW, D)],
        [],
        8,
        ties,
    )


def sum_two(one, two, *ties):
    def body(one_ref, two_ref, out_ref):
        out_ref[...] = (one_ref[...].astype(F32) + two_ref[...].astype(F32)).astype(BF16)

    return call(body, "sum_two", [one, two], [like(WINDOW, D)], [], 6, ties)


def to_half(block, upper):
    return swap(block, 16, lambda d: (d // 16 == 1) != upper)


def small_body(strips_ref, qkv_ref, proj_ref, up_ref, one_ref, two_ref, out_ref, rows_ref):
    out_ref[...] = jnp.zeros_like(out_ref)
    out_ref[0:3] = qkv_ref[0:3]
    out_ref[3:4] = proj_ref[0:1]
    out_ref[4:9] = up_ref[0:5]
    out_ref[9:11] = one_ref[0:2]
    out_ref[11:13] = two_ref[0:2]
    for j in range(WIN):
        rows_ref[24 * j : 24 * (j + 1)] = strips_ref[:, j, :]
    rows = rows_ref[...]
    high = rows.astype(BF16)
    low = (rows - high.astype(F32)).astype(BF16)
    spread = table_spread()
    wide = jnp.dot(high, spread, preferred_element_type=F32) + jnp.dot(
        low, spread, preferred_element_type=F32
    )
    total = wide[264:288]
    for j in range(WIN - 1):
        total = total + pltpu.roll(wide[24 * j : 24 * (j + 1)], 11 - j, 1)
    out_ref[16:40, 0:640] = total


def small_grads(strips, qkv, proj, up, one, two, *ties):
    return call(
        small_body,
        "small_grads",
        [strips, qkv, proj, up, one, two],
        [like(40, D, dtype=F32)],
        [pltpu.VMEM((288, 384), F32)],
        8,
        ties,
    )


def lines_body(small_ref, out_ref, table_ref, vec_ref, line_ref):
    table = jnp.concatenate([small_ref[16:40, 0:640], jnp.zeros((104, 640), F32)], 0)
    table_ref[...] = table.T
    wide = jnp.zeros((40, 384), F32)
    for q in range(16):
        rows = table_ref[pl.ds(q, 40, stride=16), :]
        padded = jnp.concatenate([rows, jnp.zeros((40, 256), F32)], 1)
        wide = wide + (pltpu.roll(padded, 24 * q, 1) if q else padded)
    line_ref[...] = jnp.zeros_like(line_ref)
    for c in range(3):
        line_ref[pl.ds(c, 40, stride=3), :] = wide[:, 128 * c : 128 * (c + 1)]
    for c in range(6):
        vec_ref[pl.ds(c, 16, stride=6), :] = small_ref[0:16, 128 * c : 128 * (c + 1)]
    rolled = pltpu.roll(vec_ref[...], 24, 1)
    lane = lax.broadcasted_iota(jnp.int32, rolled.shape, 1)
    line_ref[99:195] += jnp.where(lane >= 24, rolled, 0.0)
    line_ref[100:196] += jnp.where(lane < 24, rolled, 0.0)
    out_ref[...] = line_ref[0:192]


def small_lines(small):
    return call(
        lines_body,
        "small_lines",
        [small],
        [like(192, 128, dtype=F32)],
        [pltpu.VMEM((640, 128), F32), pltpu.VMEM((96, 128), F32), pltpu.VMEM((200, 128), F32)],
        8,
    )[0]


def adam_body(me_ref, *refs):
    terms = refs[:4]
    tail_ref, params_ref, first_ref, second_ref = refs[4:8]
    out_params, out_low, out_first, out_second, flat_ref, grad_ref, copy_ref, sems = refs[8:]
    me = me_ref[0]
    shift = me % TILE
    for which, own_terms in enumerate((terms[0:2], terms[2:3], terms[3:4])):

        @pl.when(jnp.minimum(me // 8, 2) == which)
        def _():
            copies = [
                pltpu.make_async_copy(term, copy_ref.at[z], sems.at[z])
                for z, term in enumerate(own_terms)
            ]
            if len(own_terms) == 1:
                copy_ref[1] = jnp.zeros((WINDOW, D), BF16)
            for copy in copies:
                copy.start()
            for copy in copies:
                copy.wait()

    for j in range(6):
        terms_j = [copy_ref[z, :, 128 * j : 128 * (j + 1)].astype(F32) for z in range(2)]
        flat_ref[pl.ds(j, WINDOW, stride=6), :] = terms_j[0] + terms_j[1]
    grad_ref[...] = flat_ref[pl.ds(6 * shift, 1734), :]

    @pl.when(me == 31)
    def _():
        grad_ref[1542:1734, :] += tail_ref[...]

    grad = grad_ref[...]
    position = (
        me * 221952
        + lax.broadcasted_iota(jnp.int32, grad.shape, 0) * 128
        + lax.broadcasted_iota(jnp.int32, grad.shape, 1)
    )
    step_rate = step_rates(position)
    new_first = BETA_ONE * first_ref[...] + (1.0 - BETA_ONE) * grad
    new_second = BETA_TWO * second_ref[...] + (1.0 - BETA_TWO) * grad * grad
    fixed_first = new_first / (1.0 - BETA_ONE**STEP)
    fixed_second = new_second / (1.0 - BETA_TWO**STEP)
    params = params_ref[...]
    new_params = params - step_rate * (
        fixed_first / (jnp.sqrt(fixed_second) + ADAM_EPS) + DECAY * params
    )
    out_params[...] = new_params
    out_low[...] = new_params.astype(BF16)
    out_first[...] = new_first
    out_second[...] = new_second


def adam(me, terms, tail, params, first_moment, second_moment):
    lines = (1734, 128)
    args = [one.reshape(lines) for one in (params, first_moment, second_moment)]
    outs = pl.pallas_call(
        adam_body,
        out_shape=[
            jax.ShapeDtypeStruct(lines, F32),
            jax.ShapeDtypeStruct(lines, BF16),
            jax.ShapeDtypeStruct(lines, F32),
            jax.ShapeDtypeStruct(lines, F32),
        ],
        in_specs=[SMEM_SPEC] + [ANY_SPEC] * 4 + vmem(4),
        out_specs=vmem(4),
        scratch_shapes=[
            pltpu.VMEM((6 * WINDOW, 128), F32),
            pltpu.VMEM(lines, F32),
            pltpu.VMEM((2, WINDOW, D), BF16),
            pltpu.SemaphoreType.DMA((2,)),
        ],
        compiler_params=params_call(12),
        name="adam",
    )(me, *terms, tail, *args)
    return [one.reshape(-1) for one in outs]


def shards(tokens, cotangent, valid, params, first_moment, second_moment):
    if lax.axis_size("img") != 16 or lax.axis_size("row") != 2:
        return shards_general(tokens, cotangent, valid, params, first_moment, second_moment)
    me = lax.axis_index(BOTH).astype(jnp.int32).reshape(1)
    flat_tokens = tokens.reshape(LEN, D)
    flat_cotangent = cotangent.reshape(LEN, D)
    own, spare, extra = window_of(me, params)
    mask = jnp.tile(window_mask(lax.axis_index("row") * WIN), (1, 1, 4))
    parts, places, rows = gather_windows(own, spare, extra, flat_tokens[:HALF], mask)
    windows, packed, attn, probs, near, far, w_proj, vecs, w_qkv, laid, token = attend(
        me, flat_tokens, rows, mask, parts, places
    )
    back = from_partner(far, "row", 0)
    w_up, w_down, _ = feed_weights(me, parts, places, pause(token))
    hidden, active, grad_up, sums_up, low, low_three, high_three, low_send, high_send, token = feed(
        me, valid, flat_tokens, back, near, flat_cotangent, vecs, w_up, w_down
    )
    core_high_three, core_low_three = swap(high_send, 2), swap(low_send, 2)
    grad_middle, far_grad, near_grad, sums_two, token = middle_grad(
        me, valid, flat_tokens, back, near, flat_cotangent, vecs, grad_up, w_up
    )
    far_grad = from_partner(far_grad, "row", 0)
    sent, token = sum_slots(2, [(high_three, 0), (core_high_three, 0)], pause(token))
    x_three = cross(sent, 4, 1)
    high, low_two, high_two, low_send, high_send, token = up_grad(
        me, hidden, grad_up, low, pause(token)
    )
    core_high_two, core_low_two = swap(high_send, 2), swap(low_send, 2)
    sent, three, token = split_sum(low_three, core_low_three, x_three, token)
    y_three = cross(sent, 1, 4)
    sent, token = sum_slots(2, [(high_two, 0), (core_high_two, 0)], pause(token))
    x_two = cross(sent, 4, 1)
    grad_attn, sums_proj, edge, low_one, high_one, low_send, high_send, token = proj_grad(
        me, near_grad, far_grad, attn, w_proj, high, pause(token)
    )
    core_high_one, core_low_one = swap(high_send, 2), swap(low_send, 2)
    grad_packed, strips, token = unattend(me, packed, grad_attn, attn, probs, pause(token, us=4))
    sent, two, token = split_sum(low_two, core_low_two, x_two, token)
    y_two = cross(sent, 1, 4)
    sent, token = sum_slots(2, [(high_one, 0), (core_high_one, 0)], pause(token))
    x_one = cross(sent, 4, 1)
    sums_qkv, low_zero, high_zero, low_send, high_send, token = qkv_grad(
        me, windows, edge, grad_packed, pause(token)
    )
    core_high_zero, core_low_zero = swap(high_send, 2), swap(low_send, 2)
    upper, other, token = sum_three(me, three, y_three, two, y_two, token)
    z_upper = swap(other, 8)
    sent, one, token = split_sum(low_one, core_low_one, x_one, token)
    y_one = cross(sent, 1, 4)
    sent, token = sum_slots(2, [(high_zero, 0), (core_high_zero, 0)], pause(token, us=12))
    x_zero = cross(sent, 4, 1)
    near_in, far_in, sums_one, token = token_grad(
        me, grad_packed, w_qkv, laid, vecs, pause(token)
    )
    upper, token = sum_two(upper, z_upper, token)
    far_upper = to_half(upper, True)
    one, token = sum_two(one, y_one, token)
    z_one = swap(one, 8, lambda d: d // 8 in (0, 2))
    small, token = small_grads(strips, sums_qkv, sums_proj, sums_up, sums_one, sums_two, token)
    small = small + swap(small, 2)
    sent, zero, token = split_sum(low_zero, core_low_zero, x_zero, token, small[:8, :128])
    y_zero = cross(sent, 1, 4)
    one, token = sum_two(one, z_one, token)
    far_one = swap(one, 16, lambda d: d // 8 == 3)
    zero, token = sum_two(zero, y_zero, token)
    z_zero = swap(zero, 8, lambda d: d // 8 in (1, 3))
    small = (small + swap(small, 4)) + (swap(small, 1) + swap(small, 5))
    upper, token = sum_two(upper, far_upper, token)
    one, token = sum_two(one, far_one, token)
    small = gate(small, token)
    small = small + to_half(small, True)
    zero, token = sum_two(zero, z_zero, token)
    far_zero = swap(zero, 16, lambda d: d // 8 == 2)
    small = small_lines(small + swap(small, 8, lambda d: d // 8 == 2))
    far_in = from_partner(gate(far_in, token), "row", 0)
    output, token = block_output(
        me, flat_tokens, back, near, vecs, active, w_down, token
    )
    input_grad = grad_middle + jnp.concatenate([far_in, near_in], 0).astype(F32)
    terms = [zero, far_zero, one, upper]
    new = adam(me, terms, small, params, first_moment, second_moment)
    return (output.reshape(tokens.shape), input_grad.reshape(tokens.shape), *new)


def solution(mesh):
    return jax.shard_map(
        shards,
        mesh=mesh,
        in_specs=(
            P("img", "row", None, None),
            P("img", "row", None, None),
            P("img"),
            P(("img", "row")),
            P(("img", "row")),
            P(("img", "row")),
        ),
        out_specs=(
            P("img", "row", None, None),
            P("img", "row", None, None),
            P(("img", "row")),
            P(("img", "row")),
            P(("img", "row")),
            P(("img", "row")),
        ),
        check_vma=False,
    )
```

```python
import functools
import math

import jax
import jax.numpy as jnp
from jax import lax
from jax.experimental import pallas as pl
from jax.experimental.pallas import tpu as pltpu
from jax.sharding import PartitionSpec as P

D = 768
FF = 3072
HEADS = 24
HEAD_DIM = 32
WIN = 12
SHIFT = 6
SIDE = 24
STEP = 4
TABLE_ROWS = 529


EPSILON = 1e-05
MASKED = -100.0
DECAY = 0.05
ADAM_EPS = 1e-08
BETA_ONE = 0.5
BETA_TWO = 0.5


def from_partner(block, axis, apart):
    count = lax.axis_size(axis)
    route = []
    for low in range(count):
        high = low | 1 << apart
        if high != low and high < count:
            route += [(low, high), (high, low)]
    return lax.ppermute(block, axis, route)


def piece_shapes():
    return [
        (D, 3 * D),
        (D, D),
        (D, FF),
        (FF, D),
        (TABLE_ROWS, HEADS),
        (3 * D,),
        (D,),
        (FF,),
        (D,),
        (D,),
        (D,),
        (D,),
        (D,),
    ]


def unpack(flat_vec):
    pieces = []
    offset = 0
    for shape_one in piece_shapes():
        amount = math.prod(shape_one)
        pieces.append(lax.slice_in_dim(flat_vec, offset, offset + amount).reshape(shape_one))
        offset = offset + amount
    return pieces


def step_rates(position):
    rate_list = [
        D ** (-0.5),
        4.0 * D ** (-0.5),
        D ** (-0.5),
        FF ** (-0.5),
        1.0,
        0.3,
        0.3,
        0.3,
        0.3,
        0.4,
        0.3,
        0.4,
        0.3,
    ]
    result = jnp.zeros(position.shape, jnp.float32)
    offset = 0
    for shape_one, rate_one in zip(piece_shapes(), rate_list):
        amount = math.prod(shape_one)
        inside = (position >= offset) & (position < offset + amount)
        result = jnp.where(inside, jnp.float32(rate_one), result)
        offset = offset + amount
    return result


def layer_norm(values, gain_vec, shift_vec):
    centre = jnp.mean(values, -1, keepdims=True)
    centred = values - centre
    spread = jnp.mean(centred * centred, -1, keepdims=True)
    return centred * lax.rsqrt(spread + EPSILON) * gain_vec + shift_vec


def region_of(coord):
    return jnp.where(coord < SIDE - WIN, 0, jnp.where(coord < SIDE - SHIFT, 1, 2))


def relative_index():
    cell_index = jnp.arange(WIN * WIN, dtype=jnp.int32)
    row_part = cell_index // WIN
    col_part = cell_index % WIN
    return (row_part[:, None] - row_part[None, :] + WIN - 1) * (2 * WIN - 1) + (
        col_part[:, None] - col_part[None, :] + WIN - 1
    )


def window_mask(row_first):
    row_coord = row_first + jnp.arange(WIN, dtype=jnp.int32)
    col_coord = jnp.arange(SIDE, dtype=jnp.int32)
    region_ids = 3 * region_of(row_coord)[:, None] + region_of(col_coord)[None, :]
    region_ids = (
        region_ids.reshape(WIN, SIDE // WIN, WIN).transpose(1, 0, 2).reshape(SIDE // WIN, WIN * WIN)
    )
    same = region_ids[:, :, None] == region_ids[:, None, :]
    return jnp.where(same, 0.0, MASKED).astype(jnp.float32)


def to_windows(grid_rows):
    img_count = grid_rows.shape[0]
    width = grid_rows.shape[-1]
    shaped = grid_rows.reshape(img_count, WIN, SIDE // WIN, WIN, width).transpose(0, 2, 1, 3, 4)
    return shaped.reshape(img_count * (SIDE // WIN), WIN * WIN, width)


def from_windows(window_rows, img_count):
    width = window_rows.shape[-1]
    shaped = window_rows.reshape(img_count, SIDE // WIN, WIN, WIN, width).transpose(0, 2, 1, 3, 4)
    return shaped.reshape(img_count, WIN, SIDE, width)


BF16 = jnp.bfloat16
F32 = jnp.float32
BOTH = ("img", "row")
ROWS = 9248
TILE = 16
WINDOW = 304
WIDE = 2 * D // 4
VMEM_MOST = 60 * 1024 * 1024


def contract_rows(left_op, right_op):
    summed_dims = tuple(range(left_op.ndim - 1))
    return lax.dot_general(
        left_op,
        right_op,
        ((summed_dims, summed_dims), ((), ())),
        preferred_element_type=jnp.float32,
    )


def times_transposed(left_op, right_op):
    return lax.dot_general(
        left_op,
        right_op,
        (((left_op.ndim - 1,), (1,)), ((), ())),
        preferred_element_type=jnp.float32,
    )


def scores_of(queries, keys_all, bias_full, region_mask):
    raw_scores = jnp.einsum(
        "wqhd,wkhd->whqk", queries, keys_all, preferred_element_type=jnp.float32
    )
    return raw_scores * HEAD_DIM ** (-0.5) + bias_full[None] + region_mask[:, None]


def shards_general(tokens, cotangent, valid, params, first_moment, second_moment):
    img_count = tokens.shape[0]
    win_count = img_count * (SIDE // WIN)
    tile_len = WIN * WIN
    gathered = lax.all_gather(params.astype(jnp.bfloat16), ("img", "row"), axis=0, tiled=True)
    (
        w_qkv,
        w_proj,
        w_up,
        w_down,
        bias_table,
        b_qkv,
        b_proj,
        b_up,
        b_down,
        gain_one,
        shift_one,
        gain_two,
        shift_two,
    ) = unpack(gathered)
    images = tokens.astype(jnp.float32)
    normed, norm_pull = jax.vjp(
        layer_norm, images, gain_one.astype(jnp.float32), shift_one.astype(jnp.float32)
    )
    normed_low = normed.astype(jnp.bfloat16)
    incoming = from_partner(normed_low[:, :SHIFT], "row", 0)
    shifted = jnp.roll(jnp.concatenate([normed_low[:, SHIFT:], incoming], 1), -SHIFT, 2)
    windows = to_windows(shifted)
    packed = (
        jnp.dot(windows, w_qkv, preferred_element_type=jnp.float32) + b_qkv.astype(jnp.float32)
    ).astype(jnp.bfloat16)
    heads_view = packed.reshape(win_count, tile_len, 3, HEADS, HEAD_DIM)
    queries = heads_view[:, :, 0]
    keys_all = heads_view[:, :, 1]
    values_all = heads_view[:, :, 2]
    rel_index = relative_index()
    bias_full = bias_table.astype(jnp.float32)[rel_index].transpose(2, 0, 1)
    region_mask = jnp.tile(window_mask(lax.axis_index("row") * WIN), (img_count, 1, 1))
    scores = scores_of(queries, keys_all, bias_full, region_mask)
    row_top = jnp.max(scores, -1, keepdims=True)
    exponent = jnp.exp(scores - row_top)
    row_total = jnp.sum(exponent, -1, keepdims=True)
    log_total = row_top + jnp.log(row_total)
    attn_probs = (exponent / row_total).astype(jnp.bfloat16)
    attn_mixed = jnp.einsum(
        "whqk,wkhd->wqhd", attn_probs, values_all, preferred_element_type=jnp.float32
    )
    attn_mixed = attn_mixed.astype(jnp.bfloat16).reshape(win_count, tile_len, D)
    branch = (
        jnp.dot(attn_mixed, w_proj, preferred_element_type=jnp.float32) + b_proj.astype(jnp.float32)
    ).astype(jnp.bfloat16)
    branch_grid = jnp.roll(from_windows(branch, img_count), SHIFT, 2)
    returned = from_partner(branch_grid[:, SHIFT:], "row", 0)
    middle = images + jnp.concatenate([returned, branch_grid[:, :SHIFT]], 1).astype(jnp.float32)
    normed_two, norm_two_pull = jax.vjp(
        layer_norm, middle, gain_two.astype(jnp.float32), shift_two.astype(jnp.float32)
    )
    hidden_in = normed_two.astype(jnp.bfloat16)
    upward = jnp.dot(hidden_in, w_up, preferred_element_type=jnp.float32) + b_up.astype(jnp.float32)
    active_full, gelu_pull = jax.vjp(lambda values: jax.nn.gelu(values, approximate=False), upward)
    active = active_full.astype(jnp.bfloat16)
    output = (
        middle
        + jnp.dot(active, w_down, preferred_element_type=jnp.float32)
        + b_down.astype(jnp.float32)
    )
    regathered = lax.all_gather(params.astype(jnp.bfloat16), ("img", "row"), axis=0, tiled=True)
    fresh = unpack(regathered)
    w_qkv, w_proj, w_up, w_down = (fresh[0], fresh[1], fresh[2], fresh[3])
    grad_out = cotangent * valid.astype(jnp.bfloat16)[:, None, None, None]
    grad_w_down = contract_rows(active, grad_out)
    grad_b_down = jnp.sum(grad_out.astype(jnp.float32), (0, 1, 2))
    grad_active = times_transposed(grad_out, w_down)
    grad_up = gelu_pull(grad_active)[0].astype(jnp.bfloat16)
    grad_w_up = contract_rows(hidden_in, grad_up)
    grad_b_up = jnp.sum(grad_up.astype(jnp.float32), (0, 1, 2))
    grad_hidden = times_transposed(grad_up, w_up)
    grad_middle_ln, grad_gain_two, grad_shift_two = norm_two_pull(grad_hidden)
    grad_middle = grad_out.astype(jnp.float32) + grad_middle_ln
    middle_low = grad_middle.astype(jnp.bfloat16)
    arrived = from_partner(middle_low[:, :SHIFT], "row", 0)
    grad_grid = jnp.roll(jnp.concatenate([middle_low[:, SHIFT:], arrived], 1), -SHIFT, 2)
    grad_branch = to_windows(grad_grid)
    grad_w_proj = contract_rows(attn_mixed, grad_branch)
    grad_b_proj = jnp.sum(grad_branch.astype(jnp.float32), (0, 1))
    grad_attn = times_transposed(grad_branch, w_proj).astype(jnp.bfloat16)
    grad_attn = grad_attn.reshape(win_count, tile_len, HEADS, HEAD_DIM)
    again_scores = scores_of(queries, keys_all, bias_full, region_mask)
    again_probs = jnp.exp(again_scores - log_total)
    grad_values = jnp.einsum(
        "whqk,wqhd->wkhd",
        again_probs.astype(jnp.bfloat16),
        grad_attn,
        preferred_element_type=jnp.float32,
    )
    grad_probs = jnp.einsum(
        "wqhd,wkhd->whqk", grad_attn, values_all, preferred_element_type=jnp.float32
    )
    grad_scores = again_probs * (grad_probs - jnp.sum(again_probs * grad_probs, -1, keepdims=True))
    pair_sums = jnp.sum(grad_scores, 0).transpose(1, 2, 0).reshape(tile_len * tile_len, HEADS)
    grad_table = jax.ops.segment_sum(pair_sums, rel_index.reshape(-1), TABLE_ROWS)
    grad_raw = (grad_scores * HEAD_DIM ** (-0.5)).astype(jnp.bfloat16)
    grad_queries = jnp.einsum(
        "whqk,wkhd->wqhd", grad_raw, keys_all, preferred_element_type=jnp.float32
    )
    grad_keys = jnp.einsum("whqk,wqhd->wkhd", grad_raw, queries, preferred_element_type=jnp.float32)
    grad_packed = jnp.stack([grad_queries, grad_keys, grad_values], 2).astype(jnp.bfloat16)
    grad_packed = grad_packed.reshape(win_count, tile_len, 3 * D)
    grad_w_qkv = contract_rows(windows, grad_packed)
    grad_b_qkv = jnp.sum(grad_packed.astype(jnp.float32), (0, 1))
    grad_windows = times_transposed(grad_packed, w_qkv).astype(jnp.bfloat16)
    grad_shifted = jnp.roll(from_windows(grad_windows, img_count), SHIFT, 2)
    arrived_two = from_partner(grad_shifted[:, SHIFT:], "row", 0)
    grad_normed = jnp.concatenate([arrived_two, grad_shifted[:, :SHIFT]], 1).astype(jnp.float32)
    grad_images_ln, grad_gain_one, grad_shift_one = norm_pull(grad_normed)
    input_grad = grad_middle + grad_images_ln
    grad_list = [
        grad_w_qkv,
        grad_w_proj,
        grad_w_up,
        grad_w_down,
        grad_table,
        grad_b_qkv,
        grad_b_proj,
        grad_b_up,
        grad_b_down,
        grad_gain_one,
        grad_shift_one,
        grad_gain_two,
        grad_shift_two,
    ]
    grad_flat = jnp.concatenate([grad_one.reshape(-1) for grad_one in grad_list])
    grad_flat = jnp.pad(grad_flat, (0, gathered.shape[0] - grad_flat.shape[0]))
    grad_shard = lax.psum_scatter(grad_flat, ("img", "row"), scatter_dimension=0, tiled=True)
    shard_len = params.shape[0]
    position = lax.axis_index(("img", "row")) * shard_len + jnp.arange(shard_len, dtype=jnp.int32)
    step_rate = step_rates(position)
    new_first = BETA_ONE * first_moment + (1.0 - BETA_ONE) * grad_shard
    new_second = BETA_TWO * second_moment + (1.0 - BETA_TWO) * grad_shard * grad_shard
    fixed_first = new_first / (1.0 - BETA_ONE**STEP)
    fixed_second = new_second / (1.0 - BETA_TWO**STEP)
    new_params = params - step_rate * (
        fixed_first / (jnp.sqrt(fixed_second) + ADAM_EPS) + DECAY * params
    )
    return (
        output.astype(jnp.bfloat16),
        input_grad,
        new_params,
        new_params.astype(jnp.bfloat16),
        new_first,
        new_second,
    )


BF16 = jnp.bfloat16
F32 = jnp.float32
BOTH = ("img", "row")
TILE = 16
WINDOW = 304
LEN = 2 * WIN * WIN
QUADS = HEADS // 4
SPAN = 4 * WIN * WIN


def swap(block, mask, only=None):
    count = lax.axis_size(BOTH)
    route = [(d, d ^ mask) for d in range(count) if only is None or only(d)]
    return lax.ppermute(block, BOTH, route)


def params_call(mebibytes):
    return pltpu.CompilerParams(vmem_limit_bytes=mebibytes << 20)


def vmem(count):
    return [pl.BlockSpec(memory_space=pltpu.VMEM)] * count


SMEM_SPEC = pl.BlockSpec(memory_space=pltpu.SMEM)
ANY_SPEC = pl.BlockSpec(memory_space=pl.ANY)


def first_tile(device):
    return (289 * device) // TILE


def prep_body(me_ref, own_ref, out_ref, spare_ref, extra_ref, wide_ref):
    shift = me_ref[0] % TILE
    wide_ref[0:96] = jnp.zeros((96, 128), F32)
    wide_ref[1824:1920] = jnp.zeros((96, 128), F32)
    wide_ref[96:1830] = own_ref[...]
    for j in range(6):
        picked = wide_ref[pl.ds(96 - 6 * shift + j, WINDOW, stride=6), :]
        out_ref[:, 128 * j : 128 * (j + 1)] = picked.astype(BF16)
        spare_ref[:, 128 * j : 128 * (j + 1)] = picked.astype(BF16)
        extra_ref[:, 128 * j : 128 * (j + 1)] = picked.astype(BF16)


def window_of(me, own_flat):
    return pl.pallas_call(
        prep_body,
        out_shape=[jax.ShapeDtypeStruct((WINDOW, D), BF16)] * 3,
        in_specs=[SMEM_SPEC] + vmem(1),
        out_specs=vmem(3),
        scratch_shapes=[pltpu.VMEM((1920, 128), F32)],
        compiler_params=params_call(8),
        name="own_window",
    )(me, own_flat.reshape(-1, 128))


def mixer(groups, per):
    size = groups * per
    row = lax.broadcasted_iota(jnp.int32, (size, size), 0)
    col = lax.broadcasted_iota(jnp.int32, (size, size), 1)
    return (col == groups * (row % per) + row // per).astype(F32).astype(BF16)


def unmixer(groups, per):
    size = groups * per
    row = lax.broadcasted_iota(jnp.int32, (size, size), 0)
    col = lax.broadcasted_iota(jnp.int32, (size, size), 1)
    return (row == groups * (col % per) + col // per).astype(F32).astype(BF16)


def plane_rows(plane):
    low = first_tile(8 * plane) * TILE
    high = first_tile(8 * plane + 7) * TILE + WINDOW
    return low, high


def gate(value, *others):
    def body(*refs):
        pass

    return pl.pallas_call(
        body,
        out_shape=jax.ShapeDtypeStruct(value.shape, value.dtype),
        in_specs=[ANY_SPEC] * (1 + len(others)),
        out_specs=ANY_SPEC,
        input_output_aliases={0: 0},
        cost_estimate=cost(0),
        name="gate",
    )(value, *others)


def cross(block, zero, one):
    count = lax.axis_size(BOTH)
    return lax.ppermute(block, BOTH, [(d, d ^ (one if d & 2 else zero)) for d in range(count)])


def gather_windows(own, spare, extra, rows, *early):
    got = {0: own}
    first, second, third = {}, {}, {}

    def exchange(z):
        first[z] = cross(got[z], 4, 1)
        second[z] = cross(got[z], 1, 4)
        third[z] = cross(first[z], 1, 4)

    got[8] = swap(own, 8)
    first[0] = cross(own, 4, 1)
    second[0] = cross(own, 1, 4)
    spare = gate(spare, got[8])
    got[16] = swap(spare, 16)
    first[0] = gate(first[0], spare)
    third[0] = cross(first[0], 1, 4)
    got_rows = from_partner(rows, "row", 0)
    got[8] = gate(got[8], first[0], second[0])
    exchange(8)
    got[24] = swap(gate(extra, got[16]), 24)
    got[16] = gate(got[16], first[8], second[8], third[0], got_rows)
    exchange(16)
    got[24] = gate(got[24], first[16], second[16], third[8], *early)
    exchange(24)
    blocks, places = [], []
    for z in (0, 8, 16, 24):
        own_some = [got[z], first[z], second[z], third[z]]
        masks = ((z, z), (z | 4, z | 1), (z | 1, z | 4), (z | 5, z | 5))
        if z == 24:
            places.append((len(blocks), None, *masks[3]))
            places.append((len(blocks) + 1, None, masks[3][1] | 2, masks[3][0] | 2))
            last = own_some.pop()
            blocks += [last, swap(last, 2)]
        own_some = stacked(own_some)
        for n in range(own_some.shape[0]):
            zero, one = masks[n]
            places.append((len(blocks), n, zero, one))
            places.append((len(blocks) + 1, n, one | 2, zero | 2))
        blocks += [own_some, swap(own_some, 2)]
    return blocks, places, got_rows


def stacked_body(*refs):
    for i, ref in enumerate(refs[:-1]):
        refs[-1][i] = ref[...]


def stacked(blocks):
    return pl.pallas_call(
        stacked_body,
        out_shape=like(len(blocks), WINDOW, D),
        in_specs=vmem(len(blocks)),
        out_specs=vmem(1)[0],
        compiler_params=params_call(4),
        cost_estimate=cost(0),
        name="stacked",
    )(*blocks)


def load_windows(me, parts, places, first, last, flat_ref):
    base = first_tile(first) * TILE
    for device in (first, 16):
        if first <= device <= last:
            at = first_tile(device) * TILE - base
            flat_ref[at : at + TILE] = jnp.zeros((TILE, D), BF16)

    def each(act):
        for block, slot, zero, one in places:
            device = me ^ jnp.where((me & 2) == 0, zero, one)
            start = pl.multiple_of(first_tile(device) * TILE - base, TILE)
            part = parts[block] if slot is None else parts[block].at[slot]

            @pl.when((device >= first) & (device <= last))
            def _():
                act(part, start)

    def main(part, start):
        def step(i, carry):
            at = pl.multiple_of(48 * i + TILE, TILE)
            to = pl.multiple_of(start + at, TILE)
            flat_ref[pl.ds(to, 48)] = part[pl.ds(at, 48)]
            return carry

        lax.fori_loop(0, 6, step, 0)

    def edge(part, start):
        flat_ref[pl.ds(start, TILE)] += part[0:TILE]

    each(main)
    each(edge)


def load_small(me, parts, places, tail_ref):
    for block, slot, zero, one in places:
        part = parts[block] if slot is None else parts[block].at[slot]

        @pl.when(me ^ jnp.where((me & 2) == 0, zero, one) == 31)
        def _():
            tail_ref[...] = part[WINDOW - 32 : WINDOW]


def flat_scratch(first, last):
    return pltpu.VMEM(
        (first_tile(last) * TILE + WINDOW - first_tile(first) * TILE, D), BF16
    )


def unmix_rows(flat_ref, out_ref, base, groups, per, steps):
    mix = mixer(groups, per)
    size = groups * per
    for t in range(steps):
        rows = flat_ref[base + size * t : base + size * (t + 1)]
        out = jnp.dot(mix, rows, preferred_element_type=F32).astype(BF16)
        for j in range(groups):
            out_ref[j, per * t : per * (t + 1)] = out[per * j : per * (j + 1)]


def mix_rows(in_ref, flat_ref, base, groups, per, steps):
    mix = unmixer(groups, per)
    size = groups * per
    for t in range(steps):
        rows = jnp.concatenate([in_ref[j, per * t : per * (t + 1)] for j in range(groups)], 0)
        out = jnp.dot(mix, rows, preferred_element_type=F32).astype(BF16)
        flat_ref[base + size * t : base + size * (t + 1)] = out


def cut_windows(me, plane, flat_ref, base, keeps, sends):
    for flip in (2, 0):
        for s in range(4):
            first = jnp.where(((me ^ flip) & 2) == 0, 4, 1)
            away = (first if s & 2 else 0) + (5 - first if s & 1 else 0)
            device = 8 * plane + ((me & 7) ^ (away | flip))
            start = pl.multiple_of(first_tile(device) * TILE - base, TILE)
            window = flat_ref[pl.ds(start, WINDOW)]
            (sends if flip else keeps)[s // 2][s % 2] = window


def cost(microseconds):
    return pl.CostEstimate(
        flops=int(1e9 * microseconds),
        bytes_accessed=int(3.2e6 * microseconds),
        transcendentals=0,
    )


WINDOWS = [jax.ShapeDtypeStruct((2, WINDOW, D), BF16)] * 4


def like(*shape, dtype=BF16):
    return jax.ShapeDtypeStruct(shape, dtype)


def call(body, name, ins, outs, scratch, limit, ties=(), us=0, far=0):
    n_in, n_tie, n_out = len(ins), len(ties), len(outs)
    first_out = n_in + n_tie

    def wrapped(*refs):
        body(*refs[:n_in], *refs[first_out : first_out + n_out], *refs[first_out + n_out + 1 :])
        token_ref = refs[first_out + n_out]
        token_ref[...] = jnp.zeros_like(token_ref)

    specs = [SMEM_SPEC if one.dtype == jnp.int32 else vmem(1)[0] for one in ins]
    return pl.pallas_call(
        wrapped,
        out_shape=[*outs, like(8, 128, dtype=F32)],
        in_specs=specs + vmem(n_tie),
        out_specs=vmem(n_out - far)
        + [pl.BlockSpec(memory_space=pltpu.HBM)] * far
        + vmem(1),
        scratch_shapes=scratch,
        compiler_params=params_call(limit),
        cost_estimate=cost(us),
        name=name,
    )(*ins, *ties)


def pause(*ties, us=4):
    return call(lambda: None, "pause", [], [], [], 4, ties, us)[0]


def normal_parts(values):
    centre = jnp.mean(values, -1, keepdims=True)
    centred = values - centre
    spread = jnp.mean(centred * centred, -1, keepdims=True)
    scale = lax.rsqrt(spread + EPSILON)
    return centred * scale, scale


def normal_pull(n, scale, grad, gain):
    e = grad * gain
    return scale * (
        e - jnp.mean(e, -1, keepdims=True) - n * jnp.mean(e * n, -1, keepdims=True)
    )


def over_heads(block):
    head = lax.broadcasted_iota(jnp.int32, block.shape, 1) // HEAD_DIM
    return jnp.concatenate([jnp.where(head == h, block, jnp.zeros_like(block)) for h in range(4)], 0)


def own_columns(block):
    head = lax.broadcasted_iota(jnp.int32, (144, 128), 1) // HEAD_DIM
    out = block[0:144]
    for h in range(1, 4):
        out = jnp.where(head == h, block[144 * h : 144 * (h + 1)], out)
    return out


def contract(one, two, a, b):
    return lax.dot_general(one, two, (((a,), (b,)), ((), ())), preferred_element_type=F32)


def lay(out_ref, near, far):
    for i in range(WIN):
        ref, k = (near, 24 * i) if i < SHIFT else (far, 24 * (i - SHIFT))
        out_ref[12 * i : 12 * i + 12] = ref[k + 6 : k + 18]
        out_ref[144 + 12 * i : 150 + 12 * i] = ref[k + 18 : k + 24]
        out_ref[150 + 12 * i : 156 + 12 * i] = ref[k : k + 6]


def unlay(ref, near, far):
    for i in range(WIN):
        out_ref, k = (near, 24 * i) if i < SHIFT else (far, 24 * (i - SHIFT))
        out_ref[k + 6 : k + 18] = ref[12 * i : 12 * i + 12]
        out_ref[k + 18 : k + 24] = ref[144 + 12 * i : 150 + 12 * i]
        out_ref[k : k + 6] = ref[150 + 12 * i : 156 + 12 * i]


HALF = LEN // 2
LAY_SCRATCH = [pltpu.VMEM((LEN, D), F32), pltpu.VMEM((HALF, D), F32), pltpu.VMEM((HALF, D), F32)]


def unpack_small(tail_ref, vecs_ref, strips_ref, wide_ref, shift_ref):
    tail = tail_ref[...].astype(F32)
    rolled = pltpu.roll(tail, 360, 1)
    below = pltpu.roll(rolled, 31, 0)
    lane = lax.broadcasted_iota(jnp.int32, (16, D), 1)
    vecs_ref[...] = jnp.where(lane < 360, rolled[16:32], below[16:32])
    cell = lax.broadcasted_iota(jnp.int32, (32, D), 1) // HEADS
    which = lax.broadcasted_iota(jnp.int32, (32, D), 0)
    for r in range(17):
        row = jnp.broadcast_to(tail[r : r + 1], (32, D))
        wide_ref[32 * r : 32 * (r + 1)] = jnp.where(cell == which, row, 0.0).astype(BF16)
    lane = lax.broadcasted_iota(jnp.int32, (D, 128), 0)
    head = lax.broadcasted_iota(jnp.int32, (D, 128), 1)
    pick = (lane % HEADS == head).astype(F32).astype(BF16)
    table = jnp.dot(wide_ref[0:544], pick, preferred_element_type=F32)
    row = lax.broadcasted_iota(jnp.int32, table.shape, 0)
    table = jnp.where(row < TABLE_ROWS, table, 0.0)
    table = jnp.concatenate([table, jnp.zeros((96, 128), F32)], 0).T[0:HEADS]
    for j in range(WIN):
        moved = pltpu.roll(table, 629 + j, 1) if j < 11 else table
        shift_ref[24 * j : 24 * (j + 1), 0:640] = moved
    strips = contract(shift_ref[:, 0:640].astype(BF16), table_spread(), 1, 1)
    for j in range(WIN):
        strips_ref[:, j, :] = strips[24 * j : 24 * (j + 1)]


def table_spread():
    m = lax.broadcasted_iota(jnp.int32, (384, 640), 0)
    n = lax.broadcasted_iota(jnp.int32, (384, 640), 1)
    return ((n == 23 * (m // WIN) + m % WIN) & (m < 276)).astype(F32).astype(BF16)


def attend_body(places, me_ref, tokens_ref, rows_ref, mask_ref, *refs):
    parts = refs[:10]
    windows_ref, packed_ref, attn_ref, probs_ref, near_ref, far_ref, proj_ref, vecs_ref, qkv_out, laid_out = refs[10:20]
    flat_ref, wide_ref, one_ref, two_ref, bias_ref, qkv_ref, laid_ref, sems, tail_ref, strips_ref = refs[20:]
    load_small(me_ref[0], parts, places, tail_ref)
    unpack_small(tail_ref, vecs_ref, strips_ref, flat_ref, wide_ref)
    load_windows(me_ref[0], parts, places, 0, 10, flat_ref)
    one_ref[...] = tokens_ref[HALF:LEN].astype(F32)
    two_ref[...] = rows_ref[...].astype(F32)
    lay(wide_ref, one_ref, two_ref)
    laid = wide_ref[...]
    laid_ref[...] = laid.astype(BF16)
    n, _ = normal_parts(laid)
    windows_ref[...] = (n * vecs_ref[9:10] + vecs_ref[10:11]).astype(BF16)
    unmix_rows(flat_ref, qkv_ref, 0, 3, 64, 12)
    copies = [
        pltpu.make_async_copy(qkv_ref, qkv_out, sems.at[0]),
        pltpu.make_async_copy(laid_ref, laid_out, sems.at[1]),
    ]
    for copy in copies:
        copy.start()
    proj_ref[...] = flat_ref[2304:3072]

    def project(j, carry):
        packed_ref[j] = (
            jnp.dot(windows_ref[...], qkv_ref[j], preferred_element_type=F32)
            + vecs_ref[pl.ds(j, 1)]
        ).astype(BF16)
        return carry

    lax.fori_loop(0, 3, project, 0)

    def quad(g, carry):
        lanes = pl.ds(pl.multiple_of(128 * g, 128), 128)
        for h in range(4):
            for i in range(WIN):
                low = 12 * (11 - i)
                bias_ref[12 * i : 12 * i + 12, 144 * h : 144 * (h + 1)] = strips_ref[
                    4 * g + h, 0:12, low : low + 144
                ]
        for w in range(2):
            rows = pl.ds(144 * w, 144)
            queries = over_heads(packed_ref[0, rows, lanes])
            scores = contract(packed_ref[1, rows, lanes], queries, 1, 1)
            scores = scores * HEAD_DIM ** (-0.5) + bias_ref[...] + mask_ref[w]
            top = jnp.max(scores, 0, keepdims=True)
            exponent = jnp.exp(scores - top)
            total = jnp.sum(exponent, 0, keepdims=True)
            probs = (exponent * (1.0 / total)).astype(BF16)
            probs_ref[2 * g + w] = probs
            mixed = contract(probs, packed_ref[2, rows, lanes], 0, 0)
            attn_ref[rows, lanes] = own_columns(mixed).astype(BF16)
        return carry

    lax.fori_loop(0, QUADS, quad, 0)
    wide_ref[...] = (
        jnp.dot(attn_ref[...], proj_ref[...], preferred_element_type=F32) + vecs_ref[3:4]
    )
    unlay(wide_ref, one_ref, two_ref)
    near_ref[...] = one_ref[...].astype(BF16)
    far_ref[...] = two_ref[...].astype(BF16)
    for copy in copies:
        copy.wait()


def attend(me, tokens, rows, mask, parts, places):
    return call(
        functools.partial(attend_body, places),
        "attention_forward",
        [me, tokens, rows, mask, *parts],
        [
            like(LEN, D),
            like(3, LEN, D),
            like(LEN, D),
            like(2 * QUADS, 144, SPAN),
            like(HALF, D),
            like(HALF, D),
            like(D, D),
            like(16, D, dtype=F32),
            like(3, D, D),
            like(LEN, D),
        ],
        [flat_scratch(0, 10)]
        + LAY_SCRATCH
        + [
            pltpu.VMEM((144, SPAN), F32),
            pltpu.VMEM((3, D, D), BF16),
            pltpu.VMEM((LEN, D), BF16),
            pltpu.SemaphoreType.DMA((2,)),
            pltpu.VMEM((32, D), BF16),
            pltpu.VMEM((HEADS, WIN, 384), F32),
        ],
        22,
        far=2,
    )


def middle_of(tokens_ref, back_ref, near_ref):
    branch = jnp.concatenate([back_ref[...].astype(F32), near_ref[...].astype(F32)], 0)
    return tokens_ref[...].astype(F32) + branch


def feed_weights_body(places, me_ref, *refs):
    parts = refs[:10]
    up_ref, down_ref, flat_ref = refs[10:]
    load_windows(me_ref[0], parts, places, 10, 31, flat_ref)
    base = first_tile(10) * TILE
    unmix_rows(flat_ref, up_ref, 3072 - base, 4, 48, 16)

    def step(i, carry):
        at = pl.multiple_of(64 * i, 64)
        down_ref[pl.ds(at, 64)] = flat_ref[pl.ds(pl.multiple_of(6144 - base + at, TILE), 64)]
        return carry

    lax.fori_loop(0, 48, step, 0)


def feed_weights(me, parts, places, *ties):
    return call(
        functools.partial(feed_weights_body, places),
        "feed_weights",
        [me, *parts],
        [like(4, D, D), like(FF, D)],
        [flat_scratch(10, 31)],
        20,
        ties,
    )


def feed_body(me_ref, valid_ref, tokens_ref, back_ref, near_ref, cotangent_ref, vecs_ref, up_ref, down_ref, hidden_ref, active_ref, gradup_ref, sums_ref, low_ref, low_keep, high_keep, low_send, high_send, grad_ref):
    me = me_ref[0]
    n, _ = normal_parts(middle_of(tokens_ref, back_ref, near_ref))
    hidden_ref[...] = (n * vecs_ref[11:12] + vecs_ref[12:13]).astype(BF16)
    grad_out = cotangent_ref[...] * valid_ref[0].astype(F32).astype(BF16)
    grad_ref[3072:3104] = jnp.zeros((32, D), BF16)

    def step(j, carry):
        at = pl.multiple_of(D * j, D)
        down = down_ref[pl.ds(at, D)]
        upward = jnp.dot(hidden_ref[...], up_ref[j], preferred_element_type=F32)
        upward = upward + vecs_ref[pl.ds(4 + j, 1)]
        grad_active = contract(grad_out, down, 1, 1)
        share = 0.5 * (1.0 + lax.erf(upward * (0.5**0.5)))
        density = jnp.exp(-0.5 * upward * upward) * ((2.0 * math.pi) ** (-0.5))
        active = (upward * share).astype(BF16)
        grad_up = (grad_active * (share + upward * density)).astype(BF16)
        active_ref[j] = active
        gradup_ref[j] = grad_up
        sums_ref[pl.ds(j, 1)] = jnp.sum(grad_up.astype(F32), 0, keepdims=True)
        grad_ref[pl.ds(at, D)] = contract(active, grad_out, 0, 0).astype(BF16)
        return carry

    lax.fori_loop(0, 4, step, 0)
    cut_windows(me, 3, grad_ref, 6144, (low_keep, high_keep), (low_send, high_send))
    low_ref[...] = grad_ref[0:800]
    sums_ref[4:5] = jnp.sum(grad_out.astype(F32), 0, keepdims=True)


def feed(me, valid, tokens, back, near, cotangent, vecs, w_up, w_down):
    return call(
        feed_body,
        "feed_forward",
        [me, valid, tokens, back, near, cotangent, vecs, w_up, w_down],
        [
            like(LEN, D),
            like(4, LEN, D),
            like(4, LEN, D),
            like(8, D, dtype=F32),
            like(800, D),
            *WINDOWS,
        ],
        [pltpu.VMEM((3104, D), BF16)],
        16,
    )


def middle_body(me_ref, valid_ref, tokens_ref, back_ref, near_ref, cotangent_ref, vecs_ref, gradup_ref, up_ref, grad_ref, far_out, near_out, sums_ref):
    n, scale = normal_parts(middle_of(tokens_ref, back_ref, near_ref))
    grad_hidden = contract(gradup_ref[0], up_ref[0], 1, 1)
    for j in range(1, 4):
        grad_hidden = grad_hidden + contract(gradup_ref[j], up_ref[j], 1, 1)
    sums_ref[0:1] = jnp.sum(grad_hidden * n, 0, keepdims=True)
    sums_ref[1:2] = jnp.sum(grad_hidden, 0, keepdims=True)
    grad_out = (cotangent_ref[...] * valid_ref[0].astype(F32).astype(BF16)).astype(F32)
    grad = grad_out + normal_pull(n, scale, grad_hidden, vecs_ref[11:12])
    grad_ref[...] = grad
    far_out[...] = grad[:HALF].astype(BF16)
    near_out[...] = grad[HALF:].astype(BF16)


def middle_grad(me, valid, tokens, back, near, cotangent, vecs, grad_up, w_up):
    return call(
        middle_body,
        "middle_grad",
        [me, valid, tokens, back, near, cotangent, vecs, grad_up, w_up],
        [like(LEN, D, dtype=F32), like(HALF, D), like(HALF, D), like(8, D, dtype=F32)],
        [],
        12,
    )


def up_body(me_ref, hidden_ref, gradup_ref, low_ref, proj_ref, low_keep, high_keep, low_send, high_send, quad_ref, flat_ref):
    me = me_ref[0]

    def step(j, carry):
        quad_ref[j] = contract(hidden_ref[...], gradup_ref[j], 0, 0).astype(BF16)
        return carry

    lax.fori_loop(0, 4, step, 0)
    flat_ref[3072:3872] = low_ref[...]
    mix_rows(quad_ref, flat_ref, 0, 4, 48, 16)
    cut_windows(me, 2, flat_ref, 3072, (low_keep, high_keep), (low_send, high_send))
    proj_ref[...] = flat_ref[0:1552]


def up_grad(me, hidden, grad_up, low, *ties):
    return call(
        up_body,
        "up_grad",
        [me, hidden, grad_up, low],
        [like(1552, D), *WINDOWS],
        [pltpu.VMEM((4, D, D), BF16), pltpu.VMEM((3872, D), BF16)],
        16,
        ties,
    )


def proj_body(me_ref, near_ref, far_ref, attn_ref, proj_ref, high_ref, back_ref, sums_ref, edge_ref, low_keep, high_keep, low_send, high_send, flat_ref, wide_ref, one_ref, two_ref):
    me = me_ref[0]
    one_ref[...] = near_ref[...].astype(F32)
    two_ref[...] = far_ref[...].astype(F32)
    lay(wide_ref, one_ref, two_ref)
    grad = wide_ref[...].astype(BF16)
    flat_ref[0:768] = contract(attn_ref[...], grad, 0, 0).astype(BF16)
    flat_ref[768:2320] = high_ref[...]
    cut_windows(me, 1, flat_ref, 2304, (low_keep, high_keep), (low_send, high_send))
    edge_ref[...] = flat_ref[0:16]
    back_ref[...] = contract(grad, proj_ref[...], 1, 1).astype(BF16)
    sums_ref[0:1] = jnp.sum(grad.astype(F32), 0, keepdims=True)


def proj_grad(me, near, far, attn, w_proj, high, *ties):
    return call(
        proj_body,
        "proj_grad",
        [me, near, far, attn, w_proj, high],
        [like(LEN, D), like(8, D, dtype=F32), like(16, D), *WINDOWS],
        [pltpu.VMEM((2320, D), BF16)] + LAY_SCRATCH,
        12,
        ties,
    )


def unattend_quads(quads, packed_ref, grad_ref, attn_ref, probs_ref, back_ref, strips_ref, pairs_ref):
    strips_ref[...] = jnp.zeros_like(strips_ref)

    def quad(g, carry):
        lanes = pl.ds(pl.multiple_of(128 * g, 128), 128)
        for w in range(2):
            rows = pl.ds(144 * w, 144)
            queries = over_heads(packed_ref[0, rows, lanes])
            keys = packed_ref[1, rows, lanes]
            values = packed_ref[2, rows, lanes]
            grad = grad_ref[rows, lanes]
            product = -(attn_ref[rows, lanes].astype(F32) * grad.astype(F32)).astype(BF16)
            grads = over_heads(grad)
            left = jnp.concatenate([values, jnp.ones_like(values)], 1)
            right = jnp.concatenate([grads, over_heads(product)], 1)
            probs = probs_ref[2 * g + w]
            grad_scores = probs.astype(F32) * contract(left, right, 1, 1)
            if w == 0:
                pairs_ref[...] = grad_scores
            else:
                pairs_ref[...] += grad_scores
            raw = (grad_scores * HEAD_DIM ** (-0.5)).astype(BF16)
            back_ref[0, rows, lanes] = own_columns(contract(raw, keys, 0, 0)).astype(BF16)
            back_ref[1, rows, lanes] = jnp.dot(
                raw, queries, preferred_element_type=F32
            ).astype(BF16)
            back_ref[2, rows, lanes] = jnp.dot(
                probs, grads, preferred_element_type=F32
            ).astype(BF16)
        for h in range(4):
            for i in range(WIN):
                low = 12 * (11 - i)
                strips_ref[4 * (g - quads[0]) + h, 0:12, low : low + 144] += pairs_ref[
                    12 * i : 12 * i + 12, 144 * h : 144 * (h + 1)
                ]
        return carry

    lax.fori_loop(*quads, quad, 0)


def unattend_body(me_ref, packed_ref, grad_ref, attn_ref, probs_ref, back_ref, strips_ref, pairs_ref):
    unattend_quads((0, QUADS), packed_ref, grad_ref, attn_ref, probs_ref, back_ref, strips_ref, pairs_ref)


def qkv_body(me_ref, windows_ref, edge_ref, back_ref, sums_ref, low_keep, high_keep, low_send, high_send, trio_ref, flat_ref):
    me = me_ref[0]

    def step(j, carry):
        trio_ref[j] = contract(windows_ref[...], back_ref[j], 0, 0).astype(BF16)
        sums_ref[pl.ds(j, 1)] = jnp.sum(back_ref[j].astype(F32), 0, keepdims=True)
        return carry

    lax.fori_loop(0, 3, step, 0)
    mix_rows(trio_ref, flat_ref, 0, 3, 64, 12)
    flat_ref[2304:2320] = edge_ref[...]
    cut_windows(me, 0, flat_ref, 0, (low_keep, high_keep), (low_send, high_send))


def unattend(me, packed, grad, attn, probs, *ties):
    return call(
        unattend_body,
        "attention_backward",
        [me, packed, grad, attn, probs],
        [like(3, LEN, D), like(HEADS, WIN, 384, dtype=F32)],
        [pltpu.VMEM((144, SPAN), F32)],
        10,
        ties,
    )


def qkv_grad(me, windows, edge, back, *ties):
    return call(
        qkv_body,
        "qkv_grad",
        [me, windows, edge, back],
        [like(8, D, dtype=F32), *WINDOWS],
        [pltpu.VMEM((3, D, D), BF16), pltpu.VMEM((2320, D), BF16)],
        12,
        ties,
    )


def token_body(me_ref, back_ref, qkv_ref, laid_ref, vecs_ref, near_out, far_out, sums_ref, wide_ref, one_ref, two_ref):
    grad = contract(back_ref[0], qkv_ref[0], 1, 1)
    for j in (1, 2):
        grad = grad + contract(back_ref[j], qkv_ref[j], 1, 1)
    n, scale = normal_parts(laid_ref[...].astype(F32))
    sums_ref[0:1] = jnp.sum(grad * n, 0, keepdims=True)
    sums_ref[1:2] = jnp.sum(grad, 0, keepdims=True)
    wide_ref[...] = normal_pull(n, scale, grad, vecs_ref[9:10])
    unlay(wide_ref, one_ref, two_ref)
    near_out[...] = one_ref[...].astype(BF16)
    far_out[...] = two_ref[...].astype(BF16)


def token_grad(me, back, w_qkv, laid, vecs, *ties):
    return call(
        token_body,
        "token_grad",
        [me, back, w_qkv, laid, vecs],
        [like(HALF, D), like(HALF, D), like(8, D, dtype=F32)],
        LAY_SCRATCH,
        10,
        ties,
    )


def output_body(me_ref, tokens_ref, back_ref, near_ref, vecs_ref, active_ref, down_ref, out_ref):
    total = middle_of(tokens_ref, back_ref, near_ref) + vecs_ref[8:9]
    for j in range(4):
        total = total + jnp.dot(
            active_ref[j], down_ref[D * j : D * (j + 1)], preferred_element_type=F32
        )
    out_ref[...] = total.astype(BF16)


def block_output(me, tokens, back, near, vecs, active, w_down, *ties):
    return call(
        output_body,
        "block_output",
        [me, tokens, back, near, vecs, active, w_down],
        [like(LEN, D)],
        [],
        10,
        ties,
    )


def sum_body(slots, lows, *refs):
    for i in range(slots):
        total = refs[0][lows[0] + i].astype(F32)
        for ref, low in zip(refs[1 : len(lows)], lows[1:]):
            total = total + ref[low + i].astype(F32)
        refs[-1][i] = total.astype(BF16)


def sum_slots(slots, terms, *ties):
    return call(
        functools.partial(sum_body, slots, [low for _, low in terms]),
        "sum_slots",
        [one for one, _ in terms],
        [like(slots, WINDOW, D)],
        [],
        6,
        ties,
    )


def split_body(low_ref, core_ref, x_ref, sent_ref, kept_ref):
    for slot, ref in ((1, sent_ref), (0, kept_ref)):
        total = low_ref[slot].astype(F32) + core_ref[slot].astype(F32)
        ref[...] = (total + x_ref[slot].astype(F32)).astype(BF16)


def split_sum(low, core, x, *ties):
    return call(
        split_body, "split_sum", [low, core, x], [like(WINDOW, D), like(WINDOW, D)], [], 6, ties
    )


def arranged_body(me_ref, high_ref, low_ref, small_ref, own_ref, other_ref, sum_ref):
    me = me_ref[0]
    odd = (me // 8) % 2 == 1
    sum_ref[...] = high_ref[...].astype(F32)

    @pl.when(me % 8 == 7)
    def _():
        sum_ref[WINDOW - 32 : WINDOW] += small_ref[...]

    high = sum_ref[...].astype(BF16)
    low = low_ref[...]

    @pl.when(odd)
    def _():
        own_ref[...] = high
        other_ref[...] = low

    @pl.when(jnp.logical_not(odd))
    def _():
        own_ref[...] = low
        other_ref[...] = high


def arranged(me, high, low, small, *ties):
    return call(
        arranged_body,
        "arranged",
        [me, high, low, small],
        [like(WINDOW, D), like(WINDOW, D)],
        [pltpu.VMEM((WINDOW, D), F32)],
        8,
        ties,
    )


def sum_two(one, two, *ties):
    def body(one_ref, two_ref, out_ref):
        out_ref[...] = (one_ref[...].astype(F32) + two_ref[...].astype(F32)).astype(BF16)

    return call(body, "sum_two", [one, two], [like(WINDOW, D)], [], 6, ties)


def to_half(block, upper):
    return swap(block, 16, lambda d: (d // 16 == 1) != upper)


def small_body(strips_ref, qkv_ref, proj_ref, up_ref, one_ref, two_ref, out_ref, rows_ref):
    out_ref[...] = jnp.zeros_like(out_ref)
    out_ref[0:3] = qkv_ref[0:3]
    out_ref[3:4] = proj_ref[0:1]
    out_ref[4:9] = up_ref[0:5]
    out_ref[9:11] = one_ref[0:2]
    out_ref[11:13] = two_ref[0:2]
    for j in range(WIN):
        rows_ref[24 * j : 24 * (j + 1)] = strips_ref[:, j, :]
    rows = rows_ref[...]
    high = rows.astype(BF16)
    low = (rows - high.astype(F32)).astype(BF16)
    spread = table_spread()
    wide = jnp.dot(high, spread, preferred_element_type=F32) + jnp.dot(
        low, spread, preferred_element_type=F32
    )
    total = wide[264:288]
    for j in range(WIN - 1):
        total = total + pltpu.roll(wide[24 * j : 24 * (j + 1)], 11 - j, 1)
    out_ref[16:40, 0:640] = total


def small_grads(strips, qkv, proj, up, one, two, *ties):
    return call(
        small_body,
        "small_grads",
        [strips, qkv, proj, up, one, two],
        [like(40, D, dtype=F32)],
        [pltpu.VMEM((288, 384), F32)],
        8,
        ties,
    )


def lines_body(small_ref, out_ref, table_ref, vec_ref, line_ref):
    table = jnp.concatenate([small_ref[16:40, 0:640], jnp.zeros((104, 640), F32)], 0)
    table_ref[...] = table.T
    wide = jnp.zeros((40, 384), F32)
    for q in range(16):
        rows = table_ref[pl.ds(q, 40, stride=16), :]
        padded = jnp.concatenate([rows, jnp.zeros((40, 256), F32)], 1)
        wide = wide + (pltpu.roll(padded, 24 * q, 1) if q else padded)
    line_ref[...] = jnp.zeros_like(line_ref)
    for c in range(3):
        line_ref[pl.ds(c, 40, stride=3), :] = wide[:, 128 * c : 128 * (c + 1)]
    for c in range(6):
        vec_ref[pl.ds(c, 16, stride=6), :] = small_ref[0:16, 128 * c : 128 * (c + 1)]
    rolled = pltpu.roll(vec_ref[...], 24, 1)
    lane = lax.broadcasted_iota(jnp.int32, rolled.shape, 1)
    line_ref[99:195] += jnp.where(lane >= 24, rolled, 0.0)
    line_ref[100:196] += jnp.where(lane < 24, rolled, 0.0)
    for c in range(6):
        out_ref[:, 128 * c : 128 * (c + 1)] = line_ref[pl.ds(c, 32, stride=6), :]


def small_lines(small, *ties):
    return call(
        lines_body,
        "small_lines",
        [small],
        [like(32, D, dtype=F32)],
        [pltpu.VMEM((640, 128), F32), pltpu.VMEM((96, 128), F32), pltpu.VMEM((200, 128), F32)],
        8,
        ties,
    )


CUTS = (0, 576, 1152, 1734)


def adam_body(me_ref, *refs):
    terms = refs[:4]
    params_ref, first_ref, second_ref = refs[4:7]
    outs = refs[7:11]
    flat_ref, copy_ref, sems, out_sems, params_out, low_out, first_out, second_out = refs[11:]
    me = me_ref[0]
    shift = me % TILE
    for which, own_terms in enumerate((terms[0:2], terms[2:3], terms[3:4])):

        @pl.when(jnp.minimum(me // 8, 2) == which)
        def _():
            copies = [
                pltpu.make_async_copy(term, copy_ref.at[z], sems.at[z])
                for z, term in enumerate(own_terms)
            ]
            if len(own_terms) == 1:
                copy_ref[1] = jnp.zeros((WINDOW, D), BF16)
            for copy in copies:
                copy.start()
            for copy in copies:
                copy.wait()

    for j in range(6):
        terms_j = [copy_ref[z, :, 128 * j : 128 * (j + 1)].astype(F32) for z in range(2)]
        flat_ref[pl.ds(j, WINDOW, stride=6), :] = terms_j[0] + terms_j[1]
    copies = []
    for n, (low, high) in enumerate(zip(CUTS[:-1], CUTS[1:])):
        grad = flat_ref[pl.ds(6 * shift + low, high - low), :]
        line = me * 1734 + low + lax.broadcasted_iota(jnp.int32, grad.shape, 0)
        rate = jnp.full(grad.shape, D ** (-0.5), F32)
        rate = jnp.where((line >= 13824) & (line < 18432), 4.0 * D ** (-0.5), rate)
        rate = jnp.where(line >= 36864, FF ** (-0.5), rate)
        if n == len(CUTS) - 2:
            lane = lax.broadcasted_iota(jnp.int32, (192, 128), 1)
            fine = step_rates(line[-192:] * 128 + lane)
            rate = jnp.concatenate([rate[:-192], fine], 0)
        params = params_ref[low:high]
        new_first = BETA_ONE * first_ref[low:high] + (1.0 - BETA_ONE) * grad
        new_second = BETA_TWO * second_ref[low:high] + (1.0 - BETA_TWO) * grad * grad
        fixed_first = new_first / (1.0 - BETA_ONE**STEP)
        fixed_second = new_second / (1.0 - BETA_TWO**STEP)
        new_params = params - rate * (
            fixed_first / (jnp.sqrt(fixed_second) + ADAM_EPS) + DECAY * params
        )
        params_out[low:high] = new_params
        low_out[low:high] = new_params.astype(BF16)
        first_out[low:high] = new_first
        second_out[low:high] = new_second
        for k, one in enumerate((params_out, low_out, first_out, second_out)):
            copies.append(
                pltpu.make_async_copy(
                    one.at[pl.ds(low, high - low)],
                    outs[k].at[pl.ds(low, high - low)],
                    out_sems.at[n, k],
                )
            )
            copies[-1].start()
    for copy in copies:
        copy.wait()


def adam(me, terms, params, first_moment, second_moment):
    lines = (1734, 128)
    args = [one.reshape(lines) for one in (params, first_moment, second_moment)]
    outs = pl.pallas_call(
        adam_body,
        out_shape=[
            jax.ShapeDtypeStruct(lines, F32),
            jax.ShapeDtypeStruct(lines, BF16),
            jax.ShapeDtypeStruct(lines, F32),
            jax.ShapeDtypeStruct(lines, F32),
        ],
        in_specs=[SMEM_SPEC] + [ANY_SPEC] * 4 + vmem(3),
        out_specs=[ANY_SPEC] * 4,
        scratch_shapes=[
            pltpu.VMEM((6 * WINDOW, 128), F32),
            pltpu.VMEM((2, WINDOW, D), BF16),
            pltpu.SemaphoreType.DMA((2,)),
            pltpu.SemaphoreType.DMA((3, 4)),
            pltpu.VMEM(lines, F32),
            pltpu.VMEM(lines, BF16),
            pltpu.VMEM(lines, F32),
            pltpu.VMEM(lines, F32),
        ],
        compiler_params=params_call(16),
        name="adam",
    )(me, *terms, *args)
    return [one.reshape(-1) for one in outs]


def shards(tokens, cotangent, valid, params, first_moment, second_moment):
    if lax.axis_size("img") != 16 or lax.axis_size("row") != 2:
        return shards_general(tokens, cotangent, valid, params, first_moment, second_moment)
    me = lax.axis_index(BOTH).astype(jnp.int32).reshape(1)
    flat_tokens = tokens.reshape(LEN, D)
    flat_cotangent = cotangent.reshape(LEN, D)
    own, spare, extra = window_of(me, params)
    mask = jnp.tile(window_mask(lax.axis_index("row") * WIN), (1, 1, 4))
    parts, places, rows = gather_windows(own, spare, extra, flat_tokens[:HALF], mask)
    windows, packed, attn, probs, near, far, w_proj, vecs, w_qkv, laid, token = attend(
        me, flat_tokens, rows, mask, parts, places
    )
    back = from_partner(far, "row", 0)
    w_up, w_down, _ = feed_weights(me, parts, places, pause(token))
    hidden, active, grad_up, sums_up, low, low_three, high_three, low_send, high_send, token = feed(
        me, valid, flat_tokens, back, near, flat_cotangent, vecs, w_up, w_down
    )
    core_high_three, core_low_three = swap(high_send, 2), swap(low_send, 2)
    grad_middle, far_grad, near_grad, sums_two, token = middle_grad(
        me, valid, flat_tokens, back, near, flat_cotangent, vecs, grad_up, w_up
    )
    far_grad = from_partner(far_grad, "row", 0)
    sent, token = sum_slots(2, [(high_three, 0), (core_high_three, 0)], pause(token))
    x_three = cross(sent, 4, 1)
    high, low_two, high_two, low_send, high_send, token = up_grad(
        me, hidden, grad_up, low, pause(token)
    )
    core_high_two, core_low_two = swap(high_send, 2), swap(low_send, 2)
    sent, three, token = split_sum(low_three, core_low_three, x_three, token)
    y_three = cross(sent, 1, 4)
    sent, token = sum_slots(2, [(high_two, 0), (core_high_two, 0)], pause(token))
    x_two = cross(sent, 4, 1)
    grad_attn, sums_proj, edge, low_one, high_one, low_send, high_send, token = proj_grad(
        me, near_grad, far_grad, attn, w_proj, high, pause(token)
    )
    core_high_one, core_low_one = swap(high_send, 2), swap(low_send, 2)
    grad_packed, strips, token = unattend(me, packed, grad_attn, attn, probs, pause(token, us=4))
    sent, two, token = split_sum(low_two, core_low_two, x_two, token)
    y_two = cross(sent, 1, 4)
    sent, token = sum_slots(2, [(high_one, 0), (core_high_one, 0)], pause(token))
    x_one = cross(sent, 4, 1)
    sums_qkv, low_zero, high_zero, low_send, high_send, token = qkv_grad(
        me, windows, edge, grad_packed, pause(token)
    )
    core_high_zero, core_low_zero = swap(high_send, 2), swap(low_send, 2)
    near_in, far_in, sums_one, token = token_grad(me, grad_packed, w_qkv, laid, vecs, token)
    small, token = small_grads(strips, sums_qkv, sums_proj, sums_up, sums_one, sums_two, token)
    small = small + swap(small, 2)
    three, token = sum_two(three, y_three, token)
    two, token = sum_two(two, y_two, token)
    small = (small + swap(small, 4)) + (swap(small, 1) + swap(small, 5))
    sent, one, token = split_sum(low_one, core_low_one, x_one, token, small[:8, :128])
    y_one = cross(sent, 1, 4)
    sent, token = sum_slots(2, [(high_zero, 0), (core_high_zero, 0)], pause(token, us=12))
    x_zero = cross(sent, 4, 1)
    small, token = small_lines(small, pause(token))
    upper, other, token = arranged(me, three, two, small, token)
    z_upper = swap(other, 8)
    one, token = sum_two(one, y_one, token)
    z_one = swap(one, 8, lambda d: d // 8 in (0, 2))
    sent, zero, token = split_sum(low_zero, core_low_zero, x_zero, token)
    y_zero = cross(sent, 1, 4)
    one, token = sum_two(one, z_one, token)
    upper, token = sum_two(upper, z_upper, token)
    far_one = swap(one, 16, lambda d: d // 8 == 3)
    far_upper = to_half(gate(upper, token), True)
    zero, token = sum_two(zero, y_zero, token)
    z_zero = swap(zero, 8, lambda d: d // 8 in (1, 3))
    zero, token = sum_two(zero, z_zero, token)
    far_zero = swap(zero, 16, lambda d: d // 8 == 2)
    upper, token = sum_two(upper, far_upper, token)
    one, token = sum_two(one, far_one, token)
    far_in = from_partner(gate(far_in, token), "row", 0)
    output, token = block_output(
        me, flat_tokens, back, near, vecs, active, w_down, token
    )
    input_grad = grad_middle + jnp.concatenate([far_in, near_in], 0).astype(F32)
    terms = [zero, far_zero, one, upper]
    new = adam(me, terms, params, first_moment, second_moment)
    return (output.reshape(tokens.shape), input_grad.reshape(tokens.shape), *new)


def solution(mesh):
    return jax.shard_map(
        shards,
        mesh=mesh,
        in_specs=(
            P("img", "row", None, None),
            P("img", "row", None, None),
            P("img"),
            P(("img", "row")),
            P(("img", "row")),
            P(("img", "row")),
        ),
        out_specs=(
            P("img", "row", None, None),
            P("img", "row", None, None),
            P(("img", "row")),
            P(("img", "row")),
            P(("img", "row")),
            P(("img", "row")),
        ),
        check_vma=False,
    )
```

```python
import functools
import math

import jax
import jax.numpy as jnp
from jax import lax
from jax.experimental import pallas as pl
from jax.experimental.pallas import tpu as pltpu
from jax.sharding import PartitionSpec as P

D = 768
FF = 3072
HEADS = 24
HEAD_DIM = 32
WIN = 12
SHIFT = 6
SIDE = 24
STEP = 4
TABLE_ROWS = 529


EPSILON = 1e-05
MASKED = -100.0
DECAY = 0.05
ADAM_EPS = 1e-08
BETA_ONE = 0.5
BETA_TWO = 0.5


def from_partner(block, axis, apart):
    count = lax.axis_size(axis)
    route = []
    for low in range(count):
        high = low | 1 << apart
        if high != low and high < count:
            route += [(low, high), (high, low)]
    return lax.ppermute(block, axis, route)


def piece_shapes():
    return [
        (D, 3 * D),
        (D, D),
        (D, FF),
        (FF, D),
        (TABLE_ROWS, HEADS),
        (3 * D,),
        (D,),
        (FF,),
        (D,),
        (D,),
        (D,),
        (D,),
        (D,),
    ]


def unpack(flat_vec):
    pieces = []
    offset = 0
    for shape_one in piece_shapes():
        amount = math.prod(shape_one)
        pieces.append(lax.slice_in_dim(flat_vec, offset, offset + amount).reshape(shape_one))
        offset = offset + amount
    return pieces


def step_rates(position):
    rate_list = [
        D ** (-0.5),
        4.0 * D ** (-0.5),
        D ** (-0.5),
        FF ** (-0.5),
        1.0,
        0.3,
        0.3,
        0.3,
        0.3,
        0.4,
        0.3,
        0.4,
        0.3,
    ]
    result = jnp.zeros(position.shape, jnp.float32)
    offset = 0
    for shape_one, rate_one in zip(piece_shapes(), rate_list):
        amount = math.prod(shape_one)
        inside = (position >= offset) & (position < offset + amount)
        result = jnp.where(inside, jnp.float32(rate_one), result)
        offset = offset + amount
    return result


def layer_norm(values, gain_vec, shift_vec):
    centre = jnp.mean(values, -1, keepdims=True)
    centred = values - centre
    spread = jnp.mean(centred * centred, -1, keepdims=True)
    return centred * lax.rsqrt(spread + EPSILON) * gain_vec + shift_vec


def region_of(coord):
    return jnp.where(coord < SIDE - WIN, 0, jnp.where(coord < SIDE - SHIFT, 1, 2))


def relative_index():
    cell_index = jnp.arange(WIN * WIN, dtype=jnp.int32)
    row_part = cell_index // WIN
    col_part = cell_index % WIN
    return (row_part[:, None] - row_part[None, :] + WIN - 1) * (2 * WIN - 1) + (
        col_part[:, None] - col_part[None, :] + WIN - 1
    )


def window_mask(row_first):
    row_coord = row_first + jnp.arange(WIN, dtype=jnp.int32)
    col_coord = jnp.arange(SIDE, dtype=jnp.int32)
    region_ids = 3 * region_of(row_coord)[:, None] + region_of(col_coord)[None, :]
    region_ids = (
        region_ids.reshape(WIN, SIDE // WIN, WIN).transpose(1, 0, 2).reshape(SIDE // WIN, WIN * WIN)
    )
    same = region_ids[:, :, None] == region_ids[:, None, :]
    return jnp.where(same, 0.0, MASKED).astype(jnp.float32)


def to_windows(grid_rows):
    img_count = grid_rows.shape[0]
    width = grid_rows.shape[-1]
    shaped = grid_rows.reshape(img_count, WIN, SIDE // WIN, WIN, width).transpose(0, 2, 1, 3, 4)
    return shaped.reshape(img_count * (SIDE // WIN), WIN * WIN, width)


def from_windows(window_rows, img_count):
    width = window_rows.shape[-1]
    shaped = window_rows.reshape(img_count, SIDE // WIN, WIN, WIN, width).transpose(0, 2, 1, 3, 4)
    return shaped.reshape(img_count, WIN, SIDE, width)


BF16 = jnp.bfloat16
F32 = jnp.float32
BOTH = ("img", "row")
ROWS = 9248
TILE = 16
WINDOW = 304
WIDE = 2 * D // 4
VMEM_MOST = 60 * 1024 * 1024


def contract_rows(left_op, right_op):
    summed_dims = tuple(range(left_op.ndim - 1))
    return lax.dot_general(
        left_op,
        right_op,
        ((summed_dims, summed_dims), ((), ())),
        preferred_element_type=jnp.float32,
    )


def times_transposed(left_op, right_op):
    return lax.dot_general(
        left_op,
        right_op,
        (((left_op.ndim - 1,), (1,)), ((), ())),
        preferred_element_type=jnp.float32,
    )


def scores_of(queries, keys_all, bias_full, region_mask):
    raw_scores = jnp.einsum(
        "wqhd,wkhd->whqk", queries, keys_all, preferred_element_type=jnp.float32
    )
    return raw_scores * HEAD_DIM ** (-0.5) + bias_full[None] + region_mask[:, None]


def shards_general(tokens, cotangent, valid, params, first_moment, second_moment):
    img_count = tokens.shape[0]
    win_count = img_count * (SIDE // WIN)
    tile_len = WIN * WIN
    gathered = lax.all_gather(params.astype(jnp.bfloat16), ("img", "row"), axis=0, tiled=True)
    (
        w_qkv,
        w_proj,
        w_up,
        w_down,
        bias_table,
        b_qkv,
        b_proj,
        b_up,
        b_down,
        gain_one,
        shift_one,
        gain_two,
        shift_two,
    ) = unpack(gathered)
    images = tokens.astype(jnp.float32)
    normed, norm_pull = jax.vjp(
        layer_norm, images, gain_one.astype(jnp.float32), shift_one.astype(jnp.float32)
    )
    normed_low = normed.astype(jnp.bfloat16)
    incoming = from_partner(normed_low[:, :SHIFT], "row", 0)
    shifted = jnp.roll(jnp.concatenate([normed_low[:, SHIFT:], incoming], 1), -SHIFT, 2)
    windows = to_windows(shifted)
    packed = (
        jnp.dot(windows, w_qkv, preferred_element_type=jnp.float32) + b_qkv.astype(jnp.float32)
    ).astype(jnp.bfloat16)
    heads_view = packed.reshape(win_count, tile_len, 3, HEADS, HEAD_DIM)
    queries = heads_view[:, :, 0]
    keys_all = heads_view[:, :, 1]
    values_all = heads_view[:, :, 2]
    rel_index = relative_index()
    bias_full = bias_table.astype(jnp.float32)[rel_index].transpose(2, 0, 1)
    region_mask = jnp.tile(window_mask(lax.axis_index("row") * WIN), (img_count, 1, 1))
    scores = scores_of(queries, keys_all, bias_full, region_mask)
    row_top = jnp.max(scores, -1, keepdims=True)
    exponent = jnp.exp(scores - row_top)
    row_total = jnp.sum(exponent, -1, keepdims=True)
    log_total = row_top + jnp.log(row_total)
    attn_probs = (exponent / row_total).astype(jnp.bfloat16)
    attn_mixed = jnp.einsum(
        "whqk,wkhd->wqhd", attn_probs, values_all, preferred_element_type=jnp.float32
    )
    attn_mixed = attn_mixed.astype(jnp.bfloat16).reshape(win_count, tile_len, D)
    branch = (
        jnp.dot(attn_mixed, w_proj, preferred_element_type=jnp.float32) + b_proj.astype(jnp.float32)
    ).astype(jnp.bfloat16)
    branch_grid = jnp.roll(from_windows(branch, img_count), SHIFT, 2)
    returned = from_partner(branch_grid[:, SHIFT:], "row", 0)
    middle = images + jnp.concatenate([returned, branch_grid[:, :SHIFT]], 1).astype(jnp.float32)
    normed_two, norm_two_pull = jax.vjp(
        layer_norm, middle, gain_two.astype(jnp.float32), shift_two.astype(jnp.float32)
    )
    hidden_in = normed_two.astype(jnp.bfloat16)
    upward = jnp.dot(hidden_in, w_up, preferred_element_type=jnp.float32) + b_up.astype(jnp.float32)
    active_full, gelu_pull = jax.vjp(lambda values: jax.nn.gelu(values, approximate=False), upward)
    active = active_full.astype(jnp.bfloat16)
    output = (
        middle
        + jnp.dot(active, w_down, preferred_element_type=jnp.float32)
        + b_down.astype(jnp.float32)
    )
    regathered = lax.all_gather(params.astype(jnp.bfloat16), ("img", "row"), axis=0, tiled=True)
    fresh = unpack(regathered)
    w_qkv, w_proj, w_up, w_down = (fresh[0], fresh[1], fresh[2], fresh[3])
    grad_out = cotangent * valid.astype(jnp.bfloat16)[:, None, None, None]
    grad_w_down = contract_rows(active, grad_out)
    grad_b_down = jnp.sum(grad_out.astype(jnp.float32), (0, 1, 2))
    grad_active = times_transposed(grad_out, w_down)
    grad_up = gelu_pull(grad_active)[0].astype(jnp.bfloat16)
    grad_w_up = contract_rows(hidden_in, grad_up)
    grad_b_up = jnp.sum(grad_up.astype(jnp.float32), (0, 1, 2))
    grad_hidden = times_transposed(grad_up, w_up)
    grad_middle_ln, grad_gain_two, grad_shift_two = norm_two_pull(grad_hidden)
    grad_middle = grad_out.astype(jnp.float32) + grad_middle_ln
    middle_low = grad_middle.astype(jnp.bfloat16)
    arrived = from_partner(middle_low[:, :SHIFT], "row", 0)
    grad_grid = jnp.roll(jnp.concatenate([middle_low[:, SHIFT:], arrived], 1), -SHIFT, 2)
    grad_branch = to_windows(grad_grid)
    grad_w_proj = contract_rows(attn_mixed, grad_branch)
    grad_b_proj = jnp.sum(grad_branch.astype(jnp.float32), (0, 1))
    grad_attn = times_transposed(grad_branch, w_proj).astype(jnp.bfloat16)
    grad_attn = grad_attn.reshape(win_count, tile_len, HEADS, HEAD_DIM)
    again_scores = scores_of(queries, keys_all, bias_full, region_mask)
    again_probs = jnp.exp(again_scores - log_total)
    grad_values = jnp.einsum(
        "whqk,wqhd->wkhd",
        again_probs.astype(jnp.bfloat16),
        grad_attn,
        preferred_element_type=jnp.float32,
    )
    grad_probs = jnp.einsum(
        "wqhd,wkhd->whqk", grad_attn, values_all, preferred_element_type=jnp.float32
    )
    grad_scores = again_probs * (grad_probs - jnp.sum(again_probs * grad_probs, -1, keepdims=True))
    pair_sums = jnp.sum(grad_scores, 0).transpose(1, 2, 0).reshape(tile_len * tile_len, HEADS)
    grad_table = jax.ops.segment_sum(pair_sums, rel_index.reshape(-1), TABLE_ROWS)
    grad_raw = (grad_scores * HEAD_DIM ** (-0.5)).astype(jnp.bfloat16)
    grad_queries = jnp.einsum(
        "whqk,wkhd->wqhd", grad_raw, keys_all, preferred_element_type=jnp.float32
    )
    grad_keys = jnp.einsum("whqk,wqhd->wkhd", grad_raw, queries, preferred_element_type=jnp.float32)
    grad_packed = jnp.stack([grad_queries, grad_keys, grad_values], 2).astype(jnp.bfloat16)
    grad_packed = grad_packed.reshape(win_count, tile_len, 3 * D)
    grad_w_qkv = contract_rows(windows, grad_packed)
    grad_b_qkv = jnp.sum(grad_packed.astype(jnp.float32), (0, 1))
    grad_windows = times_transposed(grad_packed, w_qkv).astype(jnp.bfloat16)
    grad_shifted = jnp.roll(from_windows(grad_windows, img_count), SHIFT, 2)
    arrived_two = from_partner(grad_shifted[:, SHIFT:], "row", 0)
    grad_normed = jnp.concatenate([arrived_two, grad_shifted[:, :SHIFT]], 1).astype(jnp.float32)
    grad_images_ln, grad_gain_one, grad_shift_one = norm_pull(grad_normed)
    input_grad = grad_middle + grad_images_ln
    grad_list = [
        grad_w_qkv,
        grad_w_proj,
        grad_w_up,
        grad_w_down,
        grad_table,
        grad_b_qkv,
        grad_b_proj,
        grad_b_up,
        grad_b_down,
        grad_gain_one,
        grad_shift_one,
        grad_gain_two,
        grad_shift_two,
    ]
    grad_flat = jnp.concatenate([grad_one.reshape(-1) for grad_one in grad_list])
    grad_flat = jnp.pad(grad_flat, (0, gathered.shape[0] - grad_flat.shape[0]))
    grad_shard = lax.psum_scatter(grad_flat, ("img", "row"), scatter_dimension=0, tiled=True)
    shard_len = params.shape[0]
    position = lax.axis_index(("img", "row")) * shard_len + jnp.arange(shard_len, dtype=jnp.int32)
    step_rate = step_rates(position)
    new_first = BETA_ONE * first_moment + (1.0 - BETA_ONE) * grad_shard
    new_second = BETA_TWO * second_moment + (1.0 - BETA_TWO) * grad_shard * grad_shard
    fixed_first = new_first / (1.0 - BETA_ONE**STEP)
    fixed_second = new_second / (1.0 - BETA_TWO**STEP)
    new_params = params - step_rate * (
        fixed_first / (jnp.sqrt(fixed_second) + ADAM_EPS) + DECAY * params
    )
    return (
        output.astype(jnp.bfloat16),
        input_grad,
        new_params,
        new_params.astype(jnp.bfloat16),
        new_first,
        new_second,
    )


BF16 = jnp.bfloat16
F32 = jnp.float32
BOTH = ("img", "row")
TILE = 16
WINDOW = 304
LEN = 2 * WIN * WIN
QUADS = HEADS // 4
SPAN = 4 * WIN * WIN


def swap(block, mask, only=None):
    count = lax.axis_size(BOTH)
    route = [(d, d ^ mask) for d in range(count) if only is None or only(d)]
    return lax.ppermute(block, BOTH, route)


def params_call(mebibytes):
    return pltpu.CompilerParams(vmem_limit_bytes=mebibytes << 20)


def vmem(count):
    return [pl.BlockSpec(memory_space=pltpu.VMEM)] * count


SMEM_SPEC = pl.BlockSpec(memory_space=pltpu.SMEM)
ANY_SPEC = pl.BlockSpec(memory_space=pl.ANY)


def first_tile(device):
    return (289 * device) // TILE


def prep_body(me_ref, own_ref, out_ref, spare_ref, extra_ref, wide_ref):
    shift = me_ref[0] % TILE
    wide_ref[0:96] = jnp.zeros((96, 128), F32)
    wide_ref[1824:1920] = jnp.zeros((96, 128), F32)
    wide_ref[96:1830] = own_ref[...]
    for j in range(6):
        picked = wide_ref[pl.ds(96 - 6 * shift + j, WINDOW, stride=6), :]
        out_ref[:, 128 * j : 128 * (j + 1)] = picked.astype(BF16)
        spare_ref[:, 128 * j : 128 * (j + 1)] = picked.astype(BF16)
        extra_ref[:, 128 * j : 128 * (j + 1)] = picked.astype(BF16)


def window_of(me, own_flat):
    return pl.pallas_call(
        prep_body,
        out_shape=[jax.ShapeDtypeStruct((WINDOW, D), BF16)] * 3,
        in_specs=[SMEM_SPEC] + vmem(1),
        out_specs=vmem(3),
        scratch_shapes=[pltpu.VMEM((1920, 128), F32)],
        compiler_params=params_call(8),
        name="own_window",
    )(me, own_flat.reshape(-1, 128))


def mixer(groups, per):
    size = groups * per
    row = lax.broadcasted_iota(jnp.int32, (size, size), 0)
    col = lax.broadcasted_iota(jnp.int32, (size, size), 1)
    return (col == groups * (row % per) + row // per).astype(F32).astype(BF16)


def unmixer(groups, per):
    size = groups * per
    row = lax.broadcasted_iota(jnp.int32, (size, size), 0)
    col = lax.broadcasted_iota(jnp.int32, (size, size), 1)
    return (row == groups * (col % per) + col // per).astype(F32).astype(BF16)


def plane_rows(plane):
    low = first_tile(8 * plane) * TILE
    high = first_tile(8 * plane + 7) * TILE + WINDOW
    return low, high


def gate(value, *others):
    def body(*refs):
        pass

    return pl.pallas_call(
        body,
        out_shape=jax.ShapeDtypeStruct(value.shape, value.dtype),
        in_specs=[ANY_SPEC] * (1 + len(others)),
        out_specs=ANY_SPEC,
        input_output_aliases={0: 0},
        cost_estimate=cost(0),
        name="gate",
    )(value, *others)


def cross(block, zero, one):
    count = lax.axis_size(BOTH)
    return lax.ppermute(block, BOTH, [(d, d ^ (one if d & 2 else zero)) for d in range(count)])


def gather_windows(own, spare, extra, rows, *early):
    got = {0: own}
    first, second, third = {}, {}, {}

    def exchange(z):
        first[z] = cross(got[z], 4, 1)
        second[z] = cross(got[z], 1, 4)
        third[z] = cross(first[z], 1, 4)

    got[8] = swap(own, 8)
    first[0] = cross(own, 4, 1)
    second[0] = cross(own, 1, 4)
    spare = gate(spare, got[8])
    got[16] = swap(spare, 16)
    first[0] = gate(first[0], spare)
    third[0] = cross(first[0], 1, 4)
    got_rows = from_partner(rows, "row", 0)
    got[8] = gate(got[8], first[0], second[0])
    exchange(8)
    got[24] = swap(gate(extra, got[16]), 24)
    got[16] = gate(got[16], first[8], second[8], third[0], got_rows)
    exchange(16)
    got[24] = gate(got[24], first[16], second[16], third[8], *early)
    exchange(24)
    blocks, places = [], []
    for z in (0, 8, 16, 24):
        own_some = [got[z], first[z], second[z], third[z]]
        masks = ((z, z), (z | 4, z | 1), (z | 1, z | 4), (z | 5, z | 5))
        if z == 24:
            places.append((len(blocks), None, *masks[3]))
            places.append((len(blocks) + 1, None, masks[3][1] | 2, masks[3][0] | 2))
            last = own_some.pop()
            blocks += [last, swap(last, 2)]
        own_some = stacked(own_some)
        for n in range(own_some.shape[0]):
            zero, one = masks[n]
            places.append((len(blocks), n, zero, one))
            places.append((len(blocks) + 1, n, one | 2, zero | 2))
        blocks += [own_some, swap(own_some, 2)]
    return blocks, places, got_rows


def stacked_body(*refs):
    for i, ref in enumerate(refs[:-1]):
        refs[-1][i] = ref[...]


def stacked(blocks):
    return pl.pallas_call(
        stacked_body,
        out_shape=like(len(blocks), WINDOW, D),
        in_specs=vmem(len(blocks)),
        out_specs=vmem(1)[0],
        compiler_params=params_call(4),
        cost_estimate=cost(0),
        name="stacked",
    )(*blocks)


def load_windows(me, parts, places, first, last, flat_ref):
    base = first_tile(first) * TILE
    for device in (first, 16):
        if first <= device <= last:
            at = first_tile(device) * TILE - base
            flat_ref[at : at + TILE] = jnp.zeros((TILE, D), BF16)

    def each(act):
        for block, slot, zero, one in places:
            device = me ^ jnp.where((me & 2) == 0, zero, one)
            start = pl.multiple_of(first_tile(device) * TILE - base, TILE)
            part = parts[block] if slot is None else parts[block].at[slot]

            @pl.when((device >= first) & (device <= last))
            def _():
                act(part, start)

    def main(part, start):
        def step(i, carry):
            at = pl.multiple_of(48 * i + TILE, TILE)
            to = pl.multiple_of(start + at, TILE)
            flat_ref[pl.ds(to, 48)] = part[pl.ds(at, 48)]
            return carry

        lax.fori_loop(0, 6, step, 0)

    def edge(part, start):
        flat_ref[pl.ds(start, TILE)] += part[0:TILE]

    each(main)
    each(edge)


def load_small(me, parts, places, tail_ref):
    for block, slot, zero, one in places:
        part = parts[block] if slot is None else parts[block].at[slot]

        @pl.when(me ^ jnp.where((me & 2) == 0, zero, one) == 31)
        def _():
            tail_ref[...] = part[WINDOW - 32 : WINDOW]


def flat_scratch(first, last):
    return pltpu.VMEM(
        (first_tile(last) * TILE + WINDOW - first_tile(first) * TILE, D), BF16
    )


def unmix_rows(flat_ref, out_ref, base, groups, per, steps):
    mix = mixer(groups, per)
    size = groups * per
    for t in range(steps):
        rows = flat_ref[base + size * t : base + size * (t + 1)]
        out = jnp.dot(mix, rows, preferred_element_type=F32).astype(BF16)
        for j in range(groups):
            out_ref[j, per * t : per * (t + 1)] = out[per * j : per * (j + 1)]


def mix_rows(in_ref, flat_ref, base, groups, per, steps):
    mix = unmixer(groups, per)
    size = groups * per
    for t in range(steps):
        rows = jnp.concatenate([in_ref[j, per * t : per * (t + 1)] for j in range(groups)], 0)
        out = jnp.dot(mix, rows, preferred_element_type=F32).astype(BF16)
        flat_ref[base + size * t : base + size * (t + 1)] = out


def cut_windows(me, plane, flat_ref, base, keeps, sends):
    for flip in (2, 0):
        for s in range(4):
            first = jnp.where(((me ^ flip) & 2) == 0, 4, 1)
            away = (first if s & 2 else 0) + (5 - first if s & 1 else 0)
            device = 8 * plane + ((me & 7) ^ (away | flip))
            start = pl.multiple_of(first_tile(device) * TILE - base, TILE)
            window = flat_ref[pl.ds(start, WINDOW)]
            (sends if flip else keeps)[s // 2][s % 2] = window


def cost(microseconds):
    return pl.CostEstimate(
        flops=int(1e9 * microseconds),
        bytes_accessed=int(3.2e6 * microseconds),
        transcendentals=0,
    )


WINDOWS = [jax.ShapeDtypeStruct((2, WINDOW, D), BF16)] * 4


def like(*shape, dtype=BF16):
    return jax.ShapeDtypeStruct(shape, dtype)


def call(body, name, ins, outs, scratch, limit, ties=(), us=0, far=0):
    n_in, n_tie, n_out = len(ins), len(ties), len(outs)
    first_out = n_in + n_tie

    def wrapped(*refs):
        body(*refs[:n_in], *refs[first_out : first_out + n_out], *refs[first_out + n_out + 1 :])
        token_ref = refs[first_out + n_out]
        token_ref[...] = jnp.zeros_like(token_ref)

    specs = [SMEM_SPEC if one.dtype == jnp.int32 else vmem(1)[0] for one in ins]
    return pl.pallas_call(
        wrapped,
        out_shape=[*outs, like(8, 128, dtype=F32)],
        in_specs=specs + vmem(n_tie),
        out_specs=vmem(n_out - far)
        + [pl.BlockSpec(memory_space=pltpu.HBM)] * far
        + vmem(1),
        scratch_shapes=scratch,
        compiler_params=params_call(limit),
        cost_estimate=cost(us),
        name=name,
    )(*ins, *ties)


def pause(*ties, us=4):
    return call(lambda: None, "pause", [], [], [], 4, ties, us)[0]


def normal_parts(values):
    centre = jnp.mean(values, -1, keepdims=True)
    centred = values - centre
    spread = jnp.mean(centred * centred, -1, keepdims=True)
    scale = lax.rsqrt(spread + EPSILON)
    return centred * scale, scale


def normal_pull(n, scale, grad, gain):
    e = grad * gain
    return scale * (
        e - jnp.mean(e, -1, keepdims=True) - n * jnp.mean(e * n, -1, keepdims=True)
    )


def over_heads(block):
    head = lax.broadcasted_iota(jnp.int32, block.shape, 1) // HEAD_DIM
    return jnp.concatenate([jnp.where(head == h, block, jnp.zeros_like(block)) for h in range(4)], 0)


def own_columns(block):
    head = lax.broadcasted_iota(jnp.int32, (144, 128), 1) // HEAD_DIM
    out = block[0:144]
    for h in range(1, 4):
        out = jnp.where(head == h, block[144 * h : 144 * (h + 1)], out)
    return out


def contract(one, two, a, b):
    return lax.dot_general(one, two, (((a,), (b,)), ((), ())), preferred_element_type=F32)


def lay(out_ref, near, far):
    for i in range(WIN):
        ref, k = (near, 24 * i) if i < SHIFT else (far, 24 * (i - SHIFT))
        out_ref[12 * i : 12 * i + 12] = ref[k + 6 : k + 18]
        out_ref[144 + 12 * i : 150 + 12 * i] = ref[k + 18 : k + 24]
        out_ref[150 + 12 * i : 156 + 12 * i] = ref[k : k + 6]


def unlay(ref, near, far):
    for i in range(WIN):
        out_ref, k = (near, 24 * i) if i < SHIFT else (far, 24 * (i - SHIFT))
        out_ref[k + 6 : k + 18] = ref[12 * i : 12 * i + 12]
        out_ref[k + 18 : k + 24] = ref[144 + 12 * i : 150 + 12 * i]
        out_ref[k : k + 6] = ref[150 + 12 * i : 156 + 12 * i]


HALF = LEN // 2
LAY_SCRATCH = [pltpu.VMEM((LEN, D), F32), pltpu.VMEM((HALF, D), F32), pltpu.VMEM((HALF, D), F32)]


def unpack_small(tail_ref, vecs_ref, strips_ref, wide_ref, shift_ref):
    tail = tail_ref[...].astype(F32)
    rolled = pltpu.roll(tail, 360, 1)
    below = pltpu.roll(rolled, 31, 0)
    lane = lax.broadcasted_iota(jnp.int32, (16, D), 1)
    vecs_ref[...] = jnp.where(lane < 360, rolled[16:32], below[16:32])
    cell = lax.broadcasted_iota(jnp.int32, (32, D), 1) // HEADS
    which = lax.broadcasted_iota(jnp.int32, (32, D), 0)
    for r in range(17):
        row = jnp.broadcast_to(tail[r : r + 1], (32, D))
        wide_ref[32 * r : 32 * (r + 1)] = jnp.where(cell == which, row, 0.0).astype(BF16)
    lane = lax.broadcasted_iota(jnp.int32, (D, 128), 0)
    head = lax.broadcasted_iota(jnp.int32, (D, 128), 1)
    pick = (lane % HEADS == head).astype(F32).astype(BF16)
    table = jnp.dot(wide_ref[0:544], pick, preferred_element_type=F32)
    row = lax.broadcasted_iota(jnp.int32, table.shape, 0)
    table = jnp.where(row < TABLE_ROWS, table, 0.0)
    table = jnp.concatenate([table, jnp.zeros((96, 128), F32)], 0).T[0:HEADS]
    for j in range(WIN):
        moved = pltpu.roll(table, 629 + j, 1) if j < 11 else table
        shift_ref[24 * j : 24 * (j + 1), 0:640] = moved
    strips = contract(shift_ref[:, 0:640].astype(BF16), table_spread(), 1, 1)
    for j in range(WIN):
        strips_ref[:, j, :] = strips[24 * j : 24 * (j + 1)]


def table_spread():
    m = lax.broadcasted_iota(jnp.int32, (384, 640), 0)
    n = lax.broadcasted_iota(jnp.int32, (384, 640), 1)
    return ((n == 23 * (m // WIN) + m % WIN) & (m < 276)).astype(F32).astype(BF16)


def attend_body(places, me_ref, tokens_ref, rows_ref, mask_ref, *refs):
    parts = refs[:10]
    windows_ref, packed_ref, attn_ref, probs_ref, near_ref, far_ref, proj_ref, vecs_ref, qkv_out, laid_out = refs[10:20]
    flat_ref, wide_ref, one_ref, two_ref, bias_ref, qkv_ref, laid_ref, sems, tail_ref, strips_ref = refs[20:]
    load_small(me_ref[0], parts, places, tail_ref)
    unpack_small(tail_ref, vecs_ref, strips_ref, flat_ref, wide_ref)
    load_windows(me_ref[0], parts, places, 0, 10, flat_ref)
    one_ref[...] = tokens_ref[HALF:LEN].astype(F32)
    two_ref[...] = rows_ref[...].astype(F32)
    lay(wide_ref, one_ref, two_ref)
    laid = wide_ref[...]
    laid_ref[...] = laid.astype(BF16)
    n, _ = normal_parts(laid)
    windows_ref[...] = (n * vecs_ref[9:10] + vecs_ref[10:11]).astype(BF16)
    unmix_rows(flat_ref, qkv_ref, 0, 3, 64, 12)
    copies = [
        pltpu.make_async_copy(qkv_ref, qkv_out, sems.at[0]),
        pltpu.make_async_copy(laid_ref, laid_out, sems.at[1]),
    ]
    for copy in copies:
        copy.start()
    proj_ref[...] = flat_ref[2304:3072]

    def project(j, carry):
        packed_ref[j] = (
            jnp.dot(windows_ref[...], qkv_ref[j], preferred_element_type=F32)
            + vecs_ref[pl.ds(j, 1)]
        ).astype(BF16)
        return carry

    lax.fori_loop(0, 3, project, 0)

    def quad(g, carry):
        lanes = pl.ds(pl.multiple_of(128 * g, 128), 128)
        for h in range(4):
            for i in range(WIN):
                low = 12 * (11 - i)
                bias_ref[12 * i : 12 * i + 12, 144 * h : 144 * (h + 1)] = strips_ref[
                    4 * g + h, 0:12, low : low + 144
                ]
        for w in range(2):
            rows = pl.ds(144 * w, 144)
            queries = over_heads(packed_ref[0, rows, lanes])
            scores = contract(packed_ref[1, rows, lanes], queries, 1, 1)
            scores = scores * HEAD_DIM ** (-0.5) + bias_ref[...] + mask_ref[w]
            top = jnp.max(scores, 0, keepdims=True)
            exponent = jnp.exp(scores - top)
            total = jnp.sum(exponent, 0, keepdims=True)
            probs = (exponent * (1.0 / total)).astype(BF16)
            probs_ref[2 * g + w] = probs
            mixed = contract(probs, packed_ref[2, rows, lanes], 0, 0)
            attn_ref[rows, lanes] = own_columns(mixed).astype(BF16)
        return carry

    lax.fori_loop(0, QUADS, quad, 0)
    wide_ref[...] = (
        jnp.dot(attn_ref[...], proj_ref[...], preferred_element_type=F32) + vecs_ref[3:4]
    )
    unlay(wide_ref, one_ref, two_ref)
    near_ref[...] = one_ref[...].astype(BF16)
    far_ref[...] = two_ref[...].astype(BF16)
    for copy in copies:
        copy.wait()


def attend(me, tokens, rows, mask, parts, places):
    return call(
        functools.partial(attend_body, places),
        "attention_forward",
        [me, tokens, rows, mask, *parts],
        [
            like(LEN, D),
            like(3, LEN, D),
            like(LEN, D),
            like(2 * QUADS, 144, SPAN),
            like(HALF, D),
            like(HALF, D),
            like(D, D),
            like(16, D, dtype=F32),
            like(3, D, D),
            like(LEN, D),
        ],
        [flat_scratch(0, 10)]
        + LAY_SCRATCH
        + [
            pltpu.VMEM((144, SPAN), F32),
            pltpu.VMEM((3, D, D), BF16),
            pltpu.VMEM((LEN, D), BF16),
            pltpu.SemaphoreType.DMA((2,)),
            pltpu.VMEM((32, D), BF16),
            pltpu.VMEM((HEADS, WIN, 384), F32),
        ],
        22,
        far=2,
    )


def middle_of(tokens_ref, back_ref, near_ref):
    branch = jnp.concatenate([back_ref[...].astype(F32), near_ref[...].astype(F32)], 0)
    return tokens_ref[...].astype(F32) + branch


def feed_weights_body(places, me_ref, *refs):
    parts = refs[:10]
    up_ref, down_ref, flat_ref = refs[10:]
    load_windows(me_ref[0], parts, places, 10, 31, flat_ref)
    base = first_tile(10) * TILE
    unmix_rows(flat_ref, up_ref, 3072 - base, 4, 48, 16)

    def step(i, carry):
        at = pl.multiple_of(64 * i, 64)
        down_ref[pl.ds(at, 64)] = flat_ref[pl.ds(pl.multiple_of(6144 - base + at, TILE), 64)]
        return carry

    lax.fori_loop(0, 48, step, 0)


def feed_weights(me, parts, places, *ties):
    return call(
        functools.partial(feed_weights_body, places),
        "feed_weights",
        [me, *parts],
        [like(4, D, D), like(FF, D)],
        [flat_scratch(10, 31)],
        20,
        ties,
    )


def feed_body(me_ref, valid_ref, tokens_ref, back_ref, near_ref, cotangent_ref, vecs_ref, up_ref, down_ref, hidden_ref, active_ref, gradup_ref, sums_ref, low_ref, low_keep, high_keep, low_send, high_send, grad_ref):
    me = me_ref[0]
    n, _ = normal_parts(middle_of(tokens_ref, back_ref, near_ref))
    hidden_ref[...] = (n * vecs_ref[11:12] + vecs_ref[12:13]).astype(BF16)
    grad_out = cotangent_ref[...] * valid_ref[0].astype(F32).astype(BF16)
    grad_ref[3072:3104] = jnp.zeros((32, D), BF16)

    def step(j, carry):
        at = pl.multiple_of(D * j, D)
        down = down_ref[pl.ds(at, D)]
        upward = jnp.dot(hidden_ref[...], up_ref[j], preferred_element_type=F32)
        upward = upward + vecs_ref[pl.ds(4 + j, 1)]
        grad_active = contract(grad_out, down, 1, 1)
        share = 0.5 * (1.0 + lax.erf(upward * (0.5**0.5)))
        density = jnp.exp(-0.5 * upward * upward) * ((2.0 * math.pi) ** (-0.5))
        active = (upward * share).astype(BF16)
        grad_up = (grad_active * (share + upward * density)).astype(BF16)
        active_ref[j] = active
        gradup_ref[j] = grad_up
        sums_ref[pl.ds(j, 1)] = jnp.sum(grad_up.astype(F32), 0, keepdims=True)
        grad_ref[pl.ds(at, D)] = contract(active, grad_out, 0, 0).astype(BF16)
        return carry

    lax.fori_loop(0, 4, step, 0)
    cut_windows(me, 3, grad_ref, 6144, (low_keep, high_keep), (low_send, high_send))
    low_ref[...] = grad_ref[0:800]
    sums_ref[4:5] = jnp.sum(grad_out.astype(F32), 0, keepdims=True)


def feed(me, valid, tokens, back, near, cotangent, vecs, w_up, w_down):
    return call(
        feed_body,
        "feed_forward",
        [me, valid, tokens, back, near, cotangent, vecs, w_up, w_down],
        [
            like(LEN, D),
            like(4, LEN, D),
            like(4, LEN, D),
            like(8, D, dtype=F32),
            like(800, D),
            *WINDOWS,
        ],
        [pltpu.VMEM((3104, D), BF16)],
        16,
    )


def middle_body(me_ref, valid_ref, tokens_ref, back_ref, near_ref, cotangent_ref, vecs_ref, gradup_ref, up_ref, grad_ref, far_out, near_out, sums_ref):
    n, scale = normal_parts(middle_of(tokens_ref, back_ref, near_ref))
    grad_hidden = contract(gradup_ref[0], up_ref[0], 1, 1)
    for j in range(1, 4):
        grad_hidden = grad_hidden + contract(gradup_ref[j], up_ref[j], 1, 1)
    sums_ref[0:1] = jnp.sum(grad_hidden * n, 0, keepdims=True)
    sums_ref[1:2] = jnp.sum(grad_hidden, 0, keepdims=True)
    grad_out = (cotangent_ref[...] * valid_ref[0].astype(F32).astype(BF16)).astype(F32)
    grad = grad_out + normal_pull(n, scale, grad_hidden, vecs_ref[11:12])
    grad_ref[...] = grad
    far_out[...] = grad[:HALF].astype(BF16)
    near_out[...] = grad[HALF:].astype(BF16)


def middle_grad(me, valid, tokens, back, near, cotangent, vecs, grad_up, w_up):
    return call(
        middle_body,
        "middle_grad",
        [me, valid, tokens, back, near, cotangent, vecs, grad_up, w_up],
        [like(LEN, D, dtype=F32), like(HALF, D), like(HALF, D), like(8, D, dtype=F32)],
        [],
        12,
    )


def up_body(me_ref, hidden_ref, gradup_ref, low_ref, proj_ref, low_keep, high_keep, low_send, high_send, quad_ref, flat_ref):
    me = me_ref[0]

    def step(j, carry):
        quad_ref[j] = contract(hidden_ref[...], gradup_ref[j], 0, 0).astype(BF16)
        return carry

    lax.fori_loop(0, 4, step, 0)
    flat_ref[3072:3872] = low_ref[...]
    mix_rows(quad_ref, flat_ref, 0, 4, 48, 16)
    cut_windows(me, 2, flat_ref, 3072, (low_keep, high_keep), (low_send, high_send))
    proj_ref[...] = flat_ref[0:1552]


def up_grad(me, hidden, grad_up, low, *ties):
    return call(
        up_body,
        "up_grad",
        [me, hidden, grad_up, low],
        [like(1552, D), *WINDOWS],
        [pltpu.VMEM((4, D, D), BF16), pltpu.VMEM((3872, D), BF16)],
        16,
        ties,
    )


def proj_body(me_ref, near_ref, far_ref, attn_ref, proj_ref, high_ref, back_ref, sums_ref, edge_ref, low_keep, high_keep, low_send, high_send, flat_ref, wide_ref, one_ref, two_ref):
    me = me_ref[0]
    one_ref[...] = near_ref[...].astype(F32)
    two_ref[...] = far_ref[...].astype(F32)
    lay(wide_ref, one_ref, two_ref)
    grad = wide_ref[...].astype(BF16)
    flat_ref[0:768] = contract(attn_ref[...], grad, 0, 0).astype(BF16)
    flat_ref[768:2320] = high_ref[...]
    cut_windows(me, 1, flat_ref, 2304, (low_keep, high_keep), (low_send, high_send))
    edge_ref[...] = flat_ref[0:16]
    back_ref[...] = contract(grad, proj_ref[...], 1, 1).astype(BF16)
    sums_ref[0:1] = jnp.sum(grad.astype(F32), 0, keepdims=True)


def proj_grad(me, near, far, attn, w_proj, high, *ties):
    return call(
        proj_body,
        "proj_grad",
        [me, near, far, attn, w_proj, high],
        [like(LEN, D), like(8, D, dtype=F32), like(16, D), *WINDOWS],
        [pltpu.VMEM((2320, D), BF16)] + LAY_SCRATCH,
        12,
        ties,
    )


def unattend_quads(quads, packed_ref, grad_ref, attn_ref, probs_ref, back_ref, strips_ref, pairs_ref):
    strips_ref[...] = jnp.zeros_like(strips_ref)

    def quad(g, carry):
        lanes = pl.ds(pl.multiple_of(128 * g, 128), 128)
        for w in range(2):
            rows = pl.ds(144 * w, 144)
            queries = over_heads(packed_ref[0, rows, lanes])
            keys = packed_ref[1, rows, lanes]
            values = packed_ref[2, rows, lanes]
            grad = grad_ref[rows, lanes]
            product = -(attn_ref[rows, lanes].astype(F32) * grad.astype(F32)).astype(BF16)
            grads = over_heads(grad)
            left = jnp.concatenate([values, jnp.ones_like(values)], 1)
            right = jnp.concatenate([grads, over_heads(product)], 1)
            probs = probs_ref[2 * g + w]
            grad_scores = probs.astype(F32) * contract(left, right, 1, 1)
            if w == 0:
                pairs_ref[...] = grad_scores
            else:
                pairs_ref[...] += grad_scores
            raw = (grad_scores * HEAD_DIM ** (-0.5)).astype(BF16)
            back_ref[0, rows, lanes] = own_columns(contract(raw, keys, 0, 0)).astype(BF16)
            back_ref[1, rows, lanes] = jnp.dot(
                raw, queries, preferred_element_type=F32
            ).astype(BF16)
            back_ref[2, rows, lanes] = jnp.dot(
                probs, grads, preferred_element_type=F32
            ).astype(BF16)
        for h in range(4):
            for i in range(WIN):
                low = 12 * (11 - i)
                strips_ref[4 * (g - quads[0]) + h, 0:12, low : low + 144] += pairs_ref[
                    12 * i : 12 * i + 12, 144 * h : 144 * (h + 1)
                ]
        return carry

    lax.fori_loop(*quads, quad, 0)


def unattend_body(me_ref, packed_ref, grad_ref, attn_ref, probs_ref, back_ref, strips_ref, sums_ref, pairs_ref):
    unattend_quads((0, QUADS), packed_ref, grad_ref, attn_ref, probs_ref, back_ref, strips_ref, pairs_ref)
    for j in range(3):
        sums_ref[j : j + 1] = jnp.sum(back_ref[j].astype(F32), 0, keepdims=True)


def qkv_body(me_ref, windows_ref, edge_ref, back_ref, low_keep, high_keep, low_send, high_send, trio_ref, flat_ref):
    me = me_ref[0]

    def step(j, carry):
        trio_ref[j] = contract(windows_ref[...], back_ref[j], 0, 0).astype(BF16)
        return carry

    lax.fori_loop(0, 3, step, 0)
    mix_rows(trio_ref, flat_ref, 0, 3, 64, 12)
    flat_ref[2304:2320] = edge_ref[...]
    cut_windows(me, 0, flat_ref, 0, (low_keep, high_keep), (low_send, high_send))


def unattend(me, packed, grad, attn, probs, *ties):
    return call(
        unattend_body,
        "attention_backward",
        [me, packed, grad, attn, probs],
        [like(3, LEN, D), like(HEADS, WIN, 384, dtype=F32), like(8, D, dtype=F32)],
        [pltpu.VMEM((144, SPAN), F32)],
        10,
        ties,
    )


def qkv_grad(me, windows, edge, back, *ties):
    return call(
        qkv_body,
        "qkv_grad",
        [me, windows, edge, back],
        [*WINDOWS],
        [pltpu.VMEM((3, D, D), BF16), pltpu.VMEM((2320, D), BF16)],
        12,
        ties,
    )


def token_body(me_ref, back_ref, qkv_ref, laid_ref, vecs_ref, near_out, far_out, sums_ref, wide_ref, one_ref, two_ref):
    grad = contract(back_ref[0], qkv_ref[0], 1, 1)
    for j in (1, 2):
        grad = grad + contract(back_ref[j], qkv_ref[j], 1, 1)
    n, scale = normal_parts(laid_ref[...].astype(F32))
    sums_ref[0:1] = jnp.sum(grad * n, 0, keepdims=True)
    sums_ref[1:2] = jnp.sum(grad, 0, keepdims=True)
    wide_ref[...] = normal_pull(n, scale, grad, vecs_ref[9:10])
    unlay(wide_ref, one_ref, two_ref)
    near_out[...] = one_ref[...].astype(BF16)
    far_out[...] = two_ref[...].astype(BF16)


def token_grad(me, back, w_qkv, laid, vecs, *ties):
    return call(
        token_body,
        "token_grad",
        [me, back, w_qkv, laid, vecs],
        [like(HALF, D), like(HALF, D), like(8, D, dtype=F32)],
        LAY_SCRATCH,
        10,
        ties,
    )


def output_body(me_ref, tokens_ref, back_ref, near_ref, vecs_ref, active_ref, down_ref, out_ref):
    total = middle_of(tokens_ref, back_ref, near_ref) + vecs_ref[8:9]
    for j in range(4):
        total = total + jnp.dot(
            active_ref[j], down_ref[D * j : D * (j + 1)], preferred_element_type=F32
        )
    out_ref[...] = total.astype(BF16)


def block_output(me, tokens, back, near, vecs, active, w_down, *ties):
    return call(
        output_body,
        "block_output",
        [me, tokens, back, near, vecs, active, w_down],
        [like(LEN, D)],
        [],
        10,
        ties,
    )


def sum_body(slots, lows, *refs):
    for i in range(slots):
        total = refs[0][lows[0] + i].astype(F32)
        for ref, low in zip(refs[1 : len(lows)], lows[1:]):
            total = total + ref[low + i].astype(F32)
        refs[-1][i] = total.astype(BF16)


def sum_slots(slots, terms, *ties):
    return call(
        functools.partial(sum_body, slots, [low for _, low in terms]),
        "sum_slots",
        [one for one, _ in terms],
        [like(slots, WINDOW, D)],
        [],
        6,
        ties,
    )


def split_body(low_ref, x_ref, sent_ref, kept_ref):
    for slot, ref in ((1, sent_ref), (0, kept_ref)):
        ref[...] = (low_ref[slot].astype(F32) + x_ref[slot].astype(F32)).astype(BF16)


def split_sum(low, x, *ties):
    return call(
        split_body, "split_sum", [low, x], [like(WINDOW, D), like(WINDOW, D)], [], 6, ties
    )


def arranged_body(me_ref, high_ref, low_ref, own_ref, other_ref):
    odd = (me_ref[0] // 8) % 2 == 1

    @pl.when(odd)
    def _():
        own_ref[...] = high_ref[...]
        other_ref[...] = low_ref[...]

    @pl.when(jnp.logical_not(odd))
    def _():
        own_ref[...] = low_ref[...]
        other_ref[...] = high_ref[...]


def arranged(me, high, low, *ties):
    return call(
        arranged_body,
        "arranged",
        [me, high, low],
        [like(WINDOW, D), like(WINDOW, D)],
        [],
        6,
        ties,
    )


def with_small_body(me_ref, own_ref, rows_ref, other_ref, out_ref):
    me = me_ref[0]
    out_ref[...] = own_ref[...]

    @pl.when((me % 8 == 7) & ((me // 8) % 2 == 1))
    def _():
        last = own_ref[WINDOW - 32 : WINDOW].astype(F32)
        out_ref[WINDOW - 32 : WINDOW] = (last + (rows_ref[...] + other_ref[...])).astype(BF16)


def with_small(me, own, rows, other, *ties):
    return call(
        with_small_body, "with_small", [me, own, rows, other], [like(WINDOW, D)], [], 6, ties
    )


def sum_two(one, two, *ties):
    def body(one_ref, two_ref, out_ref):
        out_ref[...] = (one_ref[...].astype(F32) + two_ref[...].astype(F32)).astype(BF16)

    return call(body, "sum_two", [one, two], [like(WINDOW, D)], [], 6, ties)


def to_half(block, upper):
    return swap(block, 16, lambda d: (d // 16 == 1) != upper)


def small_body(strips_ref, qkv_ref, proj_ref, up_ref, one_ref, two_ref, out_ref, rows_ref):
    out_ref[...] = jnp.zeros_like(out_ref)
    out_ref[0:3] = qkv_ref[0:3]
    out_ref[3:4] = proj_ref[0:1]
    out_ref[4:9] = up_ref[0:5]
    out_ref[9:11] = one_ref[0:2]
    out_ref[11:13] = two_ref[0:2]
    for j in range(WIN):
        rows_ref[24 * j : 24 * (j + 1)] = strips_ref[:, j, :]
    rows = rows_ref[...]
    high = rows.astype(BF16)
    low = (rows - high.astype(F32)).astype(BF16)
    spread = table_spread()
    wide = jnp.dot(high, spread, preferred_element_type=F32) + jnp.dot(
        low, spread, preferred_element_type=F32
    )
    total = wide[264:288]
    for j in range(WIN - 1):
        total = total + pltpu.roll(wide[24 * j : 24 * (j + 1)], 11 - j, 1)
    out_ref[16:40, 0:640] = total


def small_grads(strips, qkv, proj, up, one, two, *ties):
    return call(
        small_body,
        "small_grads",
        [strips, qkv, proj, up, one, two],
        [like(40, D, dtype=F32)],
        [pltpu.VMEM((288, 384), F32)],
        8,
        ties,
    )


def lines_body(small_ref, out_ref, table_ref, vec_ref, line_ref):
    table = jnp.concatenate([small_ref[16:40, 0:640], jnp.zeros((104, 640), F32)], 0)
    table_ref[...] = table.T
    wide = jnp.zeros((40, 384), F32)
    for q in range(16):
        rows = table_ref[pl.ds(q, 40, stride=16), :]
        padded = jnp.concatenate([rows, jnp.zeros((40, 256), F32)], 1)
        wide = wide + (pltpu.roll(padded, 24 * q, 1) if q else padded)
    line_ref[...] = jnp.zeros_like(line_ref)
    for c in range(3):
        line_ref[pl.ds(c, 40, stride=3), :] = wide[:, 128 * c : 128 * (c + 1)]
    for c in range(6):
        vec_ref[pl.ds(c, 16, stride=6), :] = small_ref[0:16, 128 * c : 128 * (c + 1)]
    rolled = pltpu.roll(vec_ref[...], 24, 1)
    lane = lax.broadcasted_iota(jnp.int32, rolled.shape, 1)
    line_ref[99:195] += jnp.where(lane >= 24, rolled, 0.0)
    line_ref[100:196] += jnp.where(lane < 24, rolled, 0.0)
    for c in range(6):
        out_ref[:, 128 * c : 128 * (c + 1)] = line_ref[pl.ds(c, 32, stride=6), :]


def small_sum(one, two, *ties):
    def body(one_ref, two_ref, out_ref):
        out_ref[...] = one_ref[...] + two_ref[...]

    return call(body, "small_sum", [one, two], [like(40, D, dtype=F32)], [], 4, ties)


def small_lines(small, *ties):
    return call(
        lines_body,
        "small_lines",
        [small],
        [like(32, D, dtype=F32)],
        [pltpu.VMEM((640, 128), F32), pltpu.VMEM((96, 128), F32), pltpu.VMEM((200, 128), F32)],
        8,
        ties,
    )


CUTS = (0, 576, 1152, 1734)


def adam_body(me_ref, *refs):
    terms = refs[:4]
    params_ref, first_ref, second_ref = refs[4:7]
    outs = refs[7:11]
    flat_ref, copy_ref, sems, out_sems, params_out, low_out, first_out, second_out = refs[11:]
    me = me_ref[0]
    shift = me % TILE
    for which, own_terms in enumerate((terms[0:2], terms[2:3], terms[3:4])):

        @pl.when(jnp.minimum(me // 8, 2) == which)
        def _():
            copies = [
                pltpu.make_async_copy(term, copy_ref.at[z], sems.at[z])
                for z, term in enumerate(own_terms)
            ]
            if len(own_terms) == 1:
                copy_ref[1] = jnp.zeros((WINDOW, D), BF16)
            for copy in copies:
                copy.start()
            for copy in copies:
                copy.wait()

    for j in range(6):
        terms_j = [copy_ref[z, :, 128 * j : 128 * (j + 1)].astype(F32) for z in range(2)]
        flat_ref[pl.ds(j, WINDOW, stride=6), :] = terms_j[0] + terms_j[1]
    copies = []
    for n, (low, high) in enumerate(zip(CUTS[:-1], CUTS[1:])):
        grad = flat_ref[pl.ds(6 * shift + low, high - low), :]
        line = me * 1734 + low + lax.broadcasted_iota(jnp.int32, grad.shape, 0)
        rate = jnp.full(grad.shape, D ** (-0.5), F32)
        rate = jnp.where((line >= 13824) & (line < 18432), 4.0 * D ** (-0.5), rate)
        rate = jnp.where(line >= 36864, FF ** (-0.5), rate)
        if n == len(CUTS) - 2:
            lane = lax.broadcasted_iota(jnp.int32, (192, 128), 1)
            fine = step_rates(line[-192:] * 128 + lane)
            rate = jnp.concatenate([rate[:-192], fine], 0)
        params = params_ref[low:high]
        new_first = BETA_ONE * first_ref[low:high] + (1.0 - BETA_ONE) * grad
        new_second = BETA_TWO * second_ref[low:high] + (1.0 - BETA_TWO) * grad * grad
        fixed_first = new_first / (1.0 - BETA_ONE**STEP)
        fixed_second = new_second / (1.0 - BETA_TWO**STEP)
        new_params = params - rate * (
            fixed_first / (jnp.sqrt(fixed_second) + ADAM_EPS) + DECAY * params
        )
        params_out[low:high] = new_params
        low_out[low:high] = new_params.astype(BF16)
        first_out[low:high] = new_first
        second_out[low:high] = new_second
        for k, one in enumerate((params_out, low_out, first_out, second_out)):
            copies.append(
                pltpu.make_async_copy(
                    one.at[pl.ds(low, high - low)],
                    outs[k].at[pl.ds(low, high - low)],
                    out_sems.at[n, k],
                )
            )
            copies[-1].start()
    for copy in copies:
        copy.wait()


def adam(me, terms, params, first_moment, second_moment):
    lines = (1734, 128)
    args = [one.reshape(lines) for one in (params, first_moment, second_moment)]
    outs = pl.pallas_call(
        adam_body,
        out_shape=[
            jax.ShapeDtypeStruct(lines, F32),
            jax.ShapeDtypeStruct(lines, BF16),
            jax.ShapeDtypeStruct(lines, F32),
            jax.ShapeDtypeStruct(lines, F32),
        ],
        in_specs=[SMEM_SPEC] + [ANY_SPEC] * 4 + vmem(3),
        out_specs=[ANY_SPEC] * 4,
        scratch_shapes=[
            pltpu.VMEM((6 * WINDOW, 128), F32),
            pltpu.VMEM((2, WINDOW, D), BF16),
            pltpu.SemaphoreType.DMA((2,)),
            pltpu.SemaphoreType.DMA((3, 4)),
            pltpu.VMEM(lines, F32),
            pltpu.VMEM(lines, BF16),
            pltpu.VMEM(lines, F32),
            pltpu.VMEM(lines, F32),
        ],
        compiler_params=params_call(16),
        name="adam",
    )(me, *terms, *args)
    return [one.reshape(-1) for one in outs]


def shards(tokens, cotangent, valid, params, first_moment, second_moment):
    if lax.axis_size("img") != 16 or lax.axis_size("row") != 2:
        return shards_general(tokens, cotangent, valid, params, first_moment, second_moment)
    me = lax.axis_index(BOTH).astype(jnp.int32).reshape(1)
    flat_tokens = tokens.reshape(LEN, D)
    flat_cotangent = cotangent.reshape(LEN, D)
    own, spare, extra = window_of(me, params)
    mask = jnp.tile(window_mask(lax.axis_index("row") * WIN), (1, 1, 4))
    parts, places, rows = gather_windows(own, spare, extra, flat_tokens[:HALF], mask)
    windows, packed, attn, probs, near, far, w_proj, vecs, w_qkv, laid, token = attend(
        me, flat_tokens, rows, mask, parts, places
    )
    back = from_partner(far, "row", 0)
    w_up, w_down, _ = feed_weights(me, parts, places, pause(token))
    hidden, active, grad_up, sums_up, low, low_three, high_three, low_send, high_send, token = feed(
        me, valid, flat_tokens, back, near, flat_cotangent, vecs, w_up, w_down
    )
    core_high_three, core_low_three = swap(high_send, 2), swap(low_send, 2)
    grad_middle, far_grad, near_grad, sums_two, token = middle_grad(
        me, valid, flat_tokens, back, near, flat_cotangent, vecs, grad_up, w_up
    )
    far_grad = from_partner(far_grad, "row", 0)
    sent, token = sum_slots(2, [(high_three, 0), (core_high_three, 0)], pause(token))
    x_three = cross(sent, 4, 1)
    low_three, token = sum_slots(2, [(low_three, 0), (core_low_three, 0)], token)
    high, low_two, high_two, low_send, high_send, token = up_grad(
        me, hidden, grad_up, low, pause(token)
    )
    core_high_two, core_low_two = swap(high_send, 2), swap(low_send, 2)
    sent, three, token = split_sum(low_three, x_three, token)
    y_three = cross(sent, 1, 4)
    sent, token = sum_slots(2, [(high_two, 0), (core_high_two, 0)], pause(token))
    x_two = cross(sent, 4, 1)
    low_two, token = sum_slots(2, [(low_two, 0), (core_low_two, 0)], token)
    grad_attn, sums_proj, edge, low_one, high_one, low_send, high_send, token = proj_grad(
        me, near_grad, far_grad, attn, w_proj, high, pause(token)
    )
    core_high_one, core_low_one = swap(high_send, 2), swap(low_send, 2)
    grad_packed, strips, sums_qkv, token = unattend(
        me, packed, grad_attn, attn, probs, pause(token)
    )
    sent, token = sum_slots(2, [(high_one, 0), (core_high_one, 0)], token)
    x_one = cross(sent, 4, 1)
    near_in, far_in, sums_one, token = token_grad(me, grad_packed, w_qkv, laid, vecs, token)
    small, token = small_grads(strips, sums_qkv, sums_proj, sums_up, sums_one, sums_two, token)
    three, token = sum_two(three, y_three, token)
    small, token = small_sum(small, swap(small, 2), token)
    sent, two, token = split_sum(low_two, x_two, token)
    y_two = cross(sent, 1, 4)
    low_one, token = sum_slots(2, [(low_one, 0), (core_low_one, 0)], token)
    low_zero, high_zero, low_send, high_send, token = qkv_grad(
        me, windows, edge, grad_packed, pause(token)
    )
    core_high_zero, core_low_zero = swap(high_send, 2), swap(low_send, 2)
    two, token = sum_two(two, y_two, token)
    small, token = small_sum(small, cross(small, 4, 1), token)
    upper, other, token = arranged(me, three, two, token)
    z_upper = swap(other, 8)
    sent, one, token = split_sum(low_one, x_one, token)
    y_one = cross(sent, 1, 4)
    sent, token = sum_slots(2, [(high_zero, 0), (core_high_zero, 0)], pause(token, us=12))
    x_zero = cross(sent, 4, 1)
    low_zero, token = sum_slots(2, [(low_zero, 0), (core_low_zero, 0)], token)
    upper, token = sum_two(upper, z_upper, token)
    one, token = sum_two(one, y_one, token)
    z_one = swap(one, 8, lambda d: d // 8 in (0, 2))
    sent, zero, token = split_sum(low_zero, x_zero, token)
    y_zero = cross(sent, 1, 4)
    small, token = small_sum(small, cross(small, 1, 4), token)
    rows, token = small_lines(small, token)
    z_rows = swap(rows, 8)
    one, token = sum_two(one, z_one, token)
    far_one = swap(one, 16, lambda d: d // 8 == 3)
    zero, token = sum_two(zero, y_zero, token)
    z_zero = swap(zero, 8, lambda d: d // 8 in (1, 3))
    upper, token = with_small(me, upper, rows, z_rows, token)
    far_upper = to_half(upper, True)
    zero, token = sum_two(zero, z_zero, token)
    far_zero = swap(zero, 16, lambda d: d // 8 == 2)
    upper, token = sum_two(upper, far_upper, token)
    one, token = sum_two(one, far_one, token)
    far_in = from_partner(gate(far_in, token), "row", 0)
    output, token = block_output(
        me, flat_tokens, back, near, vecs, active, w_down, token
    )
    input_grad = grad_middle + jnp.concatenate([far_in, near_in], 0).astype(F32)
    terms = [zero, far_zero, one, upper]
    new = adam(me, terms, params, first_moment, second_moment)
    return (output.reshape(tokens.shape), input_grad.reshape(tokens.shape), *new)


def solution(mesh):
    return jax.shard_map(
        shards,
        mesh=mesh,
        in_specs=(
            P("img", "row", None, None),
            P("img", "row", None, None),
            P("img"),
            P(("img", "row")),
            P(("img", "row")),
            P(("img", "row")),
        ),
        out_specs=(
            P("img", "row", None, None),
            P("img", "row", None, None),
            P(("img", "row")),
            P(("img", "row")),
            P(("img", "row")),
            P(("img", "row")),
        ),
        check_vma=False,
    )
```

```python
import functools
import math

import jax
import jax.numpy as jnp
from jax import lax
from jax.experimental import pallas as pl
from jax.experimental.pallas import tpu as pltpu
from jax.sharding import PartitionSpec as P

D = 768
FF = 3072
HEADS = 24
HEAD_DIM = 32
WIN = 12
SHIFT = 6
SIDE = 24
STEP = 4
TABLE_ROWS = 529


EPSILON = 1e-05
MASKED = -100.0
DECAY = 0.05
ADAM_EPS = 1e-08
BETA_ONE = 0.5
BETA_TWO = 0.5


def from_partner(block, axis, apart):
    count = lax.axis_size(axis)
    route = []
    for low in range(count):
        high = low | 1 << apart
        if high != low and high < count:
            route += [(low, high), (high, low)]
    return lax.ppermute(block, axis, route)


def piece_shapes():
    return [
        (D, 3 * D),
        (D, D),
        (D, FF),
        (FF, D),
        (TABLE_ROWS, HEADS),
        (3 * D,),
        (D,),
        (FF,),
        (D,),
        (D,),
        (D,),
        (D,),
        (D,),
    ]


def unpack(flat_vec):
    pieces = []
    offset = 0
    for shape_one in piece_shapes():
        amount = math.prod(shape_one)
        pieces.append(lax.slice_in_dim(flat_vec, offset, offset + amount).reshape(shape_one))
        offset = offset + amount
    return pieces


def step_rates(position):
    rate_list = [
        D ** (-0.5),
        4.0 * D ** (-0.5),
        D ** (-0.5),
        FF ** (-0.5),
        1.0,
        0.3,
        0.3,
        0.3,
        0.3,
        0.4,
        0.3,
        0.4,
        0.3,
    ]
    result = jnp.zeros(position.shape, jnp.float32)
    offset = 0
    for shape_one, rate_one in zip(piece_shapes(), rate_list):
        amount = math.prod(shape_one)
        inside = (position >= offset) & (position < offset + amount)
        result = jnp.where(inside, jnp.float32(rate_one), result)
        offset = offset + amount
    return result


def layer_norm(values, gain_vec, shift_vec):
    centre = jnp.mean(values, -1, keepdims=True)
    centred = values - centre
    spread = jnp.mean(centred * centred, -1, keepdims=True)
    return centred * lax.rsqrt(spread + EPSILON) * gain_vec + shift_vec


def region_of(coord):
    return jnp.where(coord < SIDE - WIN, 0, jnp.where(coord < SIDE - SHIFT, 1, 2))


def relative_index():
    cell_index = jnp.arange(WIN * WIN, dtype=jnp.int32)
    row_part = cell_index // WIN
    col_part = cell_index % WIN
    return (row_part[:, None] - row_part[None, :] + WIN - 1) * (2 * WIN - 1) + (
        col_part[:, None] - col_part[None, :] + WIN - 1
    )


def window_mask(row_first):
    row_coord = row_first + jnp.arange(WIN, dtype=jnp.int32)
    col_coord = jnp.arange(SIDE, dtype=jnp.int32)
    region_ids = 3 * region_of(row_coord)[:, None] + region_of(col_coord)[None, :]
    region_ids = (
        region_ids.reshape(WIN, SIDE // WIN, WIN).transpose(1, 0, 2).reshape(SIDE // WIN, WIN * WIN)
    )
    same = region_ids[:, :, None] == region_ids[:, None, :]
    return jnp.where(same, 0.0, MASKED).astype(jnp.float32)


def to_windows(grid_rows):
    img_count = grid_rows.shape[0]
    width = grid_rows.shape[-1]
    shaped = grid_rows.reshape(img_count, WIN, SIDE // WIN, WIN, width).transpose(0, 2, 1, 3, 4)
    return shaped.reshape(img_count * (SIDE // WIN), WIN * WIN, width)


def from_windows(window_rows, img_count):
    width = window_rows.shape[-1]
    shaped = window_rows.reshape(img_count, SIDE // WIN, WIN, WIN, width).transpose(0, 2, 1, 3, 4)
    return shaped.reshape(img_count, WIN, SIDE, width)


BF16 = jnp.bfloat16
F32 = jnp.float32
BOTH = ("img", "row")
ROWS = 9248
TILE = 16
WINDOW = 304
WIDE = 2 * D // 4
VMEM_MOST = 60 * 1024 * 1024


def contract_rows(left_op, right_op):
    summed_dims = tuple(range(left_op.ndim - 1))
    return lax.dot_general(
        left_op,
        right_op,
        ((summed_dims, summed_dims), ((), ())),
        preferred_element_type=jnp.float32,
    )


def times_transposed(left_op, right_op):
    return lax.dot_general(
        left_op,
        right_op,
        (((left_op.ndim - 1,), (1,)), ((), ())),
        preferred_element_type=jnp.float32,
    )


def scores_of(queries, keys_all, bias_full, region_mask):
    raw_scores = jnp.einsum(
        "wqhd,wkhd->whqk", queries, keys_all, preferred_element_type=jnp.float32
    )
    return raw_scores * HEAD_DIM ** (-0.5) + bias_full[None] + region_mask[:, None]


def shards_general(tokens, cotangent, valid, params, first_moment, second_moment):
    img_count = tokens.shape[0]
    win_count = img_count * (SIDE // WIN)
    tile_len = WIN * WIN
    gathered = lax.all_gather(params.astype(jnp.bfloat16), ("img", "row"), axis=0, tiled=True)
    (
        w_qkv,
        w_proj,
        w_up,
        w_down,
        bias_table,
        b_qkv,
        b_proj,
        b_up,
        b_down,
        gain_one,
        shift_one,
        gain_two,
        shift_two,
    ) = unpack(gathered)
    images = tokens.astype(jnp.float32)
    normed, norm_pull = jax.vjp(
        layer_norm, images, gain_one.astype(jnp.float32), shift_one.astype(jnp.float32)
    )
    normed_low = normed.astype(jnp.bfloat16)
    incoming = from_partner(normed_low[:, :SHIFT], "row", 0)
    shifted = jnp.roll(jnp.concatenate([normed_low[:, SHIFT:], incoming], 1), -SHIFT, 2)
    windows = to_windows(shifted)
    packed = (
        jnp.dot(windows, w_qkv, preferred_element_type=jnp.float32) + b_qkv.astype(jnp.float32)
    ).astype(jnp.bfloat16)
    heads_view = packed.reshape(win_count, tile_len, 3, HEADS, HEAD_DIM)
    queries = heads_view[:, :, 0]
    keys_all = heads_view[:, :, 1]
    values_all = heads_view[:, :, 2]
    rel_index = relative_index()
    bias_full = bias_table.astype(jnp.float32)[rel_index].transpose(2, 0, 1)
    region_mask = jnp.tile(window_mask(lax.axis_index("row") * WIN), (img_count, 1, 1))
    scores = scores_of(queries, keys_all, bias_full, region_mask)
    row_top = jnp.max(scores, -1, keepdims=True)
    exponent = jnp.exp(scores - row_top)
    row_total = jnp.sum(exponent, -1, keepdims=True)
    log_total = row_top + jnp.log(row_total)
    attn_probs = (exponent / row_total).astype(jnp.bfloat16)
    attn_mixed = jnp.einsum(
        "whqk,wkhd->wqhd", attn_probs, values_all, preferred_element_type=jnp.float32
    )
    attn_mixed = attn_mixed.astype(jnp.bfloat16).reshape(win_count, tile_len, D)
    branch = (
        jnp.dot(attn_mixed, w_proj, preferred_element_type=jnp.float32) + b_proj.astype(jnp.float32)
    ).astype(jnp.bfloat16)
    branch_grid = jnp.roll(from_windows(branch, img_count), SHIFT, 2)
    returned = from_partner(branch_grid[:, SHIFT:], "row", 0)
    middle = images + jnp.concatenate([returned, branch_grid[:, :SHIFT]], 1).astype(jnp.float32)
    normed_two, norm_two_pull = jax.vjp(
        layer_norm, middle, gain_two.astype(jnp.float32), shift_two.astype(jnp.float32)
    )
    hidden_in = normed_two.astype(jnp.bfloat16)
    upward = jnp.dot(hidden_in, w_up, preferred_element_type=jnp.float32) + b_up.astype(jnp.float32)
    active_full, gelu_pull = jax.vjp(lambda values: jax.nn.gelu(values, approximate=False), upward)
    active = active_full.astype(jnp.bfloat16)
    output = (
        middle
        + jnp.dot(active, w_down, preferred_element_type=jnp.float32)
        + b_down.astype(jnp.float32)
    )
    regathered = lax.all_gather(params.astype(jnp.bfloat16), ("img", "row"), axis=0, tiled=True)
    fresh = unpack(regathered)
    w_qkv, w_proj, w_up, w_down = (fresh[0], fresh[1], fresh[2], fresh[3])
    grad_out = cotangent * valid.astype(jnp.bfloat16)[:, None, None, None]
    grad_w_down = contract_rows(active, grad_out)
    grad_b_down = jnp.sum(grad_out.astype(jnp.float32), (0, 1, 2))
    grad_active = times_transposed(grad_out, w_down)
    grad_up = gelu_pull(grad_active)[0].astype(jnp.bfloat16)
    grad_w_up = contract_rows(hidden_in, grad_up)
    grad_b_up = jnp.sum(grad_up.astype(jnp.float32), (0, 1, 2))
    grad_hidden = times_transposed(grad_up, w_up)
    grad_middle_ln, grad_gain_two, grad_shift_two = norm_two_pull(grad_hidden)
    grad_middle = grad_out.astype(jnp.float32) + grad_middle_ln
    middle_low = grad_middle.astype(jnp.bfloat16)
    arrived = from_partner(middle_low[:, :SHIFT], "row", 0)
    grad_grid = jnp.roll(jnp.concatenate([middle_low[:, SHIFT:], arrived], 1), -SHIFT, 2)
    grad_branch = to_windows(grad_grid)
    grad_w_proj = contract_rows(attn_mixed, grad_branch)
    grad_b_proj = jnp.sum(grad_branch.astype(jnp.float32), (0, 1))
    grad_attn = times_transposed(grad_branch, w_proj).astype(jnp.bfloat16)
    grad_attn = grad_attn.reshape(win_count, tile_len, HEADS, HEAD_DIM)
    again_scores = scores_of(queries, keys_all, bias_full, region_mask)
    again_probs = jnp.exp(again_scores - log_total)
    grad_values = jnp.einsum(
        "whqk,wqhd->wkhd",
        again_probs.astype(jnp.bfloat16),
        grad_attn,
        preferred_element_type=jnp.float32,
    )
    grad_probs = jnp.einsum(
        "wqhd,wkhd->whqk", grad_attn, values_all, preferred_element_type=jnp.float32
    )
    grad_scores = again_probs * (grad_probs - jnp.sum(again_probs * grad_probs, -1, keepdims=True))
    pair_sums = jnp.sum(grad_scores, 0).transpose(1, 2, 0).reshape(tile_len * tile_len, HEADS)
    grad_table = jax.ops.segment_sum(pair_sums, rel_index.reshape(-1), TABLE_ROWS)
    grad_raw = (grad_scores * HEAD_DIM ** (-0.5)).astype(jnp.bfloat16)
    grad_queries = jnp.einsum(
        "whqk,wkhd->wqhd", grad_raw, keys_all, preferred_element_type=jnp.float32
    )
    grad_keys = jnp.einsum("whqk,wqhd->wkhd", grad_raw, queries, preferred_element_type=jnp.float32)
    grad_packed = jnp.stack([grad_queries, grad_keys, grad_values], 2).astype(jnp.bfloat16)
    grad_packed = grad_packed.reshape(win_count, tile_len, 3 * D)
    grad_w_qkv = contract_rows(windows, grad_packed)
    grad_b_qkv = jnp.sum(grad_packed.astype(jnp.float32), (0, 1))
    grad_windows = times_transposed(grad_packed, w_qkv).astype(jnp.bfloat16)
    grad_shifted = jnp.roll(from_windows(grad_windows, img_count), SHIFT, 2)
    arrived_two = from_partner(grad_shifted[:, SHIFT:], "row", 0)
    grad_normed = jnp.concatenate([arrived_two, grad_shifted[:, :SHIFT]], 1).astype(jnp.float32)
    grad_images_ln, grad_gain_one, grad_shift_one = norm_pull(grad_normed)
    input_grad = grad_middle + grad_images_ln
    grad_list = [
        grad_w_qkv,
        grad_w_proj,
        grad_w_up,
        grad_w_down,
        grad_table,
        grad_b_qkv,
        grad_b_proj,
        grad_b_up,
        grad_b_down,
        grad_gain_one,
        grad_shift_one,
        grad_gain_two,
        grad_shift_two,
    ]
    grad_flat = jnp.concatenate([grad_one.reshape(-1) for grad_one in grad_list])
    grad_flat = jnp.pad(grad_flat, (0, gathered.shape[0] - grad_flat.shape[0]))
    grad_shard = lax.psum_scatter(grad_flat, ("img", "row"), scatter_dimension=0, tiled=True)
    shard_len = params.shape[0]
    position = lax.axis_index(("img", "row")) * shard_len + jnp.arange(shard_len, dtype=jnp.int32)
    step_rate = step_rates(position)
    new_first = BETA_ONE * first_moment + (1.0 - BETA_ONE) * grad_shard
    new_second = BETA_TWO * second_moment + (1.0 - BETA_TWO) * grad_shard * grad_shard
    fixed_first = new_first / (1.0 - BETA_ONE**STEP)
    fixed_second = new_second / (1.0 - BETA_TWO**STEP)
    new_params = params - step_rate * (
        fixed_first / (jnp.sqrt(fixed_second) + ADAM_EPS) + DECAY * params
    )
    return (
        output.astype(jnp.bfloat16),
        input_grad,
        new_params,
        new_params.astype(jnp.bfloat16),
        new_first,
        new_second,
    )


BF16 = jnp.bfloat16
F32 = jnp.float32
BOTH = ("img", "row")
TILE = 16
WINDOW = 304
LEN = 2 * WIN * WIN
QUADS = HEADS // 4
SPAN = 4 * WIN * WIN


def swap(block, mask, only=None):
    count = lax.axis_size(BOTH)
    route = [(d, d ^ mask) for d in range(count) if only is None or only(d)]
    return lax.ppermute(block, BOTH, route)


def params_call(mebibytes):
    return pltpu.CompilerParams(vmem_limit_bytes=mebibytes << 20)


def vmem(count):
    return [pl.BlockSpec(memory_space=pltpu.VMEM)] * count


SMEM_SPEC = pl.BlockSpec(memory_space=pltpu.SMEM)
ANY_SPEC = pl.BlockSpec(memory_space=pl.ANY)


def first_tile(device):
    return (289 * device) // TILE


def prep_body(me_ref, own_ref, out_ref, spare_ref, extra_ref, wide_ref):
    shift = me_ref[0] % TILE
    wide_ref[0:96] = jnp.zeros((96, 128), F32)
    wide_ref[1824:1920] = jnp.zeros((96, 128), F32)
    wide_ref[96:1830] = own_ref[...]
    for j in range(6):
        picked = wide_ref[pl.ds(96 - 6 * shift + j, WINDOW, stride=6), :]
        out_ref[:, 128 * j : 128 * (j + 1)] = picked.astype(BF16)
        spare_ref[:, 128 * j : 128 * (j + 1)] = picked.astype(BF16)
        extra_ref[:, 128 * j : 128 * (j + 1)] = picked.astype(BF16)


def window_of(me, own_flat):
    return pl.pallas_call(
        prep_body,
        out_shape=[jax.ShapeDtypeStruct((WINDOW, D), BF16)] * 3,
        in_specs=[SMEM_SPEC] + vmem(1),
        out_specs=vmem(3),
        scratch_shapes=[pltpu.VMEM((1920, 128), F32)],
        compiler_params=params_call(8),
        name="own_window",
    )(me, own_flat.reshape(-1, 128))


def mixer(groups, per):
    size = groups * per
    row = lax.broadcasted_iota(jnp.int32, (size, size), 0)
    col = lax.broadcasted_iota(jnp.int32, (size, size), 1)
    return (col == groups * (row % per) + row // per).astype(F32).astype(BF16)


def unmixer(groups, per):
    size = groups * per
    row = lax.broadcasted_iota(jnp.int32, (size, size), 0)
    col = lax.broadcasted_iota(jnp.int32, (size, size), 1)
    return (row == groups * (col % per) + col // per).astype(F32).astype(BF16)


def plane_rows(plane):
    low = first_tile(8 * plane) * TILE
    high = first_tile(8 * plane + 7) * TILE + WINDOW
    return low, high


def gate(value, *others):
    def body(*refs):
        pass

    return pl.pallas_call(
        body,
        out_shape=jax.ShapeDtypeStruct(value.shape, value.dtype),
        in_specs=[ANY_SPEC] * (1 + len(others)),
        out_specs=ANY_SPEC,
        input_output_aliases={0: 0},
        cost_estimate=cost(0),
        name="gate",
    )(value, *others)


def cross(block, zero, one):
    count = lax.axis_size(BOTH)
    return lax.ppermute(block, BOTH, [(d, d ^ (one if d & 2 else zero)) for d in range(count)])


def gather_windows(own, spare, extra, rows, *early):
    got = {0: own}
    first, second, third = {}, {}, {}

    def exchange(z):
        first[z] = cross(got[z], 4, 1)
        second[z] = cross(got[z], 1, 4)
        third[z] = cross(first[z], 1, 4)

    got[8] = swap(own, 8)
    first[0] = cross(own, 4, 1)
    second[0] = cross(own, 1, 4)
    spare = gate(spare, got[8])
    got[16] = swap(spare, 16)
    first[0] = gate(first[0], spare)
    third[0] = cross(first[0], 1, 4)
    got_rows = from_partner(rows, "row", 0)
    got[8] = gate(got[8], first[0], second[0])
    exchange(8)
    got[24] = swap(gate(extra, got[16]), 24)
    got[16] = gate(got[16], first[8], second[8], third[0], got_rows)
    exchange(16)
    got[24] = gate(got[24], first[16], second[16], third[8], *early)
    exchange(24)
    blocks, places = [], []
    for z in (0, 8, 16, 24):
        own_some = [got[z], first[z], second[z], third[z]]
        masks = ((z, z), (z | 4, z | 1), (z | 1, z | 4), (z | 5, z | 5))
        if z == 24:
            places.append((len(blocks), None, *masks[3]))
            places.append((len(blocks) + 1, None, masks[3][1] | 2, masks[3][0] | 2))
            last = own_some.pop()
            blocks += [last, swap(last, 2)]
        own_some = stacked(own_some)
        for n in range(own_some.shape[0]):
            zero, one = masks[n]
            places.append((len(blocks), n, zero, one))
            places.append((len(blocks) + 1, n, one | 2, zero | 2))
        blocks += [own_some, swap(own_some, 2)]
    return blocks, places, got_rows


def stacked_body(*refs):
    for i, ref in enumerate(refs[:-1]):
        refs[-1][i] = ref[...]


def stacked(blocks):
    return pl.pallas_call(
        stacked_body,
        out_shape=like(len(blocks), WINDOW, D),
        in_specs=vmem(len(blocks)),
        out_specs=vmem(1)[0],
        compiler_params=params_call(4),
        cost_estimate=cost(0),
        name="stacked",
    )(*blocks)


def load_windows(me, parts, places, first, last, flat_ref):
    base = first_tile(first) * TILE
    for device in (first, 16):
        if first <= device <= last:
            at = first_tile(device) * TILE - base
            flat_ref[at : at + TILE] = jnp.zeros((TILE, D), BF16)

    def each(act):
        for block, slot, zero, one in places:
            device = me ^ jnp.where((me & 2) == 0, zero, one)
            start = pl.multiple_of(first_tile(device) * TILE - base, TILE)
            part = parts[block] if slot is None else parts[block].at[slot]

            @pl.when((device >= first) & (device <= last))
            def _():
                act(part, start)

    def main(part, start):
        def step(i, carry):
            at = pl.multiple_of(48 * i + TILE, TILE)
            to = pl.multiple_of(start + at, TILE)
            flat_ref[pl.ds(to, 48)] = part[pl.ds(at, 48)]
            return carry

        lax.fori_loop(0, 6, step, 0)

    def edge(part, start):
        flat_ref[pl.ds(start, TILE)] += part[0:TILE]

    each(main)
    each(edge)


def load_small(me, parts, places, tail_ref):
    for block, slot, zero, one in places:
        part = parts[block] if slot is None else parts[block].at[slot]

        @pl.when(me ^ jnp.where((me & 2) == 0, zero, one) == 31)
        def _():
            tail_ref[...] = part[WINDOW - 32 : WINDOW]


def flat_scratch(first, last):
    return pltpu.VMEM(
        (first_tile(last) * TILE + WINDOW - first_tile(first) * TILE, D), BF16
    )


def unmix_rows(flat_ref, out_ref, base, groups, per, steps):
    mix = mixer(groups, per)
    size = groups * per
    for t in range(steps):
        rows = flat_ref[base + size * t : base + size * (t + 1)]
        out = jnp.dot(mix, rows, preferred_element_type=F32).astype(BF16)
        for j in range(groups):
            out_ref[j, per * t : per * (t + 1)] = out[per * j : per * (j + 1)]


def mix_rows(in_ref, flat_ref, base, groups, per, steps):
    mix = unmixer(groups, per)
    size = groups * per
    for t in range(steps):
        rows = jnp.concatenate([in_ref[j, per * t : per * (t + 1)] for j in range(groups)], 0)
        out = jnp.dot(mix, rows, preferred_element_type=F32).astype(BF16)
        flat_ref[base + size * t : base + size * (t + 1)] = out


def cut_windows(me, plane, flat_ref, base, keeps, sends):
    for flip in (2, 0):
        for s in range(4):
            first = jnp.where(((me ^ flip) & 2) == 0, 4, 1)
            away = (first if s & 2 else 0) + (5 - first if s & 1 else 0)
            device = 8 * plane + ((me & 7) ^ (away | flip))
            start = pl.multiple_of(first_tile(device) * TILE - base, TILE)
            window = flat_ref[pl.ds(start, WINDOW)]
            (sends if flip else keeps)[s // 2][s % 2] = window


def cost(microseconds):
    return pl.CostEstimate(
        flops=int(1e9 * microseconds),
        bytes_accessed=int(3.2e6 * microseconds),
        transcendentals=0,
    )


WINDOWS = [jax.ShapeDtypeStruct((2, WINDOW, D), BF16)] * 4


def like(*shape, dtype=BF16):
    return jax.ShapeDtypeStruct(shape, dtype)


def call(body, name, ins, outs, scratch, limit, ties=(), us=0, far=0):
    n_in, n_tie, n_out = len(ins), len(ties), len(outs)
    first_out = n_in + n_tie

    def wrapped(*refs):
        body(*refs[:n_in], *refs[first_out : first_out + n_out], *refs[first_out + n_out + 1 :])
        token_ref = refs[first_out + n_out]
        token_ref[...] = jnp.zeros_like(token_ref)

    specs = [SMEM_SPEC if one.dtype == jnp.int32 else vmem(1)[0] for one in ins]
    return pl.pallas_call(
        wrapped,
        out_shape=[*outs, like(8, 128, dtype=F32)],
        in_specs=specs + vmem(n_tie),
        out_specs=vmem(n_out - far)
        + [pl.BlockSpec(memory_space=pltpu.HBM)] * far
        + vmem(1),
        scratch_shapes=scratch,
        compiler_params=params_call(limit),
        cost_estimate=cost(us),
        name=name,
    )(*ins, *ties)


def pause(*ties, us=4):
    return call(lambda: None, "pause", [], [], [], 4, ties, us)[0]


def normal_parts(values):
    centre = jnp.mean(values, -1, keepdims=True)
    centred = values - centre
    spread = jnp.mean(centred * centred, -1, keepdims=True)
    scale = lax.rsqrt(spread + EPSILON)
    return centred * scale, scale


def normal_pull(n, scale, grad, gain):
    e = grad * gain
    return scale * (
        e - jnp.mean(e, -1, keepdims=True) - n * jnp.mean(e * n, -1, keepdims=True)
    )


def over_heads(block):
    head = lax.broadcasted_iota(jnp.int32, block.shape, 1) // HEAD_DIM
    return jnp.concatenate([jnp.where(head == h, block, jnp.zeros_like(block)) for h in range(4)], 0)


def own_columns(block):
    head = lax.broadcasted_iota(jnp.int32, (144, 128), 1) // HEAD_DIM
    out = block[0:144]
    for h in range(1, 4):
        out = jnp.where(head == h, block[144 * h : 144 * (h + 1)], out)
    return out


def contract(one, two, a, b):
    return lax.dot_general(one, two, (((a,), (b,)), ((), ())), preferred_element_type=F32)


def lay(out_ref, near, far):
    for i in range(WIN):
        ref, k = (near, 24 * i) if i < SHIFT else (far, 24 * (i - SHIFT))
        out_ref[12 * i : 12 * i + 12] = ref[k + 6 : k + 18]
        out_ref[144 + 12 * i : 150 + 12 * i] = ref[k + 18 : k + 24]
        out_ref[150 + 12 * i : 156 + 12 * i] = ref[k : k + 6]


def unlay(ref, near, far):
    for i in range(WIN):
        out_ref, k = (near, 24 * i) if i < SHIFT else (far, 24 * (i - SHIFT))
        out_ref[k + 6 : k + 18] = ref[12 * i : 12 * i + 12]
        out_ref[k + 18 : k + 24] = ref[144 + 12 * i : 150 + 12 * i]
        out_ref[k : k + 6] = ref[150 + 12 * i : 156 + 12 * i]


HALF = LEN // 2
LAY_SCRATCH = [pltpu.VMEM((LEN, D), F32), pltpu.VMEM((HALF, D), F32), pltpu.VMEM((HALF, D), F32)]


def unpack_small(tail_ref, vecs_ref, strips_ref, wide_ref, shift_ref):
    tail = tail_ref[...].astype(F32)
    rolled = pltpu.roll(tail, 360, 1)
    below = pltpu.roll(rolled, 31, 0)
    lane = lax.broadcasted_iota(jnp.int32, (16, D), 1)
    vecs_ref[...] = jnp.where(lane < 360, rolled[16:32], below[16:32])
    cell = lax.broadcasted_iota(jnp.int32, (32, D), 1) // HEADS
    which = lax.broadcasted_iota(jnp.int32, (32, D), 0)
    for r in range(17):
        row = jnp.broadcast_to(tail[r : r + 1], (32, D))
        wide_ref[32 * r : 32 * (r + 1)] = jnp.where(cell == which, row, 0.0).astype(BF16)
    lane = lax.broadcasted_iota(jnp.int32, (D, 128), 0)
    head = lax.broadcasted_iota(jnp.int32, (D, 128), 1)
    pick = (lane % HEADS == head).astype(F32).astype(BF16)
    table = jnp.dot(wide_ref[0:544], pick, preferred_element_type=F32)
    row = lax.broadcasted_iota(jnp.int32, table.shape, 0)
    table = jnp.where(row < TABLE_ROWS, table, 0.0)
    table = jnp.concatenate([table, jnp.zeros((96, 128), F32)], 0).T[0:HEADS]
    for j in range(WIN):
        moved = pltpu.roll(table, 629 + j, 1) if j < 11 else table
        shift_ref[24 * j : 24 * (j + 1), 0:640] = moved
    strips = contract(shift_ref[:, 0:640].astype(BF16), table_spread(), 1, 1)
    for j in range(WIN):
        strips_ref[:, j, :] = strips[24 * j : 24 * (j + 1)]


def table_spread():
    m = lax.broadcasted_iota(jnp.int32, (384, 640), 0)
    n = lax.broadcasted_iota(jnp.int32, (384, 640), 1)
    return ((n == 23 * (m // WIN) + m % WIN) & (m < 276)).astype(F32).astype(BF16)


def attend_body(places, me_ref, tokens_ref, rows_ref, mask_ref, *refs):
    parts = refs[:10]
    windows_ref, packed_ref, attn_ref, probs_ref, near_ref, far_ref, proj_ref, vecs_ref, qkv_out, laid_out = refs[10:20]
    flat_ref, wide_ref, one_ref, two_ref, bias_ref, qkv_ref, laid_ref, sems, tail_ref, strips_ref = refs[20:]
    load_small(me_ref[0], parts, places, tail_ref)
    unpack_small(tail_ref, vecs_ref, strips_ref, flat_ref, wide_ref)
    load_windows(me_ref[0], parts, places, 0, 10, flat_ref)
    one_ref[...] = tokens_ref[HALF:LEN].astype(F32)
    two_ref[...] = rows_ref[...].astype(F32)
    lay(wide_ref, one_ref, two_ref)
    laid = wide_ref[...]
    laid_ref[...] = laid.astype(BF16)
    n, _ = normal_parts(laid)
    windows_ref[...] = (n * vecs_ref[9:10] + vecs_ref[10:11]).astype(BF16)
    unmix_rows(flat_ref, qkv_ref, 0, 3, 64, 12)
    copies = [
        pltpu.make_async_copy(qkv_ref, qkv_out, sems.at[0]),
        pltpu.make_async_copy(laid_ref, laid_out, sems.at[1]),
    ]
    for copy in copies:
        copy.start()
    proj_ref[...] = flat_ref[2304:3072]

    def project(j, carry):
        packed_ref[j] = (
            jnp.dot(windows_ref[...], qkv_ref[j], preferred_element_type=F32)
            + vecs_ref[pl.ds(j, 1)]
        ).astype(BF16)
        return carry

    lax.fori_loop(0, 3, project, 0, unroll=3)

    def quad(g, carry):
        lanes = pl.ds(pl.multiple_of(128 * g, 128), 128)
        for h in range(4):
            for i in range(WIN):
                low = 12 * (11 - i)
                bias_ref[12 * i : 12 * i + 12, 144 * h : 144 * (h + 1)] = strips_ref[
                    4 * g + h, 0:12, low : low + 144
                ]
        for w in range(2):
            rows = pl.ds(144 * w, 144)
            queries = over_heads(packed_ref[0, rows, lanes])
            scores = contract(packed_ref[1, rows, lanes], queries, 1, 1)
            scores = scores * HEAD_DIM ** (-0.5) + bias_ref[...] + mask_ref[w]
            top = jnp.max(scores, 0, keepdims=True)
            exponent = jnp.exp(scores - top)
            total = jnp.sum(exponent, 0, keepdims=True)
            probs = (exponent * (1.0 / total)).astype(BF16)
            probs_ref[2 * g + w] = probs
            mixed = contract(probs, packed_ref[2, rows, lanes], 0, 0)
            attn_ref[rows, lanes] = own_columns(mixed).astype(BF16)
        return carry

    lax.fori_loop(0, QUADS, quad, 0, unroll=2)
    wide_ref[...] = (
        jnp.dot(attn_ref[...], proj_ref[...], preferred_element_type=F32) + vecs_ref[3:4]
    )
    unlay(wide_ref, one_ref, two_ref)
    near_ref[...] = one_ref[...].astype(BF16)
    far_ref[...] = two_ref[...].astype(BF16)
    for copy in copies:
        copy.wait()


def attend(me, tokens, rows, mask, parts, places):
    return call(
        functools.partial(attend_body, places),
        "attention_forward",
        [me, tokens, rows, mask, *parts],
        [
            like(LEN, D),
            like(3, LEN, D),
            like(LEN, D),
            like(2 * QUADS, 144, SPAN),
            like(HALF, D),
            like(HALF, D),
            like(D, D),
            like(16, D, dtype=F32),
            like(3, D, D),
            like(LEN, D),
        ],
        [flat_scratch(0, 10)]
        + LAY_SCRATCH
        + [
            pltpu.VMEM((144, SPAN), F32),
            pltpu.VMEM((3, D, D), BF16),
            pltpu.VMEM((LEN, D), BF16),
            pltpu.SemaphoreType.DMA((2,)),
            pltpu.VMEM((32, D), BF16),
            pltpu.VMEM((HEADS, WIN, 384), F32),
        ],
        22,
        far=2,
    )


def middle_of(tokens_ref, back_ref, near_ref):
    branch = jnp.concatenate([back_ref[...].astype(F32), near_ref[...].astype(F32)], 0)
    return tokens_ref[...].astype(F32) + branch


def feed_weights_body(places, me_ref, *refs):
    parts = refs[:10]
    up_ref, down_ref, flat_ref = refs[10:]
    load_windows(me_ref[0], parts, places, 10, 31, flat_ref)
    base = first_tile(10) * TILE
    unmix_rows(flat_ref, up_ref, 3072 - base, 4, 48, 16)

    def step(i, carry):
        at = pl.multiple_of(64 * i, 64)
        down_ref[pl.ds(at, 64)] = flat_ref[pl.ds(pl.multiple_of(6144 - base + at, TILE), 64)]
        return carry

    lax.fori_loop(0, 48, step, 0)


def feed_weights(me, parts, places, *ties):
    return call(
        functools.partial(feed_weights_body, places),
        "feed_weights",
        [me, *parts],
        [like(4, D, D), like(FF, D)],
        [flat_scratch(10, 31)],
        20,
        ties,
    )


def feed_body(me_ref, valid_ref, tokens_ref, back_ref, near_ref, cotangent_ref, vecs_ref, up_ref, down_ref, hidden_ref, active_ref, gradup_ref, sums_ref, low_ref, low_keep, high_keep, low_send, high_send, grad_ref):
    me = me_ref[0]
    n, _ = normal_parts(middle_of(tokens_ref, back_ref, near_ref))
    hidden_ref[...] = (n * vecs_ref[11:12] + vecs_ref[12:13]).astype(BF16)
    grad_out = cotangent_ref[...] * valid_ref[0].astype(F32).astype(BF16)
    grad_ref[3072:3104] = jnp.zeros((32, D), BF16)

    def step(j, carry):
        at = pl.multiple_of(D * j, D)
        down = down_ref[pl.ds(at, D)]
        upward = jnp.dot(hidden_ref[...], up_ref[j], preferred_element_type=F32)
        upward = upward + vecs_ref[pl.ds(4 + j, 1)]
        grad_active = contract(grad_out, down, 1, 1)
        share = 0.5 * (1.0 + lax.erf(upward * (0.5**0.5)))
        density = jnp.exp(-0.5 * upward * upward) * ((2.0 * math.pi) ** (-0.5))
        active = (upward * share).astype(BF16)
        grad_up = (grad_active * (share + upward * density)).astype(BF16)
        active_ref[j] = active
        gradup_ref[j] = grad_up
        sums_ref[pl.ds(j, 1)] = jnp.sum(grad_up.astype(F32), 0, keepdims=True)
        grad_ref[pl.ds(at, D)] = contract(active, grad_out, 0, 0).astype(BF16)
        return carry

    lax.fori_loop(0, 4, step, 0, unroll=2)
    cut_windows(me, 3, grad_ref, 6144, (low_keep, high_keep), (low_send, high_send))
    low_ref[...] = grad_ref[0:800]
    sums_ref[4:5] = jnp.sum(grad_out.astype(F32), 0, keepdims=True)


def feed(me, valid, tokens, back, near, cotangent, vecs, w_up, w_down):
    return call(
        feed_body,
        "feed_forward",
        [me, valid, tokens, back, near, cotangent, vecs, w_up, w_down],
        [
            like(LEN, D),
            like(4, LEN, D),
            like(4, LEN, D),
            like(8, D, dtype=F32),
            like(800, D),
            *WINDOWS,
        ],
        [pltpu.VMEM((3104, D), BF16)],
        16,
    )


def middle_body(me_ref, valid_ref, tokens_ref, back_ref, near_ref, cotangent_ref, vecs_ref, gradup_ref, up_ref, grad_ref, far_out, near_out, sums_ref):
    n, scale = normal_parts(middle_of(tokens_ref, back_ref, near_ref))
    grad_hidden = contract(gradup_ref[0], up_ref[0], 1, 1)
    for j in range(1, 4):
        grad_hidden = grad_hidden + contract(gradup_ref[j], up_ref[j], 1, 1)
    sums_ref[0:1] = jnp.sum(grad_hidden * n, 0, keepdims=True)
    sums_ref[1:2] = jnp.sum(grad_hidden, 0, keepdims=True)
    grad_out = (cotangent_ref[...] * valid_ref[0].astype(F32).astype(BF16)).astype(F32)
    grad = grad_out + normal_pull(n, scale, grad_hidden, vecs_ref[11:12])
    grad_ref[...] = grad
    far_out[...] = grad[:HALF].astype(BF16)
    near_out[...] = grad[HALF:].astype(BF16)


def middle_grad(me, valid, tokens, back, near, cotangent, vecs, grad_up, w_up):
    return call(
        middle_body,
        "middle_grad",
        [me, valid, tokens, back, near, cotangent, vecs, grad_up, w_up],
        [like(LEN, D, dtype=F32), like(HALF, D), like(HALF, D), like(8, D, dtype=F32)],
        [],
        12,
    )


def up_body(me_ref, hidden_ref, gradup_ref, low_ref, proj_ref, low_keep, high_keep, low_send, high_send, quad_ref, flat_ref):
    me = me_ref[0]

    def step(j, carry):
        quad_ref[j] = contract(hidden_ref[...], gradup_ref[j], 0, 0).astype(BF16)
        return carry

    lax.fori_loop(0, 4, step, 0, unroll=2)
    flat_ref[3072:3872] = low_ref[...]
    mix_rows(quad_ref, flat_ref, 0, 4, 48, 16)
    cut_windows(me, 2, flat_ref, 3072, (low_keep, high_keep), (low_send, high_send))
    proj_ref[...] = flat_ref[0:1552]


def up_grad(me, hidden, grad_up, low, *ties):
    return call(
        up_body,
        "up_grad",
        [me, hidden, grad_up, low],
        [like(1552, D), *WINDOWS],
        [pltpu.VMEM((4, D, D), BF16), pltpu.VMEM((3872, D), BF16)],
        16,
        ties,
    )


def proj_body(me_ref, near_ref, far_ref, attn_ref, proj_ref, high_ref, back_ref, sums_ref, edge_ref, low_keep, high_keep, low_send, high_send, flat_ref, wide_ref, one_ref, two_ref):
    me = me_ref[0]
    one_ref[...] = near_ref[...].astype(F32)
    two_ref[...] = far_ref[...].astype(F32)
    lay(wide_ref, one_ref, two_ref)
    grad = wide_ref[...].astype(BF16)
    flat_ref[0:768] = contract(attn_ref[...], grad, 0, 0).astype(BF16)
    flat_ref[768:2320] = high_ref[...]
    cut_windows(me, 1, flat_ref, 2304, (low_keep, high_keep), (low_send, high_send))
    edge_ref[...] = flat_ref[0:16]
    back_ref[...] = contract(grad, proj_ref[...], 1, 1).astype(BF16)
    sums_ref[0:1] = jnp.sum(grad.astype(F32), 0, keepdims=True)


def proj_grad(me, near, far, attn, w_proj, high, *ties):
    return call(
        proj_body,
        "proj_grad",
        [me, near, far, attn, w_proj, high],
        [like(LEN, D), like(8, D, dtype=F32), like(16, D), *WINDOWS],
        [pltpu.VMEM((2320, D), BF16)] + LAY_SCRATCH,
        12,
        ties,
    )


def unattend_quads(quads, packed_ref, grad_ref, attn_ref, probs_ref, back_ref, strips_ref, pairs_ref):
    strips_ref[...] = jnp.zeros_like(strips_ref)

    def quad(g, carry):
        lanes = pl.ds(pl.multiple_of(128 * g, 128), 128)
        for w in range(2):
            rows = pl.ds(144 * w, 144)
            queries = over_heads(packed_ref[0, rows, lanes])
            keys = packed_ref[1, rows, lanes]
            values = packed_ref[2, rows, lanes]
            grad = grad_ref[rows, lanes]
            product = -(attn_ref[rows, lanes].astype(F32) * grad.astype(F32)).astype(BF16)
            grads = over_heads(grad)
            left = jnp.concatenate([values, jnp.ones_like(values)], 1)
            right = jnp.concatenate([grads, over_heads(product)], 1)
            probs = probs_ref[2 * g + w]
            grad_scores = probs.astype(F32) * contract(left, right, 1, 1)
            if w == 0:
                pairs_ref[...] = grad_scores
            else:
                pairs_ref[...] += grad_scores
            raw = (grad_scores * HEAD_DIM ** (-0.5)).astype(BF16)
            back_ref[0, rows, lanes] = own_columns(contract(raw, keys, 0, 0)).astype(BF16)
            back_ref[1, rows, lanes] = jnp.dot(
                raw, queries, preferred_element_type=F32
            ).astype(BF16)
            back_ref[2, rows, lanes] = jnp.dot(
                probs, grads, preferred_element_type=F32
            ).astype(BF16)
        for h in range(4):
            for i in range(WIN):
                low = 12 * (11 - i)
                strips_ref[4 * (g - quads[0]) + h, 0:12, low : low + 144] += pairs_ref[
                    12 * i : 12 * i + 12, 144 * h : 144 * (h + 1)
                ]
        return carry

    lax.fori_loop(*quads, quad, 0, unroll=2)


def unattend_body(me_ref, packed_ref, grad_ref, attn_ref, probs_ref, back_ref, strips_ref, sums_ref, pairs_ref):
    unattend_quads((0, QUADS), packed_ref, grad_ref, attn_ref, probs_ref, back_ref, strips_ref, pairs_ref)
    for j in range(3):
        sums_ref[j : j + 1] = jnp.sum(back_ref[j].astype(F32), 0, keepdims=True)


def qkv_body(me_ref, windows_ref, edge_ref, back_ref, low_keep, high_keep, low_send, high_send, trio_ref, flat_ref):
    me = me_ref[0]

    def step(j, carry):
        trio_ref[j] = contract(windows_ref[...], back_ref[j], 0, 0).astype(BF16)
        return carry

    lax.fori_loop(0, 3, step, 0, unroll=3)
    mix_rows(trio_ref, flat_ref, 0, 3, 64, 12)
    flat_ref[2304:2320] = edge_ref[...]
    cut_windows(me, 0, flat_ref, 0, (low_keep, high_keep), (low_send, high_send))


def unattend(me, packed, grad, attn, probs, *ties):
    return call(
        unattend_body,
        "attention_backward",
        [me, packed, grad, attn, probs],
        [like(3, LEN, D), like(HEADS, WIN, 384, dtype=F32), like(8, D, dtype=F32)],
        [pltpu.VMEM((144, SPAN), F32)],
        10,
        ties,
    )


def qkv_grad(me, windows, edge, back, *ties):
    return call(
        qkv_body,
        "qkv_grad",
        [me, windows, edge, back],
        [*WINDOWS],
        [pltpu.VMEM((3, D, D), BF16), pltpu.VMEM((2320, D), BF16)],
        12,
        ties,
    )


def token_body(me_ref, back_ref, qkv_ref, laid_ref, vecs_ref, near_out, far_out, sums_ref, wide_ref, one_ref, two_ref):
    grad = contract(back_ref[0], qkv_ref[0], 1, 1)
    for j in (1, 2):
        grad = grad + contract(back_ref[j], qkv_ref[j], 1, 1)
    n, scale = normal_parts(laid_ref[...].astype(F32))
    sums_ref[0:1] = jnp.sum(grad * n, 0, keepdims=True)
    sums_ref[1:2] = jnp.sum(grad, 0, keepdims=True)
    wide_ref[...] = normal_pull(n, scale, grad, vecs_ref[9:10])
    unlay(wide_ref, one_ref, two_ref)
    near_out[...] = one_ref[...].astype(BF16)
    far_out[...] = two_ref[...].astype(BF16)


def token_grad(me, back, w_qkv, laid, vecs, *ties):
    return call(
        token_body,
        "token_grad",
        [me, back, w_qkv, laid, vecs],
        [like(HALF, D), like(HALF, D), like(8, D, dtype=F32)],
        LAY_SCRATCH,
        10,
        ties,
    )


def output_body(me_ref, tokens_ref, back_ref, near_ref, vecs_ref, active_ref, down_ref, out_ref):
    total = middle_of(tokens_ref, back_ref, near_ref) + vecs_ref[8:9]
    for j in range(4):
        total = total + jnp.dot(
            active_ref[j], down_ref[D * j : D * (j + 1)], preferred_element_type=F32
        )
    out_ref[...] = total.astype(BF16)


def block_output(me, tokens, back, near, vecs, active, w_down, *ties):
    return call(
        output_body,
        "block_output",
        [me, tokens, back, near, vecs, active, w_down],
        [like(LEN, D)],
        [],
        10,
        ties,
    )


def sum_body(slots, lows, *refs):
    for i in range(slots):
        total = refs[0][lows[0] + i].astype(F32)
        for ref, low in zip(refs[1 : len(lows)], lows[1:]):
            total = total + ref[low + i].astype(F32)
        refs[-1][i] = total.astype(BF16)


def sum_slots(slots, terms, *ties):
    return call(
        functools.partial(sum_body, slots, [low for _, low in terms]),
        "sum_slots",
        [one for one, _ in terms],
        [like(slots, WINDOW, D)],
        [],
        6,
        ties,
    )


def split_body(low_ref, x_ref, sent_ref, kept_ref):
    for slot, ref in ((1, sent_ref), (0, kept_ref)):
        ref[...] = (low_ref[slot].astype(F32) + x_ref[slot].astype(F32)).astype(BF16)


def split_sum(low, x, *ties):
    return call(
        split_body, "split_sum", [low, x], [like(WINDOW, D), like(WINDOW, D)], [], 6, ties
    )


def arranged_body(me_ref, high_ref, low_ref, own_ref, other_ref):
    odd = (me_ref[0] // 8) % 2 == 1

    @pl.when(odd)
    def _():
        own_ref[...] = high_ref[...]
        other_ref[...] = low_ref[...]

    @pl.when(jnp.logical_not(odd))
    def _():
        own_ref[...] = low_ref[...]
        other_ref[...] = high_ref[...]


def arranged(me, high, low, *ties):
    return call(
        arranged_body,
        "arranged",
        [me, high, low],
        [like(WINDOW, D), like(WINDOW, D)],
        [],
        6,
        ties,
    )


def with_small_body(me_ref, own_ref, rows_ref, other_ref, out_ref):
    me = me_ref[0]
    out_ref[...] = own_ref[...]

    @pl.when((me % 8 == 7) & ((me // 8) % 2 == 1))
    def _():
        last = own_ref[WINDOW - 32 : WINDOW].astype(F32)
        out_ref[WINDOW - 32 : WINDOW] = (last + (rows_ref[...] + other_ref[...])).astype(BF16)


def with_small(me, own, rows, other, *ties):
    return call(
        with_small_body, "with_small", [me, own, rows, other], [like(WINDOW, D)], [], 6, ties
    )


def sum_two(one, two, *ties):
    def body(one_ref, two_ref, out_ref):
        out_ref[...] = (one_ref[...].astype(F32) + two_ref[...].astype(F32)).astype(BF16)

    return call(body, "sum_two", [one, two], [like(WINDOW, D)], [], 6, ties)


def to_half(block, upper):
    return swap(block, 16, lambda d: (d // 16 == 1) != upper)


def small_body(strips_ref, qkv_ref, proj_ref, up_ref, one_ref, two_ref, out_ref, rows_ref):
    out_ref[...] = jnp.zeros_like(out_ref)
    out_ref[0:3] = qkv_ref[0:3]
    out_ref[3:4] = proj_ref[0:1]
    out_ref[4:9] = up_ref[0:5]
    out_ref[9:11] = one_ref[0:2]
    out_ref[11:13] = two_ref[0:2]
    for j in range(WIN):
        rows_ref[24 * j : 24 * (j + 1)] = strips_ref[:, j, :]
    rows = rows_ref[...]
    high = rows.astype(BF16)
    low = (rows - high.astype(F32)).astype(BF16)
    spread = table_spread()
    wide = jnp.dot(high, spread, preferred_element_type=F32) + jnp.dot(
        low, spread, preferred_element_type=F32
    )
    total = wide[264:288]
    for j in range(WIN - 1):
        total = total + pltpu.roll(wide[24 * j : 24 * (j + 1)], 11 - j, 1)
    out_ref[16:40, 0:640] = total


def small_grads(strips, qkv, proj, up, one, two, *ties):
    return call(
        small_body,
        "small_grads",
        [strips, qkv, proj, up, one, two],
        [like(40, D, dtype=F32)],
        [pltpu.VMEM((288, 384), F32)],
        8,
        ties,
    )


def lines_body(small_ref, out_ref, table_ref, vec_ref, line_ref):
    table = jnp.concatenate([small_ref[16:40, 0:640], jnp.zeros((104, 640), F32)], 0)
    table_ref[...] = table.T
    wide = jnp.zeros((40, 384), F32)
    for q in range(16):
        rows = table_ref[pl.ds(q, 40, stride=16), :]
        padded = jnp.concatenate([rows, jnp.zeros((40, 256), F32)], 1)
        wide = wide + (pltpu.roll(padded, 24 * q, 1) if q else padded)
    line_ref[...] = jnp.zeros_like(line_ref)
    for c in range(3):
        line_ref[pl.ds(c, 40, stride=3), :] = wide[:, 128 * c : 128 * (c + 1)]
    for c in range(6):
        vec_ref[pl.ds(c, 16, stride=6), :] = small_ref[0:16, 128 * c : 128 * (c + 1)]
    rolled = pltpu.roll(vec_ref[...], 24, 1)
    lane = lax.broadcasted_iota(jnp.int32, rolled.shape, 1)
    line_ref[99:195] += jnp.where(lane >= 24, rolled, 0.0)
    line_ref[100:196] += jnp.where(lane < 24, rolled, 0.0)
    for c in range(6):
        out_ref[:, 128 * c : 128 * (c + 1)] = line_ref[pl.ds(c, 32, stride=6), :]


def small_sum(one, two, *ties):
    def body(one_ref, two_ref, out_ref):
        out_ref[...] = one_ref[...] + two_ref[...]

    return call(body, "small_sum", [one, two], [like(40, D, dtype=F32)], [], 4, ties)


def small_lines(small, *ties):
    return call(
        lines_body,
        "small_lines",
        [small],
        [like(32, D, dtype=F32)],
        [pltpu.VMEM((640, 128), F32), pltpu.VMEM((96, 128), F32), pltpu.VMEM((200, 128), F32)],
        8,
        ties,
    )


CUTS = (0, 576, 1152, 1734)


def adam_body(me_ref, *refs):
    terms = refs[:4]
    params_ref, first_ref, second_ref = refs[4:7]
    outs = refs[7:11]
    flat_ref, copy_ref, sems, out_sems, params_out, low_out, first_out, second_out = refs[11:]
    me = me_ref[0]
    shift = me % TILE
    for which, own_terms in enumerate((terms[0:2], terms[2:3], terms[3:4])):

        @pl.when(jnp.minimum(me // 8, 2) == which)
        def _():
            copies = [
                pltpu.make_async_copy(term, copy_ref.at[z], sems.at[z])
                for z, term in enumerate(own_terms)
            ]
            if len(own_terms) == 1:
                copy_ref[1] = jnp.zeros((WINDOW, D), BF16)
            for copy in copies:
                copy.start()
            for copy in copies:
                copy.wait()

    for j in range(6):
        terms_j = [copy_ref[z, :, 128 * j : 128 * (j + 1)].astype(F32) for z in range(2)]
        flat_ref[pl.ds(j, WINDOW, stride=6), :] = terms_j[0] + terms_j[1]
    copies = []
    for n, (low, high) in enumerate(zip(CUTS[:-1], CUTS[1:])):
        grad = flat_ref[pl.ds(6 * shift + low, high - low), :]
        line = me * 1734 + low + lax.broadcasted_iota(jnp.int32, grad.shape, 0)
        rate = jnp.full(grad.shape, D ** (-0.5), F32)
        rate = jnp.where((line >= 13824) & (line < 18432), 4.0 * D ** (-0.5), rate)
        rate = jnp.where(line >= 36864, FF ** (-0.5), rate)
        if n == len(CUTS) - 2:
            lane = lax.broadcasted_iota(jnp.int32, (192, 128), 1)
            fine = step_rates(line[-192:] * 128 + lane)
            rate = jnp.concatenate([rate[:-192], fine], 0)
        params = params_ref[low:high]
        new_first = BETA_ONE * first_ref[low:high] + (1.0 - BETA_ONE) * grad
        new_second = BETA_TWO * second_ref[low:high] + (1.0 - BETA_TWO) * grad * grad
        fixed_first = new_first / (1.0 - BETA_ONE**STEP)
        fixed_second = new_second / (1.0 - BETA_TWO**STEP)
        new_params = params - rate * (
            fixed_first / (jnp.sqrt(fixed_second) + ADAM_EPS) + DECAY * params
        )
        params_out[low:high] = new_params
        low_out[low:high] = new_params.astype(BF16)
        first_out[low:high] = new_first
        second_out[low:high] = new_second
        for k, one in enumerate((params_out, low_out, first_out, second_out)):
            copies.append(
                pltpu.make_async_copy(
                    one.at[pl.ds(low, high - low)],
                    outs[k].at[pl.ds(low, high - low)],
                    out_sems.at[n, k],
                )
            )
            copies[-1].start()
    for copy in copies:
        copy.wait()


def adam(me, terms, params, first_moment, second_moment):
    lines = (1734, 128)
    args = [one.reshape(lines) for one in (params, first_moment, second_moment)]
    outs = pl.pallas_call(
        adam_body,
        out_shape=[
            jax.ShapeDtypeStruct(lines, F32),
            jax.ShapeDtypeStruct(lines, BF16),
            jax.ShapeDtypeStruct(lines, F32),
            jax.ShapeDtypeStruct(lines, F32),
        ],
        in_specs=[SMEM_SPEC] + [ANY_SPEC] * 4 + vmem(3),
        out_specs=[ANY_SPEC] * 4,
        scratch_shapes=[
            pltpu.VMEM((6 * WINDOW, 128), F32),
            pltpu.VMEM((2, WINDOW, D), BF16),
            pltpu.SemaphoreType.DMA((2,)),
            pltpu.SemaphoreType.DMA((3, 4)),
            pltpu.VMEM(lines, F32),
            pltpu.VMEM(lines, BF16),
            pltpu.VMEM(lines, F32),
            pltpu.VMEM(lines, F32),
        ],
        compiler_params=params_call(16),
        name="adam",
    )(me, *terms, *args)
    return [one.reshape(-1) for one in outs]


def shards(tokens, cotangent, valid, params, first_moment, second_moment):
    if lax.axis_size("img") != 16 or lax.axis_size("row") != 2:
        return shards_general(tokens, cotangent, valid, params, first_moment, second_moment)
    me = lax.axis_index(BOTH).astype(jnp.int32).reshape(1)
    flat_tokens = tokens.reshape(LEN, D)
    flat_cotangent = cotangent.reshape(LEN, D)
    own, spare, extra = window_of(me, params)
    mask = jnp.tile(window_mask(lax.axis_index("row") * WIN), (1, 1, 4))
    parts, places, rows = gather_windows(own, spare, extra, flat_tokens[:HALF], mask)
    windows, packed, attn, probs, near, far, w_proj, vecs, w_qkv, laid, token = attend(
        me, flat_tokens, rows, mask, parts, places
    )
    back = from_partner(far, "row", 0)
    w_up, w_down, _ = feed_weights(me, parts, places, pause(token))
    hidden, active, grad_up, sums_up, low, low_three, high_three, low_send, high_send, token = feed(
        me, valid, flat_tokens, back, near, flat_cotangent, vecs, w_up, w_down
    )
    core_high_three, core_low_three = swap(high_send, 2), swap(low_send, 2)
    grad_middle, far_grad, near_grad, sums_two, token = middle_grad(
        me, valid, flat_tokens, back, near, flat_cotangent, vecs, grad_up, w_up
    )
    far_grad = from_partner(far_grad, "row", 0)
    sent, token = sum_slots(2, [(high_three, 0), (core_high_three, 0)], pause(token))
    x_three = cross(sent, 4, 1)
    low_three, token = sum_slots(2, [(low_three, 0), (core_low_three, 0)], token)
    high, low_two, high_two, low_send, high_send, token = up_grad(
        me, hidden, grad_up, low, pause(token)
    )
    core_high_two, core_low_two = swap(high_send, 2), swap(low_send, 2)
    sent, three, token = split_sum(low_three, x_three, token)
    y_three = cross(sent, 1, 4)
    sent, token = sum_slots(2, [(high_two, 0), (core_high_two, 0)], pause(token))
    x_two = cross(sent, 4, 1)
    low_two, token = sum_slots(2, [(low_two, 0), (core_low_two, 0)], token)
    grad_attn, sums_proj, edge, low_one, high_one, low_send, high_send, token = proj_grad(
        me, near_grad, far_grad, attn, w_proj, high, pause(token)
    )
    core_high_one, core_low_one = swap(high_send, 2), swap(low_send, 2)
    grad_packed, strips, sums_qkv, token = unattend(
        me, packed, grad_attn, attn, probs, pause(token)
    )
    sent, token = sum_slots(2, [(high_one, 0), (core_high_one, 0)], token)
    x_one = cross(sent, 4, 1)
    near_in, far_in, sums_one, token = token_grad(me, grad_packed, w_qkv, laid, vecs, token)
    small, token = small_grads(strips, sums_qkv, sums_proj, sums_up, sums_one, sums_two, token)
    three, token = sum_two(three, y_three, token)
    small, token = small_sum(small, swap(small, 2), token)
    sent, two, token = split_sum(low_two, x_two, token)
    y_two = cross(sent, 1, 4)
    low_one, token = sum_slots(2, [(low_one, 0), (core_low_one, 0)], token)
    low_zero, high_zero, low_send, high_send, token = qkv_grad(
        me, windows, edge, grad_packed, pause(token)
    )
    core_high_zero, core_low_zero = swap(high_send, 2), swap(low_send, 2)
    two, token = sum_two(two, y_two, token)
    small, token = small_sum(small, cross(small, 4, 1), token)
    upper, other, token = arranged(me, three, two, token)
    z_upper = swap(other, 8)
    sent, one, token = split_sum(low_one, x_one, token)
    y_one = cross(sent, 1, 4)
    sent, token = sum_slots(2, [(high_zero, 0), (core_high_zero, 0)], pause(token, us=12))
    x_zero = cross(sent, 4, 1)
    low_zero, token = sum_slots(2, [(low_zero, 0), (core_low_zero, 0)], token)
    upper, token = sum_two(upper, z_upper, token)
    one, token = sum_two(one, y_one, token)
    z_one = swap(one, 8, lambda d: d // 8 in (0, 2))
    sent, zero, token = split_sum(low_zero, x_zero, token)
    y_zero = cross(sent, 1, 4)
    small, token = small_sum(small, cross(small, 1, 4), token)
    rows, token = small_lines(small, token)
    z_rows = swap(rows, 8)
    one, token = sum_two(one, z_one, token)
    far_one = swap(one, 16, lambda d: d // 8 == 3)
    zero, token = sum_two(zero, y_zero, token)
    z_zero = swap(zero, 8, lambda d: d // 8 in (1, 3))
    upper, token = with_small(me, upper, rows, z_rows, token)
    far_upper = to_half(upper, True)
    zero, token = sum_two(zero, z_zero, token)
    far_zero = swap(zero, 16, lambda d: d // 8 == 2)
    upper, token = sum_two(upper, far_upper, token)
    one, token = sum_two(one, far_one, token)
    far_in = from_partner(gate(far_in, token), "row", 0)
    output, token = block_output(
        me, flat_tokens, back, near, vecs, active, w_down, token
    )
    input_grad = grad_middle + jnp.concatenate([far_in, near_in], 0).astype(F32)
    terms = [zero, far_zero, one, upper]
    new = adam(me, terms, params, first_moment, second_moment)
    return (output.reshape(tokens.shape), input_grad.reshape(tokens.shape), *new)


def solution(mesh):
    return jax.shard_map(
        shards,
        mesh=mesh,
        in_specs=(
            P("img", "row", None, None),
            P("img", "row", None, None),
            P("img"),
            P(("img", "row")),
            P(("img", "row")),
            P(("img", "row")),
        ),
        out_specs=(
            P("img", "row", None, None),
            P("img", "row", None, None),
            P(("img", "row")),
            P(("img", "row")),
            P(("img", "row")),
            P(("img", "row")),
        ),
        check_vma=False,
    )
```

```python
import functools
import math

import jax
import jax.numpy as jnp
from jax import lax
from jax.experimental import pallas as pl
from jax.experimental.pallas import tpu as pltpu
from jax.sharding import PartitionSpec as P

D = 768
FF = 3072
HEADS = 24
HEAD_DIM = 32
WIN = 12
SHIFT = 6
SIDE = 24
STEP = 4
TABLE_ROWS = 529


EPSILON = 1e-05
MASKED = -100.0
DECAY = 0.05
ADAM_EPS = 1e-08
BETA_ONE = 0.5
BETA_TWO = 0.5


def from_partner(block, axis, apart):
    count = lax.axis_size(axis)
    route = []
    for low in range(count):
        high = low | 1 << apart
        if high != low and high < count:
            route += [(low, high), (high, low)]
    return lax.ppermute(block, axis, route)


def piece_shapes():
    return [
        (D, 3 * D),
        (D, D),
        (D, FF),
        (FF, D),
        (TABLE_ROWS, HEADS),
        (3 * D,),
        (D,),
        (FF,),
        (D,),
        (D,),
        (D,),
        (D,),
        (D,),
    ]


def unpack(flat_vec):
    pieces = []
    offset = 0
    for shape_one in piece_shapes():
        amount = math.prod(shape_one)
        pieces.append(lax.slice_in_dim(flat_vec, offset, offset + amount).reshape(shape_one))
        offset = offset + amount
    return pieces


def step_rates(position):
    rate_list = [
        D ** (-0.5),
        4.0 * D ** (-0.5),
        D ** (-0.5),
        FF ** (-0.5),
        1.0,
        0.3,
        0.3,
        0.3,
        0.3,
        0.4,
        0.3,
        0.4,
        0.3,
    ]
    result = jnp.zeros(position.shape, jnp.float32)
    offset = 0
    for shape_one, rate_one in zip(piece_shapes(), rate_list):
        amount = math.prod(shape_one)
        inside = (position >= offset) & (position < offset + amount)
        result = jnp.where(inside, jnp.float32(rate_one), result)
        offset = offset + amount
    return result


def layer_norm(values, gain_vec, shift_vec):
    centre = jnp.mean(values, -1, keepdims=True)
    centred = values - centre
    spread = jnp.mean(centred * centred, -1, keepdims=True)
    return centred * lax.rsqrt(spread + EPSILON) * gain_vec + shift_vec


def region_of(coord):
    return jnp.where(coord < SIDE - WIN, 0, jnp.where(coord < SIDE - SHIFT, 1, 2))


def relative_index():
    cell_index = jnp.arange(WIN * WIN, dtype=jnp.int32)
    row_part = cell_index // WIN
    col_part = cell_index % WIN
    return (row_part[:, None] - row_part[None, :] + WIN - 1) * (2 * WIN - 1) + (
        col_part[:, None] - col_part[None, :] + WIN - 1
    )


def window_mask(row_first):
    row_coord = row_first + jnp.arange(WIN, dtype=jnp.int32)
    col_coord = jnp.arange(SIDE, dtype=jnp.int32)
    region_ids = 3 * region_of(row_coord)[:, None] + region_of(col_coord)[None, :]
    region_ids = (
        region_ids.reshape(WIN, SIDE // WIN, WIN).transpose(1, 0, 2).reshape(SIDE // WIN, WIN * WIN)
    )
    same = region_ids[:, :, None] == region_ids[:, None, :]
    return jnp.where(same, 0.0, MASKED).astype(jnp.float32)


def to_windows(grid_rows):
    img_count = grid_rows.shape[0]
    width = grid_rows.shape[-1]
    shaped = grid_rows.reshape(img_count, WIN, SIDE // WIN, WIN, width).transpose(0, 2, 1, 3, 4)
    return shaped.reshape(img_count * (SIDE // WIN), WIN * WIN, width)


def from_windows(window_rows, img_count):
    width = window_rows.shape[-1]
    shaped = window_rows.reshape(img_count, SIDE // WIN, WIN, WIN, width).transpose(0, 2, 1, 3, 4)
    return shaped.reshape(img_count, WIN, SIDE, width)


BF16 = jnp.bfloat16
F32 = jnp.float32
BOTH = ("img", "row")
ROWS = 9248
TILE = 16
WINDOW = 304
WIDE = 2 * D // 4
VMEM_MOST = 60 * 1024 * 1024


def contract_rows(left_op, right_op):
    summed_dims = tuple(range(left_op.ndim - 1))
    return lax.dot_general(
        left_op,
        right_op,
        ((summed_dims, summed_dims), ((), ())),
        preferred_element_type=jnp.float32,
    )


def times_transposed(left_op, right_op):
    return lax.dot_general(
        left_op,
        right_op,
        (((left_op.ndim - 1,), (1,)), ((), ())),
        preferred_element_type=jnp.float32,
    )


def scores_of(queries, keys_all, bias_full, region_mask):
    raw_scores = jnp.einsum(
        "wqhd,wkhd->whqk", queries, keys_all, preferred_element_type=jnp.float32
    )
    return raw_scores * HEAD_DIM ** (-0.5) + bias_full[None] + region_mask[:, None]


def shards_general(tokens, cotangent, valid, params, first_moment, second_moment):
    img_count = tokens.shape[0]
    win_count = img_count * (SIDE // WIN)
    tile_len = WIN * WIN
    gathered = lax.all_gather(params.astype(jnp.bfloat16), ("img", "row"), axis=0, tiled=True)
    (
        w_qkv,
        w_proj,
        w_up,
        w_down,
        bias_table,
        b_qkv,
        b_proj,
        b_up,
        b_down,
        gain_one,
        shift_one,
        gain_two,
        shift_two,
    ) = unpack(gathered)
    images = tokens.astype(jnp.float32)
    normed, norm_pull = jax.vjp(
        layer_norm, images, gain_one.astype(jnp.float32), shift_one.astype(jnp.float32)
    )
    normed_low = normed.astype(jnp.bfloat16)
    incoming = from_partner(normed_low[:, :SHIFT], "row", 0)
    shifted = jnp.roll(jnp.concatenate([normed_low[:, SHIFT:], incoming], 1), -SHIFT, 2)
    windows = to_windows(shifted)
    packed = (
        jnp.dot(windows, w_qkv, preferred_element_type=jnp.float32) + b_qkv.astype(jnp.float32)
    ).astype(jnp.bfloat16)
    heads_view = packed.reshape(win_count, tile_len, 3, HEADS, HEAD_DIM)
    queries = heads_view[:, :, 0]
    keys_all = heads_view[:, :, 1]
    values_all = heads_view[:, :, 2]
    rel_index = relative_index()
    bias_full = bias_table.astype(jnp.float32)[rel_index].transpose(2, 0, 1)
    region_mask = jnp.tile(window_mask(lax.axis_index("row") * WIN), (img_count, 1, 1))
    scores = scores_of(queries, keys_all, bias_full, region_mask)
    row_top = jnp.max(scores, -1, keepdims=True)
    exponent = jnp.exp(scores - row_top)
    row_total = jnp.sum(exponent, -1, keepdims=True)
    log_total = row_top + jnp.log(row_total)
    attn_probs = (exponent / row_total).astype(jnp.bfloat16)
    attn_mixed = jnp.einsum(
        "whqk,wkhd->wqhd", attn_probs, values_all, preferred_element_type=jnp.float32
    )
    attn_mixed = attn_mixed.astype(jnp.bfloat16).reshape(win_count, tile_len, D)
    branch = (
        jnp.dot(attn_mixed, w_proj, preferred_element_type=jnp.float32) + b_proj.astype(jnp.float32)
    ).astype(jnp.bfloat16)
    branch_grid = jnp.roll(from_windows(branch, img_count), SHIFT, 2)
    returned = from_partner(branch_grid[:, SHIFT:], "row", 0)
    middle = images + jnp.concatenate([returned, branch_grid[:, :SHIFT]], 1).astype(jnp.float32)
    normed_two, norm_two_pull = jax.vjp(
        layer_norm, middle, gain_two.astype(jnp.float32), shift_two.astype(jnp.float32)
    )
    hidden_in = normed_two.astype(jnp.bfloat16)
    upward = jnp.dot(hidden_in, w_up, preferred_element_type=jnp.float32) + b_up.astype(jnp.float32)
    active_full, gelu_pull = jax.vjp(lambda values: jax.nn.gelu(values, approximate=False), upward)
    active = active_full.astype(jnp.bfloat16)
    output = (
        middle
        + jnp.dot(active, w_down, preferred_element_type=jnp.float32)
        + b_down.astype(jnp.float32)
    )
    regathered = lax.all_gather(params.astype(jnp.bfloat16), ("img", "row"), axis=0, tiled=True)
    fresh = unpack(regathered)
    w_qkv, w_proj, w_up, w_down = (fresh[0], fresh[1], fresh[2], fresh[3])
    grad_out = cotangent * valid.astype(jnp.bfloat16)[:, None, None, None]
    grad_w_down = contract_rows(active, grad_out)
    grad_b_down = jnp.sum(grad_out.astype(jnp.float32), (0, 1, 2))
    grad_active = times_transposed(grad_out, w_down)
    grad_up = gelu_pull(grad_active)[0].astype(jnp.bfloat16)
    grad_w_up = contract_rows(hidden_in, grad_up)
    grad_b_up = jnp.sum(grad_up.astype(jnp.float32), (0, 1, 2))
    grad_hidden = times_transposed(grad_up, w_up)
    grad_middle_ln, grad_gain_two, grad_shift_two = norm_two_pull(grad_hidden)
    grad_middle = grad_out.astype(jnp.float32) + grad_middle_ln
    middle_low = grad_middle.astype(jnp.bfloat16)
    arrived = from_partner(middle_low[:, :SHIFT], "row", 0)
    grad_grid = jnp.roll(jnp.concatenate([middle_low[:, SHIFT:], arrived], 1), -SHIFT, 2)
    grad_branch = to_windows(grad_grid)
    grad_w_proj = contract_rows(attn_mixed, grad_branch)
    grad_b_proj = jnp.sum(grad_branch.astype(jnp.float32), (0, 1))
    grad_attn = times_transposed(grad_branch, w_proj).astype(jnp.bfloat16)
    grad_attn = grad_attn.reshape(win_count, tile_len, HEADS, HEAD_DIM)
    again_scores = scores_of(queries, keys_all, bias_full, region_mask)
    again_probs = jnp.exp(again_scores - log_total)
    grad_values = jnp.einsum(
        "whqk,wqhd->wkhd",
        again_probs.astype(jnp.bfloat16),
        grad_attn,
        preferred_element_type=jnp.float32,
    )
    grad_probs = jnp.einsum(
        "wqhd,wkhd->whqk", grad_attn, values_all, preferred_element_type=jnp.float32
    )
    grad_scores = again_probs * (grad_probs - jnp.sum(again_probs * grad_probs, -1, keepdims=True))
    pair_sums = jnp.sum(grad_scores, 0).transpose(1, 2, 0).reshape(tile_len * tile_len, HEADS)
    grad_table = jax.ops.segment_sum(pair_sums, rel_index.reshape(-1), TABLE_ROWS)
    grad_raw = (grad_scores * HEAD_DIM ** (-0.5)).astype(jnp.bfloat16)
    grad_queries = jnp.einsum(
        "whqk,wkhd->wqhd", grad_raw, keys_all, preferred_element_type=jnp.float32
    )
    grad_keys = jnp.einsum("whqk,wqhd->wkhd", grad_raw, queries, preferred_element_type=jnp.float32)
    grad_packed = jnp.stack([grad_queries, grad_keys, grad_values], 2).astype(jnp.bfloat16)
    grad_packed = grad_packed.reshape(win_count, tile_len, 3 * D)
    grad_w_qkv = contract_rows(windows, grad_packed)
    grad_b_qkv = jnp.sum(grad_packed.astype(jnp.float32), (0, 1))
    grad_windows = times_transposed(grad_packed, w_qkv).astype(jnp.bfloat16)
    grad_shifted = jnp.roll(from_windows(grad_windows, img_count), SHIFT, 2)
    arrived_two = from_partner(grad_shifted[:, SHIFT:], "row", 0)
    grad_normed = jnp.concatenate([arrived_two, grad_shifted[:, :SHIFT]], 1).astype(jnp.float32)
    grad_images_ln, grad_gain_one, grad_shift_one = norm_pull(grad_normed)
    input_grad = grad_middle + grad_images_ln
    grad_list = [
        grad_w_qkv,
        grad_w_proj,
        grad_w_up,
        grad_w_down,
        grad_table,
        grad_b_qkv,
        grad_b_proj,
        grad_b_up,
        grad_b_down,
        grad_gain_one,
        grad_shift_one,
        grad_gain_two,
        grad_shift_two,
    ]
    grad_flat = jnp.concatenate([grad_one.reshape(-1) for grad_one in grad_list])
    grad_flat = jnp.pad(grad_flat, (0, gathered.shape[0] - grad_flat.shape[0]))
    grad_shard = lax.psum_scatter(grad_flat, ("img", "row"), scatter_dimension=0, tiled=True)
    shard_len = params.shape[0]
    position = lax.axis_index(("img", "row")) * shard_len + jnp.arange(shard_len, dtype=jnp.int32)
    step_rate = step_rates(position)
    new_first = BETA_ONE * first_moment + (1.0 - BETA_ONE) * grad_shard
    new_second = BETA_TWO * second_moment + (1.0 - BETA_TWO) * grad_shard * grad_shard
    fixed_first = new_first / (1.0 - BETA_ONE**STEP)
    fixed_second = new_second / (1.0 - BETA_TWO**STEP)
    new_params = params - step_rate * (
        fixed_first / (jnp.sqrt(fixed_second) + ADAM_EPS) + DECAY * params
    )
    return (
        output.astype(jnp.bfloat16),
        input_grad,
        new_params,
        new_params.astype(jnp.bfloat16),
        new_first,
        new_second,
    )


BF16 = jnp.bfloat16
F32 = jnp.float32
BOTH = ("img", "row")
TILE = 16
WINDOW = 304
LEN = 2 * WIN * WIN
QUADS = HEADS // 4
SPAN = 4 * WIN * WIN


def swap(block, mask, only=None):
    count = lax.axis_size(BOTH)
    route = [(d, d ^ mask) for d in range(count) if only is None or only(d)]
    return lax.ppermute(block, BOTH, route)


def params_call(mebibytes):
    return pltpu.CompilerParams(vmem_limit_bytes=mebibytes << 20)


def vmem(count):
    return [pl.BlockSpec(memory_space=pltpu.VMEM)] * count


SMEM_SPEC = pl.BlockSpec(memory_space=pltpu.SMEM)
ANY_SPEC = pl.BlockSpec(memory_space=pl.ANY)


def first_tile(device):
    return (289 * device) // TILE


def prep_body(me_ref, own_ref, out_ref, spare_ref, extra_ref, wide_ref):
    shift = me_ref[0] % TILE
    wide_ref[0:96] = jnp.zeros((96, 128), F32)
    wide_ref[1824:1920] = jnp.zeros((96, 128), F32)
    wide_ref[96:1830] = own_ref[...]
    for j in range(6):
        picked = wide_ref[pl.ds(96 - 6 * shift + j, WINDOW, stride=6), :]
        out_ref[:, 128 * j : 128 * (j + 1)] = picked.astype(BF16)
        spare_ref[:, 128 * j : 128 * (j + 1)] = picked.astype(BF16)
        extra_ref[:, 128 * j : 128 * (j + 1)] = picked.astype(BF16)


def window_of(me, own_flat):
    return pl.pallas_call(
        prep_body,
        out_shape=[jax.ShapeDtypeStruct((WINDOW, D), BF16)] * 3,
        in_specs=[SMEM_SPEC] + vmem(1),
        out_specs=vmem(3),
        scratch_shapes=[pltpu.VMEM((1920, 128), F32)],
        compiler_params=params_call(8),
        name="own_window",
    )(me, own_flat.reshape(-1, 128))


def mixer(groups, per):
    size = groups * per
    row = lax.broadcasted_iota(jnp.int32, (size, size), 0)
    col = lax.broadcasted_iota(jnp.int32, (size, size), 1)
    return (col == groups * (row % per) + row // per).astype(F32).astype(BF16)


def unmixer(groups, per):
    size = groups * per
    row = lax.broadcasted_iota(jnp.int32, (size, size), 0)
    col = lax.broadcasted_iota(jnp.int32, (size, size), 1)
    return (row == groups * (col % per) + col // per).astype(F32).astype(BF16)


def plane_rows(plane):
    low = first_tile(8 * plane) * TILE
    high = first_tile(8 * plane + 7) * TILE + WINDOW
    return low, high


def gate(value, *others):
    def body(*refs):
        pass

    return pl.pallas_call(
        body,
        out_shape=jax.ShapeDtypeStruct(value.shape, value.dtype),
        in_specs=[ANY_SPEC] * (1 + len(others)),
        out_specs=ANY_SPEC,
        input_output_aliases={0: 0},
        cost_estimate=cost(0),
        name="gate",
    )(value, *others)


def cross(block, zero, one):
    count = lax.axis_size(BOTH)
    return lax.ppermute(block, BOTH, [(d, d ^ (one if d & 2 else zero)) for d in range(count)])


def gather_windows(own, spare, extra, rows, *early):
    got = {0: own}
    first, second, third = {}, {}, {}

    def exchange(z):
        first[z] = cross(got[z], 4, 1)
        second[z] = cross(got[z], 1, 4)
        third[z] = cross(first[z], 1, 4)

    got[8] = swap(own, 8)
    first[0] = cross(own, 4, 1)
    second[0] = cross(own, 1, 4)
    spare = gate(spare, got[8])
    got[16] = swap(spare, 16)
    first[0] = gate(first[0], spare)
    third[0] = cross(first[0], 1, 4)
    got_rows = from_partner(rows, "row", 0)
    got[8] = gate(got[8], first[0], second[0])
    exchange(8)
    got[24] = swap(gate(extra, got[16]), 24)
    got[16] = gate(got[16], first[8], second[8], third[0], got_rows)
    exchange(16)
    got[24] = gate(got[24], first[16], second[16], third[8], *early)
    exchange(24)
    blocks, places = [], []
    for z in (0, 8, 16, 24):
        own_some = [got[z], first[z], second[z], third[z]]
        masks = ((z, z), (z | 4, z | 1), (z | 1, z | 4), (z | 5, z | 5))
        if z == 24:
            places.append((len(blocks), None, *masks[3]))
            places.append((len(blocks) + 1, None, masks[3][1] | 2, masks[3][0] | 2))
            last = own_some.pop()
            blocks += [last, swap(last, 2)]
        own_some = stacked(own_some)
        for n in range(own_some.shape[0]):
            zero, one = masks[n]
            places.append((len(blocks), n, zero, one))
            places.append((len(blocks) + 1, n, one | 2, zero | 2))
        blocks += [own_some, swap(own_some, 2)]
    return blocks, places, got_rows


def stacked_body(*refs):
    for i, ref in enumerate(refs[:-1]):
        refs[-1][i] = ref[...]


def stacked(blocks):
    return pl.pallas_call(
        stacked_body,
        out_shape=like(len(blocks), WINDOW, D),
        in_specs=vmem(len(blocks)),
        out_specs=vmem(1)[0],
        compiler_params=params_call(4),
        cost_estimate=cost(0),
        name="stacked",
    )(*blocks)


def load_windows(me, parts, places, first, last, flat_ref):
    base = first_tile(first) * TILE
    for device in (first, 16):
        if first <= device <= last:
            at = first_tile(device) * TILE - base
            flat_ref[at : at + TILE] = jnp.zeros((TILE, D), BF16)

    def each(act):
        for block, slot, zero, one in places:
            device = me ^ jnp.where((me & 2) == 0, zero, one)
            start = pl.multiple_of(first_tile(device) * TILE - base, TILE)
            part = parts[block] if slot is None else parts[block].at[slot]

            @pl.when((device >= first) & (device <= last))
            def _():
                act(part, start)

    def main(part, start):
        def step(i, carry):
            at = pl.multiple_of(48 * i + TILE, TILE)
            to = pl.multiple_of(start + at, TILE)
            flat_ref[pl.ds(to, 48)] = part[pl.ds(at, 48)]
            return carry

        lax.fori_loop(0, 6, step, 0)

    def edge(part, start):
        flat_ref[pl.ds(start, TILE)] += part[0:TILE]

    each(main)
    each(edge)


def load_small(me, parts, places, tail_ref):
    for block, slot, zero, one in places:
        part = parts[block] if slot is None else parts[block].at[slot]

        @pl.when(me ^ jnp.where((me & 2) == 0, zero, one) == 31)
        def _():
            tail_ref[...] = part[WINDOW - 32 : WINDOW]


def flat_scratch(first, last):
    return pltpu.VMEM(
        (first_tile(last) * TILE + WINDOW - first_tile(first) * TILE, D), BF16
    )


def unmix_rows(flat_ref, out_ref, base, groups, per, steps):
    mix = mixer(groups, per)
    size = groups * per
    for t in range(steps):
        rows = flat_ref[base + size * t : base + size * (t + 1)]
        out = jnp.dot(mix, rows, preferred_element_type=F32).astype(BF16)
        for j in range(groups):
            out_ref[j, per * t : per * (t + 1)] = out[per * j : per * (j + 1)]


def mix_rows(in_ref, flat_ref, base, groups, per, steps):
    mix = unmixer(groups, per)
    size = groups * per
    for t in range(steps):
        rows = jnp.concatenate([in_ref[j, per * t : per * (t + 1)] for j in range(groups)], 0)
        out = jnp.dot(mix, rows, preferred_element_type=F32).astype(BF16)
        flat_ref[base + size * t : base + size * (t + 1)] = out


def cut_windows(me, plane, flat_ref, base, keeps, sends):
    for flip in (2, 0):
        for s in range(4):
            first = jnp.where(((me ^ flip) & 2) == 0, 4, 1)
            away = (first if s & 2 else 0) + (5 - first if s & 1 else 0)
            device = 8 * plane + ((me & 7) ^ (away | flip))
            start = pl.multiple_of(first_tile(device) * TILE - base, TILE)
            window = flat_ref[pl.ds(start, WINDOW)]
            (sends if flip else keeps)[s // 2][s % 2] = window


def cost(microseconds):
    return pl.CostEstimate(
        flops=int(1e9 * microseconds),
        bytes_accessed=int(3.2e6 * microseconds),
        transcendentals=0,
    )


WINDOWS = [jax.ShapeDtypeStruct((2, WINDOW, D), BF16)] * 4


def like(*shape, dtype=BF16):
    return jax.ShapeDtypeStruct(shape, dtype)


def call(body, name, ins, outs, scratch, limit, ties=(), us=0, far=0):
    n_in, n_tie, n_out = len(ins), len(ties), len(outs)
    first_out = n_in + n_tie

    def wrapped(*refs):
        body(*refs[:n_in], *refs[first_out : first_out + n_out], *refs[first_out + n_out + 1 :])
        token_ref = refs[first_out + n_out]
        token_ref[...] = jnp.zeros_like(token_ref)

    specs = [SMEM_SPEC if one.dtype == jnp.int32 else vmem(1)[0] for one in ins]
    return pl.pallas_call(
        wrapped,
        out_shape=[*outs, like(8, 128, dtype=F32)],
        in_specs=specs + vmem(n_tie),
        out_specs=vmem(n_out - far)
        + [pl.BlockSpec(memory_space=pltpu.HBM)] * far
        + vmem(1),
        scratch_shapes=scratch,
        compiler_params=params_call(limit),
        cost_estimate=cost(us),
        name=name,
    )(*ins, *ties)


def pause(*ties, us=4):
    return call(lambda: None, "pause", [], [], [], 4, ties, us)[0]


def normal_parts(values):
    centre = jnp.mean(values, -1, keepdims=True)
    centred = values - centre
    spread = jnp.mean(centred * centred, -1, keepdims=True)
    scale = lax.rsqrt(spread + EPSILON)
    return centred * scale, scale


def normal_pull(n, scale, grad, gain):
    e = grad * gain
    return scale * (
        e - jnp.mean(e, -1, keepdims=True) - n * jnp.mean(e * n, -1, keepdims=True)
    )


def over_heads(block):
    head = lax.broadcasted_iota(jnp.int32, block.shape, 1) // HEAD_DIM
    return jnp.concatenate([jnp.where(head == h, block, jnp.zeros_like(block)) for h in range(4)], 0)


def own_columns(block):
    head = lax.broadcasted_iota(jnp.int32, (144, 128), 1) // HEAD_DIM
    out = block[0:144]
    for h in range(1, 4):
        out = jnp.where(head == h, block[144 * h : 144 * (h + 1)], out)
    return out


def contract(one, two, a, b):
    return lax.dot_general(one, two, (((a,), (b,)), ((), ())), preferred_element_type=F32)


def lay(out_ref, near, far):
    for i in range(WIN):
        ref, k = (near, 24 * i) if i < SHIFT else (far, 24 * (i - SHIFT))
        out_ref[12 * i : 12 * i + 12] = ref[k + 6 : k + 18]
        out_ref[144 + 12 * i : 150 + 12 * i] = ref[k + 18 : k + 24]
        out_ref[150 + 12 * i : 156 + 12 * i] = ref[k : k + 6]


def unlay(ref, near, far):
    for i in range(WIN):
        out_ref, k = (near, 24 * i) if i < SHIFT else (far, 24 * (i - SHIFT))
        out_ref[k + 6 : k + 18] = ref[12 * i : 12 * i + 12]
        out_ref[k + 18 : k + 24] = ref[144 + 12 * i : 150 + 12 * i]
        out_ref[k : k + 6] = ref[150 + 12 * i : 156 + 12 * i]


HALF = LEN // 2
LAY_SCRATCH = [pltpu.VMEM((LEN, D), F32), pltpu.VMEM((HALF, D), F32), pltpu.VMEM((HALF, D), F32)]


def unpack_small(tail_ref, vecs_ref, strips_ref, wide_ref, shift_ref):
    tail = tail_ref[...].astype(F32)
    rolled = pltpu.roll(tail, 360, 1)
    below = pltpu.roll(rolled, 31, 0)
    lane = lax.broadcasted_iota(jnp.int32, (16, D), 1)
    vecs_ref[...] = jnp.where(lane < 360, rolled[16:32], below[16:32])
    cell = lax.broadcasted_iota(jnp.int32, (32, D), 1) // HEADS
    which = lax.broadcasted_iota(jnp.int32, (32, D), 0)
    for r in range(17):
        row = jnp.broadcast_to(tail[r : r + 1], (32, D))
        wide_ref[32 * r : 32 * (r + 1)] = jnp.where(cell == which, row, 0.0).astype(BF16)
    lane = lax.broadcasted_iota(jnp.int32, (D, 128), 0)
    head = lax.broadcasted_iota(jnp.int32, (D, 128), 1)
    pick = (lane % HEADS == head).astype(F32).astype(BF16)
    table = jnp.dot(wide_ref[0:544], pick, preferred_element_type=F32)
    row = lax.broadcasted_iota(jnp.int32, table.shape, 0)
    table = jnp.where(row < TABLE_ROWS, table, 0.0)
    table = jnp.concatenate([table, jnp.zeros((96, 128), F32)], 0).T[0:HEADS]
    for j in range(WIN):
        moved = pltpu.roll(table, 629 + j, 1) if j < 11 else table
        shift_ref[24 * j : 24 * (j + 1), 0:640] = moved
    strips = contract(shift_ref[:, 0:640].astype(BF16), table_spread(), 1, 1)
    for j in range(WIN):
        strips_ref[:, j, :] = strips[24 * j : 24 * (j + 1)]


def table_spread():
    m = lax.broadcasted_iota(jnp.int32, (384, 640), 0)
    n = lax.broadcasted_iota(jnp.int32, (384, 640), 1)
    return ((n == 23 * (m // WIN) + m % WIN) & (m < 276)).astype(F32).astype(BF16)


def attend_body(places, me_ref, tokens_ref, rows_ref, mask_ref, *refs):
    parts = refs[:10]
    windows_ref, packed_ref, attn_ref, probs_ref, near_ref, far_ref, proj_ref, vecs_ref, qkv_out, laid_out = refs[10:20]
    flat_ref, wide_ref, one_ref, two_ref, bias_ref, qkv_ref, laid_ref, sems, tail_ref, strips_ref = refs[20:]
    load_small(me_ref[0], parts, places, tail_ref)
    unpack_small(tail_ref, vecs_ref, strips_ref, flat_ref, wide_ref)
    load_windows(me_ref[0], parts, places, 0, 10, flat_ref)
    one_ref[...] = tokens_ref[HALF:LEN].astype(F32)
    two_ref[...] = rows_ref[...].astype(F32)
    lay(wide_ref, one_ref, two_ref)
    laid = wide_ref[...]
    laid_ref[...] = laid.astype(BF16)
    n, _ = normal_parts(laid)
    windows_ref[...] = (n * vecs_ref[9:10] + vecs_ref[10:11]).astype(BF16)
    unmix_rows(flat_ref, qkv_ref, 0, 3, 64, 12)
    copies = [
        pltpu.make_async_copy(qkv_ref, qkv_out, sems.at[0]),
        pltpu.make_async_copy(laid_ref, laid_out, sems.at[1]),
    ]
    for copy in copies:
        copy.start()
    proj_ref[...] = flat_ref[2304:3072]

    def project(j, carry):
        packed_ref[j] = (
            jnp.dot(windows_ref[...], qkv_ref[j], preferred_element_type=F32)
            + vecs_ref[pl.ds(j, 1)]
        ).astype(BF16)
        return carry

    lax.fori_loop(0, 3, project, 0)

    def quad(g, carry):
        lanes = pl.ds(pl.multiple_of(128 * g, 128), 128)
        for h in range(4):
            for i in range(WIN):
                low = 12 * (11 - i)
                bias_ref[12 * i : 12 * i + 12, 144 * h : 144 * (h + 1)] = strips_ref[
                    4 * g + h, 0:12, low : low + 144
                ]
        for w in range(2):
            rows = pl.ds(144 * w, 144)
            queries = over_heads(packed_ref[0, rows, lanes])
            scores = contract(packed_ref[1, rows, lanes], queries, 1, 1)
            scores = scores * HEAD_DIM ** (-0.5) + bias_ref[...] + mask_ref[w]
            top = jnp.max(scores, 0, keepdims=True)
            exponent = jnp.exp(scores - top)
            total = jnp.sum(exponent, 0, keepdims=True)
            probs = (exponent * (1.0 / total)).astype(BF16)
            probs_ref[2 * g + w] = probs
            mixed = contract(probs, packed_ref[2, rows, lanes], 0, 0)
            attn_ref[rows, lanes] = own_columns(mixed).astype(BF16)
        return carry

    lax.fori_loop(0, QUADS, quad, 0, unroll=2)
    wide_ref[...] = (
        jnp.dot(attn_ref[...], proj_ref[...], preferred_element_type=F32) + vecs_ref[3:4]
    )
    unlay(wide_ref, one_ref, two_ref)
    near_ref[...] = one_ref[...].astype(BF16)
    far_ref[...] = two_ref[...].astype(BF16)
    for copy in copies:
        copy.wait()


def attend(me, tokens, rows, mask, parts, places):
    return call(
        functools.partial(attend_body, places),
        "attention_forward",
        [me, tokens, rows, mask, *parts],
        [
            like(LEN, D),
            like(3, LEN, D),
            like(LEN, D),
            like(2 * QUADS, 144, SPAN),
            like(HALF, D),
            like(HALF, D),
            like(D, D),
            like(16, D, dtype=F32),
            like(3, D, D),
            like(LEN, D),
        ],
        [flat_scratch(0, 10)]
        + LAY_SCRATCH
        + [
            pltpu.VMEM((144, SPAN), F32),
            pltpu.VMEM((3, D, D), BF16),
            pltpu.VMEM((LEN, D), BF16),
            pltpu.SemaphoreType.DMA((2,)),
            pltpu.VMEM((32, D), BF16),
            pltpu.VMEM((HEADS, WIN, 384), F32),
        ],
        22,
        far=2,
    )


def middle_of(tokens_ref, back_ref, near_ref):
    branch = jnp.concatenate([back_ref[...].astype(F32), near_ref[...].astype(F32)], 0)
    return tokens_ref[...].astype(F32) + branch


def feed_weights_body(places, me_ref, *refs):
    parts = refs[:10]
    up_ref, down_ref, flat_ref = refs[10:]
    load_windows(me_ref[0], parts, places, 10, 31, flat_ref)
    base = first_tile(10) * TILE
    unmix_rows(flat_ref, up_ref, 3072 - base, 4, 48, 16)

    def step(i, carry):
        at = pl.multiple_of(64 * i, 64)
        down_ref[pl.ds(at, 64)] = flat_ref[pl.ds(pl.multiple_of(6144 - base + at, TILE), 64)]
        return carry

    lax.fori_loop(0, 48, step, 0)


def feed_weights(me, parts, places, *ties):
    return call(
        functools.partial(feed_weights_body, places),
        "feed_weights",
        [me, *parts],
        [like(4, D, D), like(FF, D)],
        [flat_scratch(10, 31)],
        20,
        ties,
    )


def feed_body(me_ref, valid_ref, tokens_ref, back_ref, near_ref, cotangent_ref, vecs_ref, up_ref, down_ref, hidden_ref, active_ref, gradup_ref, sums_ref, low_ref, low_keep, high_keep, low_send, high_send, grad_ref):
    me = me_ref[0]
    n, _ = normal_parts(middle_of(tokens_ref, back_ref, near_ref))
    hidden_ref[...] = (n * vecs_ref[11:12] + vecs_ref[12:13]).astype(BF16)
    grad_out = cotangent_ref[...] * valid_ref[0].astype(F32).astype(BF16)
    grad_ref[3072:3104] = jnp.zeros((32, D), BF16)

    def step(j, carry):
        at = pl.multiple_of(D * j, D)
        down = down_ref[pl.ds(at, D)]
        upward = jnp.dot(hidden_ref[...], up_ref[j], preferred_element_type=F32)
        upward = upward + vecs_ref[pl.ds(4 + j, 1)]
        grad_active = contract(grad_out, down, 1, 1)
        share = 0.5 * (1.0 + lax.erf(upward * (0.5**0.5)))
        density = jnp.exp(-0.5 * upward * upward) * ((2.0 * math.pi) ** (-0.5))
        active = (upward * share).astype(BF16)
        grad_up = (grad_active * (share + upward * density)).astype(BF16)
        active_ref[j] = active
        gradup_ref[j] = grad_up
        sums_ref[pl.ds(j, 1)] = jnp.sum(grad_up.astype(F32), 0, keepdims=True)
        grad_ref[pl.ds(at, D)] = contract(active, grad_out, 0, 0).astype(BF16)
        return carry

    lax.fori_loop(0, 4, step, 0)
    cut_windows(me, 3, grad_ref, 6144, (low_keep, high_keep), (low_send, high_send))
    low_ref[...] = grad_ref[0:800]
    sums_ref[4:5] = jnp.sum(grad_out.astype(F32), 0, keepdims=True)


def feed(me, valid, tokens, back, near, cotangent, vecs, w_up, w_down):
    return call(
        feed_body,
        "feed_forward",
        [me, valid, tokens, back, near, cotangent, vecs, w_up, w_down],
        [
            like(LEN, D),
            like(4, LEN, D),
            like(4, LEN, D),
            like(8, D, dtype=F32),
            like(800, D),
            *WINDOWS,
        ],
        [pltpu.VMEM((3104, D), BF16)],
        16,
    )


def middle_body(me_ref, valid_ref, tokens_ref, back_ref, near_ref, cotangent_ref, vecs_ref, gradup_ref, up_ref, grad_ref, far_out, near_out, sums_ref):
    n, scale = normal_parts(middle_of(tokens_ref, back_ref, near_ref))
    grad_hidden = contract(gradup_ref[0], up_ref[0], 1, 1)
    for j in range(1, 4):
        grad_hidden = grad_hidden + contract(gradup_ref[j], up_ref[j], 1, 1)
    sums_ref[0:1] = jnp.sum(grad_hidden * n, 0, keepdims=True)
    sums_ref[1:2] = jnp.sum(grad_hidden, 0, keepdims=True)
    grad_out = (cotangent_ref[...] * valid_ref[0].astype(F32).astype(BF16)).astype(F32)
    grad = grad_out + normal_pull(n, scale, grad_hidden, vecs_ref[11:12])
    grad_ref[...] = grad
    far_out[...] = grad[:HALF].astype(BF16)
    near_out[...] = grad[HALF:].astype(BF16)


def middle_grad(me, valid, tokens, back, near, cotangent, vecs, grad_up, w_up):
    return call(
        middle_body,
        "middle_grad",
        [me, valid, tokens, back, near, cotangent, vecs, grad_up, w_up],
        [like(LEN, D, dtype=F32), like(HALF, D), like(HALF, D), like(8, D, dtype=F32)],
        [],
        12,
    )


def up_body(me_ref, hidden_ref, gradup_ref, low_ref, proj_ref, low_keep, high_keep, low_send, high_send, quad_ref, flat_ref):
    me = me_ref[0]

    def step(j, carry):
        quad_ref[j] = contract(hidden_ref[...], gradup_ref[j], 0, 0).astype(BF16)
        return carry

    lax.fori_loop(0, 4, step, 0)
    flat_ref[3072:3872] = low_ref[...]
    mix_rows(quad_ref, flat_ref, 0, 4, 48, 16)
    cut_windows(me, 2, flat_ref, 3072, (low_keep, high_keep), (low_send, high_send))
    proj_ref[...] = flat_ref[0:1552]


def up_grad(me, hidden, grad_up, low, *ties):
    return call(
        up_body,
        "up_grad",
        [me, hidden, grad_up, low],
        [like(1552, D), *WINDOWS],
        [pltpu.VMEM((4, D, D), BF16), pltpu.VMEM((3872, D), BF16)],
        16,
        ties,
    )


def proj_body(me_ref, near_ref, far_ref, attn_ref, proj_ref, high_ref, back_ref, sums_ref, edge_ref, low_keep, high_keep, low_send, high_send, flat_ref, wide_ref, one_ref, two_ref):
    me = me_ref[0]
    one_ref[...] = near_ref[...].astype(F32)
    two_ref[...] = far_ref[...].astype(F32)
    lay(wide_ref, one_ref, two_ref)
    grad = wide_ref[...].astype(BF16)
    flat_ref[0:768] = contract(attn_ref[...], grad, 0, 0).astype(BF16)
    flat_ref[768:2320] = high_ref[...]
    cut_windows(me, 1, flat_ref, 2304, (low_keep, high_keep), (low_send, high_send))
    edge_ref[...] = flat_ref[0:16]
    back_ref[...] = contract(grad, proj_ref[...], 1, 1).astype(BF16)
    sums_ref[0:1] = jnp.sum(grad.astype(F32), 0, keepdims=True)


def proj_grad(me, near, far, attn, w_proj, high, *ties):
    return call(
        proj_body,
        "proj_grad",
        [me, near, far, attn, w_proj, high],
        [like(LEN, D), like(8, D, dtype=F32), like(16, D), *WINDOWS],
        [pltpu.VMEM((2320, D), BF16)] + LAY_SCRATCH,
        12,
        ties,
    )


def unattend_quads(quads, packed_ref, grad_ref, attn_ref, probs_ref, back_ref, strips_ref, pairs_ref):
    strips_ref[...] = jnp.zeros_like(strips_ref)

    def quad(g, carry):
        lanes = pl.ds(pl.multiple_of(128 * g, 128), 128)
        for w in range(2):
            rows = pl.ds(144 * w, 144)
            queries = over_heads(packed_ref[0, rows, lanes])
            keys = packed_ref[1, rows, lanes]
            values = packed_ref[2, rows, lanes]
            grad = grad_ref[rows, lanes]
            product = -(attn_ref[rows, lanes].astype(F32) * grad.astype(F32)).astype(BF16)
            grads = over_heads(grad)
            left = jnp.concatenate([values, jnp.ones_like(values)], 1)
            right = jnp.concatenate([grads, over_heads(product)], 1)
            probs = probs_ref[2 * g + w]
            grad_scores = probs.astype(F32) * contract(left, right, 1, 1)
            if w == 0:
                pairs_ref[...] = grad_scores
            else:
                pairs_ref[...] += grad_scores
            raw = (grad_scores * HEAD_DIM ** (-0.5)).astype(BF16)
            back_ref[0, rows, lanes] = own_columns(contract(raw, keys, 0, 0)).astype(BF16)
            back_ref[1, rows, lanes] = jnp.dot(
                raw, queries, preferred_element_type=F32
            ).astype(BF16)
            back_ref[2, rows, lanes] = jnp.dot(
                probs, grads, preferred_element_type=F32
            ).astype(BF16)
        for h in range(4):
            for i in range(WIN):
                low = 12 * (11 - i)
                strips_ref[4 * (g - quads[0]) + h, 0:12, low : low + 144] += pairs_ref[
                    12 * i : 12 * i + 12, 144 * h : 144 * (h + 1)
                ]
        return carry

    lax.fori_loop(*quads, quad, 0)


def unattend_body(me_ref, packed_ref, grad_ref, attn_ref, probs_ref, back_ref, strips_ref, sums_ref, pairs_ref):
    unattend_quads((0, QUADS), packed_ref, grad_ref, attn_ref, probs_ref, back_ref, strips_ref, pairs_ref)
    for j in range(3):
        sums_ref[j : j + 1] = jnp.sum(back_ref[j].astype(F32), 0, keepdims=True)


def qkv_body(me_ref, windows_ref, edge_ref, back_ref, low_keep, high_keep, low_send, high_send, trio_ref, flat_ref):
    me = me_ref[0]

    def step(j, carry):
        trio_ref[j] = contract(windows_ref[...], back_ref[j], 0, 0).astype(BF16)
        return carry

    lax.fori_loop(0, 3, step, 0)
    mix_rows(trio_ref, flat_ref, 0, 3, 64, 12)
    flat_ref[2304:2320] = edge_ref[...]
    cut_windows(me, 0, flat_ref, 0, (low_keep, high_keep), (low_send, high_send))


def unattend(me, packed, grad, attn, probs, *ties):
    return call(
        unattend_body,
        "attention_backward",
        [me, packed, grad, attn, probs],
        [like(3, LEN, D), like(HEADS, WIN, 384, dtype=F32), like(8, D, dtype=F32)],
        [pltpu.VMEM((144, SPAN), F32)],
        10,
        ties,
    )


def qkv_grad(me, windows, edge, back, *ties):
    return call(
        qkv_body,
        "qkv_grad",
        [me, windows, edge, back],
        [*WINDOWS],
        [pltpu.VMEM((3, D, D), BF16), pltpu.VMEM((2320, D), BF16)],
        12,
        ties,
    )


def token_body(me_ref, back_ref, qkv_ref, laid_ref, vecs_ref, near_out, far_out, sums_ref, wide_ref, one_ref, two_ref):
    grad = contract(back_ref[0], qkv_ref[0], 1, 1)
    for j in (1, 2):
        grad = grad + contract(back_ref[j], qkv_ref[j], 1, 1)
    n, scale = normal_parts(laid_ref[...].astype(F32))
    sums_ref[0:1] = jnp.sum(grad * n, 0, keepdims=True)
    sums_ref[1:2] = jnp.sum(grad, 0, keepdims=True)
    wide_ref[...] = normal_pull(n, scale, grad, vecs_ref[9:10])
    unlay(wide_ref, one_ref, two_ref)
    near_out[...] = one_ref[...].astype(BF16)
    far_out[...] = two_ref[...].astype(BF16)


def token_grad(me, back, w_qkv, laid, vecs, *ties):
    return call(
        token_body,
        "token_grad",
        [me, back, w_qkv, laid, vecs],
        [like(HALF, D), like(HALF, D), like(8, D, dtype=F32)],
        LAY_SCRATCH,
        10,
        ties,
    )


def output_body(me_ref, tokens_ref, back_ref, near_ref, vecs_ref, active_ref, down_ref, out_ref):
    total = middle_of(tokens_ref, back_ref, near_ref) + vecs_ref[8:9]
    for j in range(4):
        total = total + jnp.dot(
            active_ref[j], down_ref[D * j : D * (j + 1)], preferred_element_type=F32
        )
    out_ref[...] = total.astype(BF16)


def block_output(me, tokens, back, near, vecs, active, w_down, *ties):
    return call(
        output_body,
        "block_output",
        [me, tokens, back, near, vecs, active, w_down],
        [like(LEN, D)],
        [],
        10,
        ties,
    )


def sum_body(slots, lows, *refs):
    for i in range(slots):
        total = refs[0][lows[0] + i].astype(F32)
        for ref, low in zip(refs[1 : len(lows)], lows[1:]):
            total = total + ref[low + i].astype(F32)
        refs[-1][i] = total.astype(BF16)


def sum_slots(slots, terms, *ties):
    return call(
        functools.partial(sum_body, slots, [low for _, low in terms]),
        "sum_slots",
        [one for one, _ in terms],
        [like(slots, WINDOW, D)],
        [],
        6,
        ties,
    )


def split_body(low_ref, x_ref, sent_ref, kept_ref):
    for slot, ref in ((1, sent_ref), (0, kept_ref)):
        ref[...] = (low_ref[slot].astype(F32) + x_ref[slot].astype(F32)).astype(BF16)


def split_sum(low, x, *ties):
    return call(
        split_body, "split_sum", [low, x], [like(WINDOW, D), like(WINDOW, D)], [], 6, ties
    )


def arranged_body(me_ref, high_ref, low_ref, own_ref, other_ref):
    odd = (me_ref[0] // 8) % 2 == 1

    @pl.when(odd)
    def _():
        own_ref[...] = high_ref[...]
        other_ref[...] = low_ref[...]

    @pl.when(jnp.logical_not(odd))
    def _():
        own_ref[...] = low_ref[...]
        other_ref[...] = high_ref[...]


def arranged(me, high, low, *ties):
    return call(
        arranged_body,
        "arranged",
        [me, high, low],
        [like(WINDOW, D), like(WINDOW, D)],
        [],
        6,
        ties,
    )


def with_small_body(me_ref, own_ref, rows_ref, other_ref, out_ref):
    me = me_ref[0]
    out_ref[...] = own_ref[...]

    @pl.when((me % 8 == 7) & ((me // 8) % 2 == 1))
    def _():
        last = own_ref[WINDOW - 32 : WINDOW].astype(F32)
        out_ref[WINDOW - 32 : WINDOW] = (last + (rows_ref[...] + other_ref[...])).astype(BF16)


def with_small(me, own, rows, other, *ties):
    return call(
        with_small_body, "with_small", [me, own, rows, other], [like(WINDOW, D)], [], 6, ties
    )


def sum_two(one, two, *ties):
    def body(one_ref, two_ref, out_ref):
        out_ref[...] = (one_ref[...].astype(F32) + two_ref[...].astype(F32)).astype(BF16)

    return call(body, "sum_two", [one, two], [like(WINDOW, D)], [], 6, ties)


def to_half(block, upper):
    return swap(block, 16, lambda d: (d // 16 == 1) != upper)


def small_body(strips_ref, qkv_ref, proj_ref, up_ref, one_ref, two_ref, out_ref, rows_ref):
    out_ref[...] = jnp.zeros_like(out_ref)
    out_ref[0:3] = qkv_ref[0:3]
    out_ref[3:4] = proj_ref[0:1]
    out_ref[4:9] = up_ref[0:5]
    out_ref[9:11] = one_ref[0:2]
    out_ref[11:13] = two_ref[0:2]
    for j in range(WIN):
        rows_ref[24 * j : 24 * (j + 1)] = strips_ref[:, j, :]
    rows = rows_ref[...]
    high = rows.astype(BF16)
    low = (rows - high.astype(F32)).astype(BF16)
    spread = table_spread()
    wide = jnp.dot(high, spread, preferred_element_type=F32) + jnp.dot(
        low, spread, preferred_element_type=F32
    )
    total = wide[264:288]
    for j in range(WIN - 1):
        total = total + pltpu.roll(wide[24 * j : 24 * (j + 1)], 11 - j, 1)
    out_ref[16:40, 0:640] = total


def small_grads(strips, qkv, proj, up, one, two, *ties):
    return call(
        small_body,
        "small_grads",
        [strips, qkv, proj, up, one, two],
        [like(40, D, dtype=F32)],
        [pltpu.VMEM((288, 384), F32)],
        8,
        ties,
    )


def lines_body(small_ref, out_ref, table_ref, vec_ref, line_ref):
    table = jnp.concatenate([small_ref[16:40, 0:640], jnp.zeros((104, 640), F32)], 0)
    table_ref[...] = table.T
    wide = jnp.zeros((40, 384), F32)
    for q in range(16):
        rows = table_ref[pl.ds(q, 40, stride=16), :]
        padded = jnp.concatenate([rows, jnp.zeros((40, 256), F32)], 1)
        wide = wide + (pltpu.roll(padded, 24 * q, 1) if q else padded)
    line_ref[...] = jnp.zeros_like(line_ref)
    for c in range(3):
        line_ref[pl.ds(c, 40, stride=3), :] = wide[:, 128 * c : 128 * (c + 1)]
    for c in range(6):
        vec_ref[pl.ds(c, 16, stride=6), :] = small_ref[0:16, 128 * c : 128 * (c + 1)]
    rolled = pltpu.roll(vec_ref[...], 24, 1)
    lane = lax.broadcasted_iota(jnp.int32, rolled.shape, 1)
    line_ref[99:195] += jnp.where(lane >= 24, rolled, 0.0)
    line_ref[100:196] += jnp.where(lane < 24, rolled, 0.0)
    for c in range(6):
        out_ref[:, 128 * c : 128 * (c + 1)] = line_ref[pl.ds(c, 32, stride=6), :]


def small_sum(one, two, *ties):
    def body(one_ref, two_ref, out_ref):
        out_ref[...] = one_ref[...] + two_ref[...]

    return call(body, "small_sum", [one, two], [like(40, D, dtype=F32)], [], 4, ties)


def small_lines(small, *ties):
    return call(
        lines_body,
        "small_lines",
        [small],
        [like(32, D, dtype=F32)],
        [pltpu.VMEM((640, 128), F32), pltpu.VMEM((96, 128), F32), pltpu.VMEM((200, 128), F32)],
        8,
        ties,
    )


CUTS = (0, 576, 1152, 1734)


def adam_body(me_ref, *refs):
    terms = refs[:4]
    params_ref, first_ref, second_ref = refs[4:7]
    outs = refs[7:11]
    flat_ref, copy_ref, sems, out_sems, params_out, low_out, first_out, second_out = refs[11:]
    me = me_ref[0]
    shift = me % TILE
    for which, own_terms in enumerate((terms[0:2], terms[2:3], terms[3:4])):

        @pl.when(jnp.minimum(me // 8, 2) == which)
        def _():
            copies = [
                pltpu.make_async_copy(term, copy_ref.at[z], sems.at[z])
                for z, term in enumerate(own_terms)
            ]
            if len(own_terms) == 1:
                copy_ref[1] = jnp.zeros((WINDOW, D), BF16)
            for copy in copies:
                copy.start()
            for copy in copies:
                copy.wait()

    for j in range(6):
        terms_j = [copy_ref[z, :, 128 * j : 128 * (j + 1)].astype(F32) for z in range(2)]
        flat_ref[pl.ds(j, WINDOW, stride=6), :] = terms_j[0] + terms_j[1]
    copies = []
    for n, (low, high) in enumerate(zip(CUTS[:-1], CUTS[1:])):
        grad = flat_ref[pl.ds(6 * shift + low, high - low), :]
        line = me * 1734 + low + lax.broadcasted_iota(jnp.int32, grad.shape, 0)
        rate = jnp.full(grad.shape, D ** (-0.5), F32)
        rate = jnp.where((line >= 13824) & (line < 18432), 4.0 * D ** (-0.5), rate)
        rate = jnp.where(line >= 36864, FF ** (-0.5), rate)
        if n == len(CUTS) - 2:
            lane = lax.broadcasted_iota(jnp.int32, (192, 128), 1)
            fine = step_rates(line[-192:] * 128 + lane)
            rate = jnp.concatenate([rate[:-192], fine], 0)
        params = params_ref[low:high]
        new_first = BETA_ONE * first_ref[low:high] + (1.0 - BETA_ONE) * grad
        new_second = BETA_TWO * second_ref[low:high] + (1.0 - BETA_TWO) * grad * grad
        fixed_first = new_first / (1.0 - BETA_ONE**STEP)
        fixed_second = new_second / (1.0 - BETA_TWO**STEP)
        new_params = params - rate * (
            fixed_first / (jnp.sqrt(fixed_second) + ADAM_EPS) + DECAY * params
        )
        params_out[low:high] = new_params
        low_out[low:high] = new_params.astype(BF16)
        first_out[low:high] = new_first
        second_out[low:high] = new_second
        for k, one in enumerate((params_out, low_out, first_out, second_out)):
            copies.append(
                pltpu.make_async_copy(
                    one.at[pl.ds(low, high - low)],
                    outs[k].at[pl.ds(low, high - low)],
                    out_sems.at[n, k],
                )
            )
            copies[-1].start()
    for copy in copies:
        copy.wait()


def adam(me, terms, params, first_moment, second_moment):
    lines = (1734, 128)
    args = [one.reshape(lines) for one in (params, first_moment, second_moment)]
    outs = pl.pallas_call(
        adam_body,
        out_shape=[
            jax.ShapeDtypeStruct(lines, F32),
            jax.ShapeDtypeStruct(lines, BF16),
            jax.ShapeDtypeStruct(lines, F32),
            jax.ShapeDtypeStruct(lines, F32),
        ],
        in_specs=[SMEM_SPEC] + [ANY_SPEC] * 4 + vmem(3),
        out_specs=[ANY_SPEC] * 4,
        scratch_shapes=[
            pltpu.VMEM((6 * WINDOW, 128), F32),
            pltpu.VMEM((2, WINDOW, D), BF16),
            pltpu.SemaphoreType.DMA((2,)),
            pltpu.SemaphoreType.DMA((3, 4)),
            pltpu.VMEM(lines, F32),
            pltpu.VMEM(lines, BF16),
            pltpu.VMEM(lines, F32),
            pltpu.VMEM(lines, F32),
        ],
        compiler_params=params_call(16),
        name="adam",
    )(me, *terms, *args)
    return [one.reshape(-1) for one in outs]


def shards(tokens, cotangent, valid, params, first_moment, second_moment):
    if lax.axis_size("img") != 16 or lax.axis_size("row") != 2:
        return shards_general(tokens, cotangent, valid, params, first_moment, second_moment)
    me = lax.axis_index(BOTH).astype(jnp.int32).reshape(1)
    flat_tokens = tokens.reshape(LEN, D)
    flat_cotangent = cotangent.reshape(LEN, D)
    own, spare, extra = window_of(me, params)
    mask = jnp.tile(window_mask(lax.axis_index("row") * WIN), (1, 1, 4))
    parts, places, rows = gather_windows(own, spare, extra, flat_tokens[:HALF], mask)
    windows, packed, attn, probs, near, far, w_proj, vecs, w_qkv, laid, token = attend(
        me, flat_tokens, rows, mask, parts, places
    )
    back = from_partner(far, "row", 0)
    w_up, w_down, _ = feed_weights(me, parts, places, pause(token))
    hidden, active, grad_up, sums_up, low, low_three, high_three, low_send, high_send, token = feed(
        me, valid, flat_tokens, back, near, flat_cotangent, vecs, w_up, w_down
    )
    core_high_three, core_low_three = swap(high_send, 2), swap(low_send, 2)
    grad_middle, far_grad, near_grad, sums_two, token = middle_grad(
        me, valid, flat_tokens, back, near, flat_cotangent, vecs, grad_up, w_up
    )
    far_grad = from_partner(far_grad, "row", 0)
    sent, token = sum_slots(2, [(high_three, 0), (core_high_three, 0)], pause(token))
    x_three = cross(sent, 4, 1)
    low_three, token = sum_slots(2, [(low_three, 0), (core_low_three, 0)], token)
    high, low_two, high_two, low_send, high_send, token = up_grad(
        me, hidden, grad_up, low, pause(token)
    )
    core_high_two, core_low_two = swap(high_send, 2), swap(low_send, 2)
    sent, three, token = split_sum(low_three, x_three, token)
    y_three = cross(sent, 1, 4)
    sent, token = sum_slots(2, [(high_two, 0), (core_high_two, 0)], pause(token))
    x_two = cross(sent, 4, 1)
    low_two, token = sum_slots(2, [(low_two, 0), (core_low_two, 0)], token)
    grad_attn, sums_proj, edge, low_one, high_one, low_send, high_send, token = proj_grad(
        me, near_grad, far_grad, attn, w_proj, high, pause(token)
    )
    core_high_one, core_low_one = swap(high_send, 2), swap(low_send, 2)
    grad_packed, strips, sums_qkv, token = unattend(
        me, packed, grad_attn, attn, probs, pause(token)
    )
    sent, token = sum_slots(2, [(high_one, 0), (core_high_one, 0)], token)
    x_one = cross(sent, 4, 1)
    near_in, far_in, sums_one, token = token_grad(me, grad_packed, w_qkv, laid, vecs, token)
    small, token = small_grads(strips, sums_qkv, sums_proj, sums_up, sums_one, sums_two, token)
    three, token = sum_two(three, y_three, token)
    small, token = small_sum(small, swap(small, 2), token)
    sent, two, token = split_sum(low_two, x_two, token)
    y_two = cross(sent, 1, 4)
    low_one, token = sum_slots(2, [(low_one, 0), (core_low_one, 0)], token)
    low_zero, high_zero, low_send, high_send, token = qkv_grad(
        me, windows, edge, grad_packed, pause(token)
    )
    core_high_zero, core_low_zero = swap(high_send, 2), swap(low_send, 2)
    two, token = sum_two(two, y_two, token)
    small, token = small_sum(small, cross(small, 4, 1), token)
    upper, other, token = arranged(me, three, two, token)
    z_upper = swap(other, 8)
    sent, one, token = split_sum(low_one, x_one, token)
    y_one = cross(sent, 1, 4)
    sent, token = sum_slots(2, [(high_zero, 0), (core_high_zero, 0)], pause(token, us=12))
    x_zero = cross(sent, 4, 1)
    low_zero, token = sum_slots(2, [(low_zero, 0), (core_low_zero, 0)], token)
    upper, token = sum_two(upper, z_upper, token)
    one, token = sum_two(one, y_one, token)
    z_one = swap(one, 8, lambda d: d // 8 in (0, 2))
    sent, zero, token = split_sum(low_zero, x_zero, token)
    y_zero = cross(sent, 1, 4)
    small, token = small_sum(small, cross(small, 1, 4), token)
    rows, token = small_lines(small, token)
    z_rows = swap(rows, 8)
    one, token = sum_two(one, z_one, token)
    far_one = swap(one, 16, lambda d: d // 8 == 3)
    zero, token = sum_two(zero, y_zero, token)
    z_zero = swap(zero, 8, lambda d: d // 8 in (1, 3))
    upper, token = with_small(me, upper, rows, z_rows, token)
    far_upper = to_half(upper, True)
    zero, token = sum_two(zero, z_zero, token)
    far_zero = swap(zero, 16, lambda d: d // 8 == 2)
    upper, token = sum_two(upper, far_upper, token)
    one, token = sum_two(one, far_one, token)
    far_in = from_partner(gate(far_in, token), "row", 0)
    output, token = block_output(
        me, flat_tokens, back, near, vecs, active, w_down, token
    )
    input_grad = grad_middle + jnp.concatenate([far_in, near_in], 0).astype(F32)
    terms = [zero, far_zero, one, upper]
    new = adam(me, terms, params, first_moment, second_moment)
    return (output.reshape(tokens.shape), input_grad.reshape(tokens.shape), *new)


def solution(mesh):
    return jax.shard_map(
        shards,
        mesh=mesh,
        in_specs=(
            P("img", "row", None, None),
            P("img", "row", None, None),
            P("img"),
            P(("img", "row")),
            P(("img", "row")),
            P(("img", "row")),
        ),
        out_specs=(
            P("img", "row", None, None),
            P("img", "row", None, None),
            P(("img", "row")),
            P(("img", "row")),
            P(("img", "row")),
            P(("img", "row")),
        ),
        check_vma=False,
    )
```
